32 devices in a mesh: grp: 2 (over y), row: 4 (over z), inner: 4 (over x, core).
Axes of the slice: x: 2, y: 2, z: 4, core: 2. Of those that a mesh axis runs over, the one named last changes fastest.
Arguments:
- density: bfloat16 [128, 8, 128, 128], P(('grp', 'row', 'inner')), parts along dimension 0
- inverse_start: bfloat16 [128, 8, 128, 128], P(('grp', 'row', 'inner')), parts along dimension 0
- block_cols: int32 [128, 8], P(('grp', 'row', 'inner')), parts along dimension 0, may hold values from 0 to 63, as said below
Outputs:
- density_next: bfloat16 [128, 8, 128, 128], P(('grp', 'row', 'inner')), parts along dimension 0
- inverse_next: bfloat16 [128, 8, 128, 128], P(('grp', 'row', 'inner')), parts along dimension 0
The draws below stay inside these ranges and needn't reach their ends.
There are 2 independent parts, one for each index of `grp`. The reference program is written for one: setup_inputs(seed, part) draws one part's arguments, and reference() takes and returns one part's arrays. A program takes and returns all parts, laid end to end along the dimension named above; each array names one. Nothing has to cross between parts.
Inputs may be any that keep to these rules, and one draw needn't show every extreme that they name: `block_cols`: row i holds 8 distinct block-columns (i + d) mod 64 with d from -4 to 4, in increasing d; d = 0 is always among them.
All inputs are finite; a program needn't handle non-finite values.
Results may differ from the reference program's by a relative error of at most 0.0071.
Values may be sent and summed in bfloat16 or wider, within the bound.
No kernel may reach another device: no remote copies, remote signals or barrier semaphores. Data moves between devices by JAX's collectives and lax.ppermute only.
A program may use at most 64 MiB of HBM per device.

```python
import jax
import jax.numpy as jnp
from jax import lax

BS = 128
K = 8
SWEEPS = 2
HB = 4
NBR = 64


def band_columns(key):
    dropped = jax.random.randint(jax.random.fold_in(key, 7), (NBR, 1), 0, K)
    dropped = dropped + (dropped >= HB).astype(jnp.int32)
    slot_index = jnp.arange(K, dtype=jnp.int32)[None, :]
    positions = slot_index + (slot_index >= dropped).astype(jnp.int32)
    row_ids = jnp.arange(NBR, dtype=jnp.int32)[:, None]
    return jnp.mod(row_ids + positions - HB, NBR).astype(jnp.int32)


def levels(key):
    level_key = jax.random.fold_in(key, 17)
    magnitude = jax.random.uniform(jax.random.fold_in(level_key, 1), (NBR,), jnp.float32, 0.15, 0.4)
    flipped = jax.random.randint(jax.random.fold_in(level_key, 2), (NBR,), 0, 2)
    occupation = 0.5 + (2.0 * flipped.astype(jnp.float32) - 1.0) * magnitude
    gain_rows = jax.random.uniform(jax.random.fold_in(level_key, 3), (NBR,), jnp.float32, 0.2, 0.5)
    return (occupation, gain_rows)


def coefficient_blocks(columns, diagonal_level, coupling):
    row_ids = jnp.arange(NBR, dtype=jnp.int32)[:, None]
    marked = (columns == row_ids).astype(jnp.float32)
    coefficient = marked * diagonal_level[:, None] + (1.0 - marked) * coupling
    return coefficient[:, :, None, None] * jnp.eye(BS, dtype=jnp.float32)


def rough_part(key, full_shape):
    return jnp.clip(jax.random.normal(key, full_shape, jnp.float32), -4.0, 4.0)


def draw_block_cols(key, part):
    return band_columns(key)


def draw_density(key, part):
    columns = band_columns(key)
    occupation, gain_rows = levels(key)
    key = jax.random.fold_in(key, 11)
    coupling = jax.random.uniform(jax.random.fold_in(key, 1), (NBR, K), jnp.float32, -0.15, 0.15)
    full_shape = (NBR, K, BS, BS)
    spread = 0.2 / (K * BS) ** 0.5
    random_part = rough_part(jax.random.fold_in(key, 2), full_shape)
    return (spread * random_part + coefficient_blocks(columns, occupation, coupling)).astype(jnp.bfloat16)


def draw_inverse_start(key, part):
    columns = band_columns(key)
    occupation, gain_rows = levels(key)
    shifted_level = 2.0 * occupation * occupation - 2.0 * occupation + 1.0
    diagonal_level = gain_rows / shifted_level
    key = jax.random.fold_in(key, 13)
    coupling = diagonal_level[:, None] * jax.random.uniform(jax.random.fold_in(key, 1), (NBR, K), jnp.float32, -0.15, 0.15)
    full_shape = (NBR, K, BS, BS)
    spread = 0.3 / (K * BS) ** 0.5
    random_part = rough_part(jax.random.fold_in(key, 2), full_shape)
    return (spread * random_part + coefficient_blocks(columns, diagonal_level, coupling)).astype(jnp.bfloat16)


def setup_inputs(seed: int = 0, part: int = 0) -> dict:
    keys = jax.random.split(jax.random.key(seed), 4)
    part_keys = jax.random.split(jax.random.fold_in(keys[3], part), 4)
    return {
        "density": draw_density(jax.random.fold_in(jax.random.fold_in(keys[3], part), 71), part),
        "inverse_start": draw_inverse_start(jax.random.fold_in(jax.random.fold_in(keys[3], part), 71), part),
        "block_cols": draw_block_cols(jax.random.fold_in(jax.random.fold_in(keys[3], part), 71), part),
    }


def restricted(left_blocks, right_blocks, block_cols):
    def single_row(operands):
        block_row, column_row = operands
        neighbours = right_blocks[column_row].reshape(K * K, BS, BS)
        neighbour_cols = block_cols[column_row]
        matches = neighbour_cols[:, None, :] == column_row[None, :, None]
        present = jnp.any(matches, axis=2)
        column_slot = jnp.argmax(matches, axis=2).astype(jnp.int32)
        picked_index = jnp.arange(K, dtype=jnp.int32)[:, None] * K + column_slot
        selected = neighbours[picked_index]
        selected = jnp.where(present[:, :, None, None], selected, jnp.zeros((), selected.dtype))
        return jnp.einsum('tab,tsbc->sac', block_row.astype(jnp.float32), selected.astype(jnp.float32))
    return lax.map(single_row, (left_blocks, block_cols))


def reference(density, inverse_start, block_cols):
    row_ids = jnp.arange(NBR, dtype=jnp.int32)
    diagonal = (block_cols == row_ids[:, None]).astype(jnp.float32)[:, :, None, None] * jnp.eye(BS, dtype=jnp.float32)
    square_sum = restricted(density, density, block_cols)
    square = square_sum.astype(jnp.bfloat16)
    shifted = (2.0 * square_sum - 2.0 * density.astype(jnp.float32) + diagonal).astype(jnp.bfloat16)
    inverse = inverse_start
    for sweep_index in range(SWEEPS):
        correction = restricted(shifted, inverse, block_cols).astype(jnp.bfloat16)
        update = restricted(inverse, correction, block_cols)
        inverse = (2.0 * inverse.astype(jnp.float32) - update).astype(jnp.bfloat16)
    density_next = restricted(square, inverse, block_cols).astype(jnp.bfloat16)
    return density_next, inverse
```

```python
import functools

import jax
import jax.numpy as jnp
from jax import lax
from jax.experimental import pallas as pl
from jax.experimental.pallas import tpu as pltpu
from jax.sharding import PartitionSpec as P

SWEEPS = 2
RING = ("row", "inner")
VMEM_BYTES = 48 * 1024 * 1024


def shifted_by(x, by):
    size = lax.axis_size(RING)
    return lax.ppermute(x, RING, [(i, (i + by) % size) for i in range(size)])


class Frame:
    def __init__(self, half, order):
        self.h = half
        self.b = order
        self.k = 2 * half
        self.rows = 3 * half
        self.pairs = self.rows // 2
        self.reach = half // 2
        self.own_pairs = range(half // 2, half)

    def tiles(self, columns):
        for col in columns:
            for row in range(max(0, col - self.reach), min(self.pairs, col + self.reach + 1)):
                yield row, col

    def inner(self, row, col):
        return max(row, col) - self.reach, min(row, col) + self.reach + 1


def starts(counts):
    out = [0]
    for c in counts:
        out.append(out[-1] + c)
    return out


def near_below_counts(h):
    return [h + 1 + k for k in range(h)]


def near_above_counts(h):
    return [2 * h - k for k in range(h)]


def far_below_counts(h):
    return [k + 1 for k in range(h)]


def far_above_counts(h):
    return [h - k for k in range(h)]


def last_slots(rows, counts):
    width = rows.shape[1]
    return jnp.concatenate([rows[k, width - c :] for k, c in enumerate(counts)], axis=0)


def first_slots(rows, counts):
    return jnp.concatenate([rows[k, :c] for k, c in enumerate(counts)], axis=0)


def block_at(slots_of, offset, dropped, slot_limit):
    slot = jnp.minimum(offset - (offset > dropped).astype(jnp.int32), slot_limit)
    value = slots_of(slot)
    return jnp.where(offset == dropped, jnp.zeros_like(value), value)


def fill_row(f, dest, row, row_shift, slots_of, dropped, lo_col, hi_col):
    b = f.b
    first = 2 * (row // 2) - 2 * f.reach
    for col in range(max(lo_col, first), min(hi_col, first + 4 * f.reach + 2)):
        offset = col - row + f.h
        place = (
            pl.ds((row + row_shift) * b, b),
            pl.ds((col + row_shift) * b, b),
        )
        if 0 <= offset <= f.k:
            dest[place] = block_at(slots_of, offset, dropped, f.k - 1)
        else:
            dest[place] = jnp.zeros((b, b), dest.dtype)


def masked(f, tile, row, col, drop_ref):
    b = f.b
    parts = []
    for i in range(2):
        r = 2 * row + i
        line = []
        for j in range(2):
            offset = 2 * col + j - r + f.h
            piece = tile[i * b : (i + 1) * b, j * b : (j + 1) * b]
            if 0 <= offset <= f.k:
                piece = jnp.where(drop_ref[r + f.h] == offset, 0.0, piece)
            else:
                piece = jnp.zeros_like(piece)
            line.append(piece)
        parts.append(jnp.concatenate(line, axis=1))
    return jnp.concatenate(parts, axis=0)


def band_place(f, row, lo, hi):
    t = 2 * f.b
    return pl.ds(row * t, t), pl.ds((lo - row + f.reach) * t, (hi - lo) * t)


def dense_place(f, row_lo, row_hi, col_lo, col_hi):
    t = 2 * f.b
    return pl.ds(row_lo * t, (row_hi - row_lo) * t), pl.ds(col_lo * t, (col_hi - col_lo) * t)


def dot(a, b):
    return jnp.dot(a, b, preferred_element_type=jnp.float32)


def square_kernel(f, drop_ref, own, below, above, far_below, far_above, square, shifted, wide):
    h, k = f.h, f.k
    for r in range(h):
        for source, row in ((below, r), (own, h + r), (above, 2 * h + r)):
            fill_row(
                f, wide, row, h, lambda s, source=source, r=r: source[r, s], drop_ref[row + h], -h, 4 * h
            )
    low, high = starts(far_below_counts(h)), starts(far_above_counts(h))
    for r in range(h):
        base = low[r] - (k - (r + 1))
        fill_row(
            f, wide, r - h, h,
            lambda s, base=base, lo=k - (r + 1): far_below[base + jnp.maximum(s, lo)],
            drop_ref[r], 0, r + 1,
        )
        for col in range(r + 1, 2 * (r // 2) + 2):
            wide[pl.ds(r * f.b, f.b), pl.ds((col + h) * f.b, f.b)] = jnp.zeros((f.b, f.b), wide.dtype)
        fill_row(
            f, wide, 3 * h + r, h,
            lambda s, base=high[r], hi=h - r - 1: far_above[base + jnp.minimum(s, hi)],
            drop_ref[4 * h + r], 2 * h + r, 3 * h,
        )
        for col in range(2 * h + 2 * (r // 2), 2 * h + r):
            wide[pl.ds((4 * h + r) * f.b, f.b), pl.ds((col + h) * f.b, f.b)] = jnp.zeros(
                (f.b, f.b), wide.dtype
            )
    t = 2 * f.b
    shift = h // 2
    unit = (
        lax.broadcasted_iota(jnp.int32, (t, t), 0) == lax.broadcasted_iota(jnp.int32, (t, t), 1)
    ).astype(jnp.float32)
    for row, col in f.tiles(range(f.pairs)):
        lo, hi = f.inner(row, col)
        lo, hi = lo + shift, hi + shift
        total = dot(
            wide[dense_place(f, row + shift, row + shift + 1, lo, hi)],
            wide[dense_place(f, lo, hi, col + shift, col + shift + 1)],
        )
        total = masked(f, total, row, col, drop_ref)
        here = wide[dense_place(f, row + shift, row + shift + 1, col + shift, col + shift + 1)]
        moved = 2.0 * total - 2.0 * here.astype(jnp.float32)
        if row == col:
            moved = moved + unit
        place = band_place(f, row, col, col + 1)
        square[place] = total.astype(square.dtype)
        shifted[place] = moved.astype(shifted.dtype)


def clipped(f, row, col):
    lo, hi = f.inner(row, col)
    return max(lo, 0), min(hi, f.pairs)


def local(f, col):
    return col - f.h // 2


def own_place(f, lo, hi, col):
    return dense_place(f, lo, hi, local(f, col), local(f, col) + 1)


def sweep_kernel(f, drop_ref, shifted, own, below, above, fresh, to_next, to_prev, wide, correction):
    h, k, b = f.h, f.k, f.b
    low, high = starts(near_below_counts(h)), starts(near_above_counts(h))
    for r in range(h):
        lo = k - near_below_counts(h)[r]
        fill_row(
            f, wide, r, 0,
            lambda s, base=low[r] - lo, lo=lo: below[base + jnp.maximum(s, lo)],
            drop_ref[r + h], 0, 3 * h,
        )
        fill_row(f, wide, h + r, 0, lambda s, r=r: own[r, s], drop_ref[r + 2 * h], 0, 3 * h)
        fill_row(
            f, wide, 2 * h + r, 0,
            lambda s, base=high[r], hi=near_above_counts(h)[r] - 1: above[base + jnp.minimum(s, hi)],
            drop_ref[r + 3 * h], 0, 3 * h,
        )
    for row, col in f.tiles(f.own_pairs):
        lo, hi = clipped(f, row, col)
        total = dot(shifted[band_place(f, row, lo, hi)], wide[dense_place(f, lo, hi, col, col + 1)])
        correction[own_place(f, row, row + 1, col)] = masked(f, total, row, col, drop_ref).astype(
            correction.dtype
        )
    for row, col in f.tiles(f.own_pairs):
        lo, hi = clipped(f, row, col)
        total = dot(wide[dense_place(f, row, row + 1, lo, hi)], correction[own_place(f, lo, hi, col)])
        total = masked(f, total, row, col, drop_ref)
        here = wide[dense_place(f, row, row + 1, col, col + 1)].astype(jnp.float32)
        fresh[own_place(f, row, row + 1, col)] = (2.0 * here - total).astype(fresh.dtype)
    at = 0
    for c in range(h):
        for r in range(h, h + h + 1 + c):
            to_next[at] = fresh[pl.ds(r * b, b), pl.ds(c * b, b)]
            at += 1
    at = 0
    for c in range(h):
        for r in range(c, 2 * h):
            to_prev[at] = fresh[pl.ds(r * b, b), pl.ds(c * b, b)]
            at += 1


def right_kernel(f, drop_ref, left, right, out):
    for row, col in f.tiles(f.own_pairs):
        lo, hi = clipped(f, row, col)
        total = dot(left[band_place(f, row, lo, hi)], right[own_place(f, lo, hi, col)])
        out[own_place(f, row, row + 1, col)] = masked(f, total, row, col, drop_ref).astype(out.dtype)


def edge_blocks(f, matrix, to_next, to_prev):
    h, b = f.h, f.b
    at = 0
    for c in range(h):
        for r in range(2 * h, 2 * h + c + 1):
            to_next[at] = matrix[pl.ds(r * b, b), pl.ds(c * b, b)]
            at += 1
    at = 0
    for c in range(h):
        for r in range(c, h):
            to_prev[at] = matrix[pl.ds(r * b, b), pl.ds(c * b, b)]
            at += 1


def last_sweep_kernel(f, drop_ref, own, below, above, correction, fresh, to_next, to_prev, low, high):
    h, b = f.h, f.b
    zero = jnp.zeros((b, b), low.dtype)
    at = 0
    for c in range(h):
        for r in range(h + 1 + c):
            low[pl.ds(r * b, b), pl.ds(c * b, b)] = below[at]
            at += 1
        for r in range(h + 1 + c, 2 * (c // 2) + h + 2):
            low[pl.ds(r * b, b), pl.ds(c * b, b)] = zero
    at = 0
    for c in range(h):
        for r in range(2 * (c // 2), c):
            high[pl.ds(r * b, b), pl.ds(c * b, b)] = zero
        for r in range(c, 2 * h):
            high[pl.ds(r * b, b), pl.ds(c * b, b)] = above[at]
            at += 1
    s = h // 2
    for row, col in f.tiles(f.own_pairs):
        lo, hi = clipped(f, row, col)
        total = None
        for source, first, last, row_shift in ((low, 0, s, 0), (own, s, 2 * s, 0), (high, 2 * s, 3 * s, s)):
            a, z = max(lo, first), min(hi, last)
            if a >= z:
                continue
            part = dot(
                source[dense_place(f, row - row_shift, row - row_shift + 1, a - first, z - first)],
                correction[own_place(f, a, z, col)],
            )
            total = part if total is None else total + part
        total = masked(f, total, row, col, drop_ref)
        here = own[own_place(f, row, row + 1, col)].astype(jnp.float32)
        fresh[own_place(f, row, row + 1, col)] = (2.0 * here - total).astype(fresh.dtype)
    edge_blocks(f, fresh, to_next, to_prev)


def density_kernel(f, drop_ref, square, inverse, out, to_next, to_prev):
    right_kernel(f, drop_ref, square, inverse, out)
    edge_blocks(f, out, to_next, to_prev)


def rows_kernel(f, drop_ref, *refs):
    h, k, b = f.h, f.k, f.b
    low = starts([h - c for c in range(h)])
    low = starts([c + 1 for c in range(h)])
    high = starts([h - c for c in range(h)])
    half = len(refs) // 2
    outs = refs[-2:]
    for which in range(2):
        own, below, above = refs[3 * which : 3 * which + 3]
        out = outs[which]
        for r in range(h):
            dropped = drop_ref[r + 2 * h]

            def at_offset(offset, r=r, own=own, below=below, above=above):
                col = r + offset
                if col < h:
                    return below[low[col] + r]
                if col < 2 * h:
                    return own[pl.ds((h + r) * b, b), pl.ds((col - h) * b, b)]
                return above[high[col - 2 * h] + r - (col - 2 * h)]

            for s in range(k):
                out[r, s] = jnp.where(dropped <= s, at_offset(s + 1), at_offset(s))


def call(kernel, out_shapes, scratch, flops, drop, *args):
    vmem = pl.BlockSpec(memory_space=pltpu.VMEM)
    moved = sum(a.size * a.dtype.itemsize for a in args)
    moved += sum(s.size * s.dtype.itemsize for s in out_shapes)
    return pl.pallas_call(
        kernel,
        out_shape=out_shapes,
        in_specs=[pl.BlockSpec(memory_space=pltpu.SMEM)] + [vmem] * len(args),
        out_specs=[vmem] * len(out_shapes),
        scratch_shapes=scratch,
        compiler_params=pltpu.CompilerParams(vmem_limit_bytes=VMEM_BYTES),
        cost_estimate=pl.CostEstimate(flops=flops, bytes_accessed=moved, transcendentals=0),
    )(drop, *args)


def on_device(density, inverse_start, block_cols):
    rows, width, order, _ = density.shape
    half = width // 2
    assert rows == half and half % 2 == 0
    f = Frame(half, order)
    total_rows = rows * lax.axis_size(RING)
    kind = density.dtype

    below = shifted_by(density, 1)
    above = shifted_by(density, -1)
    inverse_below = shifted_by(last_slots(inverse_start, near_below_counts(half)), 1)
    inverse_above = shifted_by(first_slots(inverse_start, near_above_counts(half)), -1)

    own_ids = lax.axis_index(RING) * rows + jnp.arange(rows, dtype=jnp.int32)
    positions = jnp.mod(block_cols - own_ids[:, None] + half, total_rows)
    dropped = width * (width + 1) // 2 - jnp.sum(positions, axis=1)
    drop = jnp.concatenate(
        [shifted_by(dropped, 2), shifted_by(dropped, 1), dropped, shifted_by(dropped, -1), shifted_by(dropped, -2)]
    )

    far_below = shifted_by(last_slots(below, far_below_counts(half)), 1)
    far_above = shifted_by(first_slots(above, far_above_counts(half)), -1)

    tile_flops = 2 * (2 * order) ** 3
    span = f.rows * order
    band = jax.ShapeDtypeStruct((span, (2 * f.reach + 1) * 2 * order), kind)
    columns = jax.ShapeDtypeStruct((span, half * order), kind)
    near = jax.ShapeDtypeStruct((sum(near_below_counts(half)), order, order), kind)
    edge = jax.ShapeDtypeStruct((sum(far_below_counts(half)), order, order), kind)
    square, shifted = call(
        functools.partial(square_kernel, f),
        [band, band],
        [pltpu.VMEM((5 * half * order, 5 * half * order), kind)],
        94 * tile_flops,
        drop, density, below, above, far_below, far_above,
    )
    inverse, to_next, to_prev = call(
        functools.partial(sweep_kernel, f),
        [columns, near, near],
        [pltpu.VMEM((span, span), kind), pltpu.VMEM((span, half * order), kind)],
        76 * tile_flops,
        drop, shifted, inverse_start, inverse_below, inverse_above,
    )
    inverse_below = shifted_by(to_next, 1)
    inverse_above = shifted_by(to_prev, -1)
    (correction,) = call(
        functools.partial(right_kernel, f), [columns], [], 38 * tile_flops, drop, shifted, inverse
    )
    inverse, to_next, to_prev = call(
        functools.partial(last_sweep_kernel, f),
        [columns, edge, edge],
        [pltpu.VMEM((2 * half * order, half * order), kind), pltpu.VMEM((2 * half * order, half * order), kind)],
        38 * tile_flops,
        drop, inverse, inverse_below, inverse_above, correction,
    )
    inverse_parts = (inverse, shifted_by(to_next, 1), shifted_by(to_prev, -1))
    density_columns, to_next, to_prev = call(
        functools.partial(density_kernel, f), [columns, edge, edge], [], 38 * tile_flops, drop, square, inverse
    )
    density_parts = (density_columns, shifted_by(to_next, 1), shifted_by(to_prev, -1))
    out = jax.ShapeDtypeStruct(density.shape, kind)
    return tuple(
        call(functools.partial(rows_kernel, f), [out, out], [], 0, drop, *density_parts, *inverse_parts)
    )


def solution(mesh):
    blocks = P(("grp", "row", "inner"), None, None, None)
    return jax.shard_map(
        on_device,
        mesh=mesh,
        in_specs=(blocks, blocks, P(("grp", "row", "inner"), None)),
        out_specs=(blocks, blocks),
        check_vma=False,
    )
```

```python
import functools

import jax
import jax.numpy as jnp
from jax import lax
from jax.experimental import pallas as pl
from jax.experimental.pallas import tpu as pltpu
from jax.sharding import PartitionSpec as P

RING = ("row", "inner")
MIB = 1024 * 1024


class Frame:
    def __init__(self, half, order):
        self.h = half
        self.b = order
        self.k = 2 * half
        self.p = half // 2
        self.t = 2 * order
        self.group = half * order
        self.pairs = 3 * self.p
        self.own_pairs = range(self.p, 2 * self.p)
        self.edge_rows = [*range(self.p), *range(2 * self.p, 3 * self.p)]

    def tiles(self, columns):
        for col in columns:
            for row in range(max(0, col - self.p), min(self.pairs, col + self.p + 1)):
                yield row, col

    def inner(self, row, col):
        return max(row, col) - self.p, min(row, col) + self.p + 1

    def clipped(self, row, col):
        lo, hi = self.inner(row, col)
        return max(lo, 0), min(hi, self.pairs)

    def split(self, row, col):
        lo, hi = self.clipped(row, col)
        for g in range(3):
            a, z = max(lo, g * self.p), min(hi, (g + 1) * self.p)
            if a < z:
                yield g, a - g * self.p, z - g * self.p


def under(h):
    return [(r, c) for r in range(h) for c in range(r + 1)]


def over(h):
    return [(r, c) for r in range(h) for c in range(r, h)]


def at(f, row_lo, row_hi, col_lo, col_hi):
    t = f.t
    return pl.ds(row_lo * t, (row_hi - row_lo) * t), pl.ds(col_lo * t, (col_hi - col_lo) * t)


def block(f, r, c):
    return pl.ds(r * f.b, f.b), pl.ds(c * f.b, f.b)


def banded(f, row, lo, hi):
    return at(f, row, row + 1, lo - row + f.p, hi - row + f.p)


def dot(a, b):
    return jnp.dot(a, b, preferred_element_type=jnp.float32)


def stored(rows, r, offset, dropped):
    slot = jnp.minimum(offset - (offset > dropped).astype(jnp.int32), rows.shape[1] - 1)
    value = rows[r, slot]
    return jnp.where(offset == dropped, jnp.zeros_like(value), value)


def spread(f, dest, row, col, packed, places):
    index = {place: i for i, place in enumerate(places)}
    for r in range(f.h):
        for c in range(f.h):
            i = index.get((r, c))
            value = jnp.zeros((f.b, f.b), dest.dtype) if i is None else packed[i]
            dest[block(f, row + r, col + c)] = value


def pack(f, source, row, packed, places):
    for i, (r, c) in enumerate(places):
        packed[i] = source[block(f, row + r, c)]


def masked(f, tile, row, col, drop_ref):
    b = f.b
    parts = []
    for i in range(2):
        r = 2 * row + i
        line = []
        for j in range(2):
            offset = 2 * col + j - r + f.h
            piece = tile[i * b : (i + 1) * b, j * b : (j + 1) * b]
            if 0 <= offset <= f.k:
                piece = jnp.where(drop_ref[r] == offset, 0.0, piece)
            else:
                piece = jnp.zeros_like(piece)
            line.append(piece)
        parts.append(jnp.concatenate(line, axis=1))
    return jnp.concatenate(parts, axis=0)


def slabs_kernel(f, drop_ref, own, corner, up, down):
    h = f.h
    for r in range(h):
        for c in range(h):
            corner[block(f, r, c)] = stored(own, r, c - r + h, drop_ref[r])
    for i, (r, c) in enumerate(under(h)):
        up[i] = stored(own, r, 2 * h + c - r, drop_ref[r])
    for i, (r, c) in enumerate(over(h)):
        down[i] = stored(own, r, c - r, drop_ref[r])


def forward_kernel(f, drop_ref, below, above, *refs):
    h = f.h
    far_up, far_down = refs[3:5]
    odd = drop_ref[3 * h] == 1

    def send(rows, first):
        for i, (r, c) in enumerate(under(h)):
            far_up[i] = stored(rows, r, 2 * h + c - r, drop_ref[first + r])
        for i, (r, c) in enumerate(over(h)):
            far_down[i] = stored(rows, r, c - r, drop_ref[first + r])

    @pl.when(odd)
    def _():
        send(above, 2 * h)

    @pl.when(jnp.logical_not(odd))
    def _():
        send(below, 0)


def square_kernel(f, drop_ref, own, below, above, far_below, far_above, square, shifted, wide):
    h, p = f.h, f.p
    for g, source in enumerate((below, own, above)):
        for r in range(h):
            row = g * h + r
            first = 2 * (row // 2) - h
            for col in range(first, first + 2 * h + 2):
                offset = col - row + h
                if 0 <= offset <= f.k:
                    value = stored(source, r, offset, drop_ref[row])
                else:
                    value = jnp.zeros((f.b, f.b), wide.dtype)
                wide[block(f, row + h, col + h)] = value
    spread(f, wide, 0, h, far_below, under(h))
    spread(f, wide, 4 * h, 3 * h, far_above, over(h))
    unit = (
        lax.broadcasted_iota(jnp.int32, (f.t, f.t), 0) == lax.broadcasted_iota(jnp.int32, (f.t, f.t), 1)
    ).astype(jnp.float32)
    for row, col in f.tiles(range(f.pairs)):
        lo, hi = f.inner(row, col)
        lo, hi = lo + p, hi + p
        total = dot(
            wide[at(f, row + p, row + p + 1, lo, hi)], wide[at(f, lo, hi, col + p, col + p + 1)]
        )
        total = masked(f, total, row, col, drop_ref)
        here = wide[at(f, row + p, row + p + 1, col + p, col + p + 1)]
        moved = 2.0 * total - 2.0 * here.astype(jnp.float32)
        if row == col:
            moved = moved + unit
        place = banded(f, row, col, col + 1)
        square[place] = total.astype(square.dtype)
        shifted[place] = moved.astype(shifted.dtype)


def right_tile(f, left, right, row, col):
    lo, hi = f.clipped(row, col)
    return dot(left[banded(f, row, lo, hi)], right[at(f, lo, hi, col - f.p, col - f.p + 1)])


def first_sweep_kernel(
    f, drop_ref, shifted, corner, up, down, from_below, from_above, correction, fresh, partial, whole, before, after
):
    h, p = f.h, f.p
    spread(f, whole, 0, 0, from_below, under(h))
    for i in range(h):
        rows = pl.ds(i * f.b, f.b)
        whole[pl.ds((h + i) * f.b, f.b), :] = corner[rows, :]
    spread(f, whole, 2 * h, 0, from_above, over(h))
    spread(f, before, 0, 0, down, over(h))
    spread(f, after, 0, 0, up, under(h))
    for row, col in f.tiles(f.own_pairs):
        total = masked(f, right_tile(f, shifted, whole, row, col), row, col, drop_ref)
        correction[at(f, row, row + 1, col - p, col - p + 1)] = total.astype(correction.dtype)
    for row, col in f.tiles(f.own_pairs):
        c = col - p
        own_row = row in f.own_pairs
        total = 2.0 * whole[at(f, row, row + 1, c, c + 1)].astype(jnp.float32)
        for g, a, z in f.split(row, col):
            if g == 1:
                left = whole[at(f, row, row + 1, a, z)]
            elif own_row:
                left = (before, None, after)[g][at(f, row - p, row - p + 1, a, z)]
            else:
                continue
            total = total - dot(left, correction[at(f, g * p + a, g * p + z, c, c + 1)])
        if own_row:
            total = masked(f, total, row, col, drop_ref)
            fresh[at(f, row - p, row - p + 1, c, c + 1)] = total.astype(fresh.dtype)
        else:
            place = row if row < p else row - p
            partial[at(f, place, place + 1, c, c + 1)] = total


def edges(f, drop_ref, corner_below, corner_above, correction, start, low, high):
    p = f.p
    for row, col in f.tiles(f.own_pairs):
        if row in f.own_pairs:
            continue
        c = col - p
        side = 0 if row < p else 2
        corner, dest = ((corner_below, low), None, (corner_above, high))[side]
        local = row - side * p
        total = start(row, col)
        for g, a, z in f.split(row, col):
            if g == side:
                total = total - dot(
                    corner[at(f, local, local + 1, a, z)], correction[at(f, g * p + a, g * p + z, c, c + 1)]
                )
        total = masked(f, total, row, col, drop_ref)
        dest[at(f, local, local + 1, c, c + 1)] = total.astype(dest.dtype)


def first_edges_kernel(f, drop_ref, corner_below, corner_above, correction, partial, low, high, to_prev, to_next):
    p = f.p

    def start(row, col):
        place = row if row < p else row - p
        return partial[at(f, place, place + 1, col - p, col - p + 1)]

    edges(f, drop_ref, corner_below, corner_above, correction, start, low, high)
    pack(f, low, 0, to_prev, under(f.h))
    pack(f, high, 0, to_next, over(f.h))


def gather(f, whole, low, own, high):
    for g, source in enumerate((low, own, high)):
        for i in range(f.h):
            whole[pl.ds(g * f.group + i * f.b, f.b), :] = source[pl.ds(i * f.b, f.b), :]


def correction_kernel(f, drop_ref, shifted, low, own, high, correction, whole):
    p = f.p
    gather(f, whole, low, own, high)
    for row, col in f.tiles(f.own_pairs):
        total = masked(f, right_tile(f, shifted, whole, row, col), row, col, drop_ref)
        correction[at(f, row, row + 1, col - p, col - p + 1)] = total.astype(correction.dtype)


def second_edges_kernel(
    f, drop_ref, corner_below, corner_above, correction, low, high, new_low, new_high, to_prev, to_next
):
    p = f.p

    def start(row, col):
        c = col - p
        source, local = (low, row) if row < p else (high, row - 2 * p)
        total = 2.0 * source[at(f, local, local + 1, c, c + 1)].astype(jnp.float32)
        for g, a, z in f.split(row, col):
            if g == 1:
                total = total - dot(
                    source[at(f, local, local + 1, a, z)], correction[at(f, p + a, p + z, c, c + 1)]
                )
        return total

    edges(f, drop_ref, corner_below, corner_above, correction, start, new_low, new_high)
    pack(f, new_low, 0, to_prev, under(f.h))
    pack(f, new_high, 0, to_next, over(f.h))


def density_edges_kernel(
    f, drop_ref, own, from_below, from_above, correction, new_low, new_high, square, whole, to_prev, to_next,
    before, after, low, high,
):
    h, p = f.h, f.p
    spread(f, before, 0, 0, from_below, over(h))
    spread(f, after, 0, 0, from_above, under(h))
    for row, col in f.tiles(f.own_pairs):
        if row not in f.own_pairs:
            continue
        c, local = col - p, row - p
        total = 2.0 * own[at(f, local, local + 1, c, c + 1)].astype(jnp.float32)
        for g, a, z in f.split(row, col):
            left = (before, own, after)[g][at(f, local, local + 1, a, z)]
            total = total - dot(left, correction[at(f, g * p + a, g * p + z, c, c + 1)])
        total = masked(f, total, row, col, drop_ref)
        whole[at(f, row, row + 1, c, c + 1)] = total.astype(whole.dtype)
    for i in range(h):
        rows = pl.ds(i * f.b, f.b)
        whole[pl.ds(i * f.b, f.b), :] = new_low[rows, :]
        whole[pl.ds(2 * f.group + i * f.b, f.b), :] = new_high[rows, :]
    for row, col in f.tiles(f.own_pairs):
        if row in f.own_pairs:
            continue
        total = masked(f, right_tile(f, square, whole, row, col), row, col, drop_ref)
        dest, local = (low, row) if row < p else (high, row - 2 * p)
        dest[at(f, local, local + 1, col - p, col - p + 1)] = total.astype(dest.dtype)
    pack(f, low, 0, to_prev, under(h))
    pack(f, high, 0, to_next, over(h))


def density_own_kernel(f, drop_ref, square, whole, out):
    p = f.p
    for row, col in f.tiles(f.own_pairs):
        if row in f.own_pairs:
            total = masked(f, right_tile(f, square, whole, row, col), row, col, drop_ref)
            out[at(f, row - p, row - p + 1, col - p, col - p + 1)] = total.astype(out.dtype)


def rows_kernel(f, first, drop_ref, own, from_below, from_above, out):
    h = f.h
    over_index = {place: i for i, place in enumerate(over(h))}
    under_index = {place: i for i, place in enumerate(under(h))}
    for r in range(h):
        dropped = drop_ref[h + r]

        def at_offset(offset, r=r):
            col = r + offset
            if col < h:
                return from_below[over_index[r, col]]
            if col < 2 * h:
                return own[block(f, first + r, col - h)]
            return from_above[under_index[r, col - 2 * h]]

        for s in range(f.k):
            out[r, s] = jnp.where(dropped <= s, at_offset(s + 1), at_offset(s))


VMEM = pl.BlockSpec(memory_space=pltpu.VMEM)
SMEM = pl.BlockSpec(memory_space=pltpu.SMEM)
ANY = pl.BlockSpec(memory_space=pl.ANY)


def call(kernel, outs, scratch, flops, limit, drop, *args, passed=()):
    moved = sum(a.size * a.dtype.itemsize for a in args) + sum(s.size * s.dtype.itemsize for s in outs)
    n = len(args)
    return pl.pallas_call(
        kernel,
        out_shape=[*outs, *[jax.ShapeDtypeStruct(a.shape, a.dtype) for a in passed]],
        in_specs=[SMEM] + [VMEM] * n + [ANY] * len(passed),
        out_specs=[VMEM] * len(outs) + [ANY] * len(passed),
        scratch_shapes=scratch,
        input_output_aliases={1 + n + i: len(outs) + i for i in range(len(passed))},
        compiler_params=pltpu.CompilerParams(vmem_limit_bytes=limit * MIB),
        cost_estimate=pl.CostEstimate(flops=flops, bytes_accessed=moved, transcendentals=0),
    )(drop, *args, *passed)


def permuted(x, step):
    size = lax.axis_size(RING)
    return lax.ppermute(x, RING, [(i, (i + step(i)) % size) for i in range(size)])


def to_next(x):
    return permuted(x, lambda i: 1)


def to_prev(x):
    return permuted(x, lambda i: -1)


def on_device(density, inverse_start, block_cols):
    rows, width, order, _ = density.shape
    half = width // 2
    ring = lax.axis_size(RING)
    assert rows == half and half % 2 == 0 and ring % 2 == 0
    f = Frame(half, order)
    kind = density.dtype
    me = lax.axis_index(RING)

    def absent(columns, first):
        ids = first + jnp.arange(columns.shape[0], dtype=jnp.int32)
        positions = jnp.mod(columns - ids[:, None] + half, rows * ring)
        return width * (width + 1) // 2 - jnp.sum(positions, axis=1)

    below, above = to_next(density), to_prev(density)
    near_cols = jnp.concatenate([to_next(block_cols), block_cols, to_prev(block_cols)], axis=0)
    drop = jnp.concatenate([absent(near_cols, (me - 1) * rows), jnp.reshape(me % 2, (1,))])
    own_drop = absent(block_cols, me * rows)

    unit = 2 * f.t**3
    square_group = jax.ShapeDtypeStruct((f.group, f.group), kind)
    columns = jax.ShapeDtypeStruct((3 * f.group, f.group), kind)
    band = jax.ShapeDtypeStruct((3 * f.group, (2 * f.p + 1) * f.t), kind)
    triangle = jax.ShapeDtypeStruct((half * (half + 1) // 2, order, order), kind)
    partial_sums = jax.ShapeDtypeStruct((2 * f.group, f.group), jnp.float32)
    group_scratch = pltpu.VMEM((f.group, f.group), kind)
    whole_scratch = pltpu.VMEM((3 * f.group, f.group), kind)

    def run(kernel, outs, scratch, tiles, limit, *args, **kw):
        return call(functools.partial(kernel, f), outs, scratch, tiles * unit, limit, *args, **kw)

    corner, up, down = run(
        slabs_kernel, [square_group, triangle, triangle], [], 0, 8, own_drop, inverse_start
    )
    far_up, far_down, corner, up, down = run(
        forward_kernel, [triangle, triangle], [], 0, 8, drop, below, above, passed=(corner, up, down)
    )
    far_below = permuted(far_up, lambda i: 1 + 2 * (i % 2))
    far_above = permuted(far_down, lambda i: -3 + 2 * (i % 2))
    from_below, from_above = to_next(up), to_prev(down)
    corner_below, corner_above = to_next(corner), to_prev(corner)

    square, shifted = run(
        square_kernel,
        [band, band],
        [pltpu.VMEM((5 * f.group, 5 * f.group), kind)],
        94, 28, drop, density, below, above, far_below, far_above,
    )
    correction, own, partial = run(
        first_sweep_kernel,
        [columns, square_group, partial_sums],
        [whole_scratch, group_scratch, group_scratch],
        66, 20, drop, shifted, corner, up, down, from_below, from_above,
    )
    next_corner_below, next_corner_above = to_next(own), to_prev(own)
    low, high, back, forth = run(
        first_edges_kernel,
        [square_group, square_group, triangle, triangle],
        [],
        10, 12, drop, corner_below, corner_above, correction, partial,
    )
    from_above, from_below = to_prev(back), to_next(forth)
    (correction,) = run(
        correction_kernel, [columns], [whole_scratch], 38, 16, drop, shifted, low, own, high
    )
    new_low, new_high, back, forth = run(
        second_edges_kernel,
        [square_group, square_group, triangle, triangle],
        [],
        20, 12, drop, next_corner_below, next_corner_above, correction, low, high,
    )
    inverse_above, inverse_below = to_prev(back), to_next(forth)
    whole, back, forth = run(
        density_edges_kernel,
        [columns, triangle, triangle],
        [group_scratch] * 4,
        38, 20, drop, own, from_below, from_above, correction, new_low, new_high, square,
    )
    density_above, density_below = to_prev(back), to_next(forth)
    (density_own,) = run(density_own_kernel, [square_group], [], 18, 12, drop, square, whole)
    out = jax.ShapeDtypeStruct(density.shape, kind)

    def assembled(own, first, from_below, from_above):
        kernel = functools.partial(rows_kernel, f, first)
        return call(kernel, [out], [], 0, 8, drop, own, from_below, from_above)[0]

    inverse_next = assembled(whole, half, inverse_below, inverse_above)
    density_next = assembled(density_own, 0, density_below, density_above)
    return density_next, inverse_next


def solution(mesh):
    blocks = P(("grp", "row", "inner"), None, None, None)
    return jax.shard_map(
        on_device,
        mesh=mesh,
        in_specs=(blocks, blocks, P(("grp", "row", "inner"), None)),
        out_specs=(blocks, blocks),
        check_vma=False,
    )
```

```python
import functools

import jax
import jax.numpy as jnp
from jax import lax
from jax.experimental import pallas as pl
from jax.experimental.pallas import tpu as pltpu
from jax.sharding import PartitionSpec as P

RING = ("row", "inner")
MIB = 1024 * 1024
NOTE = 16


class Frame:
    def __init__(self, half, order):
        self.h = half
        self.b = order
        self.k = 2 * half
        self.p = half // 2
        self.t = 2 * order
        self.group = half * order
        self.pairs = 3 * self.p
        self.own_pairs = range(self.p, 2 * self.p)
        self.edge_rows = [*range(self.p), *range(2 * self.p, 3 * self.p)]

    def tiles(self, columns):
        for col in columns:
            for row in range(max(0, col - self.p), min(self.pairs, col + self.p + 1)):
                yield row, col

    def inner(self, row, col):
        return max(row, col) - self.p, min(row, col) + self.p + 1

    def clipped(self, row, col):
        lo, hi = self.inner(row, col)
        return max(lo, 0), min(hi, self.pairs)

    def split(self, row, col):
        lo, hi = self.clipped(row, col)
        for g in range(3):
            a, z = max(lo, g * self.p), min(hi, (g + 1) * self.p)
            if a < z:
                yield g, a - g * self.p, z - g * self.p


def under(h):
    return [(r, c) for r in range(h) for c in range(r + 1)]


def over(h):
    return [(r, c) for r in range(h) for c in range(r, h)]


def at(f, row_lo, row_hi, col_lo, col_hi):
    t = f.t
    return pl.ds(row_lo * t, (row_hi - row_lo) * t), pl.ds(col_lo * t, (col_hi - col_lo) * t)


def block(f, r, c):
    return pl.ds(r * f.b, f.b), pl.ds(c * f.b, f.b)


def banded(f, row, lo, hi):
    return at(f, row, row + 1, lo - row + f.p, hi - row + f.p)


def dot(a, b):
    return jnp.dot(a, b, preferred_element_type=jnp.float32)


def stored(rows, r, offset, dropped):
    slot = jnp.minimum(offset - (offset > dropped).astype(jnp.int32), rows.shape[1] - 1)
    value = rows[r, slot]
    return jnp.where(offset == dropped, jnp.zeros_like(value), value)


def spread(f, dest, row, col, packed, places):
    index = {place: i for i, place in enumerate(places)}
    for r in range(f.h):
        for c in range(f.h):
            i = index.get((r, c))
            value = jnp.zeros((f.b, f.b), dest.dtype) if i is None else packed[block(f, i, 0)]
            dest[block(f, row + r, col + c)] = value


def pack(f, source, row, packed, places):
    for i, (r, c) in enumerate(places):
        packed[block(f, i, 0)] = source[block(f, row + r, c)]


def masked(f, tile, row, col, drop_ref):
    b = f.b
    parts = []
    for i in range(2):
        r = 2 * row + i
        line = []
        for j in range(2):
            offset = 2 * col + j - r + f.h
            piece = tile[i * b : (i + 1) * b, j * b : (j + 1) * b]
            if 0 <= offset <= f.k:
                piece = jnp.where(drop_ref[r] == offset, 0.0, piece)
            else:
                piece = jnp.zeros_like(piece)
            line.append(piece)
        parts.append(jnp.concatenate(line, axis=1))
    return jnp.concatenate(parts, axis=0)


def slabs_kernel(f, drop_ref, own, corner, up, down):
    h = f.h
    for r in range(h):
        for c in range(h):
            corner[block(f, r, c)] = stored(own, r, c - r + h, drop_ref[r])
    for i, (r, c) in enumerate(under(h)):
        up[block(f, i, 0)] = stored(own, r, 2 * h + c - r, drop_ref[r])
    for i, (r, c) in enumerate(over(h)):
        down[block(f, i, 0)] = stored(own, r, c - r, drop_ref[r])
    line = lax.broadcasted_iota(jnp.int32, (NOTE, f.b), 0)
    note = jnp.zeros((NOTE, f.b), jnp.float32)
    for r in range(h):
        note = jnp.where(line == r, drop_ref[r].astype(jnp.float32), note)
    for packed, places in ((up, under(h)), (down, over(h))):
        packed[pl.ds(len(places) * f.b, NOTE), :] = note.astype(packed.dtype)


def forward_kernel(f, drop_ref, below, above, unused_in, far_up, far_down, unused_out):
    h = f.h
    odd = drop_ref[3 * h] == 1

    def send(rows, first):
        for i, (r, c) in enumerate(under(h)):
            far_up[block(f, i, 0)] = stored(rows, r, 2 * h + c - r, drop_ref[first + r])
        for i, (r, c) in enumerate(over(h)):
            far_down[block(f, i, 0)] = stored(rows, r, c - r, drop_ref[first + r])

    @pl.when(odd)
    def _():
        send(above, 2 * h)

    @pl.when(jnp.logical_not(odd))
    def _():
        send(below, 0)


def square_kernel(f, drop_ref, own, below, above, far_below, far_above, square, shifted, wide):
    h, p = f.h, f.p
    for g, source in enumerate((below, own, above)):
        for r in range(h):
            row = g * h + r
            first = 2 * (row // 2) - h
            for col in range(first, first + 2 * h + 2):
                offset = col - row + h
                if 0 <= offset <= f.k:
                    value = stored(source, r, offset, drop_ref[row])
                else:
                    value = jnp.zeros((f.b, f.b), wide.dtype)
                wide[block(f, row + h, col + h)] = value
    spread(f, wide, 0, h, far_below, under(h))
    spread(f, wide, 4 * h, 3 * h, far_above, over(h))
    unit = (
        lax.broadcasted_iota(jnp.int32, (f.t, f.t), 0) == lax.broadcasted_iota(jnp.int32, (f.t, f.t), 1)
    ).astype(jnp.float32)
    for row, col in f.tiles(range(f.pairs)):
        lo, hi = f.inner(row, col)
        lo, hi = lo + p, hi + p
        total = dot(
            wide[at(f, row + p, row + p + 1, lo, hi)], wide[at(f, lo, hi, col + p, col + p + 1)]
        )
        total = masked(f, total, row, col, drop_ref)
        here = wide[at(f, row + p, row + p + 1, col + p, col + p + 1)]
        moved = 2.0 * total - 2.0 * here.astype(jnp.float32)
        if row == col:
            moved = moved + unit
        place = banded(f, row, col, col + 1)
        square[place] = total.astype(square.dtype)
        shifted[place] = moved.astype(shifted.dtype)


def right_tile(f, left, right, row, col):
    lo, hi = f.clipped(row, col)
    return dot(left[banded(f, row, lo, hi)], right[at(f, lo, hi, col - f.p, col - f.p + 1)])


def first_sweep_kernel(
    f, drop_ref, shifted, corner, up, down, from_below, from_above, correction, fresh, partial, whole, before, after
):
    h, p = f.h, f.p
    spread(f, whole, 0, 0, from_below, under(h))
    for i in range(h):
        rows = pl.ds(i * f.b, f.b)
        whole[pl.ds((h + i) * f.b, f.b), :] = corner[rows, :]
    spread(f, whole, 2 * h, 0, from_above, over(h))
    spread(f, before, 0, 0, down, over(h))
    spread(f, after, 0, 0, up, under(h))
    for row, col in f.tiles(f.own_pairs):
        total = masked(f, right_tile(f, shifted, whole, row, col), row, col, drop_ref)
        correction[at(f, row, row + 1, col - p, col - p + 1)] = total.astype(correction.dtype)
    for row, col in f.tiles(f.own_pairs):
        c = col - p
        own_row = row in f.own_pairs
        total = 2.0 * whole[at(f, row, row + 1, c, c + 1)].astype(jnp.float32)
        for g, a, z in f.split(row, col):
            if g == 1:
                left = whole[at(f, row, row + 1, a, z)]
            elif own_row:
                left = (before, None, after)[g][at(f, row - p, row - p + 1, a, z)]
            else:
                continue
            total = total - dot(left, correction[at(f, g * p + a, g * p + z, c, c + 1)])
        if own_row:
            total = masked(f, total, row, col, drop_ref)
            fresh[at(f, row - p, row - p + 1, c, c + 1)] = total.astype(fresh.dtype)
        else:
            place = row if row < p else row - p
            partial[at(f, place, place + 1, c, c + 1)] = total


def edges(f, drop_ref, corner_below, corner_above, correction, start, low, high):
    p = f.p
    for row, col in f.tiles(f.own_pairs):
        if row in f.own_pairs:
            continue
        c = col - p
        side = 0 if row < p else 2
        corner, dest = ((corner_below, low), None, (corner_above, high))[side]
        local = row - side * p
        total = start(row, col)
        for g, a, z in f.split(row, col):
            if g == side:
                total = total - dot(
                    corner[at(f, local, local + 1, a, z)], correction[at(f, g * p + a, g * p + z, c, c + 1)]
                )
        total = masked(f, total, row, col, drop_ref)
        dest[at(f, local, local + 1, c, c + 1)] = total.astype(dest.dtype)


def first_edges_kernel(f, drop_ref, corner_below, corner_above, correction, partial, low, high, to_prev, to_next):
    p = f.p

    def start(row, col):
        place = row if row < p else row - p
        return partial[at(f, place, place + 1, col - p, col - p + 1)]

    edges(f, drop_ref, corner_below, corner_above, correction, start, low, high)
    pack(f, low, 0, to_prev, under(f.h))
    pack(f, high, 0, to_next, over(f.h))


def gather(f, whole, low, own, high):
    for g, source in enumerate((low, own, high)):
        for i in range(f.h):
            whole[pl.ds(g * f.group + i * f.b, f.b), :] = source[pl.ds(i * f.b, f.b), :]


def correction_kernel(f, drop_ref, shifted, low, own, high, correction, whole):
    p = f.p
    gather(f, whole, low, own, high)
    for row, col in f.tiles(f.own_pairs):
        total = masked(f, right_tile(f, shifted, whole, row, col), row, col, drop_ref)
        correction[at(f, row, row + 1, col - p, col - p + 1)] = total.astype(correction.dtype)


def second_edges_kernel(
    f, drop_ref, corner_below, corner_above, correction, low, high, new_low, new_high, to_prev, to_next
):
    p = f.p

    def start(row, col):
        c = col - p
        source, local = (low, row) if row < p else (high, row - 2 * p)
        total = 2.0 * source[at(f, local, local + 1, c, c + 1)].astype(jnp.float32)
        for g, a, z in f.split(row, col):
            if g == 1:
                total = total - dot(
                    source[at(f, local, local + 1, a, z)], correction[at(f, p + a, p + z, c, c + 1)]
                )
        return total

    edges(f, drop_ref, corner_below, corner_above, correction, start, new_low, new_high)
    pack(f, new_low, 0, to_prev, under(f.h))
    pack(f, new_high, 0, to_next, over(f.h))


def density_edges_kernel(
    f, drop_ref, own, from_below, from_above, correction, new_low, new_high, square, whole, to_prev, to_next,
    before, after, low, high,
):
    h, p = f.h, f.p
    spread(f, before, 0, 0, from_below, over(h))
    spread(f, after, 0, 0, from_above, under(h))
    for row, col in f.tiles(f.own_pairs):
        if row not in f.own_pairs:
            continue
        c, local = col - p, row - p
        total = 2.0 * own[at(f, local, local + 1, c, c + 1)].astype(jnp.float32)
        for g, a, z in f.split(row, col):
            left = (before, own, after)[g][at(f, local, local + 1, a, z)]
            total = total - dot(left, correction[at(f, g * p + a, g * p + z, c, c + 1)])
        total = masked(f, total, row, col, drop_ref)
        whole[at(f, row, row + 1, c, c + 1)] = total.astype(whole.dtype)
    for i in range(h):
        rows = pl.ds(i * f.b, f.b)
        whole[pl.ds(i * f.b, f.b), :] = new_low[rows, :]
        whole[pl.ds(2 * f.group + i * f.b, f.b), :] = new_high[rows, :]
    for row, col in f.tiles(f.own_pairs):
        if row in f.own_pairs:
            continue
        total = masked(f, right_tile(f, square, whole, row, col), row, col, drop_ref)
        dest, local = (low, row) if row < p else (high, row - 2 * p)
        dest[at(f, local, local + 1, col - p, col - p + 1)] = total.astype(dest.dtype)
    pack(f, low, 0, to_prev, under(h))
    pack(f, high, 0, to_next, over(h))


def density_own_kernel(f, drop_ref, square, whole, out):
    p = f.p
    for row, col in f.tiles(f.own_pairs):
        if row in f.own_pairs:
            total = masked(f, right_tile(f, square, whole, row, col), row, col, drop_ref)
            out[at(f, row - p, row - p + 1, col - p, col - p + 1)] = total.astype(out.dtype)


def rows_kernel(f, first, drop_ref, own, from_below, from_above, out):
    h = f.h
    over_index = {place: i for i, place in enumerate(over(h))}
    under_index = {place: i for i, place in enumerate(under(h))}
    for r in range(h):
        dropped = drop_ref[h + r]

        def at_offset(offset, r=r):
            col = r + offset
            if col < h:
                return from_below[block(f, over_index[r, col], 0)]
            if col < 2 * h:
                return own[block(f, first + r, col - h)]
            return from_above[block(f, under_index[r, col - 2 * h], 0)]

        for s in range(f.k):
            out[r, s] = jnp.where(dropped <= s, at_offset(s + 1), at_offset(s))


VMEM = pl.BlockSpec(memory_space=pltpu.VMEM)
SMEM = pl.BlockSpec(memory_space=pltpu.SMEM)
ANY = pl.BlockSpec(memory_space=pl.ANY)


def call(kernel, outs, scratch, flops, limit, drop, *args, passed=()):
    moved = sum(a.size * a.dtype.itemsize for a in args) + sum(s.size * s.dtype.itemsize for s in outs)
    n = len(args)
    return pl.pallas_call(
        kernel,
        out_shape=[*outs, *[jax.ShapeDtypeStruct(a.shape, a.dtype) for a in passed]],
        in_specs=[SMEM] + [VMEM] * n + [ANY] * len(passed),
        out_specs=[VMEM] * len(outs) + [ANY] * len(passed),
        scratch_shapes=scratch,
        input_output_aliases={1 + n + i: len(outs) + i for i in range(len(passed))},
        compiler_params=pltpu.CompilerParams(vmem_limit_bytes=limit * MIB),
        cost_estimate=pl.CostEstimate(flops=flops, bytes_accessed=moved, transcendentals=0),
    )(drop, *args, *passed)


def permuted(x, step):
    size = lax.axis_size(RING)
    return lax.ppermute(x, RING, [(i, (i + step(i)) % size) for i in range(size)])


def to_next(x):
    return permuted(x, lambda i: 1)


def to_prev(x):
    return permuted(x, lambda i: -1)


def on_device(density, inverse_start, block_cols):
    rows, width, order, _ = density.shape
    half = width // 2
    ring = lax.axis_size(RING)
    assert rows == half and half % 2 == 0 and ring % 2 == 0
    f = Frame(half, order)
    kind = density.dtype
    me = lax.axis_index(RING)
    total = rows * ring

    def absent(columns, first):
        ids = first + jnp.arange(columns.shape[0], dtype=jnp.int32)
        positions = columns - ids[:, None] + half
        positions = positions + jnp.where(positions < 0, total, jnp.where(positions >= total, -total, 0))
        return width * (width + 1) // 2 - jnp.sum(positions, axis=1)

    below, above = to_next(density), to_prev(density)
    own_drop = absent(block_cols, me * rows)

    unit = 2 * f.t**3
    square_group = jax.ShapeDtypeStruct((f.group, f.group), kind)
    columns = jax.ShapeDtypeStruct((3 * f.group, f.group), kind)
    band = jax.ShapeDtypeStruct((3 * f.group, (2 * f.p + 1) * f.t), kind)
    triangle_rows = half * (half + 1) // 2 * order
    triangle = jax.ShapeDtypeStruct((triangle_rows, order), kind)
    noted = jax.ShapeDtypeStruct((triangle_rows + NOTE, order), kind)
    partial_sums = jax.ShapeDtypeStruct((2 * f.group, f.group), jnp.float32)
    group_scratch = pltpu.VMEM((f.group, f.group), kind)
    whole_scratch = pltpu.VMEM((3 * f.group, f.group), kind)

    def run(kernel, outs, scratch, tiles, limit, *args, **kw):
        return call(functools.partial(kernel, f), outs, scratch, tiles * unit, limit, *args, **kw)

    corner, up, down = run(slabs_kernel, [square_group, noted, noted], [], 0, 8, own_drop, inverse_start)
    from_below, from_above = to_next(up), to_prev(down)

    def note(slab):
        return slab[triangle_rows : triangle_rows + rows, 0].astype(jnp.int32)

    odd = jnp.reshape(me & 1, (1,))
    drop = jnp.concatenate([note(from_below), own_drop, note(from_above), odd])
    far_up, far_down, corner = run(
        forward_kernel, [triangle, triangle], [], 0, 8, drop, below, above, passed=(corner,)
    )
    corner_below, corner_above = to_next(corner), to_prev(corner)
    far_below = permuted(far_up, lambda i: 1 + 2 * (i % 2))
    far_above = permuted(far_down, lambda i: -3 + 2 * (i % 2))

    square, shifted = run(
        square_kernel,
        [band, band],
        [pltpu.VMEM((5 * f.group, 5 * f.group), kind)],
        94, 28, drop, density, below, above, far_below, far_above,
    )
    correction, own, partial = run(
        first_sweep_kernel,
        [columns, square_group, partial_sums],
        [whole_scratch, group_scratch, group_scratch],
        66, 20, drop, shifted, corner, up, down, from_below, from_above,
    )
    next_corner_below, next_corner_above = to_next(own), to_prev(own)
    low, high, back, forth = run(
        first_edges_kernel,
        [square_group, square_group, triangle, triangle],
        [],
        10, 12, drop, corner_below, corner_above, correction, partial,
    )
    from_above, from_below = to_prev(back), to_next(forth)
    (correction,) = run(
        correction_kernel, [columns], [whole_scratch], 38, 16, drop, shifted, low, own, high
    )
    new_low, new_high, back, forth = run(
        second_edges_kernel,
        [square_group, square_group, triangle, triangle],
        [],
        20, 12, drop, next_corner_below, next_corner_above, correction, low, high,
    )
    inverse_above, inverse_below = to_prev(back), to_next(forth)
    whole, back, forth = run(
        density_edges_kernel,
        [columns, triangle, triangle],
        [group_scratch] * 4,
        38, 20, drop, own, from_below, from_above, correction, new_low, new_high, square,
    )
    density_above, density_below = to_prev(back), to_next(forth)
    (density_own,) = run(density_own_kernel, [square_group], [], 18, 12, drop, square, whole)
    out = jax.ShapeDtypeStruct(density.shape, kind)

    def assembled(own, first, from_below, from_above):
        kernel = functools.partial(rows_kernel, f, first)
        return call(kernel, [out], [], 0, 8, drop, own, from_below, from_above)[0]

    inverse_next = assembled(whole, half, inverse_below, inverse_above)
    density_next = assembled(density_own, 0, density_below, density_above)
    return density_next, inverse_next


def solution(mesh):
    blocks = P(("grp", "row", "inner"), None, None, None)
    return jax.shard_map(
        on_device,
        mesh=mesh,
        in_specs=(blocks, blocks, P(("grp", "row", "inner"), None)),
        out_specs=(blocks, blocks),
        check_vma=False,
    )
```

```python
import functools

import jax
import jax.numpy as jnp
from jax import lax
from jax.experimental import pallas as pl
from jax.experimental.pallas import tpu as pltpu
from jax.sharding import PartitionSpec as P

RING = ("row", "inner")
MIB = 1024 * 1024


class Frame:
    def __init__(self, half, order):
        self.h = half
        self.b = order
        self.k = 2 * half
        self.p = half // 2
        self.t = 2 * order
        self.group = half * order
        self.pairs = 3 * self.p
        self.own_pairs = range(self.p, 2 * self.p)
        self.edge_rows = [*range(self.p), *range(2 * self.p, 3 * self.p)]

    def tiles(self, columns):
        for col in columns:
            for row in range(max(0, col - self.p), min(self.pairs, col + self.p + 1)):
                yield row, col

    def inner(self, row, col):
        return max(row, col) - self.p, min(row, col) + self.p + 1

    def clipped(self, row, col):
        lo, hi = self.inner(row, col)
        return max(lo, 0), min(hi, self.pairs)

    def split(self, row, col):
        lo, hi = self.clipped(row, col)
        for g in range(3):
            a, z = max(lo, g * self.p), min(hi, (g + 1) * self.p)
            if a < z:
                yield g, a - g * self.p, z - g * self.p


def under(h):
    return [(r, c) for r in range(h) for c in range(r + 1)]


def over(h):
    return [(r, c) for r in range(h) for c in range(r, h)]


def full(h):
    return [(r, c) for r in range(h) for c in range(h)]


def at(f, row_lo, row_hi, col_lo, col_hi):
    t = f.t
    return pl.ds(row_lo * t, (row_hi - row_lo) * t), pl.ds(col_lo * t, (col_hi - col_lo) * t)


def block(f, r, c):
    return pl.ds(r * f.b, f.b), pl.ds(c * f.b, f.b)


def banded(f, row, lo, hi):
    return at(f, row, row + 1, lo - row + f.p, hi - row + f.p)


def dot(a, b):
    return jnp.dot(a, b, preferred_element_type=jnp.float32)


def stored(rows, r, offset, dropped, slots=None):
    last = (rows.shape[1] if slots is None else slots) - 1
    slot = jnp.minimum(offset - (offset > dropped).astype(jnp.int32), last)
    value = rows[r, slot] if slots is None else rows((r, slot))
    return jnp.where(offset == dropped, jnp.zeros_like(value), value)


def masked(f, tile, row, col, drop_ref):
    b = f.b
    parts = []
    for i in range(2):
        r = 2 * row + i
        line = []
        for j in range(2):
            offset = 2 * col + j - r + f.h
            piece = tile[i * b : (i + 1) * b, j * b : (j + 1) * b]
            if 0 <= offset <= f.k:
                piece = jnp.where(drop_ref[r] == offset, 0.0, piece)
            else:
                piece = jnp.zeros_like(piece)
            line.append(piece)
        parts.append(jnp.concatenate(line, axis=1))
    return jnp.concatenate(parts, axis=0)


def odd_place(f, drop_ref):
    return drop_ref[3 * f.h] == 1


def indexed(f, ref, first=0):
    return lambda i: ref[block(f, first + i, 0)]


def plain(ref):
    return lambda place: ref[place]


def sides(f, drop_ref, mate, cross):
    odd = odd_place(f, drop_ref)

    def below(key):
        return jnp.where(odd, mate(key), cross(key))

    def above(key):
        return jnp.where(odd, cross(key), mate(key))

    return below, above


def spread(f, dest, row, col, read, places):
    index = {place: i for i, place in enumerate(places)}
    for r in range(f.h):
        for c in range(f.h):
            i = index.get((r, c))
            dest[block(f, row + r, col + c)] = jnp.zeros((f.b, f.b), dest.dtype) if i is None else read(i)


def pack_edges(f, drop_ref, low, high, to_mate, to_cross):
    odd = odd_place(f, drop_ref)
    for i, (lower, upper) in enumerate(zip(under(f.h), over(f.h))):
        back, forth = low[block(f, *lower)], high[block(f, *upper)]
        to_mate[block(f, i, 0)] = jnp.where(odd, back, forth)
        to_cross[block(f, i, 0)] = jnp.where(odd, forth, back)


def slabs_kernel(f, drop_ref, own, corner, to_mate, to_cross):
    h = f.h
    odd = odd_place(f, drop_ref)
    n = len(under(h))
    for i, (lower, upper) in enumerate(zip(under(h), over(h))):
        (r, c), (s, d) = lower, upper
        forth = stored(own, r, 2 * h + c - r, drop_ref[h + r])
        back = stored(own, s, d - s, drop_ref[h + s])
        to_mate[block(f, i, 0)] = jnp.where(odd, back, forth)
        to_cross[block(f, i, 0)] = jnp.where(odd, forth, back)
    for i, (r, c) in enumerate(full(h)):
        value = stored(own, r, c - r + h, drop_ref[h + r])
        corner[block(f, i, 0)] = value
        to_mate[block(f, n + i, 0)] = value
        to_cross[block(f, n + i, 0)] = value


def forward_kernel(f, drop_ref, cross, *refs):
    h = f.h
    odd = odd_place(f, drop_ref)
    to_mate, to_far = refs[-2:]
    for i, (lower, upper) in enumerate(zip(under(h), over(h))):
        (r, c), (s, d) = lower, upper
        forth = stored(cross, r, 2 * h + c - r, jnp.where(odd, drop_ref[2 * h + r], drop_ref[r]))
        back = stored(cross, s, d - s, jnp.where(odd, drop_ref[2 * h + s], drop_ref[s]))
        to_mate[block(f, i, 0)] = jnp.where(odd, back, forth)
        to_far[block(f, i, 0)] = jnp.where(odd, forth, back)


def square_kernel(f, drop_ref, own, mate, cross, far_mate, far_far, square, shifted, wide):
    h, p = f.h, f.p
    below, above = sides(f, drop_ref, plain(mate), plain(cross))
    for g, read in enumerate((below, plain(own), above)):
        for r in range(h):
            row = g * h + r
            first = 2 * (row // 2) - h
            for col in range(first, first + 2 * h + 2):
                offset = col - row + h
                if 0 <= offset <= f.k:
                    value = stored(read, r, offset, drop_ref[row], f.k)
                else:
                    value = jnp.zeros((f.b, f.b), wide.dtype)
                wide[block(f, row + h, col + h)] = value
    far_below, far_above = sides(f, drop_ref, indexed(f, far_mate), indexed(f, far_far))
    spread(f, wide, 0, h, far_below, under(h))
    spread(f, wide, 4 * h, 3 * h, far_above, over(h))
    unit = (
        lax.broadcasted_iota(jnp.int32, (f.t, f.t), 0) == lax.broadcasted_iota(jnp.int32, (f.t, f.t), 1)
    ).astype(jnp.float32)
    for row, col in f.tiles(range(f.pairs)):
        lo, hi = f.inner(row, col)
        lo, hi = lo + p, hi + p
        total = dot(
            wide[at(f, row + p, row + p + 1, lo, hi)], wide[at(f, lo, hi, col + p, col + p + 1)]
        )
        total = masked(f, total, row, col, drop_ref)
        here = wide[at(f, row + p, row + p + 1, col + p, col + p + 1)]
        moved = 2.0 * total - 2.0 * here.astype(jnp.float32)
        if row == col:
            moved = moved + unit
        place = banded(f, row, col, col + 1)
        square[place] = total.astype(square.dtype)
        shifted[place] = moved.astype(shifted.dtype)


def right_tile(f, left, right, row, col):
    lo, hi = f.clipped(row, col)
    return dot(left[banded(f, row, lo, hi)], right[at(f, lo, hi, col - f.p, col - f.p + 1)])


def first_sweep_kernel(
    f, drop_ref, shifted, corner, sent_mate, sent_cross, mate, cross,
    correction, fresh, partial, whole, before, after,
):
    h, p = f.h, f.p
    from_below, from_above = sides(f, drop_ref, indexed(f, mate), indexed(f, cross))
    down, up = sides(f, drop_ref, indexed(f, sent_mate), indexed(f, sent_cross))
    spread(f, whole, 0, 0, from_below, under(h))
    spread(f, whole, h, 0, indexed(f, corner), full(h))
    spread(f, whole, 2 * h, 0, from_above, over(h))
    spread(f, before, 0, 0, down, over(h))
    spread(f, after, 0, 0, up, under(h))
    for row, col in f.tiles(f.own_pairs):
        total = masked(f, right_tile(f, shifted, whole, row, col), row, col, drop_ref)
        correction[at(f, row, row + 1, col - p, col - p + 1)] = total.astype(correction.dtype)
    for row, col in f.tiles(f.own_pairs):
        c = col - p
        own_row = row in f.own_pairs
        total = 2.0 * whole[at(f, row, row + 1, c, c + 1)].astype(jnp.float32)
        for g, a, z in f.split(row, col):
            if g == 1:
                left = whole[at(f, row, row + 1, a, z)]
            elif own_row:
                left = (before, None, after)[g][at(f, row - p, row - p + 1, a, z)]
            else:
                continue
            total = total - dot(left, correction[at(f, g * p + a, g * p + z, c, c + 1)])
        if own_row:
            total = masked(f, total, row, col, drop_ref)
            fresh[at(f, row - p, row - p + 1, c, c + 1)] = total.astype(fresh.dtype)
        else:
            place = row if row < p else row - p
            partial[at(f, place, place + 1, c, c + 1)] = total


def edges(f, drop_ref, corner_below, corner_above, correction, start, low, high):
    p = f.p
    for row, col in f.tiles(f.own_pairs):
        if row in f.own_pairs:
            continue
        c = col - p
        side = 0 if row < p else 2
        corner, dest = ((corner_below, low), None, (corner_above, high))[side]
        local = row - side * p
        total = start(row, col)
        for g, a, z in f.split(row, col):
            if g == side:
                total = total - dot(
                    corner(at(f, local, local + 1, a, z)), correction[at(f, g * p + a, g * p + z, c, c + 1)]
                )
        total = masked(f, total, row, col, drop_ref)
        dest[at(f, local, local + 1, c, c + 1)] = total.astype(dest.dtype)


def first_edges_kernel(
    f, drop_ref, mate, cross, correction, partial, low, high, to_mate, to_cross, before, after
):
    p = f.p
    n = len(under(f.h))
    below, above = sides(f, drop_ref, indexed(f, mate, n), indexed(f, cross, n))
    spread(f, before, 0, 0, below, full(f.h))
    spread(f, after, 0, 0, above, full(f.h))

    def start(row, col):
        place = row if row < p else row - p
        return partial[at(f, place, place + 1, col - p, col - p + 1)]

    edges(f, drop_ref, plain(before), plain(after), correction, start, low, high)
    pack_edges(f, drop_ref, low, high, to_mate, to_cross)


def gather(f, whole, low, own, high):
    for g, source in enumerate((low, own, high)):
        for i in range(f.h):
            whole[pl.ds(g * f.group + i * f.b, f.b), :] = source[pl.ds(i * f.b, f.b), :]


def correction_kernel(f, drop_ref, shifted, low, own, high, correction, whole):
    p = f.p
    gather(f, whole, low, own, high)
    for row, col in f.tiles(f.own_pairs):
        total = masked(f, right_tile(f, shifted, whole, row, col), row, col, drop_ref)
        correction[at(f, row, row + 1, col - p, col - p + 1)] = total.astype(correction.dtype)


def second_edges_kernel(
    f, drop_ref, mate, cross, correction, low, high, new_low, new_high, to_mate, to_cross
):
    p = f.p

    def start(row, col):
        c = col - p
        source, local = (low, row) if row < p else (high, row - 2 * p)
        total = 2.0 * source[at(f, local, local + 1, c, c + 1)].astype(jnp.float32)
        for g, a, z in f.split(row, col):
            if g == 1:
                total = total - dot(
                    source[at(f, local, local + 1, a, z)], correction[at(f, p + a, p + z, c, c + 1)]
                )
        return total

    below, above = sides(f, drop_ref, plain(mate), plain(cross))
    edges(f, drop_ref, below, above, correction, start, new_low, new_high)
    pack_edges(f, drop_ref, new_low, new_high, to_mate, to_cross)


def density_edges_kernel(
    f, drop_ref, own, mate, cross, correction, new_low, new_high, square, whole, to_mate, to_cross,
    before, after, low, high,
):
    h, p = f.h, f.p
    below, above = sides(f, drop_ref, indexed(f, mate), indexed(f, cross))
    spread(f, before, 0, 0, below, over(h))
    spread(f, after, 0, 0, above, under(h))
    for row, col in f.tiles(f.own_pairs):
        if row not in f.own_pairs:
            continue
        c, local = col - p, row - p
        total = 2.0 * own[at(f, local, local + 1, c, c + 1)].astype(jnp.float32)
        for g, a, z in f.split(row, col):
            left = (before, own, after)[g][at(f, local, local + 1, a, z)]
            total = total - dot(left, correction[at(f, g * p + a, g * p + z, c, c + 1)])
        total = masked(f, total, row, col, drop_ref)
        whole[at(f, row, row + 1, c, c + 1)] = total.astype(whole.dtype)
    for i in range(h):
        rows = pl.ds(i * f.b, f.b)
        whole[pl.ds(i * f.b, f.b), :] = new_low[rows, :]
        whole[pl.ds(2 * f.group + i * f.b, f.b), :] = new_high[rows, :]
    for row, col in f.tiles(f.own_pairs):
        if row in f.own_pairs:
            continue
        total = masked(f, right_tile(f, square, whole, row, col), row, col, drop_ref)
        dest, local = (low, row) if row < p else (high, row - 2 * p)
        dest[at(f, local, local + 1, col - p, col - p + 1)] = total.astype(dest.dtype)
    pack_edges(f, drop_ref, low, high, to_mate, to_cross)


def density_own_kernel(f, drop_ref, square, whole, out):
    p = f.p
    for row, col in f.tiles(f.own_pairs):
        if row in f.own_pairs:
            total = masked(f, right_tile(f, square, whole, row, col), row, col, drop_ref)
            out[at(f, row - p, row - p + 1, col - p, col - p + 1)] = total.astype(out.dtype)


def rows_kernel(f, first, drop_ref, own, mate, cross, out):
    h = f.h
    below, above = sides(f, drop_ref, indexed(f, mate), indexed(f, cross))
    over_index = {place: i for i, place in enumerate(over(h))}
    under_index = {place: i for i, place in enumerate(under(h))}
    for r in range(h):
        dropped = drop_ref[h + r]

        def at_offset(offset, r=r):
            col = r + offset
            if col < h:
                return below(over_index[r, col])
            if col < 2 * h:
                return own[block(f, first + r, col - h)]
            return above(under_index[r, col - 2 * h])

        for s in range(f.k):
            out[r, s] = jnp.where(dropped <= s, at_offset(s + 1), at_offset(s))


VMEM = pl.BlockSpec(memory_space=pltpu.VMEM)
SMEM = pl.BlockSpec(memory_space=pltpu.SMEM)
ANY = pl.BlockSpec(memory_space=pl.ANY)


def call(kernel, outs, scratch, flops, limit, drop, *args, passed=(), after=()):
    moved = sum(a.size * a.dtype.itemsize for a in args) + sum(s.size * s.dtype.itemsize for s in outs)
    n = len(args)
    return pl.pallas_call(
        kernel,
        out_shape=[*outs, *[jax.ShapeDtypeStruct(a.shape, a.dtype) for a in passed]],
        in_specs=[SMEM] + [VMEM] * n + [ANY] * (len(passed) + len(after)),
        out_specs=[VMEM] * len(outs) + [ANY] * len(passed),
        scratch_shapes=scratch,
        input_output_aliases={1 + n + i: len(outs) + i for i in range(len(passed))},
        compiler_params=pltpu.CompilerParams(vmem_limit_bytes=limit * MIB),
        cost_estimate=pl.CostEstimate(flops=flops, bytes_accessed=moved, transcendentals=0),
    )(drop, *args, *passed, *after)


def routed(x, step):
    size = lax.axis_size(RING)
    return lax.ppermute(x, RING, [(i, (i + step(i)) % size) for i in range(size) if step(i)])


def on_device(density, inverse_start, block_cols):
    rows, width, order, _ = density.shape
    half = width // 2
    ring = lax.axis_size(RING)
    total = rows * ring
    assert rows == half and half % 2 == 0 and ring % 2 == 0
    f = Frame(half, order)
    kind = density.dtype
    me = lax.axis_index(RING)
    odd = (me & 1) == 1

    def mate_step(i):
        return 1 - 2 * (i % 2)

    def cross_step(i):
        return 2 * (i % 2) - 1

    def to_mate(x):
        return routed(x, mate_step)

    def to_cross(x):
        return routed(x, cross_step)

    def absent(columns, first):
        ids = first + jnp.arange(columns.shape[0], dtype=jnp.int32)
        positions = columns - ids[:, None] + half
        positions = positions + jnp.where(positions < 0, total, jnp.where(positions >= total, -total, 0))
        return width * (width + 1) // 2 - jnp.sum(positions, axis=1)

    mate_cols, cross_cols = to_mate(block_cols), to_cross(block_cols)
    density_mate, density_cross = to_mate(density), to_cross(density)

    marks = jnp.reshape(me & 1, (1,))
    near_cols = jnp.concatenate(
        [jnp.where(odd, mate_cols, cross_cols), block_cols, jnp.where(odd, cross_cols, mate_cols)], axis=0
    )
    drop = jnp.concatenate([absent(near_cols, (me - 1) * rows), marks])

    unit = 2 * f.t**3
    count = half * (half + 1) // 2
    square_group = jax.ShapeDtypeStruct((f.group, f.group), kind)
    columns = jax.ShapeDtypeStruct((3 * f.group, f.group), kind)
    band = jax.ShapeDtypeStruct((3 * f.group, (2 * f.p + 1) * f.t), kind)
    triangle = jax.ShapeDtypeStruct((count * order, order), kind)
    listed = jax.ShapeDtypeStruct((half * half * order, order), kind)
    both = jax.ShapeDtypeStruct(((count + half * half) * order, order), kind)
    partial_sums = jax.ShapeDtypeStruct((2 * f.group, f.group), jnp.float32)
    group_scratch = pltpu.VMEM((f.group, f.group), kind)
    whole_scratch = pltpu.VMEM((3 * f.group, f.group), kind)

    def run(kernel, outs, scratch, tiles, limit, *args, **kw):
        return call(functools.partial(kernel, f), outs, scratch, tiles * unit, limit, *args, **kw)

    corner, slab_mate, slab_cross = run(
        slabs_kernel, [listed, both, both], [], 0, 12, drop, inverse_start
    )
    from_mate, from_cross = to_mate(slab_mate), to_cross(slab_cross)
    forward_mate, forward_far = run(
        forward_kernel, [triangle, triangle], [], 0, 8, drop, density_cross, after=(density_mate, from_mate)
    )
    far_mate = to_mate(forward_mate)
    far_far = routed(forward_far, lambda i: 3 * cross_step(i))

    square, shifted = run(
        square_kernel,
        [band, band],
        [pltpu.VMEM((5 * f.group, 5 * f.group), kind)],
        94, 28, drop, density, density_mate, density_cross, far_mate, far_far,
    )
    correction, own, partial = run(
        first_sweep_kernel,
        [columns, square_group, partial_sums],
        [whole_scratch, group_scratch, group_scratch],
        66, 24, drop, shifted, corner, slab_mate, slab_cross, from_mate, from_cross,
    )
    corner_mate, corner_cross = to_mate(own), to_cross(own)
    low, high, edge_mate, edge_cross = run(
        first_edges_kernel,
        [square_group, square_group, triangle, triangle],
        [group_scratch] * 2,
        10, 16, drop, from_mate, from_cross, correction, partial,
    )
    edge_mate, edge_cross = to_mate(edge_mate), to_cross(edge_cross)
    (correction,) = run(
        correction_kernel, [columns], [whole_scratch], 38, 16, drop, shifted, low, own, high
    )
    new_low, new_high, inverse_mate, inverse_cross = run(
        second_edges_kernel,
        [square_group, square_group, triangle, triangle],
        [],
        20, 12, drop, corner_mate, corner_cross, correction, low, high,
    )
    inverse_mate, inverse_cross = to_mate(inverse_mate), to_cross(inverse_cross)
    whole, rim_mate, rim_cross = run(
        density_edges_kernel,
        [columns, triangle, triangle],
        [group_scratch] * 4,
        38, 20, drop, own, edge_mate, edge_cross, correction, new_low, new_high, square,
    )
    rim_mate, rim_cross = to_mate(rim_mate), to_cross(rim_cross)
    (density_own,) = run(density_own_kernel, [square_group], [], 18, 12, drop, square, whole)
    out = jax.ShapeDtypeStruct(density.shape, kind)

    def assembled(own, first, mate, cross):
        return call(functools.partial(rows_kernel, f, first), [out], [], 0, 8, drop, own, mate, cross)[0]

    inverse_next = assembled(whole, half, inverse_mate, inverse_cross)
    density_next = assembled(density_own, 0, rim_mate, rim_cross)
    return density_next, inverse_next


def solution(mesh):
    blocks = P(("grp", "row", "inner"), None, None, None)
    return jax.shard_map(
        on_device,
        mesh=mesh,
        in_specs=(blocks, blocks, P(("grp", "row", "inner"), None)),
        out_specs=(blocks, blocks),
        check_vma=False,
    )
```

```python
import functools

import jax
import jax.numpy as jnp
from jax import lax
from jax.experimental import pallas as pl
from jax.experimental.pallas import tpu as pltpu
from jax.sharding import PartitionSpec as P

RING = ("row", "inner")
MIB = 1024 * 1024


class Frame:
    def __init__(self, half, order):
        self.h = half
        self.b = order
        self.k = 2 * half
        self.p = half // 2
        self.t = 2 * order
        self.group = half * order
        self.pairs = 3 * self.p
        self.own_pairs = range(self.p, 2 * self.p)
        self.edge_rows = [*range(self.p), *range(2 * self.p, 3 * self.p)]

    def tiles(self, columns):
        for col in columns:
            for row in range(max(0, col - self.p), min(self.pairs, col + self.p + 1)):
                yield row, col

    def inner(self, row, col):
        return max(row, col) - self.p, min(row, col) + self.p + 1

    def clipped(self, row, col):
        lo, hi = self.inner(row, col)
        return max(lo, 0), min(hi, self.pairs)

    def split(self, row, col):
        lo, hi = self.clipped(row, col)
        for g in range(3):
            a, z = max(lo, g * self.p), min(hi, (g + 1) * self.p)
            if a < z:
                yield g, a - g * self.p, z - g * self.p


def under(h):
    return [(r, c) for r in range(h) for c in range(r + 1)]


def over(h):
    return [(r, c) for r in range(h) for c in range(r, h)]


def full(h):
    return [(r, c) for r in range(h) for c in range(h)]


def at(f, row_lo, row_hi, col_lo, col_hi):
    t = f.t
    return pl.ds(row_lo * t, (row_hi - row_lo) * t), pl.ds(col_lo * t, (col_hi - col_lo) * t)


def block(f, r, c):
    return pl.ds(r * f.b, f.b), pl.ds(c * f.b, f.b)


def banded(f, row, lo, hi):
    return at(f, row, row + 1, lo - row + f.p, hi - row + f.p)


def dot(a, b):
    return jnp.dot(a, b, preferred_element_type=jnp.float32)


def stored(rows, r, offset, dropped, slots=None):
    last = (rows.shape[1] if slots is None else slots) - 1
    slot = jnp.minimum(offset - (offset > dropped).astype(jnp.int32), last)
    value = rows[r, slot] if slots is None else rows((r, slot))
    return jnp.where(offset == dropped, jnp.zeros_like(value), value)


def masked(f, tile, row, col, drop_ref):
    b = f.b
    parts = []
    for i in range(2):
        r = 2 * row + i
        line = []
        for j in range(2):
            offset = 2 * col + j - r + f.h
            piece = tile[i * b : (i + 1) * b, j * b : (j + 1) * b]
            if 0 <= offset <= f.k:
                piece = jnp.where(drop_ref[r] == offset, 0.0, piece)
            else:
                piece = jnp.zeros_like(piece)
            line.append(piece)
        parts.append(jnp.concatenate(line, axis=1))
    return jnp.concatenate(parts, axis=0)


def odd_place(f, drop_ref):
    return drop_ref[3 * f.h] == 1


def indexed(f, ref, first=0):
    return lambda i: ref[block(f, first + i, 0)]


def plain(ref):
    return lambda place: ref[place]


def sides(f, drop_ref, mate, cross):
    odd = odd_place(f, drop_ref)

    def below(key):
        return jnp.where(odd, mate(key), cross(key))

    def above(key):
        return jnp.where(odd, cross(key), mate(key))

    return below, above


def spread(f, dest, row, col, read, places):
    index = {place: i for i, place in enumerate(places)}
    for r in range(f.h):
        for c in range(f.h):
            i = index.get((r, c))
            dest[block(f, row + r, col + c)] = jnp.zeros((f.b, f.b), dest.dtype) if i is None else read(i)


def pack_edges(f, drop_ref, low, high, to_mate, to_cross):
    odd = odd_place(f, drop_ref)
    for i, (lower, upper) in enumerate(zip(under(f.h), over(f.h))):
        back, forth = low[block(f, *lower)], high[block(f, *upper)]
        to_mate[block(f, i, 0)] = jnp.where(odd, back, forth)
        to_cross[block(f, i, 0)] = jnp.where(odd, forth, back)


def slabs_kernel(f, drop_ref, own, corner, to_mate, to_cross):
    h = f.h
    odd = drop_ref[h] == 1
    n = len(under(h))
    for i, (lower, upper) in enumerate(zip(under(h), over(h))):
        (r, c), (s, d) = lower, upper
        forth = stored(own, r, 2 * h + c - r, drop_ref[r])
        back = stored(own, s, d - s, drop_ref[s])
        to_mate[block(f, i, 0)] = jnp.where(odd, back, forth)
        to_cross[block(f, i, 0)] = jnp.where(odd, forth, back)
    for i, (r, c) in enumerate(full(h)):
        value = stored(own, r, c - r + h, drop_ref[r])
        corner[block(f, i, 0)] = value
        to_mate[block(f, n + i, 0)] = value


def forward_kernel(f, drop_ref, cross, *refs):
    h = f.h
    odd = odd_place(f, drop_ref)
    to_mate, to_far = refs[-4:-2]
    for i, (lower, upper) in enumerate(zip(under(h), over(h))):
        (r, c), (s, d) = lower, upper
        forth = stored(cross, r, 2 * h + c - r, jnp.where(odd, drop_ref[2 * h + r], drop_ref[r]))
        back = stored(cross, s, d - s, jnp.where(odd, drop_ref[2 * h + s], drop_ref[s]))
        to_mate[block(f, i, 0)] = jnp.where(odd, back, forth)
        to_far[block(f, i, 0)] = jnp.where(odd, forth, back)


def square_kernel(f, drop_ref, own, mate, cross, far_mate, far_far, square, shifted, wide):
    h, p = f.h, f.p
    below, above = sides(f, drop_ref, plain(mate), plain(cross))
    for g, read in enumerate((below, plain(own), above)):
        for r in range(h):
            row = g * h + r
            first = 2 * (row // 2) - h
            for col in range(first, first + 2 * h + 2):
                offset = col - row + h
                if 0 <= offset <= f.k:
                    value = stored(read, r, offset, drop_ref[row], f.k)
                else:
                    value = jnp.zeros((f.b, f.b), wide.dtype)
                wide[block(f, row + h, col + h)] = value
    far_below, far_above = sides(f, drop_ref, indexed(f, far_mate), indexed(f, far_far))
    spread(f, wide, 0, h, far_below, under(h))
    spread(f, wide, 4 * h, 3 * h, far_above, over(h))
    unit = (
        lax.broadcasted_iota(jnp.int32, (f.t, f.t), 0) == lax.broadcasted_iota(jnp.int32, (f.t, f.t), 1)
    ).astype(jnp.float32)
    for row, col in f.tiles(range(f.pairs)):
        lo, hi = f.inner(row, col)
        lo, hi = lo + p, hi + p
        total = dot(
            wide[at(f, row + p, row + p + 1, lo, hi)], wide[at(f, lo, hi, col + p, col + p + 1)]
        )
        total = masked(f, total, row, col, drop_ref)
        here = wide[at(f, row + p, row + p + 1, col + p, col + p + 1)]
        moved = 2.0 * total - 2.0 * here.astype(jnp.float32)
        if row == col:
            moved = moved + unit
        place = banded(f, row, col, col + 1)
        square[place] = total.astype(square.dtype)
        shifted[place] = moved.astype(shifted.dtype)


def right_tile(f, left, right, row, col):
    lo, hi = f.clipped(row, col)
    return dot(left[banded(f, row, lo, hi)], right[at(f, lo, hi, col - f.p, col - f.p + 1)])


def first_sweep_kernel(
    f, drop_ref, shifted, corner, sent_mate, sent_cross, mate, cross,
    correction, fresh, partial, whole, before, after,
):
    h, p = f.h, f.p
    from_below, from_above = sides(f, drop_ref, indexed(f, mate), indexed(f, cross))
    down, up = sides(f, drop_ref, indexed(f, sent_mate), indexed(f, sent_cross))
    spread(f, whole, 0, 0, from_below, under(h))
    spread(f, whole, h, 0, indexed(f, corner), full(h))
    spread(f, whole, 2 * h, 0, from_above, over(h))
    spread(f, before, 0, 0, down, over(h))
    spread(f, after, 0, 0, up, under(h))
    for row, col in f.tiles(f.own_pairs):
        total = masked(f, right_tile(f, shifted, whole, row, col), row, col, drop_ref)
        correction[at(f, row, row + 1, col - p, col - p + 1)] = total.astype(correction.dtype)
    for row, col in f.tiles(f.own_pairs):
        c = col - p
        own_row = row in f.own_pairs
        total = 2.0 * whole[at(f, row, row + 1, c, c + 1)].astype(jnp.float32)
        for g, a, z in f.split(row, col):
            if g == 1:
                left = whole[at(f, row, row + 1, a, z)]
            elif own_row:
                left = (before, None, after)[g][at(f, row - p, row - p + 1, a, z)]
            else:
                continue
            total = total - dot(left, correction[at(f, g * p + a, g * p + z, c, c + 1)])
        if own_row:
            total = masked(f, total, row, col, drop_ref)
            fresh[at(f, row - p, row - p + 1, c, c + 1)] = total.astype(fresh.dtype)
        else:
            place = row if row < p else row - p
            partial[at(f, place, place + 1, c, c + 1)] = total


def edges(f, drop_ref, corner_below, corner_above, correction, start, low, high):
    p = f.p
    for row, col in f.tiles(f.own_pairs):
        if row in f.own_pairs:
            continue
        c = col - p
        side = 0 if row < p else 2
        corner, dest = ((corner_below, low), None, (corner_above, high))[side]
        local = row - side * p
        total = start(row, col)
        for g, a, z in f.split(row, col):
            if g == side:
                total = total - dot(
                    corner(at(f, local, local + 1, a, z)), correction[at(f, g * p + a, g * p + z, c, c + 1)]
                )
        total = masked(f, total, row, col, drop_ref)
        dest[at(f, local, local + 1, c, c + 1)] = total.astype(dest.dtype)


def first_edges_kernel(
    f, drop_ref, mate, cross, correction, partial, low, high, to_mate, to_cross, before, after
):
    p = f.p
    n = len(under(f.h))
    below, above = sides(f, drop_ref, indexed(f, mate, n), indexed(f, cross))
    spread(f, before, 0, 0, below, full(f.h))
    spread(f, after, 0, 0, above, full(f.h))

    def start(row, col):
        place = row if row < p else row - p
        return partial[at(f, place, place + 1, col - p, col - p + 1)]

    edges(f, drop_ref, plain(before), plain(after), correction, start, low, high)
    pack_edges(f, drop_ref, low, high, to_mate, to_cross)


def gather(f, whole, low, own, high):
    for g, source in enumerate((low, own, high)):
        for i in range(f.h):
            whole[pl.ds(g * f.group + i * f.b, f.b), :] = source[pl.ds(i * f.b, f.b), :]


def correction_kernel(f, drop_ref, shifted, low, own, high, correction, whole):
    p = f.p
    gather(f, whole, low, own, high)
    for row, col in f.tiles(f.own_pairs):
        total = masked(f, right_tile(f, shifted, whole, row, col), row, col, drop_ref)
        correction[at(f, row, row + 1, col - p, col - p + 1)] = total.astype(correction.dtype)


def second_edges_kernel(
    f, drop_ref, mate, cross, correction, low, high, new_low, new_high, to_mate, to_cross
):
    p = f.p

    def start(row, col):
        c = col - p
        source, local = (low, row) if row < p else (high, row - 2 * p)
        total = 2.0 * source[at(f, local, local + 1, c, c + 1)].astype(jnp.float32)
        for g, a, z in f.split(row, col):
            if g == 1:
                total = total - dot(
                    source[at(f, local, local + 1, a, z)], correction[at(f, p + a, p + z, c, c + 1)]
                )
        return total

    below, above = sides(f, drop_ref, plain(mate), plain(cross))
    edges(f, drop_ref, below, above, correction, start, new_low, new_high)
    pack_edges(f, drop_ref, new_low, new_high, to_mate, to_cross)


def density_edges_kernel(
    f, drop_ref, own, mate, cross, correction, new_low, new_high, square, whole, to_mate, to_cross,
    before, after, low, high,
):
    h, p = f.h, f.p
    below, above = sides(f, drop_ref, indexed(f, mate), indexed(f, cross))
    spread(f, before, 0, 0, below, over(h))
    spread(f, after, 0, 0, above, under(h))
    for row, col in f.tiles(f.own_pairs):
        if row not in f.own_pairs:
            continue
        c, local = col - p, row - p
        total = 2.0 * own[at(f, local, local + 1, c, c + 1)].astype(jnp.float32)
        for g, a, z in f.split(row, col):
            left = (before, own, after)[g][at(f, local, local + 1, a, z)]
            total = total - dot(left, correction[at(f, g * p + a, g * p + z, c, c + 1)])
        total = masked(f, total, row, col, drop_ref)
        whole[at(f, row, row + 1, c, c + 1)] = total.astype(whole.dtype)
    for i in range(h):
        rows = pl.ds(i * f.b, f.b)
        whole[pl.ds(i * f.b, f.b), :] = new_low[rows, :]
        whole[pl.ds(2 * f.group + i * f.b, f.b), :] = new_high[rows, :]
    for row, col in f.tiles(f.own_pairs):
        if row in f.own_pairs:
            continue
        total = masked(f, right_tile(f, square, whole, row, col), row, col, drop_ref)
        dest, local = (low, row) if row < p else (high, row - 2 * p)
        dest[at(f, local, local + 1, col - p, col - p + 1)] = total.astype(dest.dtype)
    pack_edges(f, drop_ref, low, high, to_mate, to_cross)


def density_own_kernel(f, drop_ref, square, whole, out):
    p = f.p
    for row, col in f.tiles(f.own_pairs):
        if row in f.own_pairs:
            total = masked(f, right_tile(f, square, whole, row, col), row, col, drop_ref)
            out[at(f, row - p, row - p + 1, col - p, col - p + 1)] = total.astype(out.dtype)


def rows_kernel(f, first, drop_ref, own, mate, cross, out):
    h = f.h
    below, above = sides(f, drop_ref, indexed(f, mate), indexed(f, cross))
    over_index = {place: i for i, place in enumerate(over(h))}
    under_index = {place: i for i, place in enumerate(under(h))}
    for r in range(h):
        dropped = drop_ref[h + r]

        def at_offset(offset, r=r):
            col = r + offset
            if col < h:
                return below(over_index[r, col])
            if col < 2 * h:
                return own[block(f, first + r, col - h)]
            return above(under_index[r, col - 2 * h])

        for s in range(f.k):
            out[r, s] = jnp.where(dropped <= s, at_offset(s + 1), at_offset(s))


VMEM = pl.BlockSpec(memory_space=pltpu.VMEM)
SMEM = pl.BlockSpec(memory_space=pltpu.SMEM)
ANY = pl.BlockSpec(memory_space=pl.ANY)


def call(kernel, outs, scratch, flops, limit, drop, *args, passed=(), after=()):
    moved = sum(a.size * a.dtype.itemsize for a in args) + sum(s.size * s.dtype.itemsize for s in outs)
    n = len(args)
    return pl.pallas_call(
        kernel,
        out_shape=[*outs, *[jax.ShapeDtypeStruct(a.shape, a.dtype) for a in passed]],
        in_specs=[SMEM] + [VMEM] * n + [ANY] * (len(passed) + len(after)),
        out_specs=[VMEM] * len(outs) + [ANY] * len(passed),
        scratch_shapes=scratch,
        input_output_aliases={1 + n + i: len(outs) + i for i in range(len(passed))},
        compiler_params=pltpu.CompilerParams(vmem_limit_bytes=limit * MIB),
        cost_estimate=pl.CostEstimate(flops=flops, bytes_accessed=moved, transcendentals=0),
    )(drop, *args, *passed, *after)


def routed(x, step):
    size = lax.axis_size(RING)
    return lax.ppermute(x, RING, [(i, (i + step(i)) % size) for i in range(size) if step(i)])


def on_device(density, inverse_start, block_cols):
    rows, width, order, _ = density.shape
    half = width // 2
    ring = lax.axis_size(RING)
    total = rows * ring
    assert rows == half and half % 2 == 0 and ring % 2 == 0
    f = Frame(half, order)
    kind = density.dtype
    me = lax.axis_index(RING)
    odd = (me & 1) == 1

    def mate_step(i):
        return 1 - 2 * (i % 2)

    def cross_step(i):
        return 2 * (i % 2) - 1

    def to_mate(x):
        return routed(x, mate_step)

    def to_cross(x):
        return routed(x, cross_step)

    positions = block_cols - (me * rows + jnp.arange(rows, dtype=jnp.int32))[:, None] + half
    positions = positions + jnp.where(positions < 0, total, jnp.where(positions >= total, -total, 0))
    own_drop = width * (width + 1) // 2 - jnp.sum(positions, axis=1)

    density_mate, density_cross = to_mate(density), to_cross(density)
    mate_drop, cross_drop = to_mate(own_drop), to_cross(own_drop)
    mark = jnp.reshape(me & 1, (1,))
    start_drop = jnp.concatenate([own_drop, mark])
    drop = jnp.concatenate(
        [jnp.where(odd, mate_drop, cross_drop), own_drop, jnp.where(odd, cross_drop, mate_drop), mark]
    )

    unit = 2 * f.t**3
    count = half * (half + 1) // 2
    square_group = jax.ShapeDtypeStruct((f.group, f.group), kind)
    columns = jax.ShapeDtypeStruct((3 * f.group, f.group), kind)
    band = jax.ShapeDtypeStruct((3 * f.group, (2 * f.p + 1) * f.t), kind)
    triangle = jax.ShapeDtypeStruct((count * order, order), kind)
    listed = jax.ShapeDtypeStruct((half * half * order, order), kind)
    both = jax.ShapeDtypeStruct(((count + half * half) * order, order), kind)
    partial_sums = jax.ShapeDtypeStruct((2 * f.group, f.group), jnp.float32)
    group_scratch = pltpu.VMEM((f.group, f.group), kind)
    whole_scratch = pltpu.VMEM((3 * f.group, f.group), kind)

    def run(kernel, outs, scratch, tiles, limit, *args, **kw):
        return call(functools.partial(kernel, f), outs, scratch, tiles * unit, limit, *args, **kw)

    corner, slab_mate, triangle_cross = run(
        slabs_kernel, [listed, both, triangle], [], 0, 12, start_drop, inverse_start
    )
    from_mate = to_mate(slab_mate)
    forward_mate, forward_far, triangle_cross, corner = run(
        forward_kernel, [triangle, triangle], [], 0, 8, drop, density_cross,
        passed=(triangle_cross, corner), after=(density_mate,),
    )
    far_mate = to_mate(forward_mate)
    far_far = routed(forward_far, lambda i: 3 * cross_step(i))
    cross_triangle, cross_corner = to_cross(triangle_cross), to_cross(corner)

    square, shifted = run(
        square_kernel,
        [band, band],
        [pltpu.VMEM((5 * f.group, 5 * f.group), kind)],
        94, 28, drop, density, density_mate, density_cross, far_mate, far_far,
    )
    correction, own, partial = run(
        first_sweep_kernel,
        [columns, square_group, partial_sums],
        [whole_scratch, group_scratch, group_scratch],
        66, 24, drop, shifted, corner, slab_mate, triangle_cross, from_mate, cross_triangle,
    )
    corner_mate, corner_cross = to_mate(own), to_cross(own)
    low, high, edge_mate, edge_cross = run(
        first_edges_kernel,
        [square_group, square_group, triangle, triangle],
        [group_scratch] * 2,
        10, 16, drop, from_mate, cross_corner, correction, partial,
    )
    edge_mate, edge_cross = to_mate(edge_mate), to_cross(edge_cross)
    (correction,) = run(
        correction_kernel, [columns], [whole_scratch], 38, 16, drop, shifted, low, own, high
    )
    new_low, new_high, inverse_mate, inverse_cross = run(
        second_edges_kernel,
        [square_group, square_group, triangle, triangle],
        [],
        20, 12, drop, corner_mate, corner_cross, correction, low, high,
    )
    inverse_mate, inverse_cross = to_mate(inverse_mate), to_cross(inverse_cross)
    whole, rim_mate, rim_cross = run(
        density_edges_kernel,
        [columns, triangle, triangle],
        [group_scratch] * 4,
        38, 20, drop, own, edge_mate, edge_cross, correction, new_low, new_high, square,
    )
    rim_mate, rim_cross = to_mate(rim_mate), to_cross(rim_cross)
    (density_own,) = run(density_own_kernel, [square_group], [], 18, 12, drop, square, whole)
    out = jax.ShapeDtypeStruct(density.shape, kind)

    def assembled(own, first, mate, cross):
        return call(functools.partial(rows_kernel, f, first), [out], [], 0, 8, drop, own, mate, cross)[0]

    inverse_next = assembled(whole, half, inverse_mate, inverse_cross)
    density_next = assembled(density_own, 0, rim_mate, rim_cross)
    return density_next, inverse_next


def solution(mesh):
    blocks = P(("grp", "row", "inner"), None, None, None)
    return jax.shard_map(
        on_device,
        mesh=mesh,
        in_specs=(blocks, blocks, P(("grp", "row", "inner"), None)),
        out_specs=(blocks, blocks),
        check_vma=False,
    )
```

```python
import functools

import jax
import jax.numpy as jnp
from jax import lax
from jax.experimental import pallas as pl
from jax.experimental.pallas import tpu as pltpu
from jax.sharding import PartitionSpec as P

RING = ("row", "inner")
MIB = 1024 * 1024


class Frame:
    def __init__(self, half, order):
        self.h = half
        self.b = order
        self.k = 2 * half
        self.p = half // 2
        self.t = 2 * order
        self.group = half * order
        self.pairs = 3 * self.p
        self.own_pairs = range(self.p, 2 * self.p)
        self.edge_rows = [*range(self.p), *range(2 * self.p, 3 * self.p)]

    def tiles(self, columns):
        for col in columns:
            for row in range(max(0, col - self.p), min(self.pairs, col + self.p + 1)):
                yield row, col

    def inner(self, row, col):
        return max(row, col) - self.p, min(row, col) + self.p + 1

    def clipped(self, row, col):
        lo, hi = self.inner(row, col)
        return max(lo, 0), min(hi, self.pairs)

    def split(self, row, col):
        lo, hi = self.clipped(row, col)
        for g in range(3):
            a, z = max(lo, g * self.p), min(hi, (g + 1) * self.p)
            if a < z:
                yield g, a - g * self.p, z - g * self.p


def under(h):
    return [(r, c) for r in range(h) for c in range(r + 1)]


def over(h):
    return [(r, c) for r in range(h) for c in range(r, h)]


def at(f, row_lo, row_hi, col_lo, col_hi):
    t = f.t
    return pl.ds(row_lo * t, (row_hi - row_lo) * t), pl.ds(col_lo * t, (col_hi - col_lo) * t)


def block(f, r, c):
    return pl.ds(r * f.b, f.b), pl.ds(c * f.b, f.b)


def banded(f, row, lo, hi):
    return at(f, row, row + 1, lo - row + f.p, hi - row + f.p)


def dot(a, b):
    return jnp.dot(a, b, preferred_element_type=jnp.float32)


def stored(rows, r, offset, dropped):
    slot = jnp.minimum(offset - (offset > dropped).astype(jnp.int32), rows.shape[1] - 1)
    value = rows[r, slot]
    return jnp.where(offset == dropped, jnp.zeros_like(value), value)


def spread(f, dest, row, col, packed, places):
    index = {place: i for i, place in enumerate(places)}
    for r in range(f.h):
        for c in range(f.h):
            i = index.get((r, c))
            value = jnp.zeros((f.b, f.b), dest.dtype) if i is None else packed[i]
            dest[block(f, row + r, col + c)] = value


def pack(f, source, row, packed, places):
    for i, (r, c) in enumerate(places):
        packed[i] = source[block(f, row + r, c)]


def masked(f, tile, row, col, drop_ref):
    b = f.b
    parts = []
    for i in range(2):
        r = 2 * row + i
        line = []
        for j in range(2):
            offset = 2 * col + j - r + f.h
            piece = tile[i * b : (i + 1) * b, j * b : (j + 1) * b]
            if 0 <= offset <= f.k:
                piece = jnp.where(drop_ref[r] == offset, 0.0, piece)
            else:
                piece = jnp.zeros_like(piece)
            line.append(piece)
        parts.append(jnp.concatenate(line, axis=1))
    return jnp.concatenate(parts, axis=0)


def slabs_kernel(f, drop_ref, own, corner, up, down):
    h = f.h
    for r in range(h):
        for c in range(h):
            corner[block(f, r, c)] = stored(own, r, c - r + h, drop_ref[r])
    for i, (r, c) in enumerate(under(h)):
        up[i] = stored(own, r, 2 * h + c - r, drop_ref[r])
    for i, (r, c) in enumerate(over(h)):
        down[i] = stored(own, r, c - r, drop_ref[r])


def forward_kernel(f, drop_ref, below, above, *refs):
    h = f.h
    far_up, far_down = refs[3:5]
    odd = drop_ref[3 * h] == 1

    def send(rows, first):
        for i, (r, c) in enumerate(under(h)):
            far_up[i] = stored(rows, r, 2 * h + c - r, drop_ref[first + r])
        for i, (r, c) in enumerate(over(h)):
            far_down[i] = stored(rows, r, c - r, drop_ref[first + r])

    @pl.when(odd)
    def _():
        send(above, 2 * h)

    @pl.when(jnp.logical_not(odd))
    def _():
        send(below, 0)


def square_kernel(f, drop_ref, own, below, above, far_below, far_above, square, shifted, wide):
    h, p = f.h, f.p
    for g, source in enumerate((below, own, above)):
        for r in range(h):
            row = g * h + r
            first = 2 * (row // 2) - h
            for col in range(first, first + 2 * h + 2):
                offset = col - row + h
                if 0 <= offset <= f.k:
                    value = stored(source, r, offset, drop_ref[row])
                else:
                    value = jnp.zeros((f.b, f.b), wide.dtype)
                wide[block(f, row + h, col + h)] = value
    spread(f, wide, 0, h, far_below, under(h))
    spread(f, wide, 4 * h, 3 * h, far_above, over(h))
    unit = (
        lax.broadcasted_iota(jnp.int32, (f.t, f.t), 0) == lax.broadcasted_iota(jnp.int32, (f.t, f.t), 1)
    ).astype(jnp.float32)
    for row, col in f.tiles(range(f.pairs)):
        lo, hi = f.inner(row, col)
        lo, hi = lo + p, hi + p
        total = dot(
            wide[at(f, row + p, row + p + 1, lo, hi)], wide[at(f, lo, hi, col + p, col + p + 1)]
        )
        total = masked(f, total, row, col, drop_ref)
        here = wide[at(f, row + p, row + p + 1, col + p, col + p + 1)]
        moved = 2.0 * total - 2.0 * here.astype(jnp.float32)
        if row == col:
            moved = moved + unit
        place = banded(f, row, col, col + 1)
        square[place] = total.astype(square.dtype)
        shifted[place] = moved.astype(shifted.dtype)


def right_tile(f, left, right, row, col):
    lo, hi = f.clipped(row, col)
    return dot(left[banded(f, row, lo, hi)], right[at(f, lo, hi, col - f.p, col - f.p + 1)])


def first_sweep_kernel(
    f, drop_ref, shifted, corner, up, down, from_below, from_above, correction, fresh, partial, whole, before, after
):
    h, p = f.h, f.p
    spread(f, whole, 0, 0, from_below, under(h))
    for i in range(h):
        rows = pl.ds(i * f.b, f.b)
        whole[pl.ds((h + i) * f.b, f.b), :] = corner[rows, :]
    spread(f, whole, 2 * h, 0, from_above, over(h))
    spread(f, before, 0, 0, down, over(h))
    spread(f, after, 0, 0, up, under(h))
    for row, col in f.tiles(f.own_pairs):
        total = masked(f, right_tile(f, shifted, whole, row, col), row, col, drop_ref)
        correction[at(f, row, row + 1, col - p, col - p + 1)] = total.astype(correction.dtype)
    for row, col in f.tiles(f.own_pairs):
        c = col - p
        own_row = row in f.own_pairs
        total = 2.0 * whole[at(f, row, row + 1, c, c + 1)].astype(jnp.float32)
        for g, a, z in f.split(row, col):
            if g == 1:
                left = whole[at(f, row, row + 1, a, z)]
            elif own_row:
                left = (before, None, after)[g][at(f, row - p, row - p + 1, a, z)]
            else:
                continue
            total = total - dot(left, correction[at(f, g * p + a, g * p + z, c, c + 1)])
        if own_row:
            total = masked(f, total, row, col, drop_ref)
            fresh[at(f, row - p, row - p + 1, c, c + 1)] = total.astype(fresh.dtype)
        else:
            place = row if row < p else row - p
            partial[at(f, place, place + 1, c, c + 1)] = total


def edges(f, drop_ref, corner_below, corner_above, correction, start, low, high):
    p = f.p
    for row, col in f.tiles(f.own_pairs):
        if row in f.own_pairs:
            continue
        c = col - p
        side = 0 if row < p else 2
        corner, dest = ((corner_below, low), None, (corner_above, high))[side]
        local = row - side * p
        total = start(row, col)
        for g, a, z in f.split(row, col):
            if g == side:
                total = total - dot(
                    corner[at(f, local, local + 1, a, z)], correction[at(f, g * p + a, g * p + z, c, c + 1)]
                )
        total = masked(f, total, row, col, drop_ref)
        dest[at(f, local, local + 1, c, c + 1)] = total.astype(dest.dtype)


def first_edges_kernel(f, drop_ref, corner_below, corner_above, correction, partial, low, high, to_prev, to_next):
    p = f.p

    def start(row, col):
        place = row if row < p else row - p
        return partial[at(f, place, place + 1, col - p, col - p + 1)]

    edges(f, drop_ref, corner_below, corner_above, correction, start, low, high)
    pack(f, low, 0, to_prev, under(f.h))
    pack(f, high, 0, to_next, over(f.h))


def gather(f, whole, low, own, high):
    for g, source in enumerate((low, own, high)):
        for i in range(f.h):
            whole[pl.ds(g * f.group + i * f.b, f.b), :] = source[pl.ds(i * f.b, f.b), :]


def correction_kernel(f, drop_ref, shifted, low, own, high, correction, whole):
    p = f.p
    gather(f, whole, low, own, high)
    for row, col in f.tiles(f.own_pairs):
        total = masked(f, right_tile(f, shifted, whole, row, col), row, col, drop_ref)
        correction[at(f, row, row + 1, col - p, col - p + 1)] = total.astype(correction.dtype)


def second_edges_kernel(
    f, drop_ref, corner_below, corner_above, correction, low, high, new_low, new_high, to_prev, to_next
):
    p = f.p

    def start(row, col):
        c = col - p
        source, local = (low, row) if row < p else (high, row - 2 * p)
        total = 2.0 * source[at(f, local, local + 1, c, c + 1)].astype(jnp.float32)
        for g, a, z in f.split(row, col):
            if g == 1:
                total = total - dot(
                    source[at(f, local, local + 1, a, z)], correction[at(f, p + a, p + z, c, c + 1)]
                )
        return total

    edges(f, drop_ref, corner_below, corner_above, correction, start, new_low, new_high)
    pack(f, new_low, 0, to_prev, under(f.h))
    pack(f, new_high, 0, to_next, over(f.h))


def density_edges_kernel(
    f, drop_ref, own, from_below, from_above, correction, new_low, new_high, square, whole, to_prev, to_next,
    before, after, low, high,
):
    h, p = f.h, f.p
    spread(f, before, 0, 0, from_below, over(h))
    spread(f, after, 0, 0, from_above, under(h))
    for row, col in f.tiles(f.own_pairs):
        if row not in f.own_pairs:
            continue
        c, local = col - p, row - p
        total = 2.0 * own[at(f, local, local + 1, c, c + 1)].astype(jnp.float32)
        for g, a, z in f.split(row, col):
            left = (before, own, after)[g][at(f, local, local + 1, a, z)]
            total = total - dot(left, correction[at(f, g * p + a, g * p + z, c, c + 1)])
        total = masked(f, total, row, col, drop_ref)
        whole[at(f, row, row + 1, c, c + 1)] = total.astype(whole.dtype)
    for i in range(h):
        rows = pl.ds(i * f.b, f.b)
        whole[pl.ds(i * f.b, f.b), :] = new_low[rows, :]
        whole[pl.ds(2 * f.group + i * f.b, f.b), :] = new_high[rows, :]
    for row, col in f.tiles(f.own_pairs):
        if row in f.own_pairs:
            continue
        total = masked(f, right_tile(f, square, whole, row, col), row, col, drop_ref)
        dest, local = (low, row) if row < p else (high, row - 2 * p)
        dest[at(f, local, local + 1, col - p, col - p + 1)] = total.astype(dest.dtype)
    pack(f, low, 0, to_prev, under(h))
    pack(f, high, 0, to_next, over(h))


def own_outputs_kernel(f, drop_ref, square, whole, density_out, inverse_out, scratch):
    p = f.p
    for row, col in f.tiles(f.own_pairs):
        if row in f.own_pairs:
            total = masked(f, right_tile(f, square, whole, row, col), row, col, drop_ref)
            scratch[at(f, row - p, row - p + 1, col - p, col - p + 1)] = total.astype(scratch.dtype)
    own_slots(f, drop_ref, lambda r, c: scratch[block(f, r, c)], density_out)
    own_slots(f, drop_ref, lambda r, c: whole[block(f, f.h + r, c)], inverse_out)


def own_slots(f, drop_ref, read, out):
    h = f.h
    for r in range(h):
        dropped = drop_ref[h + r]
        for c in range(h):
            offset = c - r + h
            slot = jnp.minimum(offset - (offset > dropped).astype(jnp.int32), f.k - 1)

            @pl.when(offset != dropped)
            def _(r=r, c=c, slot=slot):
                out[r, slot] = read(r, c)


def side_slots_kernel(f, drop_ref, from_below, from_above, *refs):
    h = f.h
    token, out, sems = refs[-3:]
    token[...] = jnp.zeros_like(token)
    copies = []
    for g, (source, places) in enumerate(((from_below, over(h)), (from_above, under(h)))):
        for i, (r, c) in enumerate(places):
            offset = c - r + 2 * h * g
            dropped = drop_ref[h + r]
            slot = jnp.minimum(offset - (offset > dropped).astype(jnp.int32), f.k - 1)
            copy = pltpu.make_async_copy(source.at[i], out.at[r, slot], sems.at[len(copies)])
            copies.append((offset != dropped, copy))
    for present, copy in copies:
        pl.when(present)(copy.start)
    for present, copy in copies:
        pl.when(present)(copy.wait)


VMEM = pl.BlockSpec(memory_space=pltpu.VMEM)
SMEM = pl.BlockSpec(memory_space=pltpu.SMEM)
ANY = pl.BlockSpec(memory_space=pl.ANY)


def call(kernel, outs, scratch, flops, limit, drop, *args, passed=(), after=()):
    n = len(args)
    return pl.pallas_call(
        kernel,
        out_shape=[*outs, *[jax.ShapeDtypeStruct(a.shape, a.dtype) for a in passed]],
        in_specs=[SMEM] + [VMEM] * n + [ANY] * (len(passed) + len(after)),
        out_specs=[VMEM] * len(outs) + [ANY] * len(passed),
        scratch_shapes=scratch,
        input_output_aliases={1 + n + i: len(outs) + i for i in range(len(passed))},
        compiler_params=pltpu.CompilerParams(vmem_limit_bytes=limit * MIB),
        cost_estimate=pl.CostEstimate(flops=flops, bytes_accessed=0, transcendentals=0),
    )(drop, *args, *passed, *after)


def permuted(x, step):
    size = lax.axis_size(RING)
    return lax.ppermute(x, RING, [(i, (i + step(i)) % size) for i in range(size)])


def to_next(x):
    return permuted(x, lambda i: 1)


def to_prev(x):
    return permuted(x, lambda i: -1)


def on_device(density, inverse_start, block_cols):
    rows, width, order, _ = density.shape
    half = width // 2
    ring = lax.axis_size(RING)
    assert rows == half and half % 2 == 0 and ring % 2 == 0
    f = Frame(half, order)
    kind = density.dtype
    me = lax.axis_index(RING)
    total = rows * ring

    positions = block_cols - (me * rows + jnp.arange(rows, dtype=jnp.int32))[:, None] + half
    positions = positions + jnp.where(positions < 0, total, jnp.where(positions >= total, -total, 0))
    own_drop = width * (width + 1) // 2 - jnp.sum(positions, axis=1)

    below, above = to_next(density), to_prev(density)
    odd = jnp.reshape(me & 1, (1,))
    drop = jnp.concatenate([to_next(own_drop), own_drop, to_prev(own_drop), odd])

    unit = 2 * f.t**3
    square_group = jax.ShapeDtypeStruct((f.group, f.group), kind)
    columns = jax.ShapeDtypeStruct((3 * f.group, f.group), kind)
    band = jax.ShapeDtypeStruct((3 * f.group, (2 * f.p + 1) * f.t), kind)
    triangle = jax.ShapeDtypeStruct((half * (half + 1) // 2, order, order), kind)
    partial_sums = jax.ShapeDtypeStruct((2 * f.group, f.group), jnp.float32)
    group_scratch = pltpu.VMEM((f.group, f.group), kind)
    whole_scratch = pltpu.VMEM((3 * f.group, f.group), kind)

    def run(kernel, outs, scratch, tiles, limit, *args, **kw):
        return call(functools.partial(kernel, f), outs, scratch, tiles * unit, limit, *args, **kw)

    corner, up, down = run(
        slabs_kernel, [square_group, triangle, triangle], [], 0, 8, own_drop, inverse_start
    )
    far_up, far_down, corner, up, down = run(
        forward_kernel, [triangle, triangle], [], 0, 8, drop, below, above, passed=(corner, up, down)
    )
    far_below = permuted(far_up, lambda i: 1 + 2 * (i % 2))
    far_above = permuted(far_down, lambda i: -3 + 2 * (i % 2))
    from_below, from_above = to_next(up), to_prev(down)
    corner_below, corner_above = to_next(corner), to_prev(corner)

    square, shifted = run(
        square_kernel,
        [band, band],
        [pltpu.VMEM((5 * f.group, 5 * f.group), kind)],
        94, 28, drop, density, below, above, far_below, far_above,
    )
    correction, own, partial = run(
        first_sweep_kernel,
        [columns, square_group, partial_sums],
        [whole_scratch, group_scratch, group_scratch],
        66, 20, drop, shifted, corner, up, down, from_below, from_above,
    )
    next_corner_below, next_corner_above = to_next(own), to_prev(own)
    low, high, back, forth = run(
        first_edges_kernel,
        [square_group, square_group, triangle, triangle],
        [],
        10, 12, drop, corner_below, corner_above, correction, partial,
    )
    from_above, from_below = to_prev(back), to_next(forth)
    (correction,) = run(
        correction_kernel, [columns], [whole_scratch], 38, 16, drop, shifted, low, own, high
    )
    new_low, new_high, back, forth = run(
        second_edges_kernel,
        [square_group, square_group, triangle, triangle],
        [],
        20, 12, drop, next_corner_below, next_corner_above, correction, low, high,
    )
    inverse_above, inverse_below = to_prev(back), to_next(forth)
    out = jax.ShapeDtypeStruct(density.shape, kind)
    whole, back, forth = run(
        density_edges_kernel,
        [columns, triangle, triangle],
        [group_scratch] * 4,
        38, 24, drop, own, from_below, from_above, correction, new_low, new_high, square,
    )
    density_above, density_below = to_prev(back), to_next(forth)
    density_own, inverse_own = run(own_outputs_kernel, [out, out], [group_scratch], 18, 16, drop, square, whole)

    def completed(own, from_below, from_above, after=()):
        sems = pltpu.SemaphoreType.DMA((2 * triangle.shape[0],))
        token = jax.ShapeDtypeStruct((8, order), jnp.float32)
        return run(
            side_slots_kernel, [token], [sems], 0, 8, drop, from_below, from_above, passed=(own,), after=after
        )

    token, inverse_next = completed(inverse_own, inverse_below, inverse_above)
    _, density_next = completed(density_own, density_below, density_above, after=(token,))
    return density_next, inverse_next


def solution(mesh):
    blocks = P(("grp", "row", "inner"), None, None, None)
    return jax.shard_map(
        on_device,
        mesh=mesh,
        in_specs=(blocks, blocks, P(("grp", "row", "inner"), None)),
        out_specs=(blocks, blocks),
        check_vma=False,
    )
```

```python
import functools

import jax
import jax.numpy as jnp
from jax import lax
from jax.experimental import pallas as pl
from jax.experimental.pallas import tpu as pltpu
from jax.sharding import PartitionSpec as P

RING = ("row", "inner")
MIB = 1024 * 1024


class Frame:
    def __init__(self, half, order):
        self.h = half
        self.b = order
        self.k = 2 * half
        self.p = half // 2
        self.t = 2 * order
        self.group = half * order
        self.pairs = 3 * self.p
        self.own_pairs = range(self.p, 2 * self.p)
        self.edge_rows = [*range(self.p), *range(2 * self.p, 3 * self.p)]

    def tiles(self, columns):
        for col in columns:
            for row in range(max(0, col - self.p), min(self.pairs, col + self.p + 1)):
                yield row, col

    def inner(self, row, col):
        return max(row, col) - self.p, min(row, col) + self.p + 1

    def clipped(self, row, col):
        lo, hi = self.inner(row, col)
        return max(lo, 0), min(hi, self.pairs)

    def split(self, row, col):
        lo, hi = self.clipped(row, col)
        for g in range(3):
            a, z = max(lo, g * self.p), min(hi, (g + 1) * self.p)
            if a < z:
                yield g, a - g * self.p, z - g * self.p


def under(h):
    return [(r, c) for r in range(h) for c in range(r + 1)]


def over(h):
    return [(r, c) for r in range(h) for c in range(r, h)]


def full(h):
    return [(r, c) for r in range(h) for c in range(h)]


def at(f, row_lo, row_hi, col_lo, col_hi):
    t = f.t
    return pl.ds(row_lo * t, (row_hi - row_lo) * t), pl.ds(col_lo * t, (col_hi - col_lo) * t)


def block(f, r, c):
    return pl.ds(r * f.b, f.b), pl.ds(c * f.b, f.b)


def banded(f, row, lo, hi):
    return at(f, row, row + 1, lo - row + f.p, hi - row + f.p)


def dot(a, b):
    return jnp.dot(a, b, preferred_element_type=jnp.float32)


def stored(rows, r, offset, dropped, slots=None):
    last = (rows.shape[1] if slots is None else slots) - 1
    slot = jnp.minimum(offset - (offset > dropped).astype(jnp.int32), last)
    value = rows[r, slot] if slots is None else rows((r, slot))
    return jnp.where(offset == dropped, jnp.zeros_like(value), value)


def masked(f, tile, row, col, drop_ref):
    b = f.b
    parts = []
    for i in range(2):
        r = 2 * row + i
        line = []
        for j in range(2):
            offset = 2 * col + j - r + f.h
            piece = tile[i * b : (i + 1) * b, j * b : (j + 1) * b]
            if 0 <= offset <= f.k:
                piece = jnp.where(drop_ref[r] == offset, 0.0, piece)
            else:
                piece = jnp.zeros_like(piece)
            line.append(piece)
        parts.append(jnp.concatenate(line, axis=1))
    return jnp.concatenate(parts, axis=0)


def odd_place(f, drop_ref):
    return drop_ref[3 * f.h] == 1


def indexed(f, ref, first=0):
    return lambda i: ref[block(f, first + i, 0)]


def plain(ref):
    return lambda place: ref[place]


def sides(f, drop_ref, mate, cross):
    odd = odd_place(f, drop_ref)

    def below(key):
        return jnp.where(odd, mate(key), cross(key))

    def above(key):
        return jnp.where(odd, cross(key), mate(key))

    return below, above


def spread(f, dest, row, col, read, places):
    index = {place: i for i, place in enumerate(places)}
    for r in range(f.h):
        for c in range(f.h):
            i = index.get((r, c))
            dest[block(f, row + r, col + c)] = jnp.zeros((f.b, f.b), dest.dtype) if i is None else read(i)


def pack(f, source, packed, places):
    for i, (r, c) in enumerate(places):
        packed[block(f, i, 0)] = source[block(f, r, c)]


def slabs_kernel(f, drop_ref, own, corner, corner_again, to_mate, to_cross):
    h = f.h
    odd = odd_place(f, drop_ref)
    n = len(under(h))
    for i, (lower, upper) in enumerate(zip(under(h), over(h))):
        (r, c), (s, d) = lower, upper
        forth = stored(own, r, 2 * h + c - r, drop_ref[h + r])
        back = stored(own, s, d - s, drop_ref[h + s])
        to_mate[block(f, i, 0)] = jnp.where(odd, back, forth)
        to_cross[block(f, i, 0)] = jnp.where(odd, forth, back)
    for i, (r, c) in enumerate(full(h)):
        value = stored(own, r, c - r + h, drop_ref[h + r])
        corner[block(f, i, 0)] = value
        corner_again[block(f, i, 0)] = value
        to_mate[block(f, n + i, 0)] = value


def forward_kernel(f, drop_ref, cross, *refs):
    h = f.h
    odd = odd_place(f, drop_ref)
    to_mate, to_far = refs[-4:-2]
    for i, (lower, upper) in enumerate(zip(under(h), over(h))):
        (r, c), (s, d) = lower, upper
        forth = stored(cross, r, 2 * h + c - r, jnp.where(odd, drop_ref[2 * h + r], drop_ref[r]))
        back = stored(cross, s, d - s, jnp.where(odd, drop_ref[2 * h + s], drop_ref[s]))
        to_mate[block(f, i, 0)] = jnp.where(odd, back, forth)
        to_far[block(f, i, 0)] = jnp.where(odd, forth, back)


def square_kernel(f, drop_ref, own, cross, mate, far_far, far_mate, square, shifted, wide):
    h, p = f.h, f.p
    below, above = sides(f, drop_ref, plain(mate), plain(cross))
    for g, read in enumerate((below, plain(own), above)):
        for r in range(h):
            row = g * h + r
            first = 2 * (row // 2) - h
            for col in range(first, first + 2 * h + 2):
                offset = col - row + h
                if 0 <= offset <= f.k:
                    value = stored(read, r, offset, drop_ref[row], f.k)
                else:
                    value = jnp.zeros((f.b, f.b), wide.dtype)
                wide[block(f, row + h, col + h)] = value
    far_below, far_above = sides(f, drop_ref, indexed(f, far_mate), indexed(f, far_far))
    spread(f, wide, 0, h, far_below, under(h))
    spread(f, wide, 4 * h, 3 * h, far_above, over(h))
    unit = (
        lax.broadcasted_iota(jnp.int32, (f.t, f.t), 0) == lax.broadcasted_iota(jnp.int32, (f.t, f.t), 1)
    ).astype(jnp.float32)
    for row, col in f.tiles(range(f.pairs)):
        lo, hi = f.inner(row, col)
        lo, hi = lo + p, hi + p
        total = dot(
            wide[at(f, row + p, row + p + 1, lo, hi)], wide[at(f, lo, hi, col + p, col + p + 1)]
        )
        total = masked(f, total, row, col, drop_ref)
        here = wide[at(f, row + p, row + p + 1, col + p, col + p + 1)]
        moved = 2.0 * total - 2.0 * here.astype(jnp.float32)
        if row == col:
            moved = moved + unit
        place = banded(f, row, col, col + 1)
        square[place] = total.astype(square.dtype)
        shifted[place] = moved.astype(shifted.dtype)


def right_tile(f, left, right, row, col):
    lo, hi = f.clipped(row, col)
    return dot(left[banded(f, row, lo, hi)], right[at(f, lo, hi, col - f.p, col - f.p + 1)])


def first_sweep_kernel(
    f, drop_ref, shifted, corner, sent_mate, sent_cross, mate, cross, unused,
    correction, fresh, partial, whole, before, after,
):
    h, p = f.h, f.p
    from_below, from_above = sides(f, drop_ref, indexed(f, mate), indexed(f, cross))
    down, up = sides(f, drop_ref, indexed(f, sent_mate), indexed(f, sent_cross))
    spread(f, whole, 0, 0, from_below, under(h))
    spread(f, whole, h, 0, indexed(f, corner), full(h))
    spread(f, whole, 2 * h, 0, from_above, over(h))
    spread(f, before, 0, 0, down, over(h))
    spread(f, after, 0, 0, up, under(h))
    for row, col in f.tiles(f.own_pairs):
        total = masked(f, right_tile(f, shifted, whole, row, col), row, col, drop_ref)
        correction[at(f, row, row + 1, col - p, col - p + 1)] = total.astype(correction.dtype)
    for row, col in f.tiles(f.own_pairs):
        c = col - p
        own_row = row in f.own_pairs
        total = 2.0 * whole[at(f, row, row + 1, c, c + 1)].astype(jnp.float32)
        for g, a, z in f.split(row, col):
            if g == 1:
                left = whole[at(f, row, row + 1, a, z)]
            elif own_row:
                left = (before, None, after)[g][at(f, row - p, row - p + 1, a, z)]
            else:
                continue
            total = total - dot(left, correction[at(f, g * p + a, g * p + z, c, c + 1)])
        if own_row:
            total = masked(f, total, row, col, drop_ref)
            fresh[at(f, row - p, row - p + 1, c, c + 1)] = total.astype(fresh.dtype)
        else:
            place = row if row < p else row - p
            partial[at(f, place, place + 1, c, c + 1)] = total


def edges(f, drop_ref, corner_below, corner_above, correction, start, low, high):
    p = f.p
    for row, col in f.tiles(f.own_pairs):
        if row in f.own_pairs:
            continue
        c = col - p
        side = 0 if row < p else 2
        corner, dest = ((corner_below, low), None, (corner_above, high))[side]
        local = row - side * p
        total = start(row, col)
        for g, a, z in f.split(row, col):
            if g == side:
                total = total - dot(
                    corner(at(f, local, local + 1, a, z)), correction[at(f, g * p + a, g * p + z, c, c + 1)]
                )
        total = masked(f, total, row, col, drop_ref)
        dest[at(f, local, local + 1, c, c + 1)] = total.astype(dest.dtype)


def first_edges_kernel(
    f, drop_ref, mate, direct, turned, correction, partial, low, high, to_prev, to_next, before, after
):
    p = f.p
    turning = drop_ref[3 * f.h + 1] == 1
    direct_corner, turned_corner = indexed(f, direct), indexed(f, turned)

    def cross(i):
        return jnp.where(turning, turned_corner(i), direct_corner(i))

    below, above = sides(f, drop_ref, indexed(f, mate, len(under(f.h))), cross)
    spread(f, before, 0, 0, below, full(f.h))
    spread(f, after, 0, 0, above, full(f.h))

    def start(row, col):
        place = row if row < p else row - p
        return partial[at(f, place, place + 1, col - p, col - p + 1)]

    edges(f, drop_ref, plain(before), plain(after), correction, start, low, high)
    pack(f, low, to_prev, under(f.h))
    pack(f, high, to_next, over(f.h))


def gather(f, whole, low, own, high):
    for g, source in enumerate((low, own, high)):
        for i in range(f.h):
            whole[pl.ds(g * f.group + i * f.b, f.b), :] = source[pl.ds(i * f.b, f.b), :]


def correction_kernel(f, drop_ref, shifted, low, own, high, correction, whole):
    p = f.p
    gather(f, whole, low, own, high)
    for row, col in f.tiles(f.own_pairs):
        total = masked(f, right_tile(f, shifted, whole, row, col), row, col, drop_ref)
        correction[at(f, row, row + 1, col - p, col - p + 1)] = total.astype(correction.dtype)


def second_edges_kernel(
    f, drop_ref, corner_below, corner_above, correction, low, high, new_low, new_high, to_prev, to_next
):
    p = f.p

    def start(row, col):
        c = col - p
        source, local = (low, row) if row < p else (high, row - 2 * p)
        total = 2.0 * source[at(f, local, local + 1, c, c + 1)].astype(jnp.float32)
        for g, a, z in f.split(row, col):
            if g == 1:
                total = total - dot(
                    source[at(f, local, local + 1, a, z)], correction[at(f, p + a, p + z, c, c + 1)]
                )
        return total

    edges(f, drop_ref, plain(corner_below), plain(corner_above), correction, start, new_low, new_high)
    pack(f, new_low, to_prev, under(f.h))
    pack(f, new_high, to_next, over(f.h))


def density_edges_kernel(
    f, drop_ref, own, from_below, from_above, correction, new_low, new_high, square, whole, to_prev, to_next,
    before, after, low, high,
):
    h, p = f.h, f.p
    spread(f, before, 0, 0, indexed(f, from_below), over(h))
    spread(f, after, 0, 0, indexed(f, from_above), under(h))
    for row, col in f.tiles(f.own_pairs):
        if row not in f.own_pairs:
            continue
        c, local = col - p, row - p
        total = 2.0 * own[at(f, local, local + 1, c, c + 1)].astype(jnp.float32)
        for g, a, z in f.split(row, col):
            left = (before, own, after)[g][at(f, local, local + 1, a, z)]
            total = total - dot(left, correction[at(f, g * p + a, g * p + z, c, c + 1)])
        total = masked(f, total, row, col, drop_ref)
        whole[at(f, row, row + 1, c, c + 1)] = total.astype(whole.dtype)
    for i in range(h):
        rows = pl.ds(i * f.b, f.b)
        whole[pl.ds(i * f.b, f.b), :] = new_low[rows, :]
        whole[pl.ds(2 * f.group + i * f.b, f.b), :] = new_high[rows, :]
    for row, col in f.tiles(f.own_pairs):
        if row in f.own_pairs:
            continue
        total = masked(f, right_tile(f, square, whole, row, col), row, col, drop_ref)
        dest, local = (low, row) if row < p else (high, row - 2 * p)
        dest[at(f, local, local + 1, col - p, col - p + 1)] = total.astype(dest.dtype)
    pack(f, low, to_prev, under(f.h))
    pack(f, high, to_next, over(f.h))


def density_own_kernel(f, drop_ref, square, whole, out):
    p = f.p
    for row, col in f.tiles(f.own_pairs):
        if row in f.own_pairs:
            total = masked(f, right_tile(f, square, whole, row, col), row, col, drop_ref)
            out[at(f, row - p, row - p + 1, col - p, col - p + 1)] = total.astype(out.dtype)


def rows_kernel(f, first, drop_ref, own, from_below, from_above, out):
    h = f.h
    below, above = indexed(f, from_below), indexed(f, from_above)
    over_index = {place: i for i, place in enumerate(over(h))}
    under_index = {place: i for i, place in enumerate(under(h))}
    for r in range(h):
        dropped = drop_ref[h + r]

        def at_offset(offset, r=r):
            col = r + offset
            if col < h:
                return below(over_index[r, col])
            if col < 2 * h:
                return own[block(f, first + r, col - h)]
            return above(under_index[r, col - 2 * h])

        for s in range(f.k):
            out[r, s] = jnp.where(dropped <= s, at_offset(s + 1), at_offset(s))


VMEM = pl.BlockSpec(memory_space=pltpu.VMEM)
SMEM = pl.BlockSpec(memory_space=pltpu.SMEM)
ANY = pl.BlockSpec(memory_space=pl.ANY)


def call(kernel, outs, scratch, flops, limit, drop, *args, passed=(), light=False):
    moved = sum(a.size * a.dtype.itemsize for a in args) + sum(s.size * s.dtype.itemsize for s in outs)
    if light:
        flops = moved = 0
    n = len(args)
    return pl.pallas_call(
        kernel,
        out_shape=[*outs, *[jax.ShapeDtypeStruct(a.shape, a.dtype) for a in passed]],
        in_specs=[SMEM] + [VMEM] * n + [ANY] * len(passed),
        out_specs=[VMEM] * len(outs) + [ANY] * len(passed),
        scratch_shapes=scratch,
        input_output_aliases={1 + n + i: len(outs) + i for i in range(len(passed))},
        compiler_params=pltpu.CompilerParams(vmem_limit_bytes=limit * MIB),
        cost_estimate=pl.CostEstimate(flops=flops, bytes_accessed=moved, transcendentals=0),
    )(drop, *args, *passed)


def routed(x, step):
    size = lax.axis_size(RING)
    return lax.ppermute(x, RING, [(i, (i + step(i)) % size) for i in range(size) if step(i)])


def on_device(density, inverse_start, block_cols):
    rows, width, order, _ = density.shape
    half = width // 2
    ring, inner = lax.axis_size(RING), lax.axis_size(RING[1])
    total = rows * ring
    assert rows == half and half % 2 == 0 and inner % 2 == 0
    f = Frame(half, order)
    kind = density.dtype
    me = lax.axis_index(RING)

    def mate_step(i):
        return 1 - 2 * (i % 2)

    def cross_step(i):
        return 2 * (i % 2) - 1

    def to_mate(x):
        return routed(x, mate_step)

    def to_cross(x):
        return routed(x, cross_step)

    def to_next(x):
        return routed(x, lambda i: 1)

    def to_prev(x):
        return routed(x, lambda i: -1)

    def turns(i):
        return i % inner in (0, inner - 1)

    cross_cols = to_cross(block_cols)
    density_cross = to_cross(density)
    mate_cols = to_mate(block_cols)
    density_mate = to_mate(density)

    even = (me & 1) == 0
    near_cols = jnp.concatenate(
        [jnp.where(even, cross_cols, mate_cols), block_cols, jnp.where(even, mate_cols, cross_cols)], axis=0
    )
    ids = (me - 1) * rows + jnp.arange(3 * rows, dtype=jnp.int32)
    positions = near_cols - ids[:, None] + half
    positions = positions + jnp.where(positions < 0, total, jnp.where(positions >= total, -total, 0))
    absent = width * (width + 1) // 2 - jnp.sum(positions, axis=1)
    place = lax.axis_index(RING[1])
    marks = jnp.stack([~even, (place == 0) | (place == inner - 1)]).astype(jnp.int32)
    drop = jnp.concatenate([absent, marks])

    unit = 2 * f.t**3
    count = half * (half + 1) // 2
    square_group = jax.ShapeDtypeStruct((f.group, f.group), kind)
    columns = jax.ShapeDtypeStruct((3 * f.group, f.group), kind)
    band = jax.ShapeDtypeStruct((3 * f.group, (2 * f.p + 1) * f.t), kind)
    triangle = jax.ShapeDtypeStruct((count * order, order), kind)
    listed = jax.ShapeDtypeStruct((half * half * order, order), kind)
    both = jax.ShapeDtypeStruct(((count + half * half) * order, order), kind)
    partial_sums = jax.ShapeDtypeStruct((2 * f.group, f.group), jnp.float32)
    group_scratch = pltpu.VMEM((f.group, f.group), kind)
    whole_scratch = pltpu.VMEM((3 * f.group, f.group), kind)

    def run(kernel, outs, scratch, tiles, limit, *args, **kw):
        return call(functools.partial(kernel, f), outs, scratch, tiles * unit, limit, *args, **kw)

    corner, corner_turning, slab_mate, triangle_cross = run(
        slabs_kernel, [listed, listed, both, triangle], [], 0, 12, drop, inverse_start
    )
    from_mate = to_mate(slab_mate)
    direct = routed(corner, lambda i: 0 if turns(i) else cross_step(i))
    forward_mate, forward_far, triangle_cross, corner_turning = run(
        forward_kernel, [triangle, triangle], [], 0, 12, drop, density_cross, density_mate, from_mate,
        passed=(triangle_cross, corner_turning),
    )
    far_mate = to_mate(forward_mate)
    far_far = routed(forward_far, lambda i: 3 * cross_step(i))
    cross_triangle = to_cross(triangle_cross)
    turned = routed(corner_turning, lambda i: cross_step(i) if turns(i) else 0)

    square, shifted = run(
        square_kernel,
        [band, band],
        [pltpu.VMEM((5 * f.group, 5 * f.group), kind)],
        94, 28, drop, density, density_cross, density_mate, far_far, far_mate, light=True,
    )
    correction, own, partial = run(
        first_sweep_kernel,
        [columns, square_group, partial_sums],
        [whole_scratch, group_scratch, group_scratch],
        66, 24, drop, shifted, corner, slab_mate, triangle_cross, from_mate, cross_triangle, direct,
    )
    next_corner_below, next_corner_above = to_next(own), to_prev(own)
    low, high, back, forth = run(
        first_edges_kernel,
        [square_group, square_group, triangle, triangle],
        [group_scratch] * 2,
        10, 16, drop, from_mate, direct, turned, correction, partial,
    )
    from_above, from_below = to_prev(back), to_next(forth)
    (correction,) = run(
        correction_kernel, [columns], [whole_scratch], 38, 16, drop, shifted, low, own, high
    )
    new_low, new_high, back, forth = run(
        second_edges_kernel,
        [square_group, square_group, triangle, triangle],
        [],
        20, 12, drop, next_corner_below, next_corner_above, correction, low, high,
    )
    inverse_above, inverse_below = to_prev(back), to_next(forth)
    whole, back, forth = run(
        density_edges_kernel,
        [columns, triangle, triangle],
        [group_scratch] * 4,
        38, 20, drop, own, from_below, from_above, correction, new_low, new_high, square,
    )
    density_above, density_below = to_prev(back), to_next(forth)
    (density_own,) = run(density_own_kernel, [square_group], [], 18, 12, drop, square, whole)
    out = jax.ShapeDtypeStruct(density.shape, kind)

    def assembled(own, first, from_below, from_above):
        kernel = functools.partial(rows_kernel, f, first)
        return call(kernel, [out], [], 0, 8, drop, own, from_below, from_above)[0]

    inverse_next = assembled(whole, half, inverse_below, inverse_above)
    density_next = assembled(density_own, 0, density_below, density_above)
    return density_next, inverse_next


def solution(mesh):
    blocks = P(("grp", "row", "inner"), None, None, None)
    return jax.shard_map(
        on_device,
        mesh=mesh,
        in_specs=(blocks, blocks, P(("grp", "row", "inner"), None)),
        out_specs=(blocks, blocks),
        check_vma=False,
    )
```

```python
import functools

import jax
import jax.numpy as jnp
from jax import lax
from jax.experimental import pallas as pl
from jax.experimental.pallas import tpu as pltpu
from jax.sharding import PartitionSpec as P

RING = ("row", "inner")
MIB = 1024 * 1024


class Frame:
    def __init__(self, half, order):
        self.h = half
        self.b = order
        self.k = 2 * half
        self.p = half // 2
        self.t = 2 * order
        self.group = half * order
        self.pairs = 3 * self.p
        self.own_pairs = range(self.p, 2 * self.p)
        self.edge_rows = [*range(self.p), *range(2 * self.p, 3 * self.p)]

    def tiles(self, columns):
        for col in columns:
            for row in range(max(0, col - self.p), min(self.pairs, col + self.p + 1)):
                yield row, col

    def inner(self, row, col):
        return max(row, col) - self.p, min(row, col) + self.p + 1

    def clipped(self, row, col):
        lo, hi = self.inner(row, col)
        return max(lo, 0), min(hi, self.pairs)

    def split(self, row, col):
        lo, hi = self.clipped(row, col)
        for g in range(3):
            a, z = max(lo, g * self.p), min(hi, (g + 1) * self.p)
            if a < z:
                yield g, a - g * self.p, z - g * self.p


def under(h):
    return [(r, c) for r in range(h) for c in range(r + 1)]


def over(h):
    return [(r, c) for r in range(h) for c in range(r, h)]


def full(h):
    return [(r, c) for r in range(h) for c in range(h)]


def at(f, row_lo, row_hi, col_lo, col_hi):
    t = f.t
    return pl.ds(row_lo * t, (row_hi - row_lo) * t), pl.ds(col_lo * t, (col_hi - col_lo) * t)


def block(f, r, c):
    return pl.ds(r * f.b, f.b), pl.ds(c * f.b, f.b)


def banded(f, row, lo, hi):
    return at(f, row, row + 1, lo - row + f.p, hi - row + f.p)


def dot(a, b):
    return jnp.dot(a, b, preferred_element_type=jnp.float32)


def stored(rows, r, offset, dropped, slots=None):
    last = (rows.shape[1] if slots is None else slots) - 1
    slot = jnp.minimum(offset - (offset > dropped).astype(jnp.int32), last)
    value = rows[r, slot] if slots is None else rows((r, slot))
    return jnp.where(offset == dropped, jnp.zeros_like(value), value)


def masked(f, tile, row, col, drop_ref):
    b = f.b
    parts = []
    for i in range(2):
        r = 2 * row + i
        line = []
        for j in range(2):
            offset = 2 * col + j - r + f.h
            piece = tile[i * b : (i + 1) * b, j * b : (j + 1) * b]
            if 0 <= offset <= f.k:
                piece = jnp.where(drop_ref[r] == offset, 0.0, piece)
            else:
                piece = jnp.zeros_like(piece)
            line.append(piece)
        parts.append(jnp.concatenate(line, axis=1))
    return jnp.concatenate(parts, axis=0)


def odd_place(f, drop_ref):
    return drop_ref[3 * f.h] == 1


def indexed(f, ref, first=0):
    return lambda i: ref[block(f, first + i, 0)]


def plain(ref):
    return lambda place: ref[place]


def sides(f, drop_ref, mate, cross):
    odd = odd_place(f, drop_ref)

    def below(key):
        return jnp.where(odd, mate(key), cross(key))

    def above(key):
        return jnp.where(odd, cross(key), mate(key))

    return below, above


def spread(f, dest, row, col, read, places):
    index = {place: i for i, place in enumerate(places)}
    for r in range(f.h):
        for c in range(f.h):
            i = index.get((r, c))
            dest[block(f, row + r, col + c)] = jnp.zeros((f.b, f.b), dest.dtype) if i is None else read(i)


def pack(f, source, packed, places):
    for i, (r, c) in enumerate(places):
        packed[block(f, i, 0)] = source[block(f, r, c)]


def slabs_kernel(f, drop_ref, own, corner, corner_again, to_mate, to_cross):
    h = f.h
    odd = drop_ref[h] == 1
    n = len(under(h))
    for i, (lower, upper) in enumerate(zip(under(h), over(h))):
        (r, c), (s, d) = lower, upper
        forth = stored(own, r, 2 * h + c - r, drop_ref[r])
        back = stored(own, s, d - s, drop_ref[s])
        to_mate[block(f, i, 0)] = jnp.where(odd, back, forth)
        to_cross[block(f, i, 0)] = jnp.where(odd, forth, back)
    for i, (r, c) in enumerate(full(h)):
        value = stored(own, r, c - r + h, drop_ref[r])
        corner[block(f, i, 0)] = value
        corner_again[block(f, i, 0)] = value
        to_mate[block(f, n + i, 0)] = value


def forward_kernel(f, drop_ref, cross, *refs):
    h = f.h
    odd = odd_place(f, drop_ref)
    to_mate, to_far = refs[-4:-2]
    for i, (lower, upper) in enumerate(zip(under(h), over(h))):
        (r, c), (s, d) = lower, upper
        forth = stored(cross, r, 2 * h + c - r, jnp.where(odd, drop_ref[2 * h + r], drop_ref[r]))
        back = stored(cross, s, d - s, jnp.where(odd, drop_ref[2 * h + s], drop_ref[s]))
        to_mate[block(f, i, 0)] = jnp.where(odd, back, forth)
        to_far[block(f, i, 0)] = jnp.where(odd, forth, back)


def square_kernel(f, drop_ref, own, cross, mate, far_far, far_mate, square, shifted, wide):
    h, p = f.h, f.p
    below, above = sides(f, drop_ref, plain(mate), plain(cross))
    for g, read in enumerate((below, plain(own), above)):
        for r in range(h):
            row = g * h + r
            first = 2 * (row // 2) - h
            for col in range(first, first + 2 * h + 2):
                offset = col - row + h
                if 0 <= offset <= f.k:
                    value = stored(read, r, offset, drop_ref[row], f.k)
                else:
                    value = jnp.zeros((f.b, f.b), wide.dtype)
                wide[block(f, row + h, col + h)] = value
    far_below, far_above = sides(f, drop_ref, indexed(f, far_mate), indexed(f, far_far))
    spread(f, wide, 0, h, far_below, under(h))
    spread(f, wide, 4 * h, 3 * h, far_above, over(h))
    unit = (
        lax.broadcasted_iota(jnp.int32, (f.t, f.t), 0) == lax.broadcasted_iota(jnp.int32, (f.t, f.t), 1)
    ).astype(jnp.float32)
    for row, col in f.tiles(range(f.pairs)):
        lo, hi = f.inner(row, col)
        lo, hi = lo + p, hi + p
        total = dot(
            wide[at(f, row + p, row + p + 1, lo, hi)], wide[at(f, lo, hi, col + p, col + p + 1)]
        )
        total = masked(f, total, row, col, drop_ref)
        here = wide[at(f, row + p, row + p + 1, col + p, col + p + 1)]
        moved = 2.0 * total - 2.0 * here.astype(jnp.float32)
        if row == col:
            moved = moved + unit
        place = banded(f, row, col, col + 1)
        square[place] = total.astype(square.dtype)
        shifted[place] = moved.astype(shifted.dtype)


def right_tile(f, left, right, row, col):
    lo, hi = f.clipped(row, col)
    return dot(left[banded(f, row, lo, hi)], right[at(f, lo, hi, col - f.p, col - f.p + 1)])


def first_sweep_kernel(
    f, drop_ref, shifted, corner, sent_mate, sent_cross, mate, cross,
    correction, fresh, partial, whole, before, after,
):
    h, p = f.h, f.p
    from_below, from_above = sides(f, drop_ref, indexed(f, mate), indexed(f, cross))
    down, up = sides(f, drop_ref, indexed(f, sent_mate), indexed(f, sent_cross))
    spread(f, whole, 0, 0, from_below, under(h))
    spread(f, whole, h, 0, indexed(f, corner), full(h))
    spread(f, whole, 2 * h, 0, from_above, over(h))
    spread(f, before, 0, 0, down, over(h))
    spread(f, after, 0, 0, up, under(h))
    for row, col in f.tiles(f.own_pairs):
        total = masked(f, right_tile(f, shifted, whole, row, col), row, col, drop_ref)
        correction[at(f, row, row + 1, col - p, col - p + 1)] = total.astype(correction.dtype)
    for row, col in f.tiles(f.own_pairs):
        c = col - p
        own_row = row in f.own_pairs
        total = 2.0 * whole[at(f, row, row + 1, c, c + 1)].astype(jnp.float32)
        for g, a, z in f.split(row, col):
            if g == 1:
                left = whole[at(f, row, row + 1, a, z)]
            elif own_row:
                left = (before, None, after)[g][at(f, row - p, row - p + 1, a, z)]
            else:
                continue
            total = total - dot(left, correction[at(f, g * p + a, g * p + z, c, c + 1)])
        if own_row:
            total = masked(f, total, row, col, drop_ref)
            fresh[at(f, row - p, row - p + 1, c, c + 1)] = total.astype(fresh.dtype)
        else:
            place = row if row < p else row - p
            partial[at(f, place, place + 1, c, c + 1)] = total


def edges(f, drop_ref, corner_below, corner_above, correction, start, low, high):
    p = f.p
    for row, col in f.tiles(f.own_pairs):
        if row in f.own_pairs:
            continue
        c = col - p
        side = 0 if row < p else 2
        corner, dest = ((corner_below, low), None, (corner_above, high))[side]
        local = row - side * p
        total = start(row, col)
        for g, a, z in f.split(row, col):
            if g == side:
                total = total - dot(
                    corner(at(f, local, local + 1, a, z)), correction[at(f, g * p + a, g * p + z, c, c + 1)]
                )
        total = masked(f, total, row, col, drop_ref)
        dest[at(f, local, local + 1, c, c + 1)] = total.astype(dest.dtype)


def first_edges_kernel(
    f, drop_ref, mate, cross, correction, partial, low, high, to_prev, to_next, before, after
):
    p = f.p
    below, above = sides(f, drop_ref, indexed(f, mate, len(under(f.h))), indexed(f, cross))
    spread(f, before, 0, 0, below, full(f.h))
    spread(f, after, 0, 0, above, full(f.h))

    def start(row, col):
        place = row if row < p else row - p
        return partial[at(f, place, place + 1, col - p, col - p + 1)]

    edges(f, drop_ref, plain(before), plain(after), correction, start, low, high)
    pack(f, low, to_prev, under(f.h))
    pack(f, high, to_next, over(f.h))


def gather(f, whole, low, own, high):
    for g, source in enumerate((low, own, high)):
        for i in range(f.h):
            whole[pl.ds(g * f.group + i * f.b, f.b), :] = source[pl.ds(i * f.b, f.b), :]


def correction_kernel(f, drop_ref, shifted, low, own, high, correction, whole):
    p = f.p
    gather(f, whole, low, own, high)
    for row, col in f.tiles(f.own_pairs):
        total = masked(f, right_tile(f, shifted, whole, row, col), row, col, drop_ref)
        correction[at(f, row, row + 1, col - p, col - p + 1)] = total.astype(correction.dtype)


def second_edges_kernel(
    f, drop_ref, corner_below, corner_above, correction, low, high, new_low, new_high, to_prev, to_next
):
    p = f.p

    def start(row, col):
        c = col - p
        source, local = (low, row) if row < p else (high, row - 2 * p)
        total = 2.0 * source[at(f, local, local + 1, c, c + 1)].astype(jnp.float32)
        for g, a, z in f.split(row, col):
            if g == 1:
                total = total - dot(
                    source[at(f, local, local + 1, a, z)], correction[at(f, p + a, p + z, c, c + 1)]
                )
        return total

    edges(f, drop_ref, plain(corner_below), plain(corner_above), correction, start, new_low, new_high)
    pack(f, new_low, to_prev, under(f.h))
    pack(f, new_high, to_next, over(f.h))


def density_edges_kernel(
    f, drop_ref, own, from_below, from_above, correction, new_low, new_high, square, whole, to_prev, to_next,
    before, after, low, high,
):
    h, p = f.h, f.p
    spread(f, before, 0, 0, indexed(f, from_below), over(h))
    spread(f, after, 0, 0, indexed(f, from_above), under(h))
    for row, col in f.tiles(f.own_pairs):
        if row not in f.own_pairs:
            continue
        c, local = col - p, row - p
        total = 2.0 * own[at(f, local, local + 1, c, c + 1)].astype(jnp.float32)
        for g, a, z in f.split(row, col):
            left = (before, own, after)[g][at(f, local, local + 1, a, z)]
            total = total - dot(left, correction[at(f, g * p + a, g * p + z, c, c + 1)])
        total = masked(f, total, row, col, drop_ref)
        whole[at(f, row, row + 1, c, c + 1)] = total.astype(whole.dtype)
    for i in range(h):
        rows = pl.ds(i * f.b, f.b)
        whole[pl.ds(i * f.b, f.b), :] = new_low[rows, :]
        whole[pl.ds(2 * f.group + i * f.b, f.b), :] = new_high[rows, :]
    for row, col in f.tiles(f.own_pairs):
        if row in f.own_pairs:
            continue
        total = masked(f, right_tile(f, square, whole, row, col), row, col, drop_ref)
        dest, local = (low, row) if row < p else (high, row - 2 * p)
        dest[at(f, local, local + 1, col - p, col - p + 1)] = total.astype(dest.dtype)
    pack(f, low, to_prev, under(f.h))
    pack(f, high, to_next, over(f.h))


def density_own_kernel(f, drop_ref, square, whole, out):
    p = f.p
    for row, col in f.tiles(f.own_pairs):
        if row in f.own_pairs:
            total = masked(f, right_tile(f, square, whole, row, col), row, col, drop_ref)
            out[at(f, row - p, row - p + 1, col - p, col - p + 1)] = total.astype(out.dtype)


def rows_kernel(f, first, drop_ref, own, from_below, from_above, out):
    h = f.h
    below, above = indexed(f, from_below), indexed(f, from_above)
    over_index = {place: i for i, place in enumerate(over(h))}
    under_index = {place: i for i, place in enumerate(under(h))}
    for r in range(h):
        dropped = drop_ref[h + r]

        def at_offset(offset, r=r):
            col = r + offset
            if col < h:
                return below(over_index[r, col])
            if col < 2 * h:
                return own[block(f, first + r, col - h)]
            return above(under_index[r, col - 2 * h])

        for s in range(f.k):
            out[r, s] = jnp.where(dropped <= s, at_offset(s + 1), at_offset(s))


VMEM = pl.BlockSpec(memory_space=pltpu.VMEM)
SMEM = pl.BlockSpec(memory_space=pltpu.SMEM)
ANY = pl.BlockSpec(memory_space=pl.ANY)


def call(kernel, outs, scratch, flops, limit, drop, *args, passed=(), light=False):
    moved = sum(a.size * a.dtype.itemsize for a in args) + sum(s.size * s.dtype.itemsize for s in outs)
    if light:
        flops = moved = 0
    n = len(args)
    return pl.pallas_call(
        kernel,
        out_shape=[*outs, *[jax.ShapeDtypeStruct(a.shape, a.dtype) for a in passed]],
        in_specs=[SMEM] + [VMEM] * n + [ANY] * len(passed),
        out_specs=[VMEM] * len(outs) + [ANY] * len(passed),
        scratch_shapes=scratch,
        input_output_aliases={1 + n + i: len(outs) + i for i in range(len(passed))},
        compiler_params=pltpu.CompilerParams(vmem_limit_bytes=limit * MIB),
        cost_estimate=pl.CostEstimate(flops=flops, bytes_accessed=moved, transcendentals=0),
    )(drop, *args, *passed)


def routed(x, step):
    size = lax.axis_size(RING)
    return lax.ppermute(x, RING, [(i, (i + step(i)) % size) for i in range(size) if step(i)])


def on_device(density, inverse_start, block_cols):
    rows, width, order, _ = density.shape
    half = width // 2
    ring = lax.axis_size(RING)
    total = rows * ring
    assert rows == half and half % 2 == 0 and ring % 2 == 0
    f = Frame(half, order)
    kind = density.dtype
    me = lax.axis_index(RING)

    def mate_step(i):
        return 1 - 2 * (i % 2)

    def cross_step(i):
        return 2 * (i % 2) - 1

    def to_mate(x):
        return routed(x, mate_step)

    def to_cross(x):
        return routed(x, cross_step)

    def to_next(x):
        return routed(x, lambda i: 1)

    def to_prev(x):
        return routed(x, lambda i: -1)

    positions = block_cols - (me * rows + jnp.arange(rows, dtype=jnp.int32))[:, None] + half
    positions = positions + jnp.where(positions < 0, total, jnp.where(positions >= total, -total, 0))
    own_drop = width * (width + 1) // 2 - jnp.sum(positions, axis=1)

    density_cross, density_mate = to_cross(density), to_mate(density)
    cross_drop, mate_drop = to_cross(own_drop), to_mate(own_drop)
    even = (me & 1) == 0
    mark = jnp.reshape(me & 1, (1,))
    start_drop = jnp.concatenate([own_drop, mark])
    drop = jnp.concatenate(
        [jnp.where(even, cross_drop, mate_drop), own_drop, jnp.where(even, mate_drop, cross_drop), mark]
    )

    unit = 2 * f.t**3
    count = half * (half + 1) // 2
    square_group = jax.ShapeDtypeStruct((f.group, f.group), kind)
    columns = jax.ShapeDtypeStruct((3 * f.group, f.group), kind)
    band = jax.ShapeDtypeStruct((3 * f.group, (2 * f.p + 1) * f.t), kind)
    triangle = jax.ShapeDtypeStruct((count * order, order), kind)
    listed = jax.ShapeDtypeStruct((half * half * order, order), kind)
    both = jax.ShapeDtypeStruct(((count + half * half) * order, order), kind)
    partial_sums = jax.ShapeDtypeStruct((2 * f.group, f.group), jnp.float32)
    group_scratch = pltpu.VMEM((f.group, f.group), kind)
    whole_scratch = pltpu.VMEM((3 * f.group, f.group), kind)

    def run(kernel, outs, scratch, tiles, limit, *args, **kw):
        return call(functools.partial(kernel, f), outs, scratch, tiles * unit, limit, *args, **kw)

    corner, corner_cross, slab_mate, triangle_cross = run(
        slabs_kernel, [listed, listed, both, triangle], [], 0, 12, start_drop, inverse_start
    )
    from_mate = to_mate(slab_mate)
    forward_mate, forward_far, triangle_cross, corner_cross = run(
        forward_kernel, [triangle, triangle], [], 0, 12, drop, density_cross, density_mate, from_mate,
        passed=(triangle_cross, corner_cross),
    )
    far_mate = to_mate(forward_mate)
    far_far = routed(forward_far, lambda i: 3 * cross_step(i))
    cross_triangle = to_cross(triangle_cross)
    cross_corner = to_cross(corner_cross)

    square, shifted = run(
        square_kernel,
        [band, band],
        [pltpu.VMEM((5 * f.group, 5 * f.group), kind)],
        94, 28, drop, density, density_cross, density_mate, far_far, far_mate, light=True,
    )
    correction, own, partial = run(
        first_sweep_kernel,
        [columns, square_group, partial_sums],
        [whole_scratch, group_scratch, group_scratch],
        66, 24, drop, shifted, corner, slab_mate, triangle_cross, from_mate, cross_triangle,
    )
    next_corner_below, next_corner_above = to_next(own), to_prev(own)
    low, high, back, forth = run(
        first_edges_kernel,
        [square_group, square_group, triangle, triangle],
        [group_scratch] * 2,
        10, 16, drop, from_mate, cross_corner, correction, partial,
    )
    from_above, from_below = to_prev(back), to_next(forth)
    (correction,) = run(
        correction_kernel, [columns], [whole_scratch], 38, 16, drop, shifted, low, own, high
    )
    new_low, new_high, back, forth = run(
        second_edges_kernel,
        [square_group, square_group, triangle, triangle],
        [],
        20, 12, drop, next_corner_below, next_corner_above, correction, low, high,
    )
    inverse_above, inverse_below = to_prev(back), to_next(forth)
    whole, back, forth = run(
        density_edges_kernel,
        [columns, triangle, triangle],
        [group_scratch] * 4,
        38, 20, drop, own, from_below, from_above, correction, new_low, new_high, square,
    )
    density_above, density_below = to_prev(back), to_next(forth)
    (density_own,) = run(density_own_kernel, [square_group], [], 18, 12, drop, square, whole)
    out = jax.ShapeDtypeStruct(density.shape, kind)

    def assembled(own, first, from_below, from_above):
        kernel = functools.partial(rows_kernel, f, first)
        return call(kernel, [out], [], 0, 8, drop, own, from_below, from_above)[0]

    inverse_next = assembled(whole, half, inverse_below, inverse_above)
    density_next = assembled(density_own, 0, density_below, density_above)
    return density_next, inverse_next


def solution(mesh):
    blocks = P(("grp", "row", "inner"), None, None, None)
    return jax.shard_map(
        on_device,
        mesh=mesh,
        in_specs=(blocks, blocks, P(("grp", "row", "inner"), None)),
        out_specs=(blocks, blocks),
        check_vma=False,
    )
```

```python
import functools

import jax
import jax.numpy as jnp
from jax import lax
from jax.experimental import pallas as pl
from jax.experimental.pallas import tpu as pltpu
from jax.sharding import PartitionSpec as P

RING = ("row", "inner")
MIB = 1024 * 1024


class Frame:
    def __init__(self, half, order):
        self.h = half
        self.b = order
        self.k = 2 * half
        self.p = half // 2
        self.t = 2 * order
        self.group = half * order
        self.pairs = 3 * self.p
        self.own_pairs = range(self.p, 2 * self.p)
        self.edge_rows = [*range(self.p), *range(2 * self.p, 3 * self.p)]

    def tiles(self, columns):
        for col in columns:
            for row in range(max(0, col - self.p), min(self.pairs, col + self.p + 1)):
                yield row, col

    def inner(self, row, col):
        return max(row, col) - self.p, min(row, col) + self.p + 1

    def clipped(self, row, col):
        lo, hi = self.inner(row, col)
        return max(lo, 0), min(hi, self.pairs)

    def split(self, row, col):
        lo, hi = self.clipped(row, col)
        for g in range(3):
            a, z = max(lo, g * self.p), min(hi, (g + 1) * self.p)
            if a < z:
                yield g, a - g * self.p, z - g * self.p


def under(h):
    return [(r, c) for r in range(h) for c in range(r + 1)]


def over(h):
    return [(r, c) for r in range(h) for c in range(r, h)]


def full(h):
    return [(r, c) for r in range(h) for c in range(h)]


def at(f, row_lo, row_hi, col_lo, col_hi):
    t = f.t
    return pl.ds(row_lo * t, (row_hi - row_lo) * t), pl.ds(col_lo * t, (col_hi - col_lo) * t)


def block(f, r, c):
    return pl.ds(r * f.b, f.b), pl.ds(c * f.b, f.b)


def banded(f, row, lo, hi):
    return at(f, row, row + 1, lo - row + f.p, hi - row + f.p)


def dot(a, b):
    return jnp.dot(a, b, preferred_element_type=jnp.float32)


def stored(rows, r, offset, dropped, slots=None):
    last = (rows.shape[1] if slots is None else slots) - 1
    slot = jnp.minimum(offset - (offset > dropped).astype(jnp.int32), last)
    value = rows[r, slot] if slots is None else rows((r, slot))
    return jnp.where(offset == dropped, jnp.zeros_like(value), value)


def masked(f, tile, row, col, drop_ref):
    b = f.b
    parts = []
    for i in range(2):
        r = 2 * row + i
        line = []
        for j in range(2):
            offset = 2 * col + j - r + f.h
            piece = tile[i * b : (i + 1) * b, j * b : (j + 1) * b]
            if 0 <= offset <= f.k:
                piece = jnp.where(drop_ref[r] == offset, 0.0, piece)
            else:
                piece = jnp.zeros_like(piece)
            line.append(piece)
        parts.append(jnp.concatenate(line, axis=1))
    return jnp.concatenate(parts, axis=0)


def odd_place(f, drop_ref):
    return drop_ref[3 * f.h] == 1


def indexed(f, ref, first=0):
    return lambda i: ref[block(f, first + i, 0)]


def plain(ref):
    return lambda place: ref[place]


def sides(f, drop_ref, mate, cross):
    odd = odd_place(f, drop_ref)

    def below(key):
        return jnp.where(odd, mate(key), cross(key))

    def above(key):
        return jnp.where(odd, cross(key), mate(key))

    return below, above


def spread(f, dest, row, col, read, places):
    index = {place: i for i, place in enumerate(places)}
    for r in range(f.h):
        for c in range(f.h):
            i = index.get((r, c))
            dest[block(f, row + r, col + c)] = jnp.zeros((f.b, f.b), dest.dtype) if i is None else read(i)


def pack(f, source, packed, places):
    for i, (r, c) in enumerate(places):
        packed[block(f, i, 0)] = source[block(f, r, c)]


def slabs_kernel(f, drop_ref, own, corner, corner_again, to_mate, to_cross):
    h = f.h
    odd = drop_ref[h] == 1
    n = len(under(h))
    for i, (lower, upper) in enumerate(zip(under(h), over(h))):
        (r, c), (s, d) = lower, upper
        forth = stored(own, r, 2 * h + c - r, drop_ref[r])
        back = stored(own, s, d - s, drop_ref[s])
        to_mate[block(f, i, 0)] = jnp.where(odd, back, forth)
        to_cross[block(f, i, 0)] = jnp.where(odd, forth, back)
    for i, (r, c) in enumerate(full(h)):
        value = stored(own, r, c - r + h, drop_ref[r])
        corner[block(f, i, 0)] = value
        corner_again[block(f, i, 0)] = value
        to_mate[block(f, n + i, 0)] = value


def forward_kernel(f, drop_ref, cross, *refs):
    h = f.h
    odd = odd_place(f, drop_ref)
    to_mate, to_far = refs[-5:-3], refs[-3]
    for i, (lower, upper) in enumerate(zip(under(h), over(h))):
        (r, c), (s, d) = lower, upper
        forth = stored(cross, r, 2 * h + c - r, jnp.where(odd, drop_ref[2 * h + r], drop_ref[r]))
        back = stored(cross, s, d - s, jnp.where(odd, drop_ref[2 * h + s], drop_ref[s]))
        part, place = i % 2, i // 2
        to_mate[part][block(f, place, 0)] = jnp.where(odd, back, forth)
        to_far[block(f, i, 0)] = jnp.where(odd, forth, back)


def square_kernel(f, drop_ref, own, cross, mate, far_far, far_mate, far_mate_too, square, shifted, wide):
    h, p = f.h, f.p
    below, above = sides(f, drop_ref, plain(mate), plain(cross))
    for g, read in enumerate((below, plain(own), above)):
        for r in range(h):
            row = g * h + r
            first = 2 * (row // 2) - h
            for col in range(first, first + 2 * h + 2):
                offset = col - row + h
                if 0 <= offset <= f.k:
                    value = stored(read, r, offset, drop_ref[row], f.k)
                else:
                    value = jnp.zeros((f.b, f.b), wide.dtype)
                wide[block(f, row + h, col + h)] = value
    far_mates = [indexed(f, far_mate), indexed(f, far_mate_too)]
    far_below, far_above = sides(f, drop_ref, lambda i: far_mates[i % 2](i // 2), indexed(f, far_far))
    spread(f, wide, 0, h, far_below, under(h))
    spread(f, wide, 4 * h, 3 * h, far_above, over(h))
    unit = (
        lax.broadcasted_iota(jnp.int32, (f.t, f.t), 0) == lax.broadcasted_iota(jnp.int32, (f.t, f.t), 1)
    ).astype(jnp.float32)
    for row, col in f.tiles(range(f.pairs)):
        lo, hi = f.inner(row, col)
        lo, hi = lo + p, hi + p
        total = dot(
            wide[at(f, row + p, row + p + 1, lo, hi)], wide[at(f, lo, hi, col + p, col + p + 1)]
        )
        total = masked(f, total, row, col, drop_ref)
        here = wide[at(f, row + p, row + p + 1, col + p, col + p + 1)]
        moved = 2.0 * total - 2.0 * here.astype(jnp.float32)
        if row == col:
            moved = moved + unit
        place = banded(f, row, col, col + 1)
        square[place] = total.astype(square.dtype)
        shifted[place] = moved.astype(shifted.dtype)


def right_tile(f, left, right, row, col):
    lo, hi = f.clipped(row, col)
    return dot(left[banded(f, row, lo, hi)], right[at(f, lo, hi, col - f.p, col - f.p + 1)])


def first_sweep_kernel(
    f, drop_ref, shifted, corner, sent_mate, sent_cross, mate, cross,
    correction, fresh, partial, whole, before, after,
):
    h, p = f.h, f.p
    from_below, from_above = sides(f, drop_ref, indexed(f, mate), indexed(f, cross))
    down, up = sides(f, drop_ref, indexed(f, sent_mate), indexed(f, sent_cross))
    spread(f, whole, 0, 0, from_below, under(h))
    spread(f, whole, h, 0, indexed(f, corner), full(h))
    spread(f, whole, 2 * h, 0, from_above, over(h))
    spread(f, before, 0, 0, down, over(h))
    spread(f, after, 0, 0, up, under(h))
    for row, col in f.tiles(f.own_pairs):
        total = masked(f, right_tile(f, shifted, whole, row, col), row, col, drop_ref)
        correction[at(f, row, row + 1, col - p, col - p + 1)] = total.astype(correction.dtype)
    for row, col in f.tiles(f.own_pairs):
        c = col - p
        own_row = row in f.own_pairs
        total = 2.0 * whole[at(f, row, row + 1, c, c + 1)].astype(jnp.float32)
        for g, a, z in f.split(row, col):
            if g == 1:
                left = whole[at(f, row, row + 1, a, z)]
            elif own_row:
                left = (before, None, after)[g][at(f, row - p, row - p + 1, a, z)]
            else:
                continue
            total = total - dot(left, correction[at(f, g * p + a, g * p + z, c, c + 1)])
        if own_row:
            total = masked(f, total, row, col, drop_ref)
            fresh[at(f, row - p, row - p + 1, c, c + 1)] = total.astype(fresh.dtype)
        else:
            place = row if row < p else row - p
            partial[at(f, place, place + 1, c, c + 1)] = total


def edges(f, drop_ref, corner_below, corner_above, correction, start, low, high):
    p = f.p
    for row, col in f.tiles(f.own_pairs):
        if row in f.own_pairs:
            continue
        c = col - p
        side = 0 if row < p else 2
        corner, dest = ((corner_below, low), None, (corner_above, high))[side]
        local = row - side * p
        total = start(row, col)
        for g, a, z in f.split(row, col):
            if g == side:
                total = total - dot(
                    corner(at(f, local, local + 1, a, z)), correction[at(f, g * p + a, g * p + z, c, c + 1)]
                )
        total = masked(f, total, row, col, drop_ref)
        dest[at(f, local, local + 1, c, c + 1)] = total.astype(dest.dtype)


def first_edges_kernel(
    f, drop_ref, mate, cross, correction, partial, low, high, to_prev, to_next, before, after
):
    p = f.p
    below, above = sides(f, drop_ref, indexed(f, mate, len(under(f.h))), indexed(f, cross))
    spread(f, before, 0, 0, below, full(f.h))
    spread(f, after, 0, 0, above, full(f.h))

    def start(row, col):
        place = row if row < p else row - p
        return partial[at(f, place, place + 1, col - p, col - p + 1)]

    edges(f, drop_ref, plain(before), plain(after), correction, start, low, high)
    pack(f, low, to_prev, under(f.h))
    pack(f, high, to_next, over(f.h))


def gather(f, whole, low, own, high):
    for g, source in enumerate((low, own, high)):
        for i in range(f.h):
            whole[pl.ds(g * f.group + i * f.b, f.b), :] = source[pl.ds(i * f.b, f.b), :]


def correction_kernel(f, drop_ref, shifted, low, own, high, correction, whole):
    p = f.p
    gather(f, whole, low, own, high)
    for row, col in f.tiles(f.own_pairs):
        total = masked(f, right_tile(f, shifted, whole, row, col), row, col, drop_ref)
        correction[at(f, row, row + 1, col - p, col - p + 1)] = total.astype(correction.dtype)


def second_edges_kernel(
    f, drop_ref, corner_below, corner_above, correction, low, high, new_low, new_high, to_prev, to_next
):
    p = f.p

    def start(row, col):
        c = col - p
        source, local = (low, row) if row < p else (high, row - 2 * p)
        total = 2.0 * source[at(f, local, local + 1, c, c + 1)].astype(jnp.float32)
        for g, a, z in f.split(row, col):
            if g == 1:
                total = total - dot(
                    source[at(f, local, local + 1, a, z)], correction[at(f, p + a, p + z, c, c + 1)]
                )
        return total

    edges(f, drop_ref, plain(corner_below), plain(corner_above), correction, start, new_low, new_high)
    pack(f, new_low, to_prev, under(f.h))
    pack(f, new_high, to_next, over(f.h))


def density_edges_kernel(
    f, drop_ref, own, from_below, from_above, correction, new_low, new_high, square, whole, to_prev, to_next,
    before, after, low, high,
):
    h, p = f.h, f.p
    spread(f, before, 0, 0, indexed(f, from_below), over(h))
    spread(f, after, 0, 0, indexed(f, from_above), under(h))
    for row, col in f.tiles(f.own_pairs):
        if row not in f.own_pairs:
            continue
        c, local = col - p, row - p
        total = 2.0 * own[at(f, local, local + 1, c, c + 1)].astype(jnp.float32)
        for g, a, z in f.split(row, col):
            left = (before, own, after)[g][at(f, local, local + 1, a, z)]
            total = total - dot(left, correction[at(f, g * p + a, g * p + z, c, c + 1)])
        total = masked(f, total, row, col, drop_ref)
        whole[at(f, row, row + 1, c, c + 1)] = total.astype(whole.dtype)
    for i in range(h):
        rows = pl.ds(i * f.b, f.b)
        whole[pl.ds(i * f.b, f.b), :] = new_low[rows, :]
        whole[pl.ds(2 * f.group + i * f.b, f.b), :] = new_high[rows, :]
    for row, col in f.tiles(f.own_pairs):
        if row in f.own_pairs:
            continue
        total = masked(f, right_tile(f, square, whole, row, col), row, col, drop_ref)
        dest, local = (low, row) if row < p else (high, row - 2 * p)
        dest[at(f, local, local + 1, col - p, col - p + 1)] = total.astype(dest.dtype)
    pack(f, low, to_prev, under(f.h))
    pack(f, high, to_next, over(f.h))


def density_own_kernel(f, drop_ref, square, whole, out):
    p = f.p
    for row, col in f.tiles(f.own_pairs):
        if row in f.own_pairs:
            total = masked(f, right_tile(f, square, whole, row, col), row, col, drop_ref)
            out[at(f, row - p, row - p + 1, col - p, col - p + 1)] = total.astype(out.dtype)


def rows_kernel(f, first, drop_ref, own, from_below, from_above, out):
    h = f.h
    below, above = indexed(f, from_below), indexed(f, from_above)
    over_index = {place: i for i, place in enumerate(over(h))}
    under_index = {place: i for i, place in enumerate(under(h))}
    for r in range(h):
        dropped = drop_ref[h + r]

        def at_offset(offset, r=r):
            col = r + offset
            if col < h:
                return below(over_index[r, col])
            if col < 2 * h:
                return own[block(f, first + r, col - h)]
            return above(under_index[r, col - 2 * h])

        for s in range(f.k):
            out[r, s] = jnp.where(dropped <= s, at_offset(s + 1), at_offset(s))


VMEM = pl.BlockSpec(memory_space=pltpu.VMEM)
SMEM = pl.BlockSpec(memory_space=pltpu.SMEM)
ANY = pl.BlockSpec(memory_space=pl.ANY)


def call(kernel, outs, scratch, flops, limit, drop, *args, passed=(), light=False):
    moved = sum(a.size * a.dtype.itemsize for a in args) + sum(s.size * s.dtype.itemsize for s in outs)
    if light:
        flops = moved = 0
    n = len(args)
    return pl.pallas_call(
        kernel,
        out_shape=[*outs, *[jax.ShapeDtypeStruct(a.shape, a.dtype) for a in passed]],
        in_specs=[SMEM] + [VMEM] * n + [ANY] * len(passed),
        out_specs=[VMEM] * len(outs) + [ANY] * len(passed),
        scratch_shapes=scratch,
        input_output_aliases={1 + n + i: len(outs) + i for i in range(len(passed))},
        compiler_params=pltpu.CompilerParams(vmem_limit_bytes=limit * MIB),
        cost_estimate=pl.CostEstimate(flops=flops, bytes_accessed=moved, transcendentals=0),
    )(drop, *args, *passed)


def routed(x, step):
    size = lax.axis_size(RING)
    return lax.ppermute(x, RING, [(i, (i + step(i)) % size) for i in range(size) if step(i)])


def on_device(density, inverse_start, block_cols):
    rows, width, order, _ = density.shape
    half = width // 2
    ring = lax.axis_size(RING)
    total = rows * ring
    assert rows == half and half % 2 == 0 and ring % 2 == 0
    f = Frame(half, order)
    kind = density.dtype
    me = lax.axis_index(RING)

    def mate_step(i):
        return 1 - 2 * (i % 2)

    def cross_step(i):
        return 2 * (i % 2) - 1

    def to_mate(x):
        return routed(x, mate_step)

    def to_cross(x):
        return routed(x, cross_step)

    def to_next(x):
        return routed(x, lambda i: 1)

    def to_prev(x):
        return routed(x, lambda i: -1)

    positions = block_cols - (me * rows + jnp.arange(rows, dtype=jnp.int32))[:, None] + half
    positions = positions + jnp.where(positions < 0, total, jnp.where(positions >= total, -total, 0))
    own_drop = width * (width + 1) // 2 - jnp.sum(positions, axis=1)

    density_cross, density_mate = to_cross(density), to_mate(density)
    cross_drop, mate_drop = to_cross(own_drop), to_mate(own_drop)
    even = (me & 1) == 0
    mark = jnp.reshape(me & 1, (1,))
    start_drop = jnp.concatenate([own_drop, mark])
    drop = jnp.concatenate(
        [jnp.where(even, cross_drop, mate_drop), own_drop, jnp.where(even, mate_drop, cross_drop), mark]
    )

    unit = 2 * f.t**3
    count = half * (half + 1) // 2
    square_group = jax.ShapeDtypeStruct((f.group, f.group), kind)
    columns = jax.ShapeDtypeStruct((3 * f.group, f.group), kind)
    band = jax.ShapeDtypeStruct((3 * f.group, (2 * f.p + 1) * f.t), kind)
    triangle = jax.ShapeDtypeStruct((count * order, order), kind)
    half_triangle = jax.ShapeDtypeStruct((count // 2 * order, order), kind)
    listed = jax.ShapeDtypeStruct((half * half * order, order), kind)
    both = jax.ShapeDtypeStruct(((count + half * half) * order, order), kind)
    partial_sums = jax.ShapeDtypeStruct((2 * f.group, f.group), jnp.float32)
    group_scratch = pltpu.VMEM((f.group, f.group), kind)
    whole_scratch = pltpu.VMEM((3 * f.group, f.group), kind)

    def run(kernel, outs, scratch, tiles, limit, *args, **kw):
        return call(functools.partial(kernel, f), outs, scratch, tiles * unit, limit, *args, **kw)

    corner, corner_cross, slab_mate, triangle_cross = run(
        slabs_kernel, [listed, listed, both, triangle], [], 0, 12, start_drop, inverse_start
    )
    from_mate = to_mate(slab_mate)
    forward_mate, forward_mate_too, forward_far, triangle_cross, corner_cross = run(
        forward_kernel, [half_triangle, half_triangle, triangle], [], 0, 12, drop, density_cross, density_mate, from_mate,
        passed=(triangle_cross, corner_cross),
    )
    far_mate, far_mate_too = to_mate(forward_mate), to_mate(forward_mate_too)
    far_far = routed(forward_far, lambda i: 3 * cross_step(i))
    cross_triangle = to_cross(triangle_cross)
    cross_corner = to_cross(corner_cross)

    square, shifted = run(
        square_kernel,
        [band, band],
        [pltpu.VMEM((5 * f.group, 5 * f.group), kind)],
        94, 28, drop, density, density_cross, density_mate, far_far, far_mate, far_mate_too, light=True,
    )
    correction, own, partial = run(
        first_sweep_kernel,
        [columns, square_group, partial_sums],
        [whole_scratch, group_scratch, group_scratch],
        66, 24, drop, shifted, corner, slab_mate, triangle_cross, from_mate, cross_triangle, light=True,
    )
    next_corner_below, next_corner_above = to_next(own), to_prev(own)
    low, high, back, forth = run(
        first_edges_kernel,
        [square_group, square_group, triangle, triangle],
        [group_scratch] * 2,
        10, 16, drop, from_mate, cross_corner, correction, partial,
    )
    from_above, from_below = to_prev(back), to_next(forth)
    (correction,) = run(
        correction_kernel, [columns], [whole_scratch], 38, 16, drop, shifted, low, own, high
    )
    new_low, new_high, back, forth = run(
        second_edges_kernel,
        [square_group, square_group, triangle, triangle],
        [],
        20, 12, drop, next_corner_below, next_corner_above, correction, low, high,
    )
    inverse_above, inverse_below = to_prev(back), to_next(forth)
    whole, back, forth = run(
        density_edges_kernel,
        [columns, triangle, triangle],
        [group_scratch] * 4,
        38, 20, drop, own, from_below, from_above, correction, new_low, new_high, square,
    )
    density_above, density_below = to_prev(back), to_next(forth)
    (density_own,) = run(density_own_kernel, [square_group], [], 18, 12, drop, square, whole)
    out = jax.ShapeDtypeStruct(density.shape, kind)

    def assembled(own, first, from_below, from_above):
        kernel = functools.partial(rows_kernel, f, first)
        return call(kernel, [out], [], 0, 8, drop, own, from_below, from_above)[0]

    inverse_next = assembled(whole, half, inverse_below, inverse_above)
    density_next = assembled(density_own, 0, density_below, density_above)
    return density_next, inverse_next


def solution(mesh):
    blocks = P(("grp", "row", "inner"), None, None, None)
    return jax.shard_map(
        on_device,
        mesh=mesh,
        in_specs=(blocks, blocks, P(("grp", "row", "inner"), None)),
        out_specs=(blocks, blocks),
        check_vma=False,
    )
```

```python
import functools

import jax
import jax.numpy as jnp
from jax import lax
from jax.experimental import pallas as pl
from jax.experimental.pallas import tpu as pltpu
from jax.sharding import PartitionSpec as P

RING = ("row", "inner")
MIB = 1024 * 1024


class Frame:
    def __init__(self, half, order):
        self.h = half
        self.b = order
        self.k = 2 * half
        self.p = half // 2
        self.t = 2 * order
        self.group = half * order
        self.pairs = 3 * self.p
        self.own_pairs = range(self.p, 2 * self.p)
        self.edge_rows = [*range(self.p), *range(2 * self.p, 3 * self.p)]

    def tiles(self, columns):
        for col in columns:
            for row in range(max(0, col - self.p), min(self.pairs, col + self.p + 1)):
                yield row, col

    def inner(self, row, col):
        return max(row, col) - self.p, min(row, col) + self.p + 1

    def clipped(self, row, col):
        lo, hi = self.inner(row, col)
        return max(lo, 0), min(hi, self.pairs)

    def split(self, row, col):
        lo, hi = self.clipped(row, col)
        for g in range(3):
            a, z = max(lo, g * self.p), min(hi, (g + 1) * self.p)
            if a < z:
                yield g, a - g * self.p, z - g * self.p


def under(h):
    return [(r, c) for r in range(h) for c in range(r + 1)]


def over(h):
    return [(r, c) for r in range(h) for c in range(r, h)]


def full(h):
    return [(r, c) for r in range(h) for c in range(h)]


def at(f, row_lo, row_hi, col_lo, col_hi):
    t = f.t
    return pl.ds(row_lo * t, (row_hi - row_lo) * t), pl.ds(col_lo * t, (col_hi - col_lo) * t)


def block(f, r, c):
    return pl.ds(r * f.b, f.b), pl.ds(c * f.b, f.b)


def banded(f, row, lo, hi):
    return at(f, row, row + 1, lo - row + f.p, hi - row + f.p)


def dot(a, b):
    return jnp.dot(a, b, preferred_element_type=jnp.float32)


def stored(rows, r, offset, dropped, slots=None):
    last = (rows.shape[1] if slots is None else slots) - 1
    slot = jnp.minimum(offset - (offset > dropped).astype(jnp.int32), last)
    value = rows[r, slot] if slots is None else rows((r, slot))
    return jnp.where(offset == dropped, jnp.zeros_like(value), value)


def masked(f, tile, row, col, drop_ref):
    b = f.b
    parts = []
    for i in range(2):
        r = 2 * row + i
        line = []
        for j in range(2):
            offset = 2 * col + j - r + f.h
            piece = tile[i * b : (i + 1) * b, j * b : (j + 1) * b]
            if 0 <= offset <= f.k:
                piece = jnp.where(drop_ref[r] == offset, 0.0, piece)
            else:
                piece = jnp.zeros_like(piece)
            line.append(piece)
        parts.append(jnp.concatenate(line, axis=1))
    return jnp.concatenate(parts, axis=0)


def odd_place(f, drop_ref):
    return drop_ref[3 * f.h] == 1


def indexed(f, ref, first=0):
    return lambda i: ref[block(f, first + i, 0)]


def plain(ref):
    return lambda place: ref[place]


def sides(f, drop_ref, mate, cross):
    odd = odd_place(f, drop_ref)

    def below(key):
        return jnp.where(odd, mate(key), cross(key))

    def above(key):
        return jnp.where(odd, cross(key), mate(key))

    return below, above


def spread(f, dest, row, col, read, places):
    index = {place: i for i, place in enumerate(places)}
    for r in range(f.h):
        for c in range(f.h):
            i = index.get((r, c))
            dest[block(f, row + r, col + c)] = jnp.zeros((f.b, f.b), dest.dtype) if i is None else read(i)


def pack_edges(f, drop_ref, low, high, to_cross, to_mate):
    odd = odd_place(f, drop_ref)
    for i, (lower, upper) in enumerate(zip(under(f.h), over(f.h))):
        back, forth = low[block(f, *lower)], high[block(f, *upper)]
        to_cross[block(f, i, 0)] = jnp.where(odd, forth, back)
        to_mate[block(f, i, 0)] = jnp.where(odd, back, forth)


def slabs_kernel(f, drop_ref, own, corner, corner_again, to_mate, to_cross):
    h = f.h
    odd = drop_ref[h] == 1
    n = len(under(h))
    for i, (lower, upper) in enumerate(zip(under(h), over(h))):
        (r, c), (s, d) = lower, upper
        forth = stored(own, r, 2 * h + c - r, drop_ref[r])
        back = stored(own, s, d - s, drop_ref[s])
        to_mate[block(f, i, 0)] = jnp.where(odd, back, forth)
        to_cross[block(f, i, 0)] = jnp.where(odd, forth, back)
    for i, (r, c) in enumerate(full(h)):
        value = stored(own, r, c - r + h, drop_ref[r])
        corner[block(f, i, 0)] = value
        corner_again[block(f, i, 0)] = value
        to_mate[block(f, n + i, 0)] = value


def forward_kernel(f, drop_ref, cross, *refs):
    h = f.h
    odd = odd_place(f, drop_ref)
    to_mate, to_far = refs[-5:-3], refs[-3]
    for i, (lower, upper) in enumerate(zip(under(h), over(h))):
        (r, c), (s, d) = lower, upper
        forth = stored(cross, r, 2 * h + c - r, jnp.where(odd, drop_ref[2 * h + r], drop_ref[r]))
        back = stored(cross, s, d - s, jnp.where(odd, drop_ref[2 * h + s], drop_ref[s]))
        part, place = i % 2, i // 2
        to_mate[part][block(f, place, 0)] = jnp.where(odd, back, forth)
        to_far[block(f, i, 0)] = jnp.where(odd, forth, back)


def square_kernel(f, drop_ref, own, cross, mate, far_far, far_mate, far_mate_too, square, shifted, wide):
    h, p = f.h, f.p
    below, above = sides(f, drop_ref, plain(mate), plain(cross))
    for g, read in enumerate((below, plain(own), above)):
        for r in range(h):
            row = g * h + r
            first = 2 * (row // 2) - h
            for col in range(first, first + 2 * h + 2):
                offset = col - row + h
                if 0 <= offset <= f.k:
                    value = stored(read, r, offset, drop_ref[row], f.k)
                else:
                    value = jnp.zeros((f.b, f.b), wide.dtype)
                wide[block(f, row + h, col + h)] = value
    far_mates = [indexed(f, far_mate), indexed(f, far_mate_too)]
    far_below, far_above = sides(f, drop_ref, lambda i: far_mates[i % 2](i // 2), indexed(f, far_far))
    spread(f, wide, 0, h, far_below, under(h))
    spread(f, wide, 4 * h, 3 * h, far_above, over(h))
    unit = (
        lax.broadcasted_iota(jnp.int32, (f.t, f.t), 0) == lax.broadcasted_iota(jnp.int32, (f.t, f.t), 1)
    ).astype(jnp.float32)
    for row, col in f.tiles(range(f.pairs)):
        lo, hi = f.inner(row, col)
        lo, hi = lo + p, hi + p
        total = dot(
            wide[at(f, row + p, row + p + 1, lo, hi)], wide[at(f, lo, hi, col + p, col + p + 1)]
        )
        total = masked(f, total, row, col, drop_ref)
        here = wide[at(f, row + p, row + p + 1, col + p, col + p + 1)]
        moved = 2.0 * total - 2.0 * here.astype(jnp.float32)
        if row == col:
            moved = moved + unit
        place = banded(f, row, col, col + 1)
        square[place] = total.astype(square.dtype)
        shifted[place] = moved.astype(shifted.dtype)


def right_tile(f, left, right, row, col):
    lo, hi = f.clipped(row, col)
    return dot(left[banded(f, row, lo, hi)], right[at(f, lo, hi, col - f.p, col - f.p + 1)])


def first_sweep_kernel(
    f, drop_ref, shifted, corner, sent_mate, sent_cross, mate, cross,
    correction, fresh, partial, whole, before, after,
):
    h, p = f.h, f.p
    from_below, from_above = sides(f, drop_ref, indexed(f, mate), indexed(f, cross))
    down, up = sides(f, drop_ref, indexed(f, sent_mate), indexed(f, sent_cross))
    spread(f, whole, 0, 0, from_below, under(h))
    spread(f, whole, h, 0, indexed(f, corner), full(h))
    spread(f, whole, 2 * h, 0, from_above, over(h))
    spread(f, before, 0, 0, down, over(h))
    spread(f, after, 0, 0, up, under(h))
    for row, col in f.tiles(f.own_pairs):
        total = masked(f, right_tile(f, shifted, whole, row, col), row, col, drop_ref)
        correction[at(f, row, row + 1, col - p, col - p + 1)] = total.astype(correction.dtype)
    for row, col in f.tiles(f.own_pairs):
        c = col - p
        own_row = row in f.own_pairs
        total = 2.0 * whole[at(f, row, row + 1, c, c + 1)].astype(jnp.float32)
        for g, a, z in f.split(row, col):
            if g == 1:
                left = whole[at(f, row, row + 1, a, z)]
            elif own_row:
                left = (before, None, after)[g][at(f, row - p, row - p + 1, a, z)]
            else:
                continue
            total = total - dot(left, correction[at(f, g * p + a, g * p + z, c, c + 1)])
        if own_row:
            total = masked(f, total, row, col, drop_ref)
            fresh[at(f, row - p, row - p + 1, c, c + 1)] = total.astype(fresh.dtype)
        else:
            place = row if row < p else row - p
            partial[at(f, place, place + 1, c, c + 1)] = total


def edges(f, drop_ref, corner_below, corner_above, correction, start, low, high):
    p = f.p
    for row, col in f.tiles(f.own_pairs):
        if row in f.own_pairs:
            continue
        c = col - p
        side = 0 if row < p else 2
        corner, dest = ((corner_below, low), None, (corner_above, high))[side]
        local = row - side * p
        total = start(row, col)
        for g, a, z in f.split(row, col):
            if g == side:
                total = total - dot(
                    corner(at(f, local, local + 1, a, z)), correction[at(f, g * p + a, g * p + z, c, c + 1)]
                )
        total = masked(f, total, row, col, drop_ref)
        dest[at(f, local, local + 1, c, c + 1)] = total.astype(dest.dtype)


def first_edges_kernel(
    f, drop_ref, mate, cross, correction, partial, low, high, to_cross, to_mate, before, after
):
    p = f.p
    below, above = sides(f, drop_ref, indexed(f, mate, len(under(f.h))), indexed(f, cross))
    spread(f, before, 0, 0, below, full(f.h))
    spread(f, after, 0, 0, above, full(f.h))

    def start(row, col):
        place = row if row < p else row - p
        return partial[at(f, place, place + 1, col - p, col - p + 1)]

    edges(f, drop_ref, plain(before), plain(after), correction, start, low, high)
    pack_edges(f, drop_ref, low, high, to_cross, to_mate)


def gather(f, whole, low, own, high):
    for g, source in enumerate((low, own, high)):
        for i in range(f.h):
            whole[pl.ds(g * f.group + i * f.b, f.b), :] = source[pl.ds(i * f.b, f.b), :]


def correction_kernel(f, drop_ref, shifted, low, own, high, correction, whole):
    p = f.p
    gather(f, whole, low, own, high)
    for row, col in f.tiles(f.own_pairs):
        total = masked(f, right_tile(f, shifted, whole, row, col), row, col, drop_ref)
        correction[at(f, row, row + 1, col - p, col - p + 1)] = total.astype(correction.dtype)


def second_edges_kernel(
    f, drop_ref, mate, cross, correction, low, high, new_low, new_high, to_cross, to_mate
):
    p = f.p

    def start(row, col):
        c = col - p
        source, local = (low, row) if row < p else (high, row - 2 * p)
        total = 2.0 * source[at(f, local, local + 1, c, c + 1)].astype(jnp.float32)
        for g, a, z in f.split(row, col):
            if g == 1:
                total = total - dot(
                    source[at(f, local, local + 1, a, z)], correction[at(f, p + a, p + z, c, c + 1)]
                )
        return total

    below, above = sides(f, drop_ref, plain(mate), plain(cross))
    edges(f, drop_ref, below, above, correction, start, new_low, new_high)
    pack_edges(f, drop_ref, new_low, new_high, to_cross, to_mate)


def density_edges_kernel(
    f, drop_ref, own, cross, mate, correction, new_low, new_high, square, whole, to_cross, to_mate,
    before, after, low, high,
):
    h, p = f.h, f.p
    below, above = sides(f, drop_ref, indexed(f, mate), indexed(f, cross))
    spread(f, before, 0, 0, below, over(h))
    spread(f, after, 0, 0, above, under(h))
    for row, col in f.tiles(f.own_pairs):
        if row not in f.own_pairs:
            continue
        c, local = col - p, row - p
        total = 2.0 * own[at(f, local, local + 1, c, c + 1)].astype(jnp.float32)
        for g, a, z in f.split(row, col):
            left = (before, own, after)[g][at(f, local, local + 1, a, z)]
            total = total - dot(left, correction[at(f, g * p + a, g * p + z, c, c + 1)])
        total = masked(f, total, row, col, drop_ref)
        whole[at(f, row, row + 1, c, c + 1)] = total.astype(whole.dtype)
    for i in range(h):
        rows = pl.ds(i * f.b, f.b)
        whole[pl.ds(i * f.b, f.b), :] = new_low[rows, :]
        whole[pl.ds(2 * f.group + i * f.b, f.b), :] = new_high[rows, :]
    for row, col in f.tiles(f.own_pairs):
        if row in f.own_pairs:
            continue
        total = masked(f, right_tile(f, square, whole, row, col), row, col, drop_ref)
        dest, local = (low, row) if row < p else (high, row - 2 * p)
        dest[at(f, local, local + 1, col - p, col - p + 1)] = total.astype(dest.dtype)
    pack_edges(f, drop_ref, low, high, to_cross, to_mate)


def density_own_kernel(f, drop_ref, square, whole, out):
    p = f.p
    for row, col in f.tiles(f.own_pairs):
        if row in f.own_pairs:
            total = masked(f, right_tile(f, square, whole, row, col), row, col, drop_ref)
            out[at(f, row - p, row - p + 1, col - p, col - p + 1)] = total.astype(out.dtype)


def rows_kernel(f, first, drop_ref, own, cross, mate, out):
    h = f.h
    below, above = sides(f, drop_ref, indexed(f, mate), indexed(f, cross))
    over_index = {place: i for i, place in enumerate(over(h))}
    under_index = {place: i for i, place in enumerate(under(h))}
    for r in range(h):
        dropped = drop_ref[h + r]

        def at_offset(offset, r=r):
            col = r + offset
            if col < h:
                return below(over_index[r, col])
            if col < 2 * h:
                return own[block(f, first + r, col - h)]
            return above(under_index[r, col - 2 * h])

        for s in range(f.k):
            out[r, s] = jnp.where(dropped <= s, at_offset(s + 1), at_offset(s))


VMEM = pl.BlockSpec(memory_space=pltpu.VMEM)
SMEM = pl.BlockSpec(memory_space=pltpu.SMEM)
ANY = pl.BlockSpec(memory_space=pl.ANY)


def call(kernel, outs, scratch, flops, limit, drop, *args, passed=(), light=False):
    moved = sum(a.size * a.dtype.itemsize for a in args) + sum(s.size * s.dtype.itemsize for s in outs)
    if light:
        flops = moved = 0
    n = len(args)
    return pl.pallas_call(
        kernel,
        out_shape=[*outs, *[jax.ShapeDtypeStruct(a.shape, a.dtype) for a in passed]],
        in_specs=[SMEM] + [VMEM] * n + [ANY] * len(passed),
        out_specs=[VMEM] * len(outs) + [ANY] * len(passed),
        scratch_shapes=scratch,
        input_output_aliases={1 + n + i: len(outs) + i for i in range(len(passed))},
        compiler_params=pltpu.CompilerParams(vmem_limit_bytes=limit * MIB),
        cost_estimate=pl.CostEstimate(flops=flops, bytes_accessed=moved, transcendentals=0),
    )(drop, *args, *passed)


def routed(x, step):
    size = lax.axis_size(RING)
    return lax.ppermute(x, RING, [(i, (i + step(i)) % size) for i in range(size) if step(i)])


def on_device(density, inverse_start, block_cols):
    rows, width, order, _ = density.shape
    half = width // 2
    ring = lax.axis_size(RING)
    total = rows * ring
    assert rows == half and half % 2 == 0 and ring % 2 == 0
    f = Frame(half, order)
    kind = density.dtype
    me = lax.axis_index(RING)

    def mate_step(i):
        return 1 - 2 * (i % 2)

    def cross_step(i):
        return 2 * (i % 2) - 1

    def to_mate(x):
        return routed(x, mate_step)

    def to_cross(x):
        return routed(x, cross_step)

    positions = block_cols - (me * rows + jnp.arange(rows, dtype=jnp.int32))[:, None] + half
    positions = positions + jnp.where(positions < 0, total, jnp.where(positions >= total, -total, 0))
    own_drop = width * (width + 1) // 2 - jnp.sum(positions, axis=1)

    density_cross, density_mate = to_cross(density), to_mate(density)
    cross_drop, mate_drop = to_cross(own_drop), to_mate(own_drop)
    even = (me & 1) == 0
    mark = jnp.reshape(me & 1, (1,))
    start_drop = jnp.concatenate([own_drop, mark])
    drop = jnp.concatenate(
        [jnp.where(even, cross_drop, mate_drop), own_drop, jnp.where(even, mate_drop, cross_drop), mark]
    )

    unit = 2 * f.t**3
    count = half * (half + 1) // 2
    square_group = jax.ShapeDtypeStruct((f.group, f.group), kind)
    columns = jax.ShapeDtypeStruct((3 * f.group, f.group), kind)
    band = jax.ShapeDtypeStruct((3 * f.group, (2 * f.p + 1) * f.t), kind)
    triangle = jax.ShapeDtypeStruct((count * order, order), kind)
    half_triangle = jax.ShapeDtypeStruct((count // 2 * order, order), kind)
    listed = jax.ShapeDtypeStruct((half * half * order, order), kind)
    both = jax.ShapeDtypeStruct(((count + half * half) * order, order), kind)
    partial_sums = jax.ShapeDtypeStruct((2 * f.group, f.group), jnp.float32)
    group_scratch = pltpu.VMEM((f.group, f.group), kind)
    whole_scratch = pltpu.VMEM((3 * f.group, f.group), kind)

    def run(kernel, outs, scratch, tiles, limit, *args, **kw):
        return call(functools.partial(kernel, f), outs, scratch, tiles * unit, limit, *args, **kw)

    corner, corner_cross, slab_mate, triangle_cross = run(
        slabs_kernel, [listed, listed, both, triangle], [], 0, 12, start_drop, inverse_start
    )
    from_mate = to_mate(slab_mate)
    forward_mate, forward_mate_too, forward_far, triangle_cross, corner_cross = run(
        forward_kernel, [half_triangle, half_triangle, triangle], [], 0, 12, drop, density_cross, density_mate, from_mate,
        passed=(triangle_cross, corner_cross),
    )
    far_mate, far_mate_too = to_mate(forward_mate), to_mate(forward_mate_too)
    far_far = routed(forward_far, lambda i: 3 * cross_step(i))
    cross_triangle = to_cross(triangle_cross)
    cross_corner = to_cross(corner_cross)

    square, shifted = run(
        square_kernel,
        [band, band],
        [pltpu.VMEM((5 * f.group, 5 * f.group), kind)],
        94, 28, drop, density, density_cross, density_mate, far_far, far_mate, far_mate_too, light=True,
    )
    correction, own, partial = run(
        first_sweep_kernel,
        [columns, square_group, partial_sums],
        [whole_scratch, group_scratch, group_scratch],
        66, 24, drop, shifted, corner, slab_mate, triangle_cross, from_mate, cross_triangle, light=True,
    )
    corner_cross, corner_mate = to_cross(own), to_mate(own)
    low, high, edge_cross, edge_mate = run(
        first_edges_kernel,
        [square_group, square_group, triangle, triangle],
        [group_scratch] * 2,
        10, 16, drop, from_mate, cross_corner, correction, partial,
    )
    edge_cross, edge_mate = to_cross(edge_cross), to_mate(edge_mate)
    (correction,) = run(
        correction_kernel, [columns], [whole_scratch], 38, 16, drop, shifted, low, own, high
    )
    new_low, new_high, inverse_cross, inverse_mate = run(
        second_edges_kernel,
        [square_group, square_group, triangle, triangle],
        [],
        20, 12, drop, corner_mate, corner_cross, correction, low, high,
    )
    inverse_cross, inverse_mate = to_cross(inverse_cross), to_mate(inverse_mate)
    whole, rim_cross, rim_mate = run(
        density_edges_kernel,
        [columns, triangle, triangle],
        [group_scratch] * 4,
        38, 20, drop, own, edge_cross, edge_mate, correction, new_low, new_high, square,
    )
    rim_cross, rim_mate = to_cross(rim_cross), to_mate(rim_mate)
    (density_own,) = run(density_own_kernel, [square_group], [], 18, 12, drop, square, whole)
    out = jax.ShapeDtypeStruct(density.shape, kind)

    def assembled(own, first, cross, mate):
        return call(functools.partial(rows_kernel, f, first), [out], [], 0, 8, drop, own, cross, mate)[0]

    inverse_next = assembled(whole, half, inverse_cross, inverse_mate)
    density_next = assembled(density_own, 0, rim_cross, rim_mate)
    return density_next, inverse_next


def solution(mesh):
    blocks = P(("grp", "row", "inner"), None, None, None)
    return jax.shard_map(
        on_device,
        mesh=mesh,
        in_specs=(blocks, blocks, P(("grp", "row", "inner"), None)),
        out_specs=(blocks, blocks),
        check_vma=False,
    )
```

```python
import functools

import jax
import jax.numpy as jnp
from jax import lax
from jax.experimental import pallas as pl
from jax.experimental.pallas import tpu as pltpu
from jax.sharding import PartitionSpec as P

RING = ("row", "inner")
MIB = 1024 * 1024


class Frame:
    def __init__(self, half, order):
        self.h = half
        self.b = order
        self.k = 2 * half
        self.p = half // 2
        self.t = 2 * order
        self.group = half * order
        self.pairs = 3 * self.p
        self.own_pairs = range(self.p, 2 * self.p)
        self.edge_rows = [*range(self.p), *range(2 * self.p, 3 * self.p)]

    def tiles(self, columns):
        for col in columns:
            for row in range(max(0, col - self.p), min(self.pairs, col + self.p + 1)):
                yield row, col

    def inner(self, row, col):
        return max(row, col) - self.p, min(row, col) + self.p + 1

    def clipped(self, row, col):
        lo, hi = self.inner(row, col)
        return max(lo, 0), min(hi, self.pairs)

    def on_corner(self, row, col):
        return max(row, col) < self.p or min(row, col) >= 2 * self.p

    def corner_place(self, row, col):
        r, c = (row, col) if row < self.p else (row - self.p, col - 2 * self.p)
        return r, r + 1, c, c + 1

    def split(self, row, col):
        lo, hi = self.clipped(row, col)
        for g in range(3):
            a, z = max(lo, g * self.p), min(hi, (g + 1) * self.p)
            if a < z:
                yield g, a - g * self.p, z - g * self.p


def under(h):
    return [(r, c) for r in range(h) for c in range(r + 1)]


def over(h):
    return [(r, c) for r in range(h) for c in range(r, h)]


def full(h):
    return [(r, c) for r in range(h) for c in range(h)]


def at(f, row_lo, row_hi, col_lo, col_hi):
    t = f.t
    return pl.ds(row_lo * t, (row_hi - row_lo) * t), pl.ds(col_lo * t, (col_hi - col_lo) * t)


def block(f, r, c):
    return pl.ds(r * f.b, f.b), pl.ds(c * f.b, f.b)


def banded(f, row, lo, hi):
    return at(f, row, row + 1, lo - row + f.p, hi - row + f.p)


def dot(a, b):
    return jnp.dot(a, b, preferred_element_type=jnp.float32)


def stored(rows, r, offset, dropped, slots=None):
    last = (rows.shape[1] if slots is None else slots) - 1
    slot = jnp.minimum(offset - (offset > dropped).astype(jnp.int32), last)
    value = rows[r, slot] if slots is None else rows((r, slot))
    return jnp.where(offset == dropped, jnp.zeros_like(value), value)


def masked(f, tile, row, col, drop_ref):
    b = f.b
    parts = []
    for i in range(2):
        r = 2 * row + i
        line = []
        for j in range(2):
            offset = 2 * col + j - r + f.h
            piece = tile[i * b : (i + 1) * b, j * b : (j + 1) * b]
            if 0 <= offset <= f.k:
                piece = jnp.where(drop_ref[r] == offset, 0.0, piece)
            else:
                piece = jnp.zeros_like(piece)
            line.append(piece)
        parts.append(jnp.concatenate(line, axis=1))
    return jnp.concatenate(parts, axis=0)


def odd_place(f, drop_ref):
    return drop_ref[3 * f.h] == 1


def indexed(f, ref, first=0):
    return lambda i: ref[block(f, first + i, 0)]


def plain(ref):
    return lambda place: ref[place]


def sides(f, drop_ref, mate, cross):
    odd = odd_place(f, drop_ref)

    def below(key):
        return jnp.where(odd, mate(key), cross(key))

    def above(key):
        return jnp.where(odd, cross(key), mate(key))

    return below, above


def spread(f, dest, row, col, read, places):
    index = {place: i for i, place in enumerate(places)}
    for r in range(f.h):
        for c in range(f.h):
            i = index.get((r, c))
            dest[block(f, row + r, col + c)] = jnp.zeros((f.b, f.b), dest.dtype) if i is None else read(i)


def pack_edges(f, drop_ref, low, high, to_cross, to_mate):
    odd = odd_place(f, drop_ref)
    for i, (lower, upper) in enumerate(zip(under(f.h), over(f.h))):
        back, forth = low[block(f, *lower)], high[block(f, *upper)]
        to_cross[block(f, i, 0)] = jnp.where(odd, forth, back)
        to_mate[block(f, i, 0)] = jnp.where(odd, back, forth)


def slabs_kernel(f, drop_ref, own, corner, corner_again, to_mate, to_cross):
    h = f.h
    odd = drop_ref[h] == 1
    n = len(under(h))
    for i, (lower, upper) in enumerate(zip(under(h), over(h))):
        (r, c), (s, d) = lower, upper
        forth = stored(own, r, 2 * h + c - r, drop_ref[r])
        back = stored(own, s, d - s, drop_ref[s])
        to_mate[block(f, i, 0)] = jnp.where(odd, back, forth)
        to_cross[block(f, i, 0)] = jnp.where(odd, forth, back)
    for i, (r, c) in enumerate(full(h)):
        value = stored(own, r, c - r + h, drop_ref[r])
        corner[block(f, i, 0)] = value
        corner_again[block(f, i, 0)] = value
        to_mate[block(f, n + i, 0)] = value


def forward_kernel(f, drop_ref, cross, *refs):
    h = f.h
    odd = odd_place(f, drop_ref)
    to_mate, to_far = refs[-5:-3], refs[-3]
    for i, (lower, upper) in enumerate(zip(under(h), over(h))):
        (r, c), (s, d) = lower, upper
        forth = stored(cross, r, 2 * h + c - r, jnp.where(odd, drop_ref[2 * h + r], drop_ref[r]))
        back = stored(cross, s, d - s, jnp.where(odd, drop_ref[2 * h + s], drop_ref[s]))
        part, place = i % 2, i // 2
        to_mate[part][block(f, place, 0)] = jnp.where(odd, back, forth)
        to_far[block(f, i, 0)] = jnp.where(odd, forth, back)


def square_kernel(f, drop_ref, own, cross, mate, square, shifted, reach, here, partial, wide):
    h, p = f.h, f.p
    below, above = sides(f, drop_ref, plain(mate), plain(cross))
    for g, read in enumerate((below, plain(own), above)):
        for r in range(h):
            row = g * h + r
            first = 2 * (row // 2) - h
            for col in range(first, first + 2 * h + 2):
                offset = col - row + h
                if 0 <= offset <= f.k:
                    value = stored(read, r, offset, drop_ref[row], f.k)
                else:
                    value = jnp.zeros((f.b, f.b), wide.dtype)
                wide[block(f, row, col + h)] = value
    for i in range(h):
        for g, row in enumerate((i, 2 * h + i)):
            rows = pl.ds((g * h + i) * f.b, f.b)
            source = pl.ds(row * f.b, f.b)
            reach[rows, :] = wide[source, pl.ds(4 * g * f.group, f.group)]
            here[rows, :] = wide[source, pl.ds((2 * g + 1) * f.group, f.group)]
    unit = unit_tile(f)
    for row, col in f.tiles(range(f.pairs)):
        lo, hi = f.clipped(row, col)
        total = dot(
            wide[at(f, row, row + 1, lo + p, hi + p)], wide[at(f, lo, hi, col + p, col + p + 1)]
        )
        if f.on_corner(row, col):
            partial[at(f, *f.corner_place(row, col))] = total
            continue
        total = masked(f, total, row, col, drop_ref)
        place = banded(f, row, col, col + 1)
        tile = wide[at(f, row, row + 1, col + p, col + p + 1)].astype(jnp.float32)
        square[place] = total.astype(square.dtype)
        shifted[place] = moved(total, tile, unit if row == col else None).astype(shifted.dtype)


def unit_tile(f):
    rows = lax.broadcasted_iota(jnp.int32, (f.t, f.t), 0)
    return (rows == lax.broadcasted_iota(jnp.int32, (f.t, f.t), 1)).astype(jnp.float32)


def moved(total, tile, unit):
    value = 2.0 * total - 2.0 * tile
    return value if unit is None else value + unit


def corners_kernel(
    f, drop_ref, far_far, far_mate, far_mate_too, reach, here, partial, square, shifted, low, high
):
    p = f.p
    far_mates = [indexed(f, far_mate), indexed(f, far_mate_too)]
    far_below, far_above = sides(f, drop_ref, lambda i: far_mates[i % 2](i // 2), indexed(f, far_far))
    spread(f, low, 0, 0, far_below, under(f.h))
    spread(f, high, 0, 0, far_above, over(f.h))
    unit = unit_tile(f)
    for row, col in f.tiles(range(f.pairs)):
        if not f.on_corner(row, col):
            continue
        place = at(f, *f.corner_place(row, col))
        r, _, c, _ = f.corner_place(row, col)
        total = partial[place]
        if row < p:
            a, z, far = max(row, col), p, low
        else:
            a, z, far = 0, min(row, col) - 2 * p + 1, high
        if a < z:
            total = total + dot(reach[at(f, r, r + 1, a, z)], far[at(f, a, z, c, c + 1)])
        total = masked(f, total, row, col, drop_ref)
        tile = here[place].astype(jnp.float32)
        square[place] = total.astype(square.dtype)
        shifted[place] = moved(total, tile, unit if row == col else None).astype(shifted.dtype)


def right_tile(f, left, corners, right, row, col):
    lo, hi = f.clipped(row, col)
    total = None
    if row < f.p:
        inside = corners[at(f, row, row + 1, lo, f.p)]
        total = dot(inside, right[at(f, lo, f.p, col - f.p, col - f.p + 1)])
        lo = f.p
    elif row >= 2 * f.p:
        inside = corners[at(f, row - f.p, row - f.p + 1, 0, hi - 2 * f.p)]
        total = dot(inside, right[at(f, 2 * f.p, hi, col - f.p, col - f.p + 1)])
        hi = 2 * f.p
    rest = dot(left[banded(f, row, lo, hi)], right[at(f, lo, hi, col - f.p, col - f.p + 1)])
    return rest if total is None else total + rest


def first_sweep_kernel(
    f, drop_ref, shifted, corners, corner, sent_mate, sent_cross, mate, cross,
    correction, fresh, partial, whole, before, after,
):
    h, p = f.h, f.p
    from_below, from_above = sides(f, drop_ref, indexed(f, mate), indexed(f, cross))
    down, up = sides(f, drop_ref, indexed(f, sent_mate), indexed(f, sent_cross))
    spread(f, whole, 0, 0, from_below, under(h))
    spread(f, whole, h, 0, indexed(f, corner), full(h))
    spread(f, whole, 2 * h, 0, from_above, over(h))
    spread(f, before, 0, 0, down, over(h))
    spread(f, after, 0, 0, up, under(h))
    for row, col in f.tiles(f.own_pairs):
        total = masked(f, right_tile(f, shifted, corners, whole, row, col), row, col, drop_ref)
        correction[at(f, row, row + 1, col - p, col - p + 1)] = total.astype(correction.dtype)
    for row, col in f.tiles(f.own_pairs):
        c = col - p
        own_row = row in f.own_pairs
        total = 2.0 * whole[at(f, row, row + 1, c, c + 1)].astype(jnp.float32)
        for g, a, z in f.split(row, col):
            if g == 1:
                left = whole[at(f, row, row + 1, a, z)]
            elif own_row:
                left = (before, None, after)[g][at(f, row - p, row - p + 1, a, z)]
            else:
                continue
            total = total - dot(left, correction[at(f, g * p + a, g * p + z, c, c + 1)])
        if own_row:
            total = masked(f, total, row, col, drop_ref)
            fresh[at(f, row - p, row - p + 1, c, c + 1)] = total.astype(fresh.dtype)
        else:
            place = row if row < p else row - p
            partial[at(f, place, place + 1, c, c + 1)] = total


def edges(f, drop_ref, corner_below, corner_above, correction, start, low, high):
    p = f.p
    for row, col in f.tiles(f.own_pairs):
        if row in f.own_pairs:
            continue
        c = col - p
        side = 0 if row < p else 2
        corner, dest = ((corner_below, low), None, (corner_above, high))[side]
        local = row - side * p
        total = start(row, col)
        for g, a, z in f.split(row, col):
            if g == side:
                total = total - dot(
                    corner(at(f, local, local + 1, a, z)), correction[at(f, g * p + a, g * p + z, c, c + 1)]
                )
        total = masked(f, total, row, col, drop_ref)
        dest[at(f, local, local + 1, c, c + 1)] = total.astype(dest.dtype)


def first_edges_kernel(
    f, drop_ref, mate, cross, correction, partial, low, high, to_cross, to_mate, before, after
):
    p = f.p
    below, above = sides(f, drop_ref, indexed(f, mate, len(under(f.h))), indexed(f, cross))
    spread(f, before, 0, 0, below, full(f.h))
    spread(f, after, 0, 0, above, full(f.h))

    def start(row, col):
        place = row if row < p else row - p
        return partial[at(f, place, place + 1, col - p, col - p + 1)]

    edges(f, drop_ref, plain(before), plain(after), correction, start, low, high)
    pack_edges(f, drop_ref, low, high, to_cross, to_mate)


def gather(f, whole, low, own, high):
    for g, source in enumerate((low, own, high)):
        for i in range(f.h):
            whole[pl.ds(g * f.group + i * f.b, f.b), :] = source[pl.ds(i * f.b, f.b), :]


def correction_kernel(f, drop_ref, shifted, corners, low, own, high, correction, whole):
    p = f.p
    gather(f, whole, low, own, high)
    for row, col in f.tiles(f.own_pairs):
        total = masked(f, right_tile(f, shifted, corners, whole, row, col), row, col, drop_ref)
        correction[at(f, row, row + 1, col - p, col - p + 1)] = total.astype(correction.dtype)


def second_edges_kernel(
    f, drop_ref, cross, mate, correction, low, high, new_low, new_high, to_cross, to_mate
):
    p = f.p

    def start(row, col):
        c = col - p
        source, local = (low, row) if row < p else (high, row - 2 * p)
        total = 2.0 * source[at(f, local, local + 1, c, c + 1)].astype(jnp.float32)
        for g, a, z in f.split(row, col):
            if g == 1:
                total = total - dot(
                    source[at(f, local, local + 1, a, z)], correction[at(f, p + a, p + z, c, c + 1)]
                )
        return total

    below, above = sides(f, drop_ref, plain(mate), plain(cross))
    edges(f, drop_ref, below, above, correction, start, new_low, new_high)
    pack_edges(f, drop_ref, new_low, new_high, to_cross, to_mate)


def density_edges_kernel(
    f, drop_ref, own, cross, mate, correction, new_low, new_high, square, corners, whole, to_cross, to_mate,
    before, after, low, high,
):
    h, p = f.h, f.p
    below, above = sides(f, drop_ref, indexed(f, mate), indexed(f, cross))
    spread(f, before, 0, 0, below, over(h))
    spread(f, after, 0, 0, above, under(h))
    for row, col in f.tiles(f.own_pairs):
        if row not in f.own_pairs:
            continue
        c, local = col - p, row - p
        total = 2.0 * own[at(f, local, local + 1, c, c + 1)].astype(jnp.float32)
        for g, a, z in f.split(row, col):
            left = (before, own, after)[g][at(f, local, local + 1, a, z)]
            total = total - dot(left, correction[at(f, g * p + a, g * p + z, c, c + 1)])
        total = masked(f, total, row, col, drop_ref)
        whole[at(f, row, row + 1, c, c + 1)] = total.astype(whole.dtype)
    for i in range(h):
        rows = pl.ds(i * f.b, f.b)
        whole[pl.ds(i * f.b, f.b), :] = new_low[rows, :]
        whole[pl.ds(2 * f.group + i * f.b, f.b), :] = new_high[rows, :]
    for row, col in f.tiles(f.own_pairs):
        if row in f.own_pairs:
            continue
        total = masked(f, right_tile(f, square, corners, whole, row, col), row, col, drop_ref)
        dest, local = (low, row) if row < p else (high, row - 2 * p)
        dest[at(f, local, local + 1, col - p, col - p + 1)] = total.astype(dest.dtype)
    pack_edges(f, drop_ref, low, high, to_cross, to_mate)


def density_own_kernel(f, drop_ref, square, whole, out):
    p = f.p
    for row, col in f.tiles(f.own_pairs):
        if row in f.own_pairs:
            total = masked(f, right_tile(f, square, None, whole, row, col), row, col, drop_ref)
            out[at(f, row - p, row - p + 1, col - p, col - p + 1)] = total.astype(out.dtype)


def rows_kernel(f, first, drop_ref, own, cross, mate, out):
    h = f.h
    below, above = sides(f, drop_ref, indexed(f, mate), indexed(f, cross))
    over_index = {place: i for i, place in enumerate(over(h))}
    under_index = {place: i for i, place in enumerate(under(h))}
    for r in range(h):
        dropped = drop_ref[h + r]

        def at_offset(offset, r=r):
            col = r + offset
            if col < h:
                return below(over_index[r, col])
            if col < 2 * h:
                return own[block(f, first + r, col - h)]
            return above(under_index[r, col - 2 * h])

        for s in range(f.k):
            out[r, s] = jnp.where(dropped <= s, at_offset(s + 1), at_offset(s))


VMEM = pl.BlockSpec(memory_space=pltpu.VMEM)
SMEM = pl.BlockSpec(memory_space=pltpu.SMEM)
ANY = pl.BlockSpec(memory_space=pl.ANY)


def call(kernel, outs, scratch, flops, limit, drop, *args, passed=(), light=False):
    moved = sum(a.size * a.dtype.itemsize for a in args) + sum(s.size * s.dtype.itemsize for s in outs)
    if light:
        flops = moved = 0
    n = len(args)
    return pl.pallas_call(
        kernel,
        out_shape=[*outs, *[jax.ShapeDtypeStruct(a.shape, a.dtype) for a in passed]],
        in_specs=[SMEM] + [VMEM] * n + [ANY] * len(passed),
        out_specs=[VMEM] * len(outs) + [ANY] * len(passed),
        scratch_shapes=scratch,
        input_output_aliases={1 + n + i: len(outs) + i for i in range(len(passed))},
        compiler_params=pltpu.CompilerParams(vmem_limit_bytes=limit * MIB),
        cost_estimate=pl.CostEstimate(flops=flops, bytes_accessed=moved, transcendentals=0),
    )(drop, *args, *passed)


def routed(x, step):
    size = lax.axis_size(RING)
    return lax.ppermute(x, RING, [(i, (i + step(i)) % size) for i in range(size) if step(i)])


def on_device(density, inverse_start, block_cols):
    rows, width, order, _ = density.shape
    half = width // 2
    ring = lax.axis_size(RING)
    total = rows * ring
    assert rows == half and half % 2 == 0 and ring % 2 == 0
    f = Frame(half, order)
    kind = density.dtype
    me = lax.axis_index(RING)

    def mate_step(i):
        return 1 - 2 * (i % 2)

    def cross_step(i):
        return 2 * (i % 2) - 1

    def to_mate(x):
        return routed(x, mate_step)

    def to_cross(x):
        return routed(x, cross_step)

    positions = block_cols - (me * rows + jnp.arange(rows, dtype=jnp.int32))[:, None] + half
    positions = positions + jnp.where(positions < 0, total, jnp.where(positions >= total, -total, 0))
    own_drop = width * (width + 1) // 2 - jnp.sum(positions, axis=1)

    density_cross, density_mate = to_cross(density), to_mate(density)
    cross_drop, mate_drop = to_cross(own_drop), to_mate(own_drop)
    even = (me & 1) == 0
    mark = jnp.reshape(me & 1, (1,))
    start_drop = jnp.concatenate([own_drop, mark])
    drop = jnp.concatenate(
        [jnp.where(even, cross_drop, mate_drop), own_drop, jnp.where(even, mate_drop, cross_drop), mark]
    )

    unit = 2 * f.t**3
    count = half * (half + 1) // 2
    square_group = jax.ShapeDtypeStruct((f.group, f.group), kind)
    columns = jax.ShapeDtypeStruct((3 * f.group, f.group), kind)
    band = jax.ShapeDtypeStruct((3 * f.group, (2 * f.p + 1) * f.t), kind)
    triangle = jax.ShapeDtypeStruct((count * order, order), kind)
    half_triangle = jax.ShapeDtypeStruct((count // 2 * order, order), kind)
    listed = jax.ShapeDtypeStruct((half * half * order, order), kind)
    both = jax.ShapeDtypeStruct(((count + half * half) * order, order), kind)
    partial_sums = jax.ShapeDtypeStruct((2 * f.group, f.group), jnp.float32)
    group_scratch = pltpu.VMEM((f.group, f.group), kind)
    whole_scratch = pltpu.VMEM((3 * f.group, f.group), kind)

    def run(kernel, outs, scratch, tiles, limit, *args, **kw):
        return call(functools.partial(kernel, f), outs, scratch, tiles * unit, limit, *args, **kw)

    corner, corner_cross, slab_mate, triangle_cross = run(
        slabs_kernel, [listed, listed, both, triangle], [], 0, 12, start_drop, inverse_start
    )
    from_mate = to_mate(slab_mate)
    forward_mate, forward_mate_too, forward_far, triangle_cross, corner_cross = run(
        forward_kernel, [half_triangle, half_triangle, triangle], [], 0, 12, drop, density_cross, density_mate, from_mate,
        passed=(triangle_cross, corner_cross),
    )
    far_mate, far_mate_too = to_mate(forward_mate), to_mate(forward_mate_too)
    far_far = routed(forward_far, lambda i: 3 * cross_step(i))
    cross_triangle = to_cross(triangle_cross)
    cross_corner = to_cross(corner_cross)

    both_corners = jax.ShapeDtypeStruct((2 * f.group, f.group), kind)
    square, shifted, reach, here, partial = run(
        square_kernel,
        [band, band, both_corners, both_corners, partial_sums],
        [pltpu.VMEM((3 * f.group, 5 * f.group), kind)],
        84, 26, drop, density, density_cross, density_mate,
    )
    square_corners, shifted_corners = run(
        corners_kernel,
        [both_corners, both_corners],
        [group_scratch] * 2,
        10, 16, drop, far_far, far_mate, far_mate_too, reach, here, partial, light=True,
    )
    correction, own, partial = run(
        first_sweep_kernel,
        [columns, square_group, partial_sums],
        [whole_scratch, group_scratch, group_scratch],
        66, 24, drop, shifted, shifted_corners, corner, slab_mate, triangle_cross, from_mate, cross_triangle, light=True,
    )
    corner_cross, corner_mate = to_cross(own), to_mate(own)
    low, high, edge_cross, edge_mate = run(
        first_edges_kernel,
        [square_group, square_group, triangle, triangle],
        [group_scratch] * 2,
        10, 16, drop, from_mate, cross_corner, correction, partial,
    )
    edge_cross, edge_mate = to_cross(edge_cross), to_mate(edge_mate)
    (correction,) = run(
        correction_kernel, [columns], [whole_scratch], 38, 16, drop, shifted, shifted_corners, low, own, high
    )
    new_low, new_high, inverse_cross, inverse_mate = run(
        second_edges_kernel,
        [square_group, square_group, triangle, triangle],
        [],
        20, 12, drop, corner_cross, corner_mate, correction, low, high,
    )
    inverse_cross, inverse_mate = to_cross(inverse_cross), to_mate(inverse_mate)
    whole, rim_cross, rim_mate = run(
        density_edges_kernel,
        [columns, triangle, triangle],
        [group_scratch] * 4,
        38, 20, drop, own, edge_cross, edge_mate, correction, new_low, new_high, square,
        square_corners,
    )
    rim_cross, rim_mate = to_cross(rim_cross), to_mate(rim_mate)
    (density_own,) = run(density_own_kernel, [square_group], [], 18, 12, drop, square, whole)
    out = jax.ShapeDtypeStruct(density.shape, kind)

    def assembled(own, first, cross, mate):
        return call(functools.partial(rows_kernel, f, first), [out], [], 0, 8, drop, own, cross, mate)[0]

    inverse_next = assembled(whole, half, inverse_cross, inverse_mate)
    density_next = assembled(density_own, 0, rim_cross, rim_mate)
    return density_next, inverse_next


def solution(mesh):
    blocks = P(("grp", "row", "inner"), None, None, None)
    return jax.shard_map(
        on_device,
        mesh=mesh,
        in_specs=(blocks, blocks, P(("grp", "row", "inner"), None)),
        out_specs=(blocks, blocks),
        check_vma=False,
    )
```

```python
import functools

import jax
import jax.numpy as jnp
from jax import lax
from jax.experimental import pallas as pl
from jax.experimental.pallas import tpu as pltpu
from jax.sharding import PartitionSpec as P

RING = ("row", "inner")
MIB = 1024 * 1024


class Frame:
    def __init__(self, half, order):
        self.h = half
        self.b = order
        self.k = 2 * half
        self.p = half // 2
        self.t = 2 * order
        self.group = half * order
        self.pairs = 3 * self.p
        self.own_pairs = range(self.p, 2 * self.p)
        self.edge_rows = [*range(self.p), *range(2 * self.p, 3 * self.p)]

    def tiles(self, columns):
        for col in columns:
            for row in range(max(0, col - self.p), min(self.pairs, col + self.p + 1)):
                yield row, col

    def inner(self, row, col):
        return max(row, col) - self.p, min(row, col) + self.p + 1

    def clipped(self, row, col):
        lo, hi = self.inner(row, col)
        return max(lo, 0), min(hi, self.pairs)

    def on_corner(self, row, col):
        return max(row, col) < self.p or min(row, col) >= 2 * self.p

    def corner_place(self, row, col):
        r, c = (row, col) if row < self.p else (row - self.p, col - 2 * self.p)
        return r, r + 1, c, c + 1

    def split(self, row, col):
        lo, hi = self.clipped(row, col)
        for g in range(3):
            a, z = max(lo, g * self.p), min(hi, (g + 1) * self.p)
            if a < z:
                yield g, a - g * self.p, z - g * self.p


def under(h):
    return [(r, c) for r in range(h) for c in range(r + 1)]


def over(h):
    return [(r, c) for r in range(h) for c in range(r, h)]


def full(h):
    return [(r, c) for r in range(h) for c in range(h)]


def at(f, row_lo, row_hi, col_lo, col_hi):
    t = f.t
    return pl.ds(row_lo * t, (row_hi - row_lo) * t), pl.ds(col_lo * t, (col_hi - col_lo) * t)


def block(f, r, c):
    return pl.ds(r * f.b, f.b), pl.ds(c * f.b, f.b)


def banded(f, row, lo, hi):
    return at(f, row, row + 1, lo - row + f.p, hi - row + f.p)


def dot(a, b):
    return jnp.dot(a, b, preferred_element_type=jnp.float32)


def stored(rows, r, offset, dropped, slots=None):
    last = (rows.shape[1] if slots is None else slots) - 1
    slot = jnp.minimum(offset - (offset > dropped).astype(jnp.int32), last)
    value = rows[r, slot] if slots is None else rows((r, slot))
    return jnp.where(offset == dropped, jnp.zeros_like(value), value)


def masked(f, tile, row, col, drop_ref):
    b = f.b
    parts = []
    for i in range(2):
        r = 2 * row + i
        line = []
        for j in range(2):
            offset = 2 * col + j - r + f.h
            piece = tile[i * b : (i + 1) * b, j * b : (j + 1) * b]
            if 0 <= offset <= f.k:
                piece = jnp.where(drop_ref[r] == offset, 0.0, piece)
            else:
                piece = jnp.zeros_like(piece)
            line.append(piece)
        parts.append(jnp.concatenate(line, axis=1))
    return jnp.concatenate(parts, axis=0)


def odd_place(f, drop_ref):
    return drop_ref[3 * f.h] == 1


def indexed(f, ref, first=0):
    return lambda i: ref[block(f, first + i, 0)]


def plain(ref):
    return lambda place: ref[place]


def sides(f, drop_ref, mate, cross):
    odd = odd_place(f, drop_ref)

    def below(key):
        return jnp.where(odd, mate(key), cross(key))

    def above(key):
        return jnp.where(odd, cross(key), mate(key))

    return below, above


def spread(f, dest, row, col, read, places):
    index = {place: i for i, place in enumerate(places)}
    for r in range(f.h):
        for c in range(f.h):
            i = index.get((r, c))
            dest[block(f, row + r, col + c)] = jnp.zeros((f.b, f.b), dest.dtype) if i is None else read(i)


def pack_edges(f, drop_ref, low, high, to_cross, to_mate):
    odd = odd_place(f, drop_ref)
    for i, (lower, upper) in enumerate(zip(under(f.h), over(f.h))):
        back, forth = low[block(f, *lower)], high[block(f, *upper)]
        to_cross[block(f, i, 0)] = jnp.where(odd, forth, back)
        to_mate[block(f, i, 0)] = jnp.where(odd, back, forth)


def slabs_kernel(f, drop_ref, own, corner, corner_again, to_mate, to_cross, to_cross_again):
    h = f.h
    odd = drop_ref[h] == 1
    n = len(under(h))
    for i, (lower, upper) in enumerate(zip(under(h), over(h))):
        (r, c), (s, d) = lower, upper
        forth = stored(own, r, 2 * h + c - r, drop_ref[r])
        back = stored(own, s, d - s, drop_ref[s])
        to_mate[block(f, i, 0)] = jnp.where(odd, back, forth)
        across = jnp.where(odd, forth, back)
        to_cross[block(f, i, 0)] = across
        to_cross_again[block(f, i, 0)] = across
    for i, (r, c) in enumerate(full(h)):
        value = stored(own, r, c - r + h, drop_ref[r])
        corner[block(f, i, 0)] = value
        corner_again[block(f, i, 0)] = value
        to_mate[block(f, n + i, 0)] = value


def forward_kernel(f, drop_ref, cross, *refs):
    h = f.h
    odd = odd_place(f, drop_ref)
    to_mate, to_far = refs[-5:-3], refs[-3]
    for i, (lower, upper) in enumerate(zip(under(h), over(h))):
        (r, c), (s, d) = lower, upper
        forth = stored(cross, r, 2 * h + c - r, jnp.where(odd, drop_ref[2 * h + r], drop_ref[r]))
        back = stored(cross, s, d - s, jnp.where(odd, drop_ref[2 * h + s], drop_ref[s]))
        part, place = i % 2, i // 2
        to_mate[part][block(f, place, 0)] = jnp.where(odd, back, forth)
        to_far[block(f, i, 0)] = jnp.where(odd, forth, back)


def square_kernel(f, drop_ref, own, cross, mate, square, shifted, reach, here, partial, wide):
    h, p = f.h, f.p
    below, above = sides(f, drop_ref, plain(mate), plain(cross))
    for g, read in enumerate((below, plain(own), above)):
        for r in range(h):
            row = g * h + r
            first = 2 * (row // 2) - h
            for col in range(first, first + 2 * h + 2):
                offset = col - row + h
                if 0 <= offset <= f.k:
                    value = stored(read, r, offset, drop_ref[row], f.k)
                else:
                    value = jnp.zeros((f.b, f.b), wide.dtype)
                wide[block(f, row, col + h)] = value
    for i in range(h):
        for g, row in enumerate((i, 2 * h + i)):
            rows = pl.ds((g * h + i) * f.b, f.b)
            source = pl.ds(row * f.b, f.b)
            reach[rows, :] = wide[source, pl.ds(4 * g * f.group, f.group)]
            here[rows, :] = wide[source, pl.ds((2 * g + 1) * f.group, f.group)]
    unit = unit_tile(f)
    for row, col in f.tiles(range(f.pairs)):
        lo, hi = f.clipped(row, col)
        total = dot(
            wide[at(f, row, row + 1, lo + p, hi + p)], wide[at(f, lo, hi, col + p, col + p + 1)]
        )
        if f.on_corner(row, col):
            partial[at(f, *f.corner_place(row, col))] = total
            continue
        total = masked(f, total, row, col, drop_ref)
        place = banded(f, row, col, col + 1)
        tile = wide[at(f, row, row + 1, col + p, col + p + 1)].astype(jnp.float32)
        square[place] = total.astype(square.dtype)
        shifted[place] = moved(total, tile, unit if row == col else None).astype(shifted.dtype)


def unit_tile(f):
    rows = lax.broadcasted_iota(jnp.int32, (f.t, f.t), 0)
    return (rows == lax.broadcasted_iota(jnp.int32, (f.t, f.t), 1)).astype(jnp.float32)


def moved(total, tile, unit):
    value = 2.0 * total - 2.0 * tile
    return value if unit is None else value + unit


def corners_kernel(
    f, drop_ref, far_far, far_mate, far_mate_too, reach, here, partial, unused, square, shifted, low, high
):
    p = f.p
    far_mates = [indexed(f, far_mate), indexed(f, far_mate_too)]
    far_below, far_above = sides(f, drop_ref, lambda i: far_mates[i % 2](i // 2), indexed(f, far_far))
    spread(f, low, 0, 0, far_below, under(f.h))
    spread(f, high, 0, 0, far_above, over(f.h))
    unit = unit_tile(f)
    for row, col in f.tiles(range(f.pairs)):
        if not f.on_corner(row, col):
            continue
        place = at(f, *f.corner_place(row, col))
        r, _, c, _ = f.corner_place(row, col)
        total = partial[place]
        if row < p:
            a, z, far = max(row, col), p, low
        else:
            a, z, far = 0, min(row, col) - 2 * p + 1, high
        if a < z:
            total = total + dot(reach[at(f, r, r + 1, a, z)], far[at(f, a, z, c, c + 1)])
        total = masked(f, total, row, col, drop_ref)
        tile = here[place].astype(jnp.float32)
        square[place] = total.astype(square.dtype)
        shifted[place] = moved(total, tile, unit if row == col else None).astype(shifted.dtype)


def right_tile(f, left, corners, right, row, col):
    lo, hi = f.clipped(row, col)
    total = None
    if row < f.p:
        inside = corners[at(f, row, row + 1, lo, f.p)]
        total = dot(inside, right[at(f, lo, f.p, col - f.p, col - f.p + 1)])
        lo = f.p
    elif row >= 2 * f.p:
        inside = corners[at(f, row - f.p, row - f.p + 1, 0, hi - 2 * f.p)]
        total = dot(inside, right[at(f, 2 * f.p, hi, col - f.p, col - f.p + 1)])
        hi = 2 * f.p
    rest = dot(left[banded(f, row, lo, hi)], right[at(f, lo, hi, col - f.p, col - f.p + 1)])
    return rest if total is None else total + rest


def first_sweep_kernel(
    f, drop_ref, shifted, corners, corner, sent_mate, sent_cross, mate, direct, turned,
    correction, fresh, partial, whole, before, after,
):
    h, p = f.h, f.p
    turning = drop_ref[3 * h + 1] == 1
    direct_block, turned_block = indexed(f, direct), indexed(f, turned)

    def cross(i):
        return jnp.where(turning, turned_block(i), direct_block(i))

    from_below, from_above = sides(f, drop_ref, indexed(f, mate), cross)
    down, up = sides(f, drop_ref, indexed(f, sent_mate), indexed(f, sent_cross))
    spread(f, whole, 0, 0, from_below, under(h))
    spread(f, whole, h, 0, indexed(f, corner), full(h))
    spread(f, whole, 2 * h, 0, from_above, over(h))
    spread(f, before, 0, 0, down, over(h))
    spread(f, after, 0, 0, up, under(h))
    for row, col in f.tiles(f.own_pairs):
        total = masked(f, right_tile(f, shifted, corners, whole, row, col), row, col, drop_ref)
        correction[at(f, row, row + 1, col - p, col - p + 1)] = total.astype(correction.dtype)
    for row, col in f.tiles(f.own_pairs):
        c = col - p
        own_row = row in f.own_pairs
        total = 2.0 * whole[at(f, row, row + 1, c, c + 1)].astype(jnp.float32)
        for g, a, z in f.split(row, col):
            if g == 1:
                left = whole[at(f, row, row + 1, a, z)]
            elif own_row:
                left = (before, None, after)[g][at(f, row - p, row - p + 1, a, z)]
            else:
                continue
            total = total - dot(left, correction[at(f, g * p + a, g * p + z, c, c + 1)])
        if own_row:
            total = masked(f, total, row, col, drop_ref)
            fresh[at(f, row - p, row - p + 1, c, c + 1)] = total.astype(fresh.dtype)
        else:
            place = row if row < p else row - p
            partial[at(f, place, place + 1, c, c + 1)] = total


def edges(f, drop_ref, corner_below, corner_above, correction, start, low, high):
    p = f.p
    for row, col in f.tiles(f.own_pairs):
        if row in f.own_pairs:
            continue
        c = col - p
        side = 0 if row < p else 2
        corner, dest = ((corner_below, low), None, (corner_above, high))[side]
        local = row - side * p
        total = start(row, col)
        for g, a, z in f.split(row, col):
            if g == side:
                total = total - dot(
                    corner(at(f, local, local + 1, a, z)), correction[at(f, g * p + a, g * p + z, c, c + 1)]
                )
        total = masked(f, total, row, col, drop_ref)
        dest[at(f, local, local + 1, c, c + 1)] = total.astype(dest.dtype)


def first_edges_kernel(
    f, drop_ref, mate, cross, correction, partial, low, high, to_cross, to_mate, before, after
):
    p = f.p
    below, above = sides(f, drop_ref, indexed(f, mate, len(under(f.h))), indexed(f, cross))
    spread(f, before, 0, 0, below, full(f.h))
    spread(f, after, 0, 0, above, full(f.h))

    def start(row, col):
        place = row if row < p else row - p
        return partial[at(f, place, place + 1, col - p, col - p + 1)]

    edges(f, drop_ref, plain(before), plain(after), correction, start, low, high)
    pack_edges(f, drop_ref, low, high, to_cross, to_mate)


def gather(f, whole, low, own, high):
    for g, source in enumerate((low, own, high)):
        for i in range(f.h):
            whole[pl.ds(g * f.group + i * f.b, f.b), :] = source[pl.ds(i * f.b, f.b), :]


def correction_kernel(f, drop_ref, shifted, corners, low, own, high, correction, whole):
    p = f.p
    gather(f, whole, low, own, high)
    for row, col in f.tiles(f.own_pairs):
        total = masked(f, right_tile(f, shifted, corners, whole, row, col), row, col, drop_ref)
        correction[at(f, row, row + 1, col - p, col - p + 1)] = total.astype(correction.dtype)


def second_edges_kernel(
    f, drop_ref, mate, cross, correction, low, high, new_low, new_high, to_cross, to_mate
):
    p = f.p

    def start(row, col):
        c = col - p
        source, local = (low, row) if row < p else (high, row - 2 * p)
        total = 2.0 * source[at(f, local, local + 1, c, c + 1)].astype(jnp.float32)
        for g, a, z in f.split(row, col):
            if g == 1:
                total = total - dot(
                    source[at(f, local, local + 1, a, z)], correction[at(f, p + a, p + z, c, c + 1)]
                )
        return total

    below, above = sides(f, drop_ref, plain(mate), plain(cross))
    edges(f, drop_ref, below, above, correction, start, new_low, new_high)
    pack_edges(f, drop_ref, new_low, new_high, to_cross, to_mate)


def density_edges_kernel(
    f, drop_ref, own, cross, mate, correction, new_low, new_high, square, corners, whole, to_cross, to_mate,
    before, after, low, high,
):
    h, p = f.h, f.p
    below, above = sides(f, drop_ref, indexed(f, mate), indexed(f, cross))
    spread(f, before, 0, 0, below, over(h))
    spread(f, after, 0, 0, above, under(h))
    for row, col in f.tiles(f.own_pairs):
        if row not in f.own_pairs:
            continue
        c, local = col - p, row - p
        total = 2.0 * own[at(f, local, local + 1, c, c + 1)].astype(jnp.float32)
        for g, a, z in f.split(row, col):
            left = (before, own, after)[g][at(f, local, local + 1, a, z)]
            total = total - dot(left, correction[at(f, g * p + a, g * p + z, c, c + 1)])
        total = masked(f, total, row, col, drop_ref)
        whole[at(f, row, row + 1, c, c + 1)] = total.astype(whole.dtype)
    for i in range(h):
        rows = pl.ds(i * f.b, f.b)
        whole[pl.ds(i * f.b, f.b), :] = new_low[rows, :]
        whole[pl.ds(2 * f.group + i * f.b, f.b), :] = new_high[rows, :]
    for row, col in f.tiles(f.own_pairs):
        if row in f.own_pairs:
            continue
        total = masked(f, right_tile(f, square, corners, whole, row, col), row, col, drop_ref)
        dest, local = (low, row) if row < p else (high, row - 2 * p)
        dest[at(f, local, local + 1, col - p, col - p + 1)] = total.astype(dest.dtype)
    pack_edges(f, drop_ref, low, high, to_cross, to_mate)


def density_own_kernel(f, drop_ref, square, whole, out):
    p = f.p
    for row, col in f.tiles(f.own_pairs):
        if row in f.own_pairs:
            total = masked(f, right_tile(f, square, None, whole, row, col), row, col, drop_ref)
            out[at(f, row - p, row - p + 1, col - p, col - p + 1)] = total.astype(out.dtype)


def rows_kernel(f, first, drop_ref, own, cross, mate, out):
    h = f.h
    below, above = sides(f, drop_ref, indexed(f, mate), indexed(f, cross))
    over_index = {place: i for i, place in enumerate(over(h))}
    under_index = {place: i for i, place in enumerate(under(h))}
    for r in range(h):
        dropped = drop_ref[h + r]

        def at_offset(offset, r=r):
            col = r + offset
            if col < h:
                return below(over_index[r, col])
            if col < 2 * h:
                return own[block(f, first + r, col - h)]
            return above(under_index[r, col - 2 * h])

        for s in range(f.k):
            out[r, s] = jnp.where(dropped <= s, at_offset(s + 1), at_offset(s))


VMEM = pl.BlockSpec(memory_space=pltpu.VMEM)
SMEM = pl.BlockSpec(memory_space=pltpu.SMEM)
ANY = pl.BlockSpec(memory_space=pl.ANY)


def call(kernel, outs, scratch, flops, limit, drop, *args, passed=(), light=False):
    moved = sum(a.size * a.dtype.itemsize for a in args) + sum(s.size * s.dtype.itemsize for s in outs)
    if light:
        flops = moved = 0
    n = len(args)
    return pl.pallas_call(
        kernel,
        out_shape=[*outs, *[jax.ShapeDtypeStruct(a.shape, a.dtype) for a in passed]],
        in_specs=[SMEM] + [VMEM] * n + [ANY] * len(passed),
        out_specs=[VMEM] * len(outs) + [ANY] * len(passed),
        scratch_shapes=scratch,
        input_output_aliases={1 + n + i: len(outs) + i for i in range(len(passed))},
        compiler_params=pltpu.CompilerParams(vmem_limit_bytes=limit * MIB),
        cost_estimate=pl.CostEstimate(flops=flops, bytes_accessed=moved, transcendentals=0),
    )(drop, *args, *passed)


def routed(x, step):
    size = lax.axis_size(RING)
    return lax.ppermute(x, RING, [(i, (i + step(i)) % size) for i in range(size) if step(i)])


def on_device(density, inverse_start, block_cols):
    rows, width, order, _ = density.shape
    half = width // 2
    ring, inner = lax.axis_size(RING), lax.axis_size(RING[1])
    total = rows * ring
    assert rows == half and half % 2 == 0 and inner % 2 == 0
    f = Frame(half, order)
    kind = density.dtype
    me = lax.axis_index(RING)

    def mate_step(i):
        return 1 - 2 * (i % 2)

    def cross_step(i):
        return 2 * (i % 2) - 1

    def to_mate(x):
        return routed(x, mate_step)

    def to_cross(x):
        return routed(x, cross_step)

    def turns(i):
        return i % inner in (0, inner - 1)

    positions = block_cols - (me * rows + jnp.arange(rows, dtype=jnp.int32))[:, None] + half
    positions = positions + jnp.where(positions < 0, total, jnp.where(positions >= total, -total, 0))
    own_drop = width * (width + 1) // 2 - jnp.sum(positions, axis=1)

    density_cross, density_mate = to_cross(density), to_mate(density)
    cross_drop, mate_drop = to_cross(own_drop), to_mate(own_drop)
    even = (me & 1) == 0
    place = lax.axis_index(RING[1])
    marks = jnp.stack([me & 1, ((place == 0) | (place == inner - 1)).astype(jnp.int32)])
    start_drop = jnp.concatenate([own_drop, marks[:1]])
    drop = jnp.concatenate(
        [jnp.where(even, cross_drop, mate_drop), own_drop, jnp.where(even, mate_drop, cross_drop), marks]
    )

    unit = 2 * f.t**3
    count = half * (half + 1) // 2
    square_group = jax.ShapeDtypeStruct((f.group, f.group), kind)
    columns = jax.ShapeDtypeStruct((3 * f.group, f.group), kind)
    band = jax.ShapeDtypeStruct((3 * f.group, (2 * f.p + 1) * f.t), kind)
    triangle = jax.ShapeDtypeStruct((count * order, order), kind)
    half_triangle = jax.ShapeDtypeStruct((count // 2 * order, order), kind)
    listed = jax.ShapeDtypeStruct((half * half * order, order), kind)
    both = jax.ShapeDtypeStruct(((count + half * half) * order, order), kind)
    partial_sums = jax.ShapeDtypeStruct((2 * f.group, f.group), jnp.float32)
    group_scratch = pltpu.VMEM((f.group, f.group), kind)
    whole_scratch = pltpu.VMEM((3 * f.group, f.group), kind)

    def run(kernel, outs, scratch, tiles, limit, *args, **kw):
        return call(functools.partial(kernel, f), outs, scratch, tiles * unit, limit, *args, **kw)

    corner, corner_cross, slab_mate, triangle_cross, triangle_turning = run(
        slabs_kernel, [listed, listed, both, triangle, triangle], [], 0, 12, start_drop, inverse_start
    )
    from_mate = to_mate(slab_mate)
    direct_triangle = routed(triangle_cross, lambda i: 0 if turns(i) else cross_step(i))
    forward_mate, forward_mate_too, forward_far, triangle_turning, corner_cross = run(
        forward_kernel, [half_triangle, half_triangle, triangle], [], 0, 12, drop, density_cross, density_mate, from_mate,
        passed=(triangle_turning, corner_cross),
    )
    far_mate, far_mate_too = to_mate(forward_mate), to_mate(forward_mate_too)
    far_far = routed(forward_far, lambda i: 3 * cross_step(i))
    turned_triangle = routed(triangle_turning, lambda i: cross_step(i) if turns(i) else 0)
    cross_corner = to_cross(corner_cross)

    both_corners = jax.ShapeDtypeStruct((2 * f.group, f.group), kind)
    square, shifted, reach, here, partial = run(
        square_kernel,
        [band, band, both_corners, both_corners, partial_sums],
        [pltpu.VMEM((3 * f.group, 5 * f.group), kind)],
        84, 26, drop, density, density_cross, density_mate, light=True,
    )
    square_corners, shifted_corners = run(
        corners_kernel,
        [both_corners, both_corners],
        [group_scratch] * 2,
        10, 16, drop, far_far, far_mate, far_mate_too, reach, here, partial,
        direct_triangle, light=True,
    )
    correction, own, partial = run(
        first_sweep_kernel,
        [columns, square_group, partial_sums],
        [whole_scratch, group_scratch, group_scratch],
        66, 24, drop, shifted, shifted_corners, corner, slab_mate, triangle_cross, from_mate,
        direct_triangle, turned_triangle, light=True,
    )
    corner_cross, corner_mate = to_cross(own), to_mate(own)
    low, high, edge_cross, edge_mate = run(
        first_edges_kernel,
        [square_group, square_group, triangle, triangle],
        [group_scratch] * 2,
        10, 16, drop, from_mate, cross_corner, correction, partial,
    )
    edge_cross, edge_mate = to_cross(edge_cross), to_mate(edge_mate)
    (correction,) = run(
        correction_kernel, [columns], [whole_scratch], 38, 16, drop, shifted, shifted_corners, low, own, high
    )
    new_low, new_high, inverse_cross, inverse_mate = run(
        second_edges_kernel,
        [square_group, square_group, triangle, triangle],
        [],
        20, 12, drop, corner_mate, corner_cross, correction, low, high,
    )
    inverse_cross, inverse_mate = to_cross(inverse_cross), to_mate(inverse_mate)
    whole, rim_cross, rim_mate = run(
        density_edges_kernel,
        [columns, triangle, triangle],
        [group_scratch] * 4,
        38, 20, drop, own, edge_cross, edge_mate, correction, new_low, new_high, square,
        square_corners,
    )
    rim_cross, rim_mate = to_cross(rim_cross), to_mate(rim_mate)
    (density_own,) = run(density_own_kernel, [square_group], [], 18, 12, drop, square, whole)
    out = jax.ShapeDtypeStruct(density.shape, kind)

    def assembled(own, first, cross, mate):
        return call(functools.partial(rows_kernel, f, first), [out], [], 0, 8, drop, own, cross, mate)[0]

    inverse_next = assembled(whole, half, inverse_cross, inverse_mate)
    density_next = assembled(density_own, 0, rim_cross, rim_mate)
    return density_next, inverse_next


def solution(mesh):
    blocks = P(("grp", "row", "inner"), None, None, None)
    return jax.shard_map(
        on_device,
        mesh=mesh,
        in_specs=(blocks, blocks, P(("grp", "row", "inner"), None)),
        out_specs=(blocks, blocks),
        check_vma=False,
    )
```

```python
import functools

import jax
import jax.numpy as jnp
from jax import lax
from jax.experimental import pallas as pl
from jax.experimental.pallas import tpu as pltpu
from jax.sharding import PartitionSpec as P

RING = ("row", "inner")
MIB = 1024 * 1024


class Frame:
    def __init__(self, half, order):
        self.h = half
        self.b = order
        self.k = 2 * half
        self.p = half // 2
        self.t = 2 * order
        self.group = half * order
        self.pairs = 3 * self.p
        self.own_pairs = range(self.p, 2 * self.p)
        self.edge_rows = [*range(self.p), *range(2 * self.p, 3 * self.p)]

    def tiles(self, columns):
        for col in columns:
            for row in range(max(0, col - self.p), min(self.pairs, col + self.p + 1)):
                yield row, col

    def inner(self, row, col):
        return max(row, col) - self.p, min(row, col) + self.p + 1

    def clipped(self, row, col):
        lo, hi = self.inner(row, col)
        return max(lo, 0), min(hi, self.pairs)

    def on_corner(self, row, col):
        return max(row, col) < self.p or min(row, col) >= 2 * self.p

    def corner_place(self, row, col):
        r, c = (row, col) if row < self.p else (row - self.p, col - 2 * self.p)
        return r, r + 1, c, c + 1

    def split(self, row, col):
        lo, hi = self.clipped(row, col)
        for g in range(3):
            a, z = max(lo, g * self.p), min(hi, (g + 1) * self.p)
            if a < z:
                yield g, a - g * self.p, z - g * self.p


def under(h):
    return [(r, c) for r in range(h) for c in range(r + 1)]


def over(h):
    return [(r, c) for r in range(h) for c in range(r, h)]


def full(h):
    return [(r, c) for r in range(h) for c in range(h)]


def at(f, row_lo, row_hi, col_lo, col_hi):
    t = f.t
    return pl.ds(row_lo * t, (row_hi - row_lo) * t), pl.ds(col_lo * t, (col_hi - col_lo) * t)


def block(f, r, c):
    return pl.ds(r * f.b, f.b), pl.ds(c * f.b, f.b)


def banded(f, row, lo, hi):
    return at(f, row, row + 1, lo - row + f.p, hi - row + f.p)


def dot(a, b):
    return jnp.dot(a, b, preferred_element_type=jnp.float32)


def stored(rows, r, offset, dropped, slots=None):
    last = (rows.shape[1] if slots is None else slots) - 1
    slot = jnp.minimum(offset - (offset > dropped).astype(jnp.int32), last)
    value = rows[r, slot] if slots is None else rows((r, slot))
    return jnp.where(offset == dropped, jnp.zeros_like(value), value)


def masked(f, tile, row, col, drop_ref):
    b = f.b
    parts = []
    for i in range(2):
        r = 2 * row + i
        line = []
        for j in range(2):
            offset = 2 * col + j - r + f.h
            piece = tile[i * b : (i + 1) * b, j * b : (j + 1) * b]
            if 0 <= offset <= f.k:
                piece = jnp.where(drop_ref[r] == offset, 0.0, piece)
            else:
                piece = jnp.zeros_like(piece)
            line.append(piece)
        parts.append(jnp.concatenate(line, axis=1))
    return jnp.concatenate(parts, axis=0)


def odd_place(f, drop_ref):
    return drop_ref[3 * f.h] == 1


def indexed(f, ref, first=0):
    return lambda i: ref[block(f, first + i, 0)]


def plain(ref):
    return lambda place: ref[place]


def sides(f, drop_ref, mate, cross):
    odd = odd_place(f, drop_ref)

    def below(key):
        return jnp.where(odd, mate(key), cross(key))

    def above(key):
        return jnp.where(odd, cross(key), mate(key))

    return below, above


def spread(f, dest, row, col, read, places):
    index = {place: i for i, place in enumerate(places)}
    for r in range(f.h):
        for c in range(f.h):
            i = index.get((r, c))
            dest[block(f, row + r, col + c)] = jnp.zeros((f.b, f.b), dest.dtype) if i is None else read(i)


def pack_edges(f, drop_ref, low, high, to_cross, to_mate):
    odd = odd_place(f, drop_ref)
    for i, (lower, upper) in enumerate(zip(under(f.h), over(f.h))):
        back, forth = low[block(f, *lower)], high[block(f, *upper)]
        to_cross[block(f, i, 0)] = jnp.where(odd, forth, back)
        to_mate[block(f, i, 0)] = jnp.where(odd, back, forth)


def slabs_kernel(f, drop_ref, own, corner, corner_again, to_mate, to_cross, to_cross_again):
    h = f.h
    odd = drop_ref[h] == 1
    n = len(under(h))
    for i, (lower, upper) in enumerate(zip(under(h), over(h))):
        (r, c), (s, d) = lower, upper
        forth = stored(own, r, 2 * h + c - r, drop_ref[r])
        back = stored(own, s, d - s, drop_ref[s])
        to_mate[block(f, i, 0)] = jnp.where(odd, back, forth)
        across = jnp.where(odd, forth, back)
        to_cross[block(f, i, 0)] = across
        to_cross_again[block(f, i, 0)] = across
    for i, (r, c) in enumerate(full(h)):
        value = stored(own, r, c - r + h, drop_ref[r])
        corner[block(f, i, 0)] = value
        corner_again[block(f, i, 0)] = value
        to_mate[block(f, n + i, 0)] = value


def forward_kernel(f, drop_ref, cross, *refs):
    h = f.h
    odd = odd_place(f, drop_ref)
    to_mate, to_far = refs[-4:-2]
    for i, (lower, upper) in enumerate(zip(under(h), over(h))):
        (r, c), (s, d) = lower, upper
        forth = stored(cross, r, 2 * h + c - r, jnp.where(odd, drop_ref[2 * h + r], drop_ref[r]))
        back = stored(cross, s, d - s, jnp.where(odd, drop_ref[2 * h + s], drop_ref[s]))
        to_mate[block(f, i, 0)] = jnp.where(odd, back, forth)
        to_far[block(f, i, 0)] = jnp.where(odd, forth, back)


def square_kernel(f, drop_ref, own, cross, mate, square, shifted, reach, here, partial, wide):
    h, p = f.h, f.p
    below, above = sides(f, drop_ref, plain(mate), plain(cross))
    for g, read in enumerate((below, plain(own), above)):
        for r in range(h):
            row = g * h + r
            first = 2 * (row // 2) - h
            for col in range(first, first + 2 * h + 2):
                offset = col - row + h
                if 0 <= offset <= f.k:
                    value = stored(read, r, offset, drop_ref[row], f.k)
                else:
                    value = jnp.zeros((f.b, f.b), wide.dtype)
                wide[block(f, row, col + h)] = value
    for i in range(h):
        for g, row in enumerate((i, 2 * h + i)):
            rows = pl.ds((g * h + i) * f.b, f.b)
            source = pl.ds(row * f.b, f.b)
            reach[rows, :] = wide[source, pl.ds(4 * g * f.group, f.group)]
            here[rows, :] = wide[source, pl.ds((2 * g + 1) * f.group, f.group)]
    unit = unit_tile(f)
    for row, col in f.tiles(range(f.pairs)):
        lo, hi = f.clipped(row, col)
        total = dot(
            wide[at(f, row, row + 1, lo + p, hi + p)], wide[at(f, lo, hi, col + p, col + p + 1)]
        )
        if f.on_corner(row, col):
            partial[at(f, *f.corner_place(row, col))] = total
            continue
        total = masked(f, total, row, col, drop_ref)
        place = banded(f, row, col, col + 1)
        tile = wide[at(f, row, row + 1, col + p, col + p + 1)].astype(jnp.float32)
        square[place] = total.astype(square.dtype)
        shifted[place] = moved(total, tile, unit if row == col else None).astype(shifted.dtype)


def unit_tile(f):
    rows = lax.broadcasted_iota(jnp.int32, (f.t, f.t), 0)
    return (rows == lax.broadcasted_iota(jnp.int32, (f.t, f.t), 1)).astype(jnp.float32)


def moved(total, tile, unit):
    value = 2.0 * total - 2.0 * tile
    return value if unit is None else value + unit


def corners_kernel(
    f, drop_ref, far_far, far_mate, reach, here, partial, unused, square, shifted, low, high
):
    p = f.p
    far_below, far_above = sides(f, drop_ref, indexed(f, far_mate), indexed(f, far_far))
    spread(f, low, 0, 0, far_below, under(f.h))
    spread(f, high, 0, 0, far_above, over(f.h))
    unit = unit_tile(f)
    for row, col in f.tiles(range(f.pairs)):
        if not f.on_corner(row, col):
            continue
        place = at(f, *f.corner_place(row, col))
        r, _, c, _ = f.corner_place(row, col)
        total = partial[place]
        if row < p:
            a, z, far = max(row, col), p, low
        else:
            a, z, far = 0, min(row, col) - 2 * p + 1, high
        if a < z:
            total = total + dot(reach[at(f, r, r + 1, a, z)], far[at(f, a, z, c, c + 1)])
        total = masked(f, total, row, col, drop_ref)
        tile = here[place].astype(jnp.float32)
        square[place] = total.astype(square.dtype)
        shifted[place] = moved(total, tile, unit if row == col else None).astype(shifted.dtype)


def right_tile(f, left, corners, right, row, col):
    lo, hi = f.clipped(row, col)
    total = None
    if row < f.p:
        inside = corners[at(f, row, row + 1, lo, f.p)]
        total = dot(inside, right[at(f, lo, f.p, col - f.p, col - f.p + 1)])
        lo = f.p
    elif row >= 2 * f.p:
        inside = corners[at(f, row - f.p, row - f.p + 1, 0, hi - 2 * f.p)]
        total = dot(inside, right[at(f, 2 * f.p, hi, col - f.p, col - f.p + 1)])
        hi = 2 * f.p
    rest = dot(left[banded(f, row, lo, hi)], right[at(f, lo, hi, col - f.p, col - f.p + 1)])
    return rest if total is None else total + rest


def first_sweep_kernel(
    f, drop_ref, shifted, corners, corner, sent_mate, sent_cross, mate, direct, turned,
    correction, fresh, partial, whole, before, after,
):
    h, p = f.h, f.p
    turning = drop_ref[3 * h + 1] == 1
    direct_block, turned_block = indexed(f, direct), indexed(f, turned)

    def cross(i):
        return jnp.where(turning, turned_block(i), direct_block(i))

    from_below, from_above = sides(f, drop_ref, indexed(f, mate), cross)
    down, up = sides(f, drop_ref, indexed(f, sent_mate), indexed(f, sent_cross))
    spread(f, whole, 0, 0, from_below, under(h))
    spread(f, whole, h, 0, indexed(f, corner), full(h))
    spread(f, whole, 2 * h, 0, from_above, over(h))
    spread(f, before, 0, 0, down, over(h))
    spread(f, after, 0, 0, up, under(h))
    for row, col in f.tiles(f.own_pairs):
        total = masked(f, right_tile(f, shifted, corners, whole, row, col), row, col, drop_ref)
        correction[at(f, row, row + 1, col - p, col - p + 1)] = total.astype(correction.dtype)
    for row, col in f.tiles(f.own_pairs):
        c = col - p
        own_row = row in f.own_pairs
        total = 2.0 * whole[at(f, row, row + 1, c, c + 1)].astype(jnp.float32)
        for g, a, z in f.split(row, col):
            if g == 1:
                left = whole[at(f, row, row + 1, a, z)]
            elif own_row:
                left = (before, None, after)[g][at(f, row - p, row - p + 1, a, z)]
            else:
                continue
            total = total - dot(left, correction[at(f, g * p + a, g * p + z, c, c + 1)])
        if own_row:
            total = masked(f, total, row, col, drop_ref)
            fresh[at(f, row - p, row - p + 1, c, c + 1)] = total.astype(fresh.dtype)
        else:
            place = row if row < p else row - p
            partial[at(f, place, place + 1, c, c + 1)] = total


def edges(f, drop_ref, corner_below, corner_above, correction, start, low, high):
    p = f.p
    for row, col in f.tiles(f.own_pairs):
        if row in f.own_pairs:
            continue
        c = col - p
        side = 0 if row < p else 2
        corner, dest = ((corner_below, low), None, (corner_above, high))[side]
        local = row - side * p
        total = start(row, col)
        for g, a, z in f.split(row, col):
            if g == side:
                total = total - dot(
                    corner(at(f, local, local + 1, a, z)), correction[at(f, g * p + a, g * p + z, c, c + 1)]
                )
        total = masked(f, total, row, col, drop_ref)
        dest[at(f, local, local + 1, c, c + 1)] = total.astype(dest.dtype)


def first_edges_kernel(
    f, drop_ref, mate, cross, correction, partial, low, high, to_cross, to_mate, before, after
):
    p = f.p
    below, above = sides(f, drop_ref, indexed(f, mate, len(under(f.h))), indexed(f, cross))
    spread(f, before, 0, 0, below, full(f.h))
    spread(f, after, 0, 0, above, full(f.h))

    def start(row, col):
        place = row if row < p else row - p
        return partial[at(f, place, place + 1, col - p, col - p + 1)]

    edges(f, drop_ref, plain(before), plain(after), correction, start, low, high)
    pack_edges(f, drop_ref, low, high, to_cross, to_mate)


def gather(f, whole, low, own, high):
    for g, source in enumerate((low, own, high)):
        for i in range(f.h):
            whole[pl.ds(g * f.group + i * f.b, f.b), :] = source[pl.ds(i * f.b, f.b), :]


def correction_kernel(f, drop_ref, shifted, corners, low, own, high, correction, whole):
    p = f.p
    gather(f, whole, low, own, high)
    for row, col in f.tiles(f.own_pairs):
        total = masked(f, right_tile(f, shifted, corners, whole, row, col), row, col, drop_ref)
        correction[at(f, row, row + 1, col - p, col - p + 1)] = total.astype(correction.dtype)


def second_edges_kernel(
    f, drop_ref, mate, cross, correction, low, high, new_low, new_high, to_cross, to_mate
):
    p = f.p

    def start(row, col):
        c = col - p
        source, local = (low, row) if row < p else (high, row - 2 * p)
        total = 2.0 * source[at(f, local, local + 1, c, c + 1)].astype(jnp.float32)
        for g, a, z in f.split(row, col):
            if g == 1:
                total = total - dot(
                    source[at(f, local, local + 1, a, z)], correction[at(f, p + a, p + z, c, c + 1)]
                )
        return total

    below, above = sides(f, drop_ref, plain(mate), plain(cross))
    edges(f, drop_ref, below, above, correction, start, new_low, new_high)
    pack_edges(f, drop_ref, new_low, new_high, to_cross, to_mate)


def density_edges_kernel(
    f, drop_ref, own, cross, mate, correction, new_low, new_high, square, corners, whole, to_cross, to_mate,
    before, after, low, high,
):
    h, p = f.h, f.p
    below, above = sides(f, drop_ref, indexed(f, mate), indexed(f, cross))
    spread(f, before, 0, 0, below, over(h))
    spread(f, after, 0, 0, above, under(h))
    for row, col in f.tiles(f.own_pairs):
        if row not in f.own_pairs:
            continue
        c, local = col - p, row - p
        total = 2.0 * own[at(f, local, local + 1, c, c + 1)].astype(jnp.float32)
        for g, a, z in f.split(row, col):
            left = (before, own, after)[g][at(f, local, local + 1, a, z)]
            total = total - dot(left, correction[at(f, g * p + a, g * p + z, c, c + 1)])
        total = masked(f, total, row, col, drop_ref)
        whole[at(f, row, row + 1, c, c + 1)] = total.astype(whole.dtype)
    for i in range(h):
        rows = pl.ds(i * f.b, f.b)
        whole[pl.ds(i * f.b, f.b), :] = new_low[rows, :]
        whole[pl.ds(2 * f.group + i * f.b, f.b), :] = new_high[rows, :]
    for row, col in f.tiles(f.own_pairs):
        if row in f.own_pairs:
            continue
        total = masked(f, right_tile(f, square, corners, whole, row, col), row, col, drop_ref)
        dest, local = (low, row) if row < p else (high, row - 2 * p)
        dest[at(f, local, local + 1, col - p, col - p + 1)] = total.astype(dest.dtype)
    pack_edges(f, drop_ref, low, high, to_cross, to_mate)


def density_own_kernel(f, drop_ref, square, whole, out):
    p = f.p
    for row, col in f.tiles(f.own_pairs):
        if row in f.own_pairs:
            total = masked(f, right_tile(f, square, None, whole, row, col), row, col, drop_ref)
            out[at(f, row - p, row - p + 1, col - p, col - p + 1)] = total.astype(out.dtype)


def rows_kernel(f, first, drop_ref, own, cross, mate, out):
    h = f.h
    below, above = sides(f, drop_ref, indexed(f, mate), indexed(f, cross))
    over_index = {place: i for i, place in enumerate(over(h))}
    under_index = {place: i for i, place in enumerate(under(h))}
    for r in range(h):
        dropped = drop_ref[h + r]

        def at_offset(offset, r=r):
            col = r + offset
            if col < h:
                return below(over_index[r, col])
            if col < 2 * h:
                return own[block(f, first + r, col - h)]
            return above(under_index[r, col - 2 * h])

        for s in range(f.k):
            out[r, s] = jnp.where(dropped <= s, at_offset(s + 1), at_offset(s))


VMEM = pl.BlockSpec(memory_space=pltpu.VMEM)
SMEM = pl.BlockSpec(memory_space=pltpu.SMEM)
ANY = pl.BlockSpec(memory_space=pl.ANY)


def call(kernel, outs, scratch, flops, limit, drop, *args, passed=(), light=False):
    moved = sum(a.size * a.dtype.itemsize for a in args) + sum(s.size * s.dtype.itemsize for s in outs)
    if light:
        flops = moved = 0
    n = len(args)
    return pl.pallas_call(
        kernel,
        out_shape=[*outs, *[jax.ShapeDtypeStruct(a.shape, a.dtype) for a in passed]],
        in_specs=[SMEM] + [VMEM] * n + [ANY] * len(passed),
        out_specs=[VMEM] * len(outs) + [ANY] * len(passed),
        scratch_shapes=scratch,
        input_output_aliases={1 + n + i: len(outs) + i for i in range(len(passed))},
        compiler_params=pltpu.CompilerParams(vmem_limit_bytes=limit * MIB),
        cost_estimate=pl.CostEstimate(flops=flops, bytes_accessed=moved, transcendentals=0),
    )(drop, *args, *passed)


def routed(x, step):
    size = lax.axis_size(RING)
    return lax.ppermute(x, RING, [(i, (i + step(i)) % size) for i in range(size) if step(i)])


def on_device(density, inverse_start, block_cols):
    rows, width, order, _ = density.shape
    half = width // 2
    ring, inner = lax.axis_size(RING), lax.axis_size(RING[1])
    total = rows * ring
    assert rows == half and half % 2 == 0 and inner % 2 == 0
    f = Frame(half, order)
    kind = density.dtype
    me = lax.axis_index(RING)

    def mate_step(i):
        return 1 - 2 * (i % 2)

    def cross_step(i):
        return 2 * (i % 2) - 1

    def to_mate(x):
        return routed(x, mate_step)

    def to_cross(x):
        return routed(x, cross_step)

    def turns(i):
        return i % inner in (0, inner - 1)

    positions = block_cols - (me * rows + jnp.arange(rows, dtype=jnp.int32))[:, None] + half
    positions = positions + jnp.where(positions < 0, total, jnp.where(positions >= total, -total, 0))
    own_drop = width * (width + 1) // 2 - jnp.sum(positions, axis=1)

    density_cross, density_mate = to_cross(density), to_mate(density)
    cross_drop, mate_drop = to_cross(own_drop), to_mate(own_drop)
    even = (me & 1) == 0
    place = lax.axis_index(RING[1])
    marks = jnp.stack([me & 1, ((place == 0) | (place == inner - 1)).astype(jnp.int32)])
    start_drop = jnp.concatenate([own_drop, marks[:1]])
    drop = jnp.concatenate(
        [jnp.where(even, cross_drop, mate_drop), own_drop, jnp.where(even, mate_drop, cross_drop), marks]
    )

    unit = 2 * f.t**3
    count = half * (half + 1) // 2
    square_group = jax.ShapeDtypeStruct((f.group, f.group), kind)
    columns = jax.ShapeDtypeStruct((3 * f.group, f.group), kind)
    band = jax.ShapeDtypeStruct((3 * f.group, (2 * f.p + 1) * f.t), kind)
    triangle = jax.ShapeDtypeStruct((count * order, order), kind)
    listed = jax.ShapeDtypeStruct((half * half * order, order), kind)
    both = jax.ShapeDtypeStruct(((count + half * half) * order, order), kind)
    partial_sums = jax.ShapeDtypeStruct((2 * f.group, f.group), jnp.float32)
    group_scratch = pltpu.VMEM((f.group, f.group), kind)
    whole_scratch = pltpu.VMEM((3 * f.group, f.group), kind)

    def run(kernel, outs, scratch, tiles, limit, *args, **kw):
        return call(functools.partial(kernel, f), outs, scratch, tiles * unit, limit, *args, **kw)

    corner, corner_cross, slab_mate, triangle_cross, triangle_turning = run(
        slabs_kernel, [listed, listed, both, triangle, triangle], [], 0, 12, start_drop, inverse_start
    )
    from_mate = to_mate(slab_mate)
    direct_triangle = routed(triangle_cross, lambda i: 0 if turns(i) else cross_step(i))
    forward_mate, forward_far, triangle_turning, corner_cross = run(
        forward_kernel, [triangle, triangle], [], 0, 12, drop, density_cross, density_mate, from_mate,
        passed=(triangle_turning, corner_cross),
    )
    far_mate = to_mate(forward_mate)
    far_far = routed(forward_far, lambda i: 3 * cross_step(i))
    turned_triangle = routed(triangle_turning, lambda i: cross_step(i) if turns(i) else 0)
    cross_corner = to_cross(corner_cross)

    both_corners = jax.ShapeDtypeStruct((2 * f.group, f.group), kind)
    square, shifted, reach, here, partial = run(
        square_kernel,
        [band, band, both_corners, both_corners, partial_sums],
        [pltpu.VMEM((3 * f.group, 5 * f.group), kind)],
        84, 26, drop, density, density_cross, density_mate, light=True,
    )
    square_corners, shifted_corners = run(
        corners_kernel,
        [both_corners, both_corners],
        [group_scratch] * 2,
        10, 16, drop, far_far, far_mate, reach, here, partial,
        direct_triangle, light=True,
    )
    correction, own, partial = run(
        first_sweep_kernel,
        [columns, square_group, partial_sums],
        [whole_scratch, group_scratch, group_scratch],
        66, 24, drop, shifted, shifted_corners, corner, slab_mate, triangle_cross, from_mate,
        direct_triangle, turned_triangle, light=True,
    )
    corner_cross, corner_mate = to_cross(own), to_mate(own)
    low, high, edge_cross, edge_mate = run(
        first_edges_kernel,
        [square_group, square_group, triangle, triangle],
        [group_scratch] * 2,
        10, 16, drop, from_mate, cross_corner, correction, partial,
    )
    edge_cross, edge_mate = to_cross(edge_cross), to_mate(edge_mate)
    (correction,) = run(
        correction_kernel, [columns], [whole_scratch], 38, 16, drop, shifted, shifted_corners, low, own, high
    )
    new_low, new_high, inverse_cross, inverse_mate = run(
        second_edges_kernel,
        [square_group, square_group, triangle, triangle],
        [],
        20, 12, drop, corner_mate, corner_cross, correction, low, high,
    )
    inverse_cross, inverse_mate = to_cross(inverse_cross), to_mate(inverse_mate)
    whole, rim_cross, rim_mate = run(
        density_edges_kernel,
        [columns, triangle, triangle],
        [group_scratch] * 4,
        38, 20, drop, own, edge_cross, edge_mate, correction, new_low, new_high, square,
        square_corners,
    )
    rim_cross, rim_mate = to_cross(rim_cross), to_mate(rim_mate)
    (density_own,) = run(density_own_kernel, [square_group], [], 18, 12, drop, square, whole)
    out = jax.ShapeDtypeStruct(density.shape, kind)

    def assembled(own, first, cross, mate):
        return call(functools.partial(rows_kernel, f, first), [out], [], 0, 8, drop, own, cross, mate)[0]

    inverse_next = assembled(whole, half, inverse_cross, inverse_mate)
    density_next = assembled(density_own, 0, rim_cross, rim_mate)
    return density_next, inverse_next


def solution(mesh):
    blocks = P(("grp", "row", "inner"), None, None, None)
    return jax.shard_map(
        on_device,
        mesh=mesh,
        in_specs=(blocks, blocks, P(("grp", "row", "inner"), None)),
        out_specs=(blocks, blocks),
        check_vma=False,
    )
```

```python
import functools

import jax
import jax.numpy as jnp
from jax import lax
from jax.experimental import pallas as pl
from jax.experimental.pallas import tpu as pltpu
from jax.sharding import PartitionSpec as P

RING = ("row", "inner")
MIB = 1024 * 1024


class Frame:
    def __init__(self, half, order):
        self.h = half
        self.b = order
        self.k = 2 * half
        self.p = half // 2
        self.t = 2 * order
        self.group = half * order
        self.pairs = 3 * self.p
        self.own_pairs = range(self.p, 2 * self.p)
        self.edge_rows = [*range(self.p), *range(2 * self.p, 3 * self.p)]

    def tiles(self, columns):
        for col in columns:
            for row in range(max(0, col - self.p), min(self.pairs, col + self.p + 1)):
                yield row, col

    def inner(self, row, col):
        return max(row, col) - self.p, min(row, col) + self.p + 1

    def clipped(self, row, col):
        lo, hi = self.inner(row, col)
        return max(lo, 0), min(hi, self.pairs)

    def on_corner(self, row, col):
        return max(row, col) < self.p or min(row, col) >= 2 * self.p

    def corner_place(self, row, col):
        r, c = (row, col) if row < self.p else (row - self.p, col - 2 * self.p)
        return r, r + 1, c, c + 1

    def split(self, row, col):
        lo, hi = self.clipped(row, col)
        for g in range(3):
            a, z = max(lo, g * self.p), min(hi, (g + 1) * self.p)
            if a < z:
                yield g, a - g * self.p, z - g * self.p


def under(h):
    return [(r, c) for r in range(h) for c in range(r + 1)]


def over(h):
    return [(r, c) for r in range(h) for c in range(r, h)]


def full(h):
    return [(r, c) for r in range(h) for c in range(h)]


def at(f, row_lo, row_hi, col_lo, col_hi):
    t = f.t
    return pl.ds(row_lo * t, (row_hi - row_lo) * t), pl.ds(col_lo * t, (col_hi - col_lo) * t)


def block(f, r, c):
    return pl.ds(r * f.b, f.b), pl.ds(c * f.b, f.b)


def banded(f, row, lo, hi):
    return at(f, row, row + 1, lo - row + f.p, hi - row + f.p)


def dot(a, b):
    return jnp.dot(a, b, preferred_element_type=jnp.float32)


def stored(rows, r, offset, dropped, slots=None):
    last = (rows.shape[1] if slots is None else slots) - 1
    slot = jnp.minimum(offset - (offset > dropped).astype(jnp.int32), last)
    value = rows[r, slot] if slots is None else rows((r, slot))
    return jnp.where(offset == dropped, jnp.zeros_like(value), value)


def masked(f, tile, row, col, drop_ref):
    b = f.b
    parts = []
    for i in range(2):
        r = 2 * row + i
        line = []
        for j in range(2):
            offset = 2 * col + j - r + f.h
            piece = tile[i * b : (i + 1) * b, j * b : (j + 1) * b]
            if 0 <= offset <= f.k:
                piece = jnp.where(drop_ref[r] == offset, 0.0, piece)
            else:
                piece = jnp.zeros_like(piece)
            line.append(piece)
        parts.append(jnp.concatenate(line, axis=1))
    return jnp.concatenate(parts, axis=0)


def odd_place(f, drop_ref):
    return drop_ref[3 * f.h] == 1


def indexed(f, ref, first=0):
    return lambda i: ref[block(f, first + i, 0)]


def plain(ref):
    return lambda place: ref[place]


def sides(f, drop_ref, mate, cross):
    odd = odd_place(f, drop_ref)

    def below(key):
        return jnp.where(odd, mate(key), cross(key))

    def above(key):
        return jnp.where(odd, cross(key), mate(key))

    return below, above


def spread(f, dest, row, col, read, places):
    index = {place: i for i, place in enumerate(places)}
    for r in range(f.h):
        for c in range(f.h):
            i = index.get((r, c))
            dest[block(f, row + r, col + c)] = jnp.zeros((f.b, f.b), dest.dtype) if i is None else read(i)


def pack_edges(f, drop_ref, low, high, to_cross, to_mate):
    odd = odd_place(f, drop_ref)
    for i, (lower, upper) in enumerate(zip(under(f.h), over(f.h))):
        back, forth = low[block(f, *lower)], high[block(f, *upper)]
        to_cross[block(f, i, 0)] = jnp.where(odd, forth, back)
        to_mate[block(f, i, 0)] = jnp.where(odd, back, forth)


def slabs_kernel(f, drop_ref, own, corner, corner_again, to_mate, to_cross):
    h = f.h
    odd = drop_ref[h] == 1
    n = len(under(h))
    for i, (lower, upper) in enumerate(zip(under(h), over(h))):
        (r, c), (s, d) = lower, upper
        forth = stored(own, r, 2 * h + c - r, drop_ref[r])
        back = stored(own, s, d - s, drop_ref[s])
        to_mate[block(f, i, 0)] = jnp.where(odd, back, forth)
        to_cross[block(f, i, 0)] = jnp.where(odd, forth, back)
    for i, (r, c) in enumerate(full(h)):
        value = stored(own, r, c - r + h, drop_ref[r])
        corner[block(f, i, 0)] = value
        corner_again[block(f, i, 0)] = value
        to_mate[block(f, n + i, 0)] = value


def forward_kernel(f, drop_ref, cross, *refs):
    h = f.h
    odd = odd_place(f, drop_ref)
    to_mate, to_far = refs[-5:-3], refs[-3]
    for i, (lower, upper) in enumerate(zip(under(h), over(h))):
        (r, c), (s, d) = lower, upper
        forth = stored(cross, r, 2 * h + c - r, jnp.where(odd, drop_ref[2 * h + r], drop_ref[r]))
        back = stored(cross, s, d - s, jnp.where(odd, drop_ref[2 * h + s], drop_ref[s]))
        part, place = i % 2, i // 2
        to_mate[part][block(f, place, 0)] = jnp.where(odd, back, forth)
        to_far[block(f, i, 0)] = jnp.where(odd, forth, back)


def square_kernel(f, drop_ref, own, cross, mate, square, shifted, reach, here, partial, wide):
    h, p = f.h, f.p
    below, above = sides(f, drop_ref, plain(mate), plain(cross))
    for g, read in enumerate((below, plain(own), above)):
        for r in range(h):
            row = g * h + r
            first = 2 * (row // 2) - h
            for col in range(first, first + 2 * h + 2):
                offset = col - row + h
                if 0 <= offset <= f.k:
                    value = stored(read, r, offset, drop_ref[row], f.k)
                else:
                    value = jnp.zeros((f.b, f.b), wide.dtype)
                wide[block(f, row, col + h)] = value
    for i in range(h):
        for g, row in enumerate((i, 2 * h + i)):
            rows = pl.ds((g * h + i) * f.b, f.b)
            source = pl.ds(row * f.b, f.b)
            reach[rows, :] = wide[source, pl.ds(4 * g * f.group, f.group)]
            here[rows, :] = wide[source, pl.ds((2 * g + 1) * f.group, f.group)]
    unit = unit_tile(f)
    for row, col in f.tiles(range(f.pairs)):
        lo, hi = f.clipped(row, col)
        total = dot(
            wide[at(f, row, row + 1, lo + p, hi + p)], wide[at(f, lo, hi, col + p, col + p + 1)]
        )
        if f.on_corner(row, col):
            partial[at(f, *f.corner_place(row, col))] = total
            continue
        total = masked(f, total, row, col, drop_ref)
        place = banded(f, row, col, col + 1)
        tile = wide[at(f, row, row + 1, col + p, col + p + 1)].astype(jnp.float32)
        square[place] = total.astype(square.dtype)
        shifted[place] = moved(total, tile, unit if row == col else None).astype(shifted.dtype)


def unit_tile(f):
    rows = lax.broadcasted_iota(jnp.int32, (f.t, f.t), 0)
    return (rows == lax.broadcasted_iota(jnp.int32, (f.t, f.t), 1)).astype(jnp.float32)


def moved(total, tile, unit):
    value = 2.0 * total - 2.0 * tile
    return value if unit is None else value + unit


def corners_kernel(
    f, drop_ref, far_far, far_mate, far_mate_too, reach, here, partial, square, shifted, low, high
):
    p = f.p
    far_mates = [indexed(f, far_mate), indexed(f, far_mate_too)]
    far_below, far_above = sides(f, drop_ref, lambda i: far_mates[i % 2](i // 2), indexed(f, far_far))
    spread(f, low, 0, 0, far_below, under(f.h))
    spread(f, high, 0, 0, far_above, over(f.h))
    unit = unit_tile(f)
    for row, col in f.tiles(range(f.pairs)):
        if not f.on_corner(row, col):
            continue
        place = at(f, *f.corner_place(row, col))
        r, _, c, _ = f.corner_place(row, col)
        total = partial[place]
        if row < p:
            a, z, far = max(row, col), p, low
        else:
            a, z, far = 0, min(row, col) - 2 * p + 1, high
        if a < z:
            total = total + dot(reach[at(f, r, r + 1, a, z)], far[at(f, a, z, c, c + 1)])
        total = masked(f, total, row, col, drop_ref)
        tile = here[place].astype(jnp.float32)
        square[place] = total.astype(square.dtype)
        shifted[place] = moved(total, tile, unit if row == col else None).astype(shifted.dtype)


def right_tile(f, left, corners, right, row, col):
    lo, hi = f.clipped(row, col)
    total = None
    if row < f.p:
        inside = corners[at(f, row, row + 1, lo, f.p)]
        total = dot(inside, right[at(f, lo, f.p, col - f.p, col - f.p + 1)])
        lo = f.p
    elif row >= 2 * f.p:
        inside = corners[at(f, row - f.p, row - f.p + 1, 0, hi - 2 * f.p)]
        total = dot(inside, right[at(f, 2 * f.p, hi, col - f.p, col - f.p + 1)])
        hi = 2 * f.p
    rest = dot(left[banded(f, row, lo, hi)], right[at(f, lo, hi, col - f.p, col - f.p + 1)])
    return rest if total is None else total + rest


def first_sweep_kernel(
    f, drop_ref, shifted, corners, corner, sent_mate, sent_cross, mate, cross,
    correction, fresh, partial, whole, before, after,
):
    h, p = f.h, f.p
    from_below, from_above = sides(f, drop_ref, indexed(f, mate), indexed(f, cross))
    down, up = sides(f, drop_ref, indexed(f, sent_mate), indexed(f, sent_cross))
    spread(f, whole, 0, 0, from_below, under(h))
    spread(f, whole, h, 0, indexed(f, corner), full(h))
    spread(f, whole, 2 * h, 0, from_above, over(h))
    spread(f, before, 0, 0, down, over(h))
    spread(f, after, 0, 0, up, under(h))
    for row, col in f.tiles(f.own_pairs):
        total = masked(f, right_tile(f, shifted, corners, whole, row, col), row, col, drop_ref)
        correction[at(f, row, row + 1, col - p, col - p + 1)] = total.astype(correction.dtype)
    for row, col in f.tiles(f.own_pairs):
        c = col - p
        own_row = row in f.own_pairs
        total = 2.0 * whole[at(f, row, row + 1, c, c + 1)].astype(jnp.float32)
        for g, a, z in f.split(row, col):
            if g == 1:
                left = whole[at(f, row, row + 1, a, z)]
            elif own_row:
                left = (before, None, after)[g][at(f, row - p, row - p + 1, a, z)]
            else:
                continue
            total = total - dot(left, correction[at(f, g * p + a, g * p + z, c, c + 1)])
        if own_row:
            total = masked(f, total, row, col, drop_ref)
            fresh[at(f, row - p, row - p + 1, c, c + 1)] = total.astype(fresh.dtype)
        else:
            place = row if row < p else row - p
            partial[at(f, place, place + 1, c, c + 1)] = total


def edges(f, drop_ref, corner_below, corner_above, correction, start, low, high):
    p = f.p
    for row, col in f.tiles(f.own_pairs):
        if row in f.own_pairs:
            continue
        c = col - p
        side = 0 if row < p else 2
        corner, dest = ((corner_below, low), None, (corner_above, high))[side]
        local = row - side * p
        total = start(row, col)
        for g, a, z in f.split(row, col):
            if g == side:
                total = total - dot(
                    corner(at(f, local, local + 1, a, z)), correction[at(f, g * p + a, g * p + z, c, c + 1)]
                )
        total = masked(f, total, row, col, drop_ref)
        dest[at(f, local, local + 1, c, c + 1)] = total.astype(dest.dtype)


def first_edges_kernel(
    f, drop_ref, mate, cross, correction, partial, low, high, to_cross, to_mate, before, after
):
    p = f.p
    below, above = sides(f, drop_ref, indexed(f, mate, len(under(f.h))), indexed(f, cross))
    spread(f, before, 0, 0, below, full(f.h))
    spread(f, after, 0, 0, above, full(f.h))

    def start(row, col):
        place = row if row < p else row - p
        return partial[at(f, place, place + 1, col - p, col - p + 1)]

    edges(f, drop_ref, plain(before), plain(after), correction, start, low, high)
    pack_edges(f, drop_ref, low, high, to_cross, to_mate)


def gather(f, whole, low, own, high):
    for g, source in enumerate((low, own, high)):
        for i in range(f.h):
            whole[pl.ds(g * f.group + i * f.b, f.b), :] = source[pl.ds(i * f.b, f.b), :]


def correction_kernel(f, drop_ref, shifted, corners, low, own, high, correction, whole):
    p = f.p
    gather(f, whole, low, own, high)
    for row, col in f.tiles(f.own_pairs):
        total = masked(f, right_tile(f, shifted, corners, whole, row, col), row, col, drop_ref)
        correction[at(f, row, row + 1, col - p, col - p + 1)] = total.astype(correction.dtype)


def second_edges_kernel(
    f, drop_ref, cross, mate, correction, low, high, new_low, new_high, to_cross, to_mate
):
    p = f.p

    def start(row, col):
        c = col - p
        source, local = (low, row) if row < p else (high, row - 2 * p)
        total = 2.0 * source[at(f, local, local + 1, c, c + 1)].astype(jnp.float32)
        for g, a, z in f.split(row, col):
            if g == 1:
                total = total - dot(
                    source[at(f, local, local + 1, a, z)], correction[at(f, p + a, p + z, c, c + 1)]
                )
        return total

    below, above = sides(f, drop_ref, plain(mate), plain(cross))
    edges(f, drop_ref, below, above, correction, start, new_low, new_high)
    pack_edges(f, drop_ref, new_low, new_high, to_cross, to_mate)


def density_edges_kernel(
    f, drop_ref, own, cross, mate, correction, new_low, new_high, square, corners, whole, to_cross, to_mate,
    before, after, low, high,
):
    h, p = f.h, f.p
    below, above = sides(f, drop_ref, indexed(f, mate), indexed(f, cross))
    spread(f, before, 0, 0, below, over(h))
    spread(f, after, 0, 0, above, under(h))
    for row, col in f.tiles(f.own_pairs):
        if row not in f.own_pairs:
            continue
        c, local = col - p, row - p
        total = 2.0 * own[at(f, local, local + 1, c, c + 1)].astype(jnp.float32)
        for g, a, z in f.split(row, col):
            left = (before, own, after)[g][at(f, local, local + 1, a, z)]
            total = total - dot(left, correction[at(f, g * p + a, g * p + z, c, c + 1)])
        total = masked(f, total, row, col, drop_ref)
        whole[at(f, row, row + 1, c, c + 1)] = total.astype(whole.dtype)
    for i in range(h):
        rows = pl.ds(i * f.b, f.b)
        whole[pl.ds(i * f.b, f.b), :] = new_low[rows, :]
        whole[pl.ds(2 * f.group + i * f.b, f.b), :] = new_high[rows, :]
    for row, col in f.tiles(f.own_pairs):
        if row in f.own_pairs:
            continue
        total = masked(f, right_tile(f, square, corners, whole, row, col), row, col, drop_ref)
        dest, local = (low, row) if row < p else (high, row - 2 * p)
        dest[at(f, local, local + 1, col - p, col - p + 1)] = total.astype(dest.dtype)
    pack_edges(f, drop_ref, low, high, to_cross, to_mate)


def density_own_kernel(f, drop_ref, square, whole, out):
    p = f.p
    for row, col in f.tiles(f.own_pairs):
        if row in f.own_pairs:
            total = masked(f, right_tile(f, square, None, whole, row, col), row, col, drop_ref)
            out[at(f, row - p, row - p + 1, col - p, col - p + 1)] = total.astype(out.dtype)


def slots_kernel(f, first, drop_ref, own, mate, out):
    h = f.h
    mate_block = indexed(f, mate)
    over_index = {place: i for i, place in enumerate(over(h))}
    under_index = {place: i for i, place in enumerate(under(h))}
    for r in range(h):
        dropped = drop_ref[h + r]

        def at_offset(offset, r=r):
            col = r + offset
            if col < h:
                return mate_block(over_index[r, col])
            if col < 2 * h:
                return own[block(f, first + r, col - h)]
            return mate_block(under_index[r, col - 2 * h])

        for s in range(f.k):
            out[r, s] = jnp.where(dropped <= s, at_offset(s + 1), at_offset(s))


def last_slots_kernel(f, drop_ref, slots, cross, out, sides_ref, sems):
    h, k = f.h, f.k
    odd = odd_place(f, drop_ref)
    cross_block = indexed(f, cross)
    over_index = {place: i for i, place in enumerate(over(h))}
    under_index = {place: i for i, place in enumerate(under(h))}
    copies = []

    def copy(source, r, lo, hi):
        there = pltpu.make_async_copy(
            source.at[r, pl.ds(lo, hi - lo)], out.at[r, pl.ds(lo, hi - lo)], sems.at[len(copies)]
        )
        there.start()
        copies.append(there)

    for r in range(h):
        copy(slots, r, h - r, k - 1 - r)
    for r in range(h):
        dropped = drop_ref[h + r]
        for lo, hi, mine in ((0, h - r, jnp.logical_not(odd)), (k - 1 - r, k, odd)):
            for s in range(lo, hi):
                here = slots[r, s]

                def at_offset(offset, r=r, low=lo == 0, here=here):
                    col = r + offset
                    if low and col < h:
                        return cross_block(over_index[r, col])
                    if not low and col >= 2 * h:
                        return cross_block(under_index[r, col - 2 * h])
                    return here

                value = jnp.where(dropped <= s, at_offset(s + 1), at_offset(s))
                sides_ref[r, s] = jnp.where(mine, value, here)
            copy(sides_ref, r, lo, hi)
    for there in copies:
        there.wait()


VMEM = pl.BlockSpec(memory_space=pltpu.VMEM)
SMEM = pl.BlockSpec(memory_space=pltpu.SMEM)
ANY = pl.BlockSpec(memory_space=pl.ANY)


def call(kernel, outs, scratch, flops, limit, drop, *args, passed=(), light=False, off=False):
    moved = sum(a.size * a.dtype.itemsize for a in args) + sum(s.size * s.dtype.itemsize for s in outs)
    if light:
        flops = moved = 0
    n = len(args)
    return pl.pallas_call(
        kernel,
        out_shape=[*outs, *[jax.ShapeDtypeStruct(a.shape, a.dtype) for a in passed]],
        in_specs=[SMEM] + [VMEM] * n + [ANY] * len(passed),
        out_specs=[ANY if off else VMEM] * len(outs) + [ANY] * len(passed),
        scratch_shapes=scratch,
        input_output_aliases={1 + n + i: len(outs) + i for i in range(len(passed))},
        compiler_params=pltpu.CompilerParams(vmem_limit_bytes=limit * MIB),
        cost_estimate=pl.CostEstimate(flops=flops, bytes_accessed=moved, transcendentals=0),
    )(drop, *args, *passed)


def routed(x, step):
    size = lax.axis_size(RING)
    return lax.ppermute(x, RING, [(i, (i + step(i)) % size) for i in range(size) if step(i)])


def on_device(density, inverse_start, block_cols):
    rows, width, order, _ = density.shape
    half = width // 2
    ring = lax.axis_size(RING)
    total = rows * ring
    assert rows == half and half % 2 == 0 and ring % 2 == 0
    f = Frame(half, order)
    kind = density.dtype
    me = lax.axis_index(RING)

    def mate_step(i):
        return 1 - 2 * (i % 2)

    def cross_step(i):
        return 2 * (i % 2) - 1

    def to_mate(x):
        return routed(x, mate_step)

    def to_cross(x):
        return routed(x, cross_step)

    positions = block_cols - (me * rows + jnp.arange(rows, dtype=jnp.int32))[:, None] + half
    positions = positions + jnp.where(positions < 0, total, jnp.where(positions >= total, -total, 0))
    own_drop = width * (width + 1) // 2 - jnp.sum(positions, axis=1)

    density_cross, density_mate = to_cross(density), to_mate(density)
    cross_drop, mate_drop = to_cross(own_drop), to_mate(own_drop)
    even = (me & 1) == 0
    mark = jnp.reshape(me & 1, (1,))
    start_drop = jnp.concatenate([own_drop, mark])
    drop = jnp.concatenate(
        [jnp.where(even, cross_drop, mate_drop), own_drop, jnp.where(even, mate_drop, cross_drop), mark]
    )

    unit = 2 * f.t**3
    count = half * (half + 1) // 2
    square_group = jax.ShapeDtypeStruct((f.group, f.group), kind)
    columns = jax.ShapeDtypeStruct((3 * f.group, f.group), kind)
    band = jax.ShapeDtypeStruct((3 * f.group, (2 * f.p + 1) * f.t), kind)
    triangle = jax.ShapeDtypeStruct((count * order, order), kind)
    half_triangle = jax.ShapeDtypeStruct((count // 2 * order, order), kind)
    listed = jax.ShapeDtypeStruct((half * half * order, order), kind)
    both = jax.ShapeDtypeStruct(((count + half * half) * order, order), kind)
    partial_sums = jax.ShapeDtypeStruct((2 * f.group, f.group), jnp.float32)
    group_scratch = pltpu.VMEM((f.group, f.group), kind)
    whole_scratch = pltpu.VMEM((3 * f.group, f.group), kind)

    def run(kernel, outs, scratch, tiles, limit, *args, **kw):
        return call(functools.partial(kernel, f), outs, scratch, tiles * unit, limit, *args, **kw)

    corner, corner_cross, slab_mate, triangle_cross = run(
        slabs_kernel, [listed, listed, both, triangle], [], 0, 12, start_drop, inverse_start
    )
    from_mate = to_mate(slab_mate)
    forward_mate, forward_mate_too, forward_far, triangle_cross, corner_cross = run(
        forward_kernel, [half_triangle, half_triangle, triangle], [], 0, 12, drop, density_cross, density_mate, from_mate,
        passed=(triangle_cross, corner_cross),
    )
    far_mate, far_mate_too = to_mate(forward_mate), to_mate(forward_mate_too)
    far_far = routed(forward_far, lambda i: 3 * cross_step(i))
    cross_triangle = to_cross(triangle_cross)
    cross_corner = to_cross(corner_cross)

    both_corners = jax.ShapeDtypeStruct((2 * f.group, f.group), kind)
    square, shifted, reach, here, partial = run(
        square_kernel,
        [band, band, both_corners, both_corners, partial_sums],
        [pltpu.VMEM((3 * f.group, 5 * f.group), kind)],
        84, 26, drop, density, density_cross, density_mate,
    )
    square_corners, shifted_corners = run(
        corners_kernel,
        [both_corners, both_corners],
        [group_scratch] * 2,
        10, 16, drop, far_far, far_mate, far_mate_too, reach, here, partial, light=True,
    )
    correction, own, partial = run(
        first_sweep_kernel,
        [columns, square_group, partial_sums],
        [whole_scratch, group_scratch, group_scratch],
        66, 24, drop, shifted, shifted_corners, corner, slab_mate, triangle_cross, from_mate, cross_triangle, light=True,
    )
    corner_cross, corner_mate = to_cross(own), to_mate(own)
    low, high, edge_cross, edge_mate = run(
        first_edges_kernel,
        [square_group, square_group, triangle, triangle],
        [group_scratch] * 2,
        10, 16, drop, from_mate, cross_corner, correction, partial,
    )
    edge_cross, edge_mate = to_cross(edge_cross), to_mate(edge_mate)
    (correction,) = run(
        correction_kernel, [columns], [whole_scratch], 38, 16, drop, shifted, shifted_corners, low, own, high
    )
    new_low, new_high, inverse_cross, inverse_mate = run(
        second_edges_kernel,
        [square_group, square_group, triangle, triangle],
        [],
        20, 12, drop, corner_cross, corner_mate, correction, low, high,
    )
    inverse_cross, inverse_mate = to_cross(inverse_cross), to_mate(inverse_mate)
    whole, rim_cross, rim_mate = run(
        density_edges_kernel,
        [columns, triangle, triangle],
        [group_scratch] * 4,
        38, 20, drop, own, edge_cross, edge_mate, correction, new_low, new_high, square,
        square_corners,
    )
    rim_cross, rim_mate = to_cross(rim_cross), to_mate(rim_mate)
    (density_own,) = run(density_own_kernel, [square_group], [], 18, 12, drop, square, whole)
    out = jax.ShapeDtypeStruct(density.shape, kind)

    def assembled(own, first, cross, mate):
        (slots,) = call(functools.partial(slots_kernel, f, first), [out], [], 0, 8, drop, own, mate)
        scratch = [pltpu.VMEM(out.shape, kind), pltpu.SemaphoreType.DMA((3 * half,))]
        return call(
            functools.partial(last_slots_kernel, f), [out], scratch, 0, 8, drop, slots, cross, off=True
        )[0]

    inverse_next = assembled(whole, half, inverse_cross, inverse_mate)
    density_next = assembled(density_own, 0, rim_cross, rim_mate)
    return density_next, inverse_next


def solution(mesh):
    blocks = P(("grp", "row", "inner"), None, None, None)
    return jax.shard_map(
        on_device,
        mesh=mesh,
        in_specs=(blocks, blocks, P(("grp", "row", "inner"), None)),
        out_specs=(blocks, blocks),
        check_vma=False,
    )
```

```python
import functools

import jax
import jax.numpy as jnp
from jax import lax
from jax.experimental import pallas as pl
from jax.experimental.pallas import tpu as pltpu
from jax.sharding import PartitionSpec as P

RING = ("row", "inner")
MIB = 1024 * 1024


class Frame:
    def __init__(self, half, order):
        self.h = half
        self.b = order
        self.k = 2 * half
        self.p = half // 2
        self.t = 2 * order
        self.group = half * order
        self.pairs = 3 * self.p
        self.own_pairs = range(self.p, 2 * self.p)
        self.edge_rows = [*range(self.p), *range(2 * self.p, 3 * self.p)]

    def tiles(self, columns):
        for col in columns:
            for row in range(max(0, col - self.p), min(self.pairs, col + self.p + 1)):
                yield row, col

    def inner(self, row, col):
        return max(row, col) - self.p, min(row, col) + self.p + 1

    def clipped(self, row, col):
        lo, hi = self.inner(row, col)
        return max(lo, 0), min(hi, self.pairs)

    def on_corner(self, row, col):
        return max(row, col) < self.p or min(row, col) >= 2 * self.p

    def corner_place(self, row, col):
        r, c = (row, col) if row < self.p else (row - self.p, col - 2 * self.p)
        return r, r + 1, c, c + 1

    def split(self, row, col):
        lo, hi = self.clipped(row, col)
        for g in range(3):
            a, z = max(lo, g * self.p), min(hi, (g + 1) * self.p)
            if a < z:
                yield g, a - g * self.p, z - g * self.p


def under(h):
    return [(r, c) for r in range(h) for c in range(r + 1)]


def over(h):
    return [(r, c) for r in range(h) for c in range(r, h)]


def full(h):
    return [(r, c) for r in range(h) for c in range(h)]


def at(f, row_lo, row_hi, col_lo, col_hi):
    t = f.t
    return pl.ds(row_lo * t, (row_hi - row_lo) * t), pl.ds(col_lo * t, (col_hi - col_lo) * t)


def block(f, r, c):
    return pl.ds(r * f.b, f.b), pl.ds(c * f.b, f.b)


def banded(f, row, lo, hi):
    return at(f, row, row + 1, lo - row + f.p, hi - row + f.p)


def dot(a, b):
    return jnp.dot(a, b, preferred_element_type=jnp.float32)


def stored(rows, r, offset, dropped, slots=None):
    last = (rows.shape[1] if slots is None else slots) - 1
    slot = jnp.minimum(offset - (offset > dropped).astype(jnp.int32), last)
    value = rows[r, slot] if slots is None else rows((r, slot))
    return jnp.where(offset == dropped, jnp.zeros_like(value), value)


def masked(f, tile, row, col, drop_ref):
    b = f.b
    parts = []
    for i in range(2):
        r = 2 * row + i
        line = []
        for j in range(2):
            offset = 2 * col + j - r + f.h
            piece = tile[i * b : (i + 1) * b, j * b : (j + 1) * b]
            if 0 <= offset <= f.k:
                piece = jnp.where(drop_ref[r] == offset, 0.0, piece)
            else:
                piece = jnp.zeros_like(piece)
            line.append(piece)
        parts.append(jnp.concatenate(line, axis=1))
    return jnp.concatenate(parts, axis=0)


def odd_place(f, drop_ref):
    return drop_ref[3 * f.h] == 1


def indexed(f, ref, first=0):
    return lambda i: ref[block(f, first + i, 0)]


def plain(ref):
    return lambda place: ref[place]


def sides(f, drop_ref, mate, cross):
    odd = odd_place(f, drop_ref)

    def below(key):
        return jnp.where(odd, mate(key), cross(key))

    def above(key):
        return jnp.where(odd, cross(key), mate(key))

    return below, above


def spread(f, dest, row, col, read, places):
    index = {place: i for i, place in enumerate(places)}
    for r in range(f.h):
        for c in range(f.h):
            i = index.get((r, c))
            dest[block(f, row + r, col + c)] = jnp.zeros((f.b, f.b), dest.dtype) if i is None else read(i)


def pack_edges(f, drop_ref, low, high, to_cross, *to_mate):
    odd = odd_place(f, drop_ref)
    parts = len(to_mate)
    for i, (lower, upper) in enumerate(zip(under(f.h), over(f.h))):
        back, forth = low[block(f, *lower)], high[block(f, *upper)]
        to_cross[block(f, i, 0)] = jnp.where(odd, forth, back)
        to_mate[i % parts][block(f, i // parts, 0)] = jnp.where(odd, back, forth)


def slabs_kernel(f, drop_ref, own, corner, corner_again, to_mate, to_cross):
    h = f.h
    odd = drop_ref[h] == 1
    n = len(under(h))
    for i, (lower, upper) in enumerate(zip(under(h), over(h))):
        (r, c), (s, d) = lower, upper
        forth = stored(own, r, 2 * h + c - r, drop_ref[r])
        back = stored(own, s, d - s, drop_ref[s])
        to_mate[block(f, i, 0)] = jnp.where(odd, back, forth)
        to_cross[block(f, i, 0)] = jnp.where(odd, forth, back)
    for i, (r, c) in enumerate(full(h)):
        value = stored(own, r, c - r + h, drop_ref[r])
        corner[block(f, i, 0)] = value
        corner_again[block(f, i, 0)] = value
        to_mate[block(f, n + i, 0)] = value


def forward_kernel(f, drop_ref, cross, *refs):
    h = f.h
    odd = odd_place(f, drop_ref)
    to_mate, to_far = refs[-5:-3], refs[-3]
    for i, (lower, upper) in enumerate(zip(under(h), over(h))):
        (r, c), (s, d) = lower, upper
        forth = stored(cross, r, 2 * h + c - r, jnp.where(odd, drop_ref[2 * h + r], drop_ref[r]))
        back = stored(cross, s, d - s, jnp.where(odd, drop_ref[2 * h + s], drop_ref[s]))
        part, place = i % 2, i // 2
        to_mate[part][block(f, place, 0)] = jnp.where(odd, back, forth)
        to_far[block(f, i, 0)] = jnp.where(odd, forth, back)


def square_kernel(f, drop_ref, own, cross, mate, square, shifted, reach, here, partial, wide):
    h, p = f.h, f.p
    below, above = sides(f, drop_ref, plain(mate), plain(cross))
    for g, read in enumerate((below, plain(own), above)):
        for r in range(h):
            row = g * h + r
            first = 2 * (row // 2) - h
            for col in range(first, first + 2 * h + 2):
                offset = col - row + h
                if 0 <= offset <= f.k:
                    value = stored(read, r, offset, drop_ref[row], f.k)
                else:
                    value = jnp.zeros((f.b, f.b), wide.dtype)
                wide[block(f, row, col + h)] = value
    for i in range(h):
        for g, row in enumerate((i, 2 * h + i)):
            rows = pl.ds((g * h + i) * f.b, f.b)
            source = pl.ds(row * f.b, f.b)
            reach[rows, :] = wide[source, pl.ds(4 * g * f.group, f.group)]
            here[rows, :] = wide[source, pl.ds((2 * g + 1) * f.group, f.group)]
    unit = unit_tile(f)
    for row, col in f.tiles(range(f.pairs)):
        lo, hi = f.clipped(row, col)
        total = dot(
            wide[at(f, row, row + 1, lo + p, hi + p)], wide[at(f, lo, hi, col + p, col + p + 1)]
        )
        if f.on_corner(row, col):
            partial[at(f, *f.corner_place(row, col))] = total
            continue
        total = masked(f, total, row, col, drop_ref)
        place = banded(f, row, col, col + 1)
        tile = wide[at(f, row, row + 1, col + p, col + p + 1)].astype(jnp.float32)
        square[place] = total.astype(square.dtype)
        shifted[place] = moved(total, tile, unit if row == col else None).astype(shifted.dtype)


def unit_tile(f):
    rows = lax.broadcasted_iota(jnp.int32, (f.t, f.t), 0)
    return (rows == lax.broadcasted_iota(jnp.int32, (f.t, f.t), 1)).astype(jnp.float32)


def moved(total, tile, unit):
    value = 2.0 * total - 2.0 * tile
    return value if unit is None else value + unit


def corners_kernel(
    f, drop_ref, far_far, far_mate, far_mate_too, reach, here, partial, square, shifted, low, high
):
    p = f.p
    far_mates = [indexed(f, far_mate), indexed(f, far_mate_too)]
    far_below, far_above = sides(f, drop_ref, lambda i: far_mates[i % 2](i // 2), indexed(f, far_far))
    spread(f, low, 0, 0, far_below, under(f.h))
    spread(f, high, 0, 0, far_above, over(f.h))
    unit = unit_tile(f)
    for row, col in f.tiles(range(f.pairs)):
        if not f.on_corner(row, col):
            continue
        place = at(f, *f.corner_place(row, col))
        r, _, c, _ = f.corner_place(row, col)
        total = partial[place]
        if row < p:
            a, z, far = max(row, col), p, low
        else:
            a, z, far = 0, min(row, col) - 2 * p + 1, high
        if a < z:
            total = total + dot(reach[at(f, r, r + 1, a, z)], far[at(f, a, z, c, c + 1)])
        total = masked(f, total, row, col, drop_ref)
        tile = here[place].astype(jnp.float32)
        square[place] = total.astype(square.dtype)
        shifted[place] = moved(total, tile, unit if row == col else None).astype(shifted.dtype)


def right_tile(f, left, corners, right, row, col):
    lo, hi = f.clipped(row, col)
    total = None
    if row < f.p:
        inside = corners[at(f, row, row + 1, lo, f.p)]
        total = dot(inside, right[at(f, lo, f.p, col - f.p, col - f.p + 1)])
        lo = f.p
    elif row >= 2 * f.p:
        inside = corners[at(f, row - f.p, row - f.p + 1, 0, hi - 2 * f.p)]
        total = dot(inside, right[at(f, 2 * f.p, hi, col - f.p, col - f.p + 1)])
        hi = 2 * f.p
    rest = dot(left[banded(f, row, lo, hi)], right[at(f, lo, hi, col - f.p, col - f.p + 1)])
    return rest if total is None else total + rest


def first_sweep_kernel(
    f, drop_ref, shifted, corners, corner, sent_mate, sent_cross, mate, cross,
    correction, fresh, partial, whole, before, after,
):
    h, p = f.h, f.p
    from_below, from_above = sides(f, drop_ref, indexed(f, mate), indexed(f, cross))
    down, up = sides(f, drop_ref, indexed(f, sent_mate), indexed(f, sent_cross))
    spread(f, whole, 0, 0, from_below, under(h))
    spread(f, whole, h, 0, indexed(f, corner), full(h))
    spread(f, whole, 2 * h, 0, from_above, over(h))
    spread(f, before, 0, 0, down, over(h))
    spread(f, after, 0, 0, up, under(h))
    for row, col in f.tiles(f.own_pairs):
        total = masked(f, right_tile(f, shifted, corners, whole, row, col), row, col, drop_ref)
        correction[at(f, row, row + 1, col - p, col - p + 1)] = total.astype(correction.dtype)
    for row, col in f.tiles(f.own_pairs):
        c = col - p
        own_row = row in f.own_pairs
        total = 2.0 * whole[at(f, row, row + 1, c, c + 1)].astype(jnp.float32)
        for g, a, z in f.split(row, col):
            if g == 1:
                left = whole[at(f, row, row + 1, a, z)]
            elif own_row:
                left = (before, None, after)[g][at(f, row - p, row - p + 1, a, z)]
            else:
                continue
            total = total - dot(left, correction[at(f, g * p + a, g * p + z, c, c + 1)])
        if own_row:
            total = masked(f, total, row, col, drop_ref)
            fresh[at(f, row - p, row - p + 1, c, c + 1)] = total.astype(fresh.dtype)
        else:
            place = row if row < p else row - p
            partial[at(f, place, place + 1, c, c + 1)] = total


def edges(f, drop_ref, corner_below, corner_above, correction, start, low, high):
    p = f.p
    for row, col in f.tiles(f.own_pairs):
        if row in f.own_pairs:
            continue
        c = col - p
        side = 0 if row < p else 2
        corner, dest = ((corner_below, low), None, (corner_above, high))[side]
        local = row - side * p
        total = start(row, col)
        for g, a, z in f.split(row, col):
            if g == side:
                total = total - dot(
                    corner(at(f, local, local + 1, a, z)), correction[at(f, g * p + a, g * p + z, c, c + 1)]
                )
        total = masked(f, total, row, col, drop_ref)
        dest[at(f, local, local + 1, c, c + 1)] = total.astype(dest.dtype)


def first_edges_kernel(
    f, drop_ref, mate, cross, correction, partial, low, high, to_cross, to_mate, before, after
):
    p = f.p
    below, above = sides(f, drop_ref, indexed(f, mate, len(under(f.h))), indexed(f, cross))
    spread(f, before, 0, 0, below, full(f.h))
    spread(f, after, 0, 0, above, full(f.h))

    def start(row, col):
        place = row if row < p else row - p
        return partial[at(f, place, place + 1, col - p, col - p + 1)]

    edges(f, drop_ref, plain(before), plain(after), correction, start, low, high)
    pack_edges(f, drop_ref, low, high, to_cross, to_mate)


def gather(f, whole, low, own, high):
    for g, source in enumerate((low, own, high)):
        for i in range(f.h):
            whole[pl.ds(g * f.group + i * f.b, f.b), :] = source[pl.ds(i * f.b, f.b), :]


def correction_kernel(f, drop_ref, shifted, corners, low, own, high, correction, whole):
    p = f.p
    gather(f, whole, low, own, high)
    for row, col in f.tiles(f.own_pairs):
        total = masked(f, right_tile(f, shifted, corners, whole, row, col), row, col, drop_ref)
        correction[at(f, row, row + 1, col - p, col - p + 1)] = total.astype(correction.dtype)


def second_edges_kernel(
    f, drop_ref, cross, mate, correction, low, high, new_low, new_high, to_cross, to_mate
):
    p = f.p

    def start(row, col):
        c = col - p
        source, local = (low, row) if row < p else (high, row - 2 * p)
        total = 2.0 * source[at(f, local, local + 1, c, c + 1)].astype(jnp.float32)
        for g, a, z in f.split(row, col):
            if g == 1:
                total = total - dot(
                    source[at(f, local, local + 1, a, z)], correction[at(f, p + a, p + z, c, c + 1)]
                )
        return total

    below, above = sides(f, drop_ref, plain(mate), plain(cross))
    edges(f, drop_ref, below, above, correction, start, new_low, new_high)
    pack_edges(f, drop_ref, new_low, new_high, to_cross, to_mate)


def density_edges_kernel(
    f, drop_ref, own, cross, mate, correction, new_low, new_high, square, corners, whole, to_cross, to_mate,
    to_mate_too, before, after, low, high,
):
    h, p = f.h, f.p
    below, above = sides(f, drop_ref, indexed(f, mate), indexed(f, cross))
    spread(f, before, 0, 0, below, over(h))
    spread(f, after, 0, 0, above, under(h))
    for row, col in f.tiles(f.own_pairs):
        if row not in f.own_pairs:
            continue
        c, local = col - p, row - p
        total = 2.0 * own[at(f, local, local + 1, c, c + 1)].astype(jnp.float32)
        for g, a, z in f.split(row, col):
            left = (before, own, after)[g][at(f, local, local + 1, a, z)]
            total = total - dot(left, correction[at(f, g * p + a, g * p + z, c, c + 1)])
        total = masked(f, total, row, col, drop_ref)
        whole[at(f, row, row + 1, c, c + 1)] = total.astype(whole.dtype)
    for i in range(h):
        rows = pl.ds(i * f.b, f.b)
        whole[pl.ds(i * f.b, f.b), :] = new_low[rows, :]
        whole[pl.ds(2 * f.group + i * f.b, f.b), :] = new_high[rows, :]
    for row, col in f.tiles(f.own_pairs):
        if row in f.own_pairs:
            continue
        total = masked(f, right_tile(f, square, corners, whole, row, col), row, col, drop_ref)
        dest, local = (low, row) if row < p else (high, row - 2 * p)
        dest[at(f, local, local + 1, col - p, col - p + 1)] = total.astype(dest.dtype)
    pack_edges(f, drop_ref, low, high, to_cross, to_mate, to_mate_too)


def density_own_kernel(f, drop_ref, square, whole, out):
    p = f.p
    for row, col in f.tiles(f.own_pairs):
        if row in f.own_pairs:
            total = masked(f, right_tile(f, square, None, whole, row, col), row, col, drop_ref)
            out[at(f, row - p, row - p + 1, col - p, col - p + 1)] = total.astype(out.dtype)


def slots_kernel(f, first, parts, drop_ref, own, *refs):
    h = f.h
    mates = [indexed(f, ref) for ref in refs[:parts]]
    slots, out, sem = refs[parts:]
    over_index = {place: i for i, place in enumerate(over(h))}
    under_index = {place: i for i, place in enumerate(under(h))}

    def mate_block(i):
        return mates[i % parts](i // parts)

    for r in range(h):
        dropped = drop_ref[h + r]

        def at_offset(offset, r=r):
            col = r + offset
            if col < h:
                return mate_block(over_index[r, col])
            if col < 2 * h:
                return own[block(f, first + r, col - h)]
            return mate_block(under_index[r, col - 2 * h])

        for s in range(f.k):
            slots[r, s] = jnp.where(dropped <= s, at_offset(s + 1), at_offset(s))
    copy = pltpu.make_async_copy(slots, out, sem)
    copy.start()
    copy.wait()


def last_slots_kernel(f, drop_ref, slots, cross, unused, out, side, sems):
    h, k = f.h, f.k
    odd = odd_place(f, drop_ref)
    cross_block = indexed(f, cross)
    over_index = {place: i for i, place in enumerate(over(h))}
    under_index = {place: i for i, place in enumerate(under(h))}

    def fill(low):
        copies = []
        for r in range(h):
            dropped = drop_ref[h + r]
            lo, hi = (0, h - r) if low else (k - 1 - r, k)
            for s in range(lo, hi):

                def at_offset(offset, r=r, s=s):
                    col = r + offset
                    if low and col < h:
                        return cross_block(over_index[r, col])
                    if not low and col >= 2 * h:
                        return cross_block(under_index[r, col - 2 * h])
                    return slots[r, s]

                side[r, s] = jnp.where(dropped <= s, at_offset(s + 1), at_offset(s))
            copy = pltpu.make_async_copy(
                side.at[r, pl.ds(lo, hi - lo)], out.at[r, pl.ds(lo, hi - lo)], sems.at[r]
            )
            copy.start()
            copies.append(copy)
        for copy in copies:
            copy.wait()

    @pl.when(odd)
    def _():
        fill(False)

    @pl.when(jnp.logical_not(odd))
    def _():
        fill(True)


VMEM = pl.BlockSpec(memory_space=pltpu.VMEM)
SMEM = pl.BlockSpec(memory_space=pltpu.SMEM)
ANY = pl.BlockSpec(memory_space=pl.ANY)


def call(kernel, outs, scratch, flops, limit, drop, *args, passed=(), light=False, off=0):
    moved = sum(a.size * a.dtype.itemsize for a in args) + sum(s.size * s.dtype.itemsize for s in outs)
    if light:
        flops = moved = 0
    n = len(args)
    return pl.pallas_call(
        kernel,
        out_shape=[*outs, *[jax.ShapeDtypeStruct(a.shape, a.dtype) for a in passed]],
        in_specs=[SMEM] + [VMEM] * n + [ANY] * len(passed),
        out_specs=[VMEM] * (len(outs) - off) + [ANY] * (off + len(passed)),
        scratch_shapes=scratch,
        input_output_aliases={1 + n + i: len(outs) + i for i in range(len(passed))},
        compiler_params=pltpu.CompilerParams(vmem_limit_bytes=limit * MIB),
        cost_estimate=pl.CostEstimate(flops=flops, bytes_accessed=moved, transcendentals=0),
    )(drop, *args, *passed)


def routed(x, step):
    size = lax.axis_size(RING)
    return lax.ppermute(x, RING, [(i, (i + step(i)) % size) for i in range(size) if step(i)])


def on_device(density, inverse_start, block_cols):
    rows, width, order, _ = density.shape
    half = width // 2
    ring = lax.axis_size(RING)
    total = rows * ring
    assert rows == half and half % 2 == 0 and ring % 2 == 0
    f = Frame(half, order)
    kind = density.dtype
    me = lax.axis_index(RING)

    def mate_step(i):
        return 1 - 2 * (i % 2)

    def cross_step(i):
        return 2 * (i % 2) - 1

    def to_mate(x):
        return routed(x, mate_step)

    def to_cross(x):
        return routed(x, cross_step)

    positions = block_cols - (me * rows + jnp.arange(rows, dtype=jnp.int32))[:, None] + half
    positions = positions + jnp.where(positions < 0, total, jnp.where(positions >= total, -total, 0))
    own_drop = width * (width + 1) // 2 - jnp.sum(positions, axis=1)

    density_cross, density_mate = to_cross(density), to_mate(density)
    cross_drop, mate_drop = to_cross(own_drop), to_mate(own_drop)
    even = (me & 1) == 0
    mark = jnp.reshape(me & 1, (1,))
    start_drop = jnp.concatenate([own_drop, mark])
    drop = jnp.concatenate(
        [jnp.where(even, cross_drop, mate_drop), own_drop, jnp.where(even, mate_drop, cross_drop), mark]
    )

    unit = 2 * f.t**3
    count = half * (half + 1) // 2
    square_group = jax.ShapeDtypeStruct((f.group, f.group), kind)
    columns = jax.ShapeDtypeStruct((3 * f.group, f.group), kind)
    band = jax.ShapeDtypeStruct((3 * f.group, (2 * f.p + 1) * f.t), kind)
    triangle = jax.ShapeDtypeStruct((count * order, order), kind)
    half_triangle = jax.ShapeDtypeStruct((count // 2 * order, order), kind)
    listed = jax.ShapeDtypeStruct((half * half * order, order), kind)
    both = jax.ShapeDtypeStruct(((count + half * half) * order, order), kind)
    partial_sums = jax.ShapeDtypeStruct((2 * f.group, f.group), jnp.float32)
    group_scratch = pltpu.VMEM((f.group, f.group), kind)
    whole_scratch = pltpu.VMEM((3 * f.group, f.group), kind)

    def run(kernel, outs, scratch, tiles, limit, *args, **kw):
        return call(functools.partial(kernel, f), outs, scratch, tiles * unit, limit, *args, **kw)

    corner, corner_cross, slab_mate, triangle_cross = run(
        slabs_kernel, [listed, listed, both, triangle], [], 0, 12, start_drop, inverse_start
    )
    from_mate = to_mate(slab_mate)
    forward_mate, forward_mate_too, forward_far, triangle_cross, corner_cross = run(
        forward_kernel, [half_triangle, half_triangle, triangle], [], 0, 12, drop, density_cross, density_mate, from_mate,
        passed=(triangle_cross, corner_cross),
    )
    far_mate, far_mate_too = to_mate(forward_mate), to_mate(forward_mate_too)
    far_far = routed(forward_far, lambda i: 3 * cross_step(i))
    cross_triangle = to_cross(triangle_cross)
    cross_corner = to_cross(corner_cross)

    both_corners = jax.ShapeDtypeStruct((2 * f.group, f.group), kind)
    square, shifted, reach, here, partial = run(
        square_kernel,
        [band, band, both_corners, both_corners, partial_sums],
        [pltpu.VMEM((3 * f.group, 5 * f.group), kind)],
        84, 26, drop, density, density_cross, density_mate,
    )
    square_corners, shifted_corners = run(
        corners_kernel,
        [both_corners, both_corners],
        [group_scratch] * 2,
        10, 16, drop, far_far, far_mate, far_mate_too, reach, here, partial, light=True,
    )
    correction, own, partial = run(
        first_sweep_kernel,
        [columns, square_group, partial_sums],
        [whole_scratch, group_scratch, group_scratch],
        66, 24, drop, shifted, shifted_corners, corner, slab_mate, triangle_cross, from_mate, cross_triangle, light=True,
    )
    corner_cross, corner_mate = to_cross(own), to_mate(own)
    low, high, edge_cross, edge_mate = run(
        first_edges_kernel,
        [square_group, square_group, triangle, triangle],
        [group_scratch] * 2,
        10, 16, drop, from_mate, cross_corner, correction, partial,
    )
    edge_cross, edge_mate = to_cross(edge_cross), to_mate(edge_mate)
    (correction,) = run(
        correction_kernel, [columns], [whole_scratch], 38, 16, drop, shifted, shifted_corners, low, own, high
    )
    new_low, new_high, inverse_cross, inverse_mate = run(
        second_edges_kernel,
        [square_group, square_group, triangle, triangle],
        [],
        20, 12, drop, corner_cross, corner_mate, correction, low, high,
    )
    inverse_cross, inverse_mate = to_cross(inverse_cross), to_mate(inverse_mate)
    whole, rim_cross, rim_mate, rim_mate_too = run(
        density_edges_kernel,
        [columns, triangle, half_triangle, half_triangle],
        [group_scratch] * 4,
        38, 20, drop, own, edge_cross, edge_mate, correction, new_low, new_high, square,
        square_corners,
    )
    rim_cross, rim_mates = to_cross(rim_cross), [to_mate(rim_mate), to_mate(rim_mate_too)]
    (density_own,) = run(density_own_kernel, [square_group], [], 18, 12, drop, square, whole)
    out = jax.ShapeDtypeStruct(density.shape, kind)

    def assembled(own, first, cross, mates):
        kernel = functools.partial(slots_kernel, f, first, len(mates))
        scratch = [pltpu.SemaphoreType.DMA(())]
        slots, early = call(kernel, [out, out], scratch, 0, 8, drop, own, *mates, light=True, off=1)
        scratch = [pltpu.VMEM(out.shape, kind), pltpu.SemaphoreType.DMA((half,))]
        kernel = functools.partial(last_slots_kernel, f)
        return call(kernel, [], scratch, 0, 8, drop, slots, cross, passed=(early,), light=True)[0]

    inverse_next = assembled(whole, half, inverse_cross, [inverse_mate])
    density_next = assembled(density_own, 0, rim_cross, rim_mates)
    return density_next, inverse_next


def solution(mesh):
    blocks = P(("grp", "row", "inner"), None, None, None)
    return jax.shard_map(
        on_device,
        mesh=mesh,
        in_specs=(blocks, blocks, P(("grp", "row", "inner"), None)),
        out_specs=(blocks, blocks),
        check_vma=False,
    )
```

```python
import functools

import jax
import jax.numpy as jnp
from jax import lax
from jax.experimental import pallas as pl
from jax.experimental.pallas import tpu as pltpu
from jax.sharding import PartitionSpec as P

RING = ("row", "inner")
MIB = 1024 * 1024


class Frame:
    def __init__(self, half, order):
        self.h = half
        self.b = order
        self.k = 2 * half
        self.p = half // 2
        self.t = 2 * order
        self.group = half * order
        self.pairs = 3 * self.p
        self.own_pairs = range(self.p, 2 * self.p)
        self.edge_rows = [*range(self.p), *range(2 * self.p, 3 * self.p)]

    def tiles(self, columns):
        for col in columns:
            for row in range(max(0, col - self.p), min(self.pairs, col + self.p + 1)):
                yield row, col

    def inner(self, row, col):
        return max(row, col) - self.p, min(row, col) + self.p + 1

    def clipped(self, row, col):
        lo, hi = self.inner(row, col)
        return max(lo, 0), min(hi, self.pairs)

    def on_corner(self, row, col):
        return max(row, col) < self.p or min(row, col) >= 2 * self.p

    def corner_place(self, row, col):
        r, c = (row, col) if row < self.p else (row - self.p, col - 2 * self.p)
        return r, r + 1, c, c + 1

    def split(self, row, col):
        lo, hi = self.clipped(row, col)
        for g in range(3):
            a, z = max(lo, g * self.p), min(hi, (g + 1) * self.p)
            if a < z:
                yield g, a - g * self.p, z - g * self.p


def under(h):
    return [(r, c) for r in range(h) for c in range(r + 1)]


def over(h):
    return [(r, c) for r in range(h) for c in range(r, h)]


def full(h):
    return [(r, c) for r in range(h) for c in range(h)]


def at(f, row_lo, row_hi, col_lo, col_hi):
    t = f.t
    return pl.ds(row_lo * t, (row_hi - row_lo) * t), pl.ds(col_lo * t, (col_hi - col_lo) * t)


def block(f, r, c):
    return pl.ds(r * f.b, f.b), pl.ds(c * f.b, f.b)


def banded(f, row, lo, hi):
    return at(f, row, row + 1, lo - row + f.p, hi - row + f.p)


def dot(a, b):
    return jnp.dot(a, b, preferred_element_type=jnp.float32)


def stored(rows, r, offset, dropped, slots=None):
    last = (rows.shape[1] if slots is None else slots) - 1
    slot = jnp.minimum(offset - (offset > dropped).astype(jnp.int32), last)
    value = rows[r, slot] if slots is None else rows((r, slot))
    return jnp.where(offset == dropped, jnp.zeros_like(value), value)


def masked(f, tile, row, col, drop_ref):
    b = f.b
    parts = []
    for i in range(2):
        r = 2 * row + i
        line = []
        for j in range(2):
            offset = 2 * col + j - r + f.h
            piece = tile[i * b : (i + 1) * b, j * b : (j + 1) * b]
            if 0 <= offset <= f.k:
                piece = jnp.where(drop_ref[r] == offset, 0.0, piece)
            else:
                piece = jnp.zeros_like(piece)
            line.append(piece)
        parts.append(jnp.concatenate(line, axis=1))
    return jnp.concatenate(parts, axis=0)


def odd_place(f, drop_ref):
    return drop_ref[3 * f.h] == 1


def indexed(f, ref, first=0):
    return lambda i: ref[block(f, first + i, 0)]


def plain(ref):
    return lambda place: ref[place]


def sides(f, drop_ref, mate, cross):
    odd = odd_place(f, drop_ref)

    def below(key):
        return jnp.where(odd, mate(key), cross(key))

    def above(key):
        return jnp.where(odd, cross(key), mate(key))

    return below, above


def spread(f, dest, row, col, read, places):
    index = {place: i for i, place in enumerate(places)}
    for r in range(f.h):
        for c in range(f.h):
            i = index.get((r, c))
            dest[block(f, row + r, col + c)] = jnp.zeros((f.b, f.b), dest.dtype) if i is None else read(i)


def pack_edges(f, drop_ref, low, high, to_cross, *to_mate):
    odd = odd_place(f, drop_ref)
    parts = len(to_mate)
    for i, (lower, upper) in enumerate(zip(under(f.h), over(f.h))):
        back, forth = low[block(f, *lower)], high[block(f, *upper)]
        to_cross[block(f, i, 0)] = jnp.where(odd, forth, back)
        to_mate[i % parts][block(f, i // parts, 0)] = jnp.where(odd, back, forth)


def slabs_kernel(f, drop_ref, own, corner, corner_again, to_mate, to_cross, to_cross_again):
    h = f.h
    odd = drop_ref[h] == 1
    n = len(under(h))
    for i, (lower, upper) in enumerate(zip(under(h), over(h))):
        (r, c), (s, d) = lower, upper
        forth = stored(own, r, 2 * h + c - r, drop_ref[r])
        back = stored(own, s, d - s, drop_ref[s])
        to_mate[block(f, i, 0)] = jnp.where(odd, back, forth)
        across = jnp.where(odd, forth, back)
        to_cross[block(f, i, 0)] = across
        to_cross_again[block(f, i, 0)] = across
    for i, (r, c) in enumerate(full(h)):
        value = stored(own, r, c - r + h, drop_ref[r])
        corner[block(f, i, 0)] = value
        corner_again[block(f, i, 0)] = value
        to_mate[block(f, n + i, 0)] = value


def forward_kernel(f, drop_ref, cross, *refs):
    h = f.h
    odd = odd_place(f, drop_ref)
    to_mate, to_far = refs[-4:-2]
    for i, (lower, upper) in enumerate(zip(under(h), over(h))):
        (r, c), (s, d) = lower, upper
        forth = stored(cross, r, 2 * h + c - r, jnp.where(odd, drop_ref[2 * h + r], drop_ref[r]))
        back = stored(cross, s, d - s, jnp.where(odd, drop_ref[2 * h + s], drop_ref[s]))
        to_mate[block(f, i, 0)] = jnp.where(odd, back, forth)
        to_far[block(f, i, 0)] = jnp.where(odd, forth, back)


def square_kernel(f, drop_ref, own, cross, mate, square, shifted, reach, here, partial, wide):
    h, p = f.h, f.p
    below, above = sides(f, drop_ref, plain(mate), plain(cross))
    for g, read in enumerate((below, plain(own), above)):
        for r in range(h):
            row = g * h + r
            first = 2 * (row // 2) - h
            for col in range(first, first + 2 * h + 2):
                offset = col - row + h
                if 0 <= offset <= f.k:
                    value = stored(read, r, offset, drop_ref[row], f.k)
                else:
                    value = jnp.zeros((f.b, f.b), wide.dtype)
                wide[block(f, row, col + h)] = value
    for i in range(h):
        for g, row in enumerate((i, 2 * h + i)):
            rows = pl.ds((g * h + i) * f.b, f.b)
            source = pl.ds(row * f.b, f.b)
            reach[rows, :] = wide[source, pl.ds(4 * g * f.group, f.group)]
            here[rows, :] = wide[source, pl.ds((2 * g + 1) * f.group, f.group)]
    unit = unit_tile(f)
    for row, col in f.tiles(range(f.pairs)):
        lo, hi = f.clipped(row, col)
        total = dot(
            wide[at(f, row, row + 1, lo + p, hi + p)], wide[at(f, lo, hi, col + p, col + p + 1)]
        )
        if f.on_corner(row, col):
            partial[at(f, *f.corner_place(row, col))] = total
            continue
        total = masked(f, total, row, col, drop_ref)
        place = banded(f, row, col, col + 1)
        tile = wide[at(f, row, row + 1, col + p, col + p + 1)].astype(jnp.float32)
        square[place] = total.astype(square.dtype)
        shifted[place] = moved(total, tile, unit if row == col else None).astype(shifted.dtype)


def unit_tile(f):
    rows = lax.broadcasted_iota(jnp.int32, (f.t, f.t), 0)
    return (rows == lax.broadcasted_iota(jnp.int32, (f.t, f.t), 1)).astype(jnp.float32)


def moved(total, tile, unit):
    value = 2.0 * total - 2.0 * tile
    return value if unit is None else value + unit


def corners_kernel(
    f, drop_ref, far_far, far_mate, reach, here, partial, unused, square, shifted, low, high
):
    p = f.p
    far_below, far_above = sides(f, drop_ref, indexed(f, far_mate), indexed(f, far_far))
    spread(f, low, 0, 0, far_below, under(f.h))
    spread(f, high, 0, 0, far_above, over(f.h))
    unit = unit_tile(f)
    for row, col in f.tiles(range(f.pairs)):
        if not f.on_corner(row, col):
            continue
        place = at(f, *f.corner_place(row, col))
        r, _, c, _ = f.corner_place(row, col)
        total = partial[place]
        if row < p:
            a, z, far = max(row, col), p, low
        else:
            a, z, far = 0, min(row, col) - 2 * p + 1, high
        if a < z:
            total = total + dot(reach[at(f, r, r + 1, a, z)], far[at(f, a, z, c, c + 1)])
        total = masked(f, total, row, col, drop_ref)
        tile = here[place].astype(jnp.float32)
        square[place] = total.astype(square.dtype)
        shifted[place] = moved(total, tile, unit if row == col else None).astype(shifted.dtype)


def right_tile(f, left, corners, right, row, col):
    lo, hi = f.clipped(row, col)
    total = None
    if row < f.p:
        inside = corners[at(f, row, row + 1, lo, f.p)]
        total = dot(inside, right[at(f, lo, f.p, col - f.p, col - f.p + 1)])
        lo = f.p
    elif row >= 2 * f.p:
        inside = corners[at(f, row - f.p, row - f.p + 1, 0, hi - 2 * f.p)]
        total = dot(inside, right[at(f, 2 * f.p, hi, col - f.p, col - f.p + 1)])
        hi = 2 * f.p
    rest = dot(left[banded(f, row, lo, hi)], right[at(f, lo, hi, col - f.p, col - f.p + 1)])
    return rest if total is None else total + rest


def first_sweep_kernel(
    f, drop_ref, shifted, corners, corner, sent_mate, sent_cross, mate, direct, turned,
    correction, fresh, partial, whole, before, after,
):
    h, p = f.h, f.p
    turning = drop_ref[3 * h + 1] == 1
    direct_block, turned_block = indexed(f, direct), indexed(f, turned)

    def cross(i):
        return jnp.where(turning, turned_block(i), direct_block(i))

    from_below, from_above = sides(f, drop_ref, indexed(f, mate), cross)
    down, up = sides(f, drop_ref, indexed(f, sent_mate), indexed(f, sent_cross))
    spread(f, whole, 0, 0, from_below, under(h))
    spread(f, whole, h, 0, indexed(f, corner), full(h))
    spread(f, whole, 2 * h, 0, from_above, over(h))
    spread(f, before, 0, 0, down, over(h))
    spread(f, after, 0, 0, up, under(h))
    for row, col in f.tiles(f.own_pairs):
        total = masked(f, right_tile(f, shifted, corners, whole, row, col), row, col, drop_ref)
        correction[at(f, row, row + 1, col - p, col - p + 1)] = total.astype(correction.dtype)
    for row, col in f.tiles(f.own_pairs):
        c = col - p
        own_row = row in f.own_pairs
        total = 2.0 * whole[at(f, row, row + 1, c, c + 1)].astype(jnp.float32)
        for g, a, z in f.split(row, col):
            if g == 1:
                left = whole[at(f, row, row + 1, a, z)]
            elif own_row:
                left = (before, None, after)[g][at(f, row - p, row - p + 1, a, z)]
            else:
                continue
            total = total - dot(left, correction[at(f, g * p + a, g * p + z, c, c + 1)])
        if own_row:
            total = masked(f, total, row, col, drop_ref)
            fresh[at(f, row - p, row - p + 1, c, c + 1)] = total.astype(fresh.dtype)
        else:
            place = row if row < p else row - p
            partial[at(f, place, place + 1, c, c + 1)] = total


def edges(f, drop_ref, corner_below, corner_above, correction, start, low, high):
    p = f.p
    for row, col in f.tiles(f.own_pairs):
        if row in f.own_pairs:
            continue
        c = col - p
        side = 0 if row < p else 2
        corner, dest = ((corner_below, low), None, (corner_above, high))[side]
        local = row - side * p
        total = start(row, col)
        for g, a, z in f.split(row, col):
            if g == side:
                total = total - dot(
                    corner(at(f, local, local + 1, a, z)), correction[at(f, g * p + a, g * p + z, c, c + 1)]
                )
        total = masked(f, total, row, col, drop_ref)
        dest[at(f, local, local + 1, c, c + 1)] = total.astype(dest.dtype)


def first_edges_kernel(
    f, drop_ref, mate, cross, correction, partial, low, high, to_cross, to_mate, before, after
):
    p = f.p
    below, above = sides(f, drop_ref, indexed(f, mate, len(under(f.h))), indexed(f, cross))
    spread(f, before, 0, 0, below, full(f.h))
    spread(f, after, 0, 0, above, full(f.h))

    def start(row, col):
        place = row if row < p else row - p
        return partial[at(f, place, place + 1, col - p, col - p + 1)]

    edges(f, drop_ref, plain(before), plain(after), correction, start, low, high)
    pack_edges(f, drop_ref, low, high, to_cross, to_mate)


def gather(f, whole, low, own, high):
    for g, source in enumerate((low, own, high)):
        for i in range(f.h):
            whole[pl.ds(g * f.group + i * f.b, f.b), :] = source[pl.ds(i * f.b, f.b), :]


def correction_kernel(f, drop_ref, shifted, corners, low, own, high, correction, whole):
    p = f.p
    gather(f, whole, low, own, high)
    for row, col in f.tiles(f.own_pairs):
        total = masked(f, right_tile(f, shifted, corners, whole, row, col), row, col, drop_ref)
        correction[at(f, row, row + 1, col - p, col - p + 1)] = total.astype(correction.dtype)


def second_edges_kernel(
    f, drop_ref, mate, cross, correction, low, high, new_low, new_high, to_cross, to_mate
):
    p = f.p

    def start(row, col):
        c = col - p
        source, local = (low, row) if row < p else (high, row - 2 * p)
        total = 2.0 * source[at(f, local, local + 1, c, c + 1)].astype(jnp.float32)
        for g, a, z in f.split(row, col):
            if g == 1:
                total = total - dot(
                    source[at(f, local, local + 1, a, z)], correction[at(f, p + a, p + z, c, c + 1)]
                )
        return total

    below, above = sides(f, drop_ref, plain(mate), plain(cross))
    edges(f, drop_ref, below, above, correction, start, new_low, new_high)
    pack_edges(f, drop_ref, new_low, new_high, to_cross, to_mate)


def density_edges_kernel(
    f, drop_ref, own, cross, mate, correction, new_low, new_high, square, corners, whole, to_cross, to_mate,
    to_mate_too, before, after, low, high,
):
    h, p = f.h, f.p
    below, above = sides(f, drop_ref, indexed(f, mate), indexed(f, cross))
    spread(f, before, 0, 0, below, over(h))
    spread(f, after, 0, 0, above, under(h))
    for row, col in f.tiles(f.own_pairs):
        if row not in f.own_pairs:
            continue
        c, local = col - p, row - p
        total = 2.0 * own[at(f, local, local + 1, c, c + 1)].astype(jnp.float32)
        for g, a, z in f.split(row, col):
            left = (before, own, after)[g][at(f, local, local + 1, a, z)]
            total = total - dot(left, correction[at(f, g * p + a, g * p + z, c, c + 1)])
        total = masked(f, total, row, col, drop_ref)
        whole[at(f, row, row + 1, c, c + 1)] = total.astype(whole.dtype)
    for i in range(h):
        rows = pl.ds(i * f.b, f.b)
        whole[pl.ds(i * f.b, f.b), :] = new_low[rows, :]
        whole[pl.ds(2 * f.group + i * f.b, f.b), :] = new_high[rows, :]
    for row, col in f.tiles(f.own_pairs):
        if row in f.own_pairs:
            continue
        total = masked(f, right_tile(f, square, corners, whole, row, col), row, col, drop_ref)
        dest, local = (low, row) if row < p else (high, row - 2 * p)
        dest[at(f, local, local + 1, col - p, col - p + 1)] = total.astype(dest.dtype)
    pack_edges(f, drop_ref, low, high, to_cross, to_mate, to_mate_too)


def density_own_kernel(f, drop_ref, square, whole, out):
    p = f.p
    for row, col in f.tiles(f.own_pairs):
        if row in f.own_pairs:
            total = masked(f, right_tile(f, square, None, whole, row, col), row, col, drop_ref)
            out[at(f, row - p, row - p + 1, col - p, col - p + 1)] = total.astype(out.dtype)


def slots_kernel(f, first, parts, drop_ref, own, *refs):
    h = f.h
    mates = [indexed(f, ref) for ref in refs[:parts]]
    slots, out, sem = refs[parts:]
    over_index = {place: i for i, place in enumerate(over(h))}
    under_index = {place: i for i, place in enumerate(under(h))}

    def mate_block(i):
        return mates[i % parts](i // parts)

    for r in range(h):
        dropped = drop_ref[h + r]

        def at_offset(offset, r=r):
            col = r + offset
            if col < h:
                return mate_block(over_index[r, col])
            if col < 2 * h:
                return own[block(f, first + r, col - h)]
            return mate_block(under_index[r, col - 2 * h])

        for s in range(f.k):
            slots[r, s] = jnp.where(dropped <= s, at_offset(s + 1), at_offset(s))
    copy = pltpu.make_async_copy(slots, out, sem)
    copy.start()
    copy.wait()


def last_slots_kernel(f, drop_ref, slots, cross, unused, out, side, sems):
    h, k = f.h, f.k
    odd = odd_place(f, drop_ref)
    cross_block = indexed(f, cross)
    over_index = {place: i for i, place in enumerate(over(h))}
    under_index = {place: i for i, place in enumerate(under(h))}

    def fill(low):
        copies = []
        for r in range(h):
            dropped = drop_ref[h + r]
            lo, hi = (0, h - r) if low else (k - 1 - r, k)
            for s in range(lo, hi):

                def at_offset(offset, r=r, s=s):
                    col = r + offset
                    if low and col < h:
                        return cross_block(over_index[r, col])
                    if not low and col >= 2 * h:
                        return cross_block(under_index[r, col - 2 * h])
                    return slots[r, s]

                side[r, s] = jnp.where(dropped <= s, at_offset(s + 1), at_offset(s))
            copy = pltpu.make_async_copy(
                side.at[r, pl.ds(lo, hi - lo)], out.at[r, pl.ds(lo, hi - lo)], sems.at[r]
            )
            copy.start()
            copies.append(copy)
        for copy in copies:
            copy.wait()

    @pl.when(odd)
    def _():
        fill(False)

    @pl.when(jnp.logical_not(odd))
    def _():
        fill(True)


VMEM = pl.BlockSpec(memory_space=pltpu.VMEM)
SMEM = pl.BlockSpec(memory_space=pltpu.SMEM)
ANY = pl.BlockSpec(memory_space=pl.ANY)


def call(kernel, outs, scratch, flops, limit, drop, *args, passed=(), light=False, off=0):
    moved = sum(a.size * a.dtype.itemsize for a in args) + sum(s.size * s.dtype.itemsize for s in outs)
    if light:
        flops = moved = 0
    n = len(args)
    return pl.pallas_call(
        kernel,
        out_shape=[*outs, *[jax.ShapeDtypeStruct(a.shape, a.dtype) for a in passed]],
        in_specs=[SMEM] + [VMEM] * n + [ANY] * len(passed),
        out_specs=[VMEM] * (len(outs) - off) + [ANY] * (off + len(passed)),
        scratch_shapes=scratch,
        input_output_aliases={1 + n + i: len(outs) + i for i in range(len(passed))},
        compiler_params=pltpu.CompilerParams(vmem_limit_bytes=limit * MIB),
        cost_estimate=pl.CostEstimate(flops=flops, bytes_accessed=moved, transcendentals=0),
    )(drop, *args, *passed)


def routed(x, step):
    size = lax.axis_size(RING)
    return lax.ppermute(x, RING, [(i, (i + step(i)) % size) for i in range(size) if step(i)])


def on_device(density, inverse_start, block_cols):
    rows, width, order, _ = density.shape
    half = width // 2
    ring, inner = lax.axis_size(RING), lax.axis_size(RING[1])
    total = rows * ring
    assert rows == half and half % 2 == 0 and inner % 2 == 0
    f = Frame(half, order)
    kind = density.dtype
    me = lax.axis_index(RING)

    def mate_step(i):
        return 1 - 2 * (i % 2)

    def cross_step(i):
        return 2 * (i % 2) - 1

    def to_mate(x):
        return routed(x, mate_step)

    def to_cross(x):
        return routed(x, cross_step)

    def turns(i):
        return i % inner in (0, inner - 1)

    positions = block_cols - (me * rows + jnp.arange(rows, dtype=jnp.int32))[:, None] + half
    positions = positions + jnp.where(positions < 0, total, jnp.where(positions >= total, -total, 0))
    own_drop = width * (width + 1) // 2 - jnp.sum(positions, axis=1)

    density_cross, density_mate = to_cross(density), to_mate(density)
    cross_drop, mate_drop = to_cross(own_drop), to_mate(own_drop)
    even = (me & 1) == 0
    place = lax.axis_index(RING[1])
    marks = jnp.stack([me & 1, ((place == 0) | (place == inner - 1)).astype(jnp.int32)])
    start_drop = jnp.concatenate([own_drop, marks[:1]])
    drop = jnp.concatenate(
        [jnp.where(even, cross_drop, mate_drop), own_drop, jnp.where(even, mate_drop, cross_drop), marks]
    )

    unit = 2 * f.t**3
    count = half * (half + 1) // 2
    square_group = jax.ShapeDtypeStruct((f.group, f.group), kind)
    columns = jax.ShapeDtypeStruct((3 * f.group, f.group), kind)
    band = jax.ShapeDtypeStruct((3 * f.group, (2 * f.p + 1) * f.t), kind)
    triangle = jax.ShapeDtypeStruct((count * order, order), kind)
    half_triangle = jax.ShapeDtypeStruct((count // 2 * order, order), kind)
    listed = jax.ShapeDtypeStruct((half * half * order, order), kind)
    both = jax.ShapeDtypeStruct(((count + half * half) * order, order), kind)
    partial_sums = jax.ShapeDtypeStruct((2 * f.group, f.group), jnp.float32)
    group_scratch = pltpu.VMEM((f.group, f.group), kind)
    whole_scratch = pltpu.VMEM((3 * f.group, f.group), kind)

    def run(kernel, outs, scratch, tiles, limit, *args, **kw):
        return call(functools.partial(kernel, f), outs, scratch, tiles * unit, limit, *args, **kw)

    corner, corner_cross, slab_mate, triangle_cross, triangle_turning = run(
        slabs_kernel, [listed, listed, both, triangle, triangle], [], 0, 12, start_drop, inverse_start
    )
    from_mate = to_mate(slab_mate)
    direct_triangle = routed(triangle_cross, lambda i: 0 if turns(i) else cross_step(i))
    forward_mate, forward_far, triangle_turning, corner_cross = run(
        forward_kernel, [triangle, triangle], [], 0, 12, drop, density_cross, density_mate, from_mate,
        passed=(triangle_turning, corner_cross),
    )
    far_mate = to_mate(forward_mate)
    far_far = routed(forward_far, lambda i: 3 * cross_step(i))
    turned_triangle = routed(triangle_turning, lambda i: cross_step(i) if turns(i) else 0)
    cross_corner = to_cross(corner_cross)

    both_corners = jax.ShapeDtypeStruct((2 * f.group, f.group), kind)
    square, shifted, reach, here, partial = run(
        square_kernel,
        [band, band, both_corners, both_corners, partial_sums],
        [pltpu.VMEM((3 * f.group, 5 * f.group), kind)],
        84, 26, drop, density, density_cross, density_mate, light=True,
    )
    square_corners, shifted_corners = run(
        corners_kernel,
        [both_corners, both_corners],
        [group_scratch] * 2,
        10, 16, drop, far_far, far_mate, reach, here, partial, direct_triangle, light=True,
    )
    correction, own, partial = run(
        first_sweep_kernel,
        [columns, square_group, partial_sums],
        [whole_scratch, group_scratch, group_scratch],
        66, 24, drop, shifted, shifted_corners, corner, slab_mate, triangle_cross, from_mate,
        direct_triangle, turned_triangle, light=True,
    )
    corner_cross, corner_mate = to_cross(own), to_mate(own)
    low, high, edge_cross, edge_mate = run(
        first_edges_kernel,
        [square_group, square_group, triangle, triangle],
        [group_scratch] * 2,
        10, 16, drop, from_mate, cross_corner, correction, partial,
    )
    edge_cross, edge_mate = to_cross(edge_cross), to_mate(edge_mate)
    (correction,) = run(
        correction_kernel, [columns], [whole_scratch], 38, 16, drop, shifted, shifted_corners, low, own, high
    )
    new_low, new_high, inverse_cross, inverse_mate = run(
        second_edges_kernel,
        [square_group, square_group, triangle, triangle],
        [],
        20, 12, drop, corner_mate, corner_cross, correction, low, high,
    )
    inverse_cross, inverse_mate = to_cross(inverse_cross), to_mate(inverse_mate)
    whole, rim_cross, rim_mate, rim_mate_too = run(
        density_edges_kernel,
        [columns, triangle, half_triangle, half_triangle],
        [group_scratch] * 4,
        38, 20, drop, own, edge_cross, edge_mate, correction, new_low, new_high, square,
        square_corners,
    )
    rim_cross, rim_mates = to_cross(rim_cross), [to_mate(rim_mate), to_mate(rim_mate_too)]
    (density_own,) = run(density_own_kernel, [square_group], [], 18, 12, drop, square, whole)
    out = jax.ShapeDtypeStruct(density.shape, kind)

    def assembled(own, first, cross, mates):
        kernel = functools.partial(slots_kernel, f, first, len(mates))
        scratch = [pltpu.SemaphoreType.DMA(())]
        slots, early = call(kernel, [out, out], scratch, 0, 8, drop, own, *mates, light=True, off=1)
        scratch = [pltpu.VMEM(out.shape, kind), pltpu.SemaphoreType.DMA((half,))]
        kernel = functools.partial(last_slots_kernel, f)
        return call(kernel, [], scratch, 0, 8, drop, slots, cross, passed=(early,), light=True)[0]

    inverse_next = assembled(whole, half, inverse_cross, [inverse_mate])
    density_next = assembled(density_own, 0, rim_cross, rim_mates)
    return density_next, inverse_next


def solution(mesh):
    blocks = P(("grp", "row", "inner"), None, None, None)
    return jax.shard_map(
        on_device,
        mesh=mesh,
        in_specs=(blocks, blocks, P(("grp", "row", "inner"), None)),
        out_specs=(blocks, blocks),
        check_vma=False,
    )
```

```python
import functools

import jax
import jax.numpy as jnp
from jax import lax
from jax.experimental import pallas as pl
from jax.experimental.pallas import tpu as pltpu
from jax.sharding import PartitionSpec as P

RING = ("row", "inner")
MIB = 1024 * 1024


class Frame:
    def __init__(self, half, order):
        self.h = half
        self.b = order
        self.k = 2 * half
        self.p = half // 2
        self.t = 2 * order
        self.group = half * order
        self.pairs = 3 * self.p
        self.own_pairs = range(self.p, 2 * self.p)
        self.edge_rows = [*range(self.p), *range(2 * self.p, 3 * self.p)]

    def tiles(self, columns):
        for col in columns:
            for row in range(max(0, col - self.p), min(self.pairs, col + self.p + 1)):
                yield row, col

    def inner(self, row, col):
        return max(row, col) - self.p, min(row, col) + self.p + 1

    def clipped(self, row, col):
        lo, hi = self.inner(row, col)
        return max(lo, 0), min(hi, self.pairs)

    def on_corner(self, row, col):
        return max(row, col) < self.p or min(row, col) >= 2 * self.p

    def corner_place(self, row, col):
        r, c = (row, col) if row < self.p else (row - self.p, col - 2 * self.p)
        return r, r + 1, c, c + 1

    def split(self, row, col):
        lo, hi = self.clipped(row, col)
        for g in range(3):
            a, z = max(lo, g * self.p), min(hi, (g + 1) * self.p)
            if a < z:
                yield g, a - g * self.p, z - g * self.p


def under(h):
    return [(r, c) for r in range(h) for c in range(r + 1)]


def over(h):
    return [(r, c) for r in range(h) for c in range(r, h)]


def full(h):
    return [(r, c) for r in range(h) for c in range(h)]


def at(f, row_lo, row_hi, col_lo, col_hi):
    t = f.t
    return pl.ds(row_lo * t, (row_hi - row_lo) * t), pl.ds(col_lo * t, (col_hi - col_lo) * t)


def block(f, r, c):
    return pl.ds(r * f.b, f.b), pl.ds(c * f.b, f.b)


def banded(f, row, lo, hi):
    return at(f, row, row + 1, lo - row + f.p, hi - row + f.p)


def dot(a, b):
    return jnp.dot(a, b, preferred_element_type=jnp.float32)


def stored(rows, r, offset, dropped, slots=None):
    last = (rows.shape[1] if slots is None else slots) - 1
    slot = jnp.minimum(offset - (offset > dropped).astype(jnp.int32), last)
    value = rows[r, slot] if slots is None else rows((r, slot))
    return jnp.where(offset == dropped, jnp.zeros_like(value), value)


def masked(f, tile, row, col, drop_ref):
    b = f.b
    parts = []
    for i in range(2):
        r = 2 * row + i
        line = []
        for j in range(2):
            offset = 2 * col + j - r + f.h
            piece = tile[i * b : (i + 1) * b, j * b : (j + 1) * b]
            if 0 <= offset <= f.k:
                piece = jnp.where(drop_ref[r] == offset, 0.0, piece)
            else:
                piece = jnp.zeros_like(piece)
            line.append(piece)
        parts.append(jnp.concatenate(line, axis=1))
    return jnp.concatenate(parts, axis=0)


def odd_place(f, drop_ref):
    return drop_ref[3 * f.h] == 1


def indexed(f, ref, first=0):
    return lambda i: ref[block(f, first + i, 0)]


def plain(ref):
    return lambda place: ref[place]


def sides(f, drop_ref, mate, cross):
    odd = odd_place(f, drop_ref)

    def below(key):
        return jnp.where(odd, mate(key), cross(key))

    def above(key):
        return jnp.where(odd, cross(key), mate(key))

    return below, above


def spread(f, dest, row, col, read, places):
    index = {place: i for i, place in enumerate(places)}
    for r in range(f.h):
        for c in range(f.h):
            i = index.get((r, c))
            dest[block(f, row + r, col + c)] = jnp.zeros((f.b, f.b), dest.dtype) if i is None else read(i)


def pack_edges(f, drop_ref, low, high, to_cross, *to_mate):
    odd = odd_place(f, drop_ref)
    parts = len(to_mate)
    for i, (lower, upper) in enumerate(zip(under(f.h), over(f.h))):
        back, forth = low[block(f, *lower)], high[block(f, *upper)]
        to_cross[block(f, i, 0)] = jnp.where(odd, forth, back)
        to_mate[i % parts][block(f, i // parts, 0)] = jnp.where(odd, back, forth)


def slabs_kernel(f, drop_ref, own, corner, corner_again, to_mate, to_cross):
    h = f.h
    odd = drop_ref[h] == 1
    n = len(under(h))
    for i, (lower, upper) in enumerate(zip(under(h), over(h))):
        (r, c), (s, d) = lower, upper
        forth = stored(own, r, 2 * h + c - r, drop_ref[r])
        back = stored(own, s, d - s, drop_ref[s])
        to_mate[block(f, i, 0)] = jnp.where(odd, back, forth)
        to_cross[block(f, i, 0)] = jnp.where(odd, forth, back)
    for i, (r, c) in enumerate(full(h)):
        value = stored(own, r, c - r + h, drop_ref[r])
        corner[block(f, i, 0)] = value
        corner_again[block(f, i, 0)] = value
        to_mate[block(f, n + i, 0)] = value


def forward_kernel(f, drop_ref, cross, *refs):
    h = f.h
    odd = odd_place(f, drop_ref)
    to_mate, to_far = refs[-5:-3], refs[-3]
    for i, (lower, upper) in enumerate(zip(under(h), over(h))):
        (r, c), (s, d) = lower, upper
        forth = stored(cross, r, 2 * h + c - r, jnp.where(odd, drop_ref[2 * h + r], drop_ref[r]))
        back = stored(cross, s, d - s, jnp.where(odd, drop_ref[2 * h + s], drop_ref[s]))
        part, place = i % 2, i // 2
        to_mate[part][block(f, place, 0)] = jnp.where(odd, back, forth)
        to_far[block(f, i, 0)] = jnp.where(odd, forth, back)


def square_kernel(f, drop_ref, own, cross, mate, square, shifted, reach, here, partial, wide):
    h, p = f.h, f.p
    below, above = sides(f, drop_ref, plain(mate), plain(cross))
    for g, read in enumerate((below, plain(own), above)):
        for r in range(h):
            row = g * h + r
            first = 2 * (row // 2) - h
            for col in range(first, first + 2 * h + 2):
                offset = col - row + h
                if 0 <= offset <= f.k:
                    value = stored(read, r, offset, drop_ref[row], f.k)
                else:
                    value = jnp.zeros((f.b, f.b), wide.dtype)
                wide[block(f, row, col + h)] = value
    for i in range(h):
        for g, row in enumerate((i, 2 * h + i)):
            rows = pl.ds((g * h + i) * f.b, f.b)
            source = pl.ds(row * f.b, f.b)
            reach[rows, :] = wide[source, pl.ds(4 * g * f.group, f.group)]
            here[rows, :] = wide[source, pl.ds((2 * g + 1) * f.group, f.group)]
    unit = unit_tile(f)
    for row, col in f.tiles(range(f.pairs)):
        lo, hi = f.clipped(row, col)
        total = dot(
            wide[at(f, row, row + 1, lo + p, hi + p)], wide[at(f, lo, hi, col + p, col + p + 1)]
        )
        if f.on_corner(row, col):
            partial[at(f, *f.corner_place(row, col))] = total
            continue
        total = masked(f, total, row, col, drop_ref)
        place = banded(f, row, col, col + 1)
        tile = wide[at(f, row, row + 1, col + p, col + p + 1)].astype(jnp.float32)
        square[place] = total.astype(square.dtype)
        shifted[place] = moved(total, tile, unit if row == col else None).astype(shifted.dtype)


def unit_tile(f):
    rows = lax.broadcasted_iota(jnp.int32, (f.t, f.t), 0)
    return (rows == lax.broadcasted_iota(jnp.int32, (f.t, f.t), 1)).astype(jnp.float32)


def moved(total, tile, unit):
    value = 2.0 * total - 2.0 * tile
    return value if unit is None else value + unit


def corners_kernel(
    f, drop_ref, far_far, far_mate, far_mate_too, reach, here, partial, square, shifted, low, high
):
    p = f.p
    far_mates = [indexed(f, far_mate), indexed(f, far_mate_too)]
    far_below, far_above = sides(f, drop_ref, lambda i: far_mates[i % 2](i // 2), indexed(f, far_far))
    spread(f, low, 0, 0, far_below, under(f.h))
    spread(f, high, 0, 0, far_above, over(f.h))
    unit = unit_tile(f)
    for row, col in f.tiles(range(f.pairs)):
        if not f.on_corner(row, col):
            continue
        place = at(f, *f.corner_place(row, col))
        r, _, c, _ = f.corner_place(row, col)
        total = partial[place]
        if row < p:
            a, z, far = max(row, col), p, low
        else:
            a, z, far = 0, min(row, col) - 2 * p + 1, high
        if a < z:
            total = total + dot(reach[at(f, r, r + 1, a, z)], far[at(f, a, z, c, c + 1)])
        total = masked(f, total, row, col, drop_ref)
        tile = here[place].astype(jnp.float32)
        square[place] = total.astype(square.dtype)
        shifted[place] = moved(total, tile, unit if row == col else None).astype(shifted.dtype)


def right_tile(f, left, corners, right, row, col):
    lo, hi = f.clipped(row, col)
    total = None
    if row < f.p:
        inside = corners[at(f, row, row + 1, lo, f.p)]
        total = dot(inside, right[at(f, lo, f.p, col - f.p, col - f.p + 1)])
        lo = f.p
    elif row >= 2 * f.p:
        inside = corners[at(f, row - f.p, row - f.p + 1, 0, hi - 2 * f.p)]
        total = dot(inside, right[at(f, 2 * f.p, hi, col - f.p, col - f.p + 1)])
        hi = 2 * f.p
    rest = dot(left[banded(f, row, lo, hi)], right[at(f, lo, hi, col - f.p, col - f.p + 1)])
    return rest if total is None else total + rest


def first_sweep_kernel(
    f, drop_ref, shifted, corners, corner, sent_mate, sent_cross, mate, cross,
    correction, fresh, partial, whole, before, after,
):
    h, p = f.h, f.p
    from_below, from_above = sides(f, drop_ref, indexed(f, mate), indexed(f, cross))
    down, up = sides(f, drop_ref, indexed(f, sent_mate), indexed(f, sent_cross))
    spread(f, whole, 0, 0, from_below, under(h))
    spread(f, whole, h, 0, indexed(f, corner), full(h))
    spread(f, whole, 2 * h, 0, from_above, over(h))
    spread(f, before, 0, 0, down, over(h))
    spread(f, after, 0, 0, up, under(h))
    for row, col in f.tiles(f.own_pairs):
        total = masked(f, right_tile(f, shifted, corners, whole, row, col), row, col, drop_ref)
        correction[at(f, row, row + 1, col - p, col - p + 1)] = total.astype(correction.dtype)
    for row, col in f.tiles(f.own_pairs):
        c = col - p
        own_row = row in f.own_pairs
        total = 2.0 * whole[at(f, row, row + 1, c, c + 1)].astype(jnp.float32)
        for g, a, z in f.split(row, col):
            if g == 1:
                left = whole[at(f, row, row + 1, a, z)]
            elif own_row:
                left = (before, None, after)[g][at(f, row - p, row - p + 1, a, z)]
            else:
                continue
            total = total - dot(left, correction[at(f, g * p + a, g * p + z, c, c + 1)])
        if own_row:
            total = masked(f, total, row, col, drop_ref)
            fresh[at(f, row - p, row - p + 1, c, c + 1)] = total.astype(fresh.dtype)
        else:
            place = row if row < p else row - p
            partial[at(f, place, place + 1, c, c + 1)] = total


def edges(f, drop_ref, corner_below, corner_above, correction, start, low, high):
    p = f.p
    for row, col in f.tiles(f.own_pairs):
        if row in f.own_pairs:
            continue
        c = col - p
        side = 0 if row < p else 2
        corner, dest = ((corner_below, low), None, (corner_above, high))[side]
        local = row - side * p
        total = start(row, col)
        for g, a, z in f.split(row, col):
            if g == side:
                total = total - dot(
                    corner(at(f, local, local + 1, a, z)), correction[at(f, g * p + a, g * p + z, c, c + 1)]
                )
        total = masked(f, total, row, col, drop_ref)
        dest[at(f, local, local + 1, c, c + 1)] = total.astype(dest.dtype)


def first_edges_kernel(
    f, drop_ref, mate, cross, correction, partial, low, high, to_cross, to_mate, before, after
):
    p = f.p
    below, above = sides(f, drop_ref, indexed(f, mate, len(under(f.h))), indexed(f, cross))
    spread(f, before, 0, 0, below, full(f.h))
    spread(f, after, 0, 0, above, full(f.h))

    def start(row, col):
        place = row if row < p else row - p
        return partial[at(f, place, place + 1, col - p, col - p + 1)]

    edges(f, drop_ref, plain(before), plain(after), correction, start, low, high)
    pack_edges(f, drop_ref, low, high, to_cross, to_mate)


def gather(f, whole, low, own, high):
    for g, source in enumerate((low, own, high)):
        for i in range(f.h):
            whole[pl.ds(g * f.group + i * f.b, f.b), :] = source[pl.ds(i * f.b, f.b), :]


def correction_kernel(f, drop_ref, shifted, corners, low, own, high, correction, whole):
    p = f.p
    gather(f, whole, low, own, high)
    for row, col in f.tiles(f.own_pairs):
        total = masked(f, right_tile(f, shifted, corners, whole, row, col), row, col, drop_ref)
        correction[at(f, row, row + 1, col - p, col - p + 1)] = total.astype(correction.dtype)


def second_edges_kernel(
    f, drop_ref, cross, mate, correction, low, high, new_low, new_high, to_cross, to_mate
):
    p = f.p

    def start(row, col):
        c = col - p
        source, local = (low, row) if row < p else (high, row - 2 * p)
        total = 2.0 * source[at(f, local, local + 1, c, c + 1)].astype(jnp.float32)
        for g, a, z in f.split(row, col):
            if g == 1:
                total = total - dot(
                    source[at(f, local, local + 1, a, z)], correction[at(f, p + a, p + z, c, c + 1)]
                )
        return total

    below, above = sides(f, drop_ref, plain(mate), plain(cross))
    edges(f, drop_ref, below, above, correction, start, new_low, new_high)
    pack_edges(f, drop_ref, new_low, new_high, to_cross, to_mate)


def density_edges_kernel(
    f, drop_ref, own, mate, cross, correction, new_low, new_high, square, corners, whole, to_cross, to_mate,
    to_mate_too, before, after, low, high,
):
    h, p = f.h, f.p
    below, above = sides(f, drop_ref, indexed(f, mate), indexed(f, cross))
    spread(f, before, 0, 0, below, over(h))
    spread(f, after, 0, 0, above, under(h))
    for row, col in f.tiles(f.own_pairs):
        if row not in f.own_pairs:
            continue
        c, local = col - p, row - p
        total = 2.0 * own[at(f, local, local + 1, c, c + 1)].astype(jnp.float32)
        for g, a, z in f.split(row, col):
            left = (before, own, after)[g][at(f, local, local + 1, a, z)]
            total = total - dot(left, correction[at(f, g * p + a, g * p + z, c, c + 1)])
        total = masked(f, total, row, col, drop_ref)
        whole[at(f, row, row + 1, c, c + 1)] = total.astype(whole.dtype)
    for i in range(h):
        rows = pl.ds(i * f.b, f.b)
        whole[pl.ds(i * f.b, f.b), :] = new_low[rows, :]
        whole[pl.ds(2 * f.group + i * f.b, f.b), :] = new_high[rows, :]
    for row, col in f.tiles(f.own_pairs):
        if row in f.own_pairs:
            continue
        total = masked(f, right_tile(f, square, corners, whole, row, col), row, col, drop_ref)
        dest, local = (low, row) if row < p else (high, row - 2 * p)
        dest[at(f, local, local + 1, col - p, col - p + 1)] = total.astype(dest.dtype)
    pack_edges(f, drop_ref, low, high, to_cross, to_mate, to_mate_too)


def density_own_kernel(f, drop_ref, square, whole, out):
    p = f.p
    for row, col in f.tiles(f.own_pairs):
        if row in f.own_pairs:
            total = masked(f, right_tile(f, square, None, whole, row, col), row, col, drop_ref)
            out[at(f, row - p, row - p + 1, col - p, col - p + 1)] = total.astype(out.dtype)


def slots_kernel(f, first, parts, drop_ref, own, *refs):
    h = f.h
    mates = [indexed(f, ref) for ref in refs[:parts]]
    slots, out, sem = refs[parts:]
    over_index = {place: i for i, place in enumerate(over(h))}
    under_index = {place: i for i, place in enumerate(under(h))}

    def mate_block(i):
        return mates[i % parts](i // parts)

    for r in range(h):
        dropped = drop_ref[h + r]

        def at_offset(offset, r=r):
            col = r + offset
            if col < h:
                return mate_block(over_index[r, col])
            if col < 2 * h:
                return own[block(f, first + r, col - h)]
            return mate_block(under_index[r, col - 2 * h])

        for s in range(f.k):
            slots[r, s] = jnp.where(dropped <= s, at_offset(s + 1), at_offset(s))
    copy = pltpu.make_async_copy(slots, out, sem)
    copy.start()
    copy.wait()


def last_slots_kernel(f, drop_ref, slots, cross, unused, out, side, sems):
    h, k = f.h, f.k
    odd = odd_place(f, drop_ref)
    cross_block = indexed(f, cross)
    over_index = {place: i for i, place in enumerate(over(h))}
    under_index = {place: i for i, place in enumerate(under(h))}

    def fill(low):
        copies = []
        for r in range(h):
            dropped = drop_ref[h + r]
            lo, hi = (0, h - r) if low else (k - 1 - r, k)
            for s in range(lo, hi):

                def at_offset(offset, r=r, s=s):
                    col = r + offset
                    if low and col < h:
                        return cross_block(over_index[r, col])
                    if not low and col >= 2 * h:
                        return cross_block(under_index[r, col - 2 * h])
                    return slots[r, s]

                side[r, s] = jnp.where(dropped <= s, at_offset(s + 1), at_offset(s))
            copy = pltpu.make_async_copy(
                side.at[r, pl.ds(lo, hi - lo)], out.at[r, pl.ds(lo, hi - lo)], sems.at[r]
            )
            copy.start()
            copies.append(copy)
        for copy in copies:
            copy.wait()

    @pl.when(odd)
    def _():
        fill(False)

    @pl.when(jnp.logical_not(odd))
    def _():
        fill(True)


VMEM = pl.BlockSpec(memory_space=pltpu.VMEM)
SMEM = pl.BlockSpec(memory_space=pltpu.SMEM)
ANY = pl.BlockSpec(memory_space=pl.ANY)


def call(kernel, outs, scratch, flops, limit, drop, *args, passed=(), light=False, off=0):
    moved = sum(a.size * a.dtype.itemsize for a in args) + sum(s.size * s.dtype.itemsize for s in outs)
    if light:
        flops = moved = 0
    n = len(args)
    return pl.pallas_call(
        kernel,
        out_shape=[*outs, *[jax.ShapeDtypeStruct(a.shape, a.dtype) for a in passed]],
        in_specs=[SMEM] + [VMEM] * n + [ANY] * len(passed),
        out_specs=[VMEM] * (len(outs) - off) + [ANY] * (off + len(passed)),
        scratch_shapes=scratch,
        input_output_aliases={1 + n + i: len(outs) + i for i in range(len(passed))},
        compiler_params=pltpu.CompilerParams(vmem_limit_bytes=limit * MIB),
        cost_estimate=pl.CostEstimate(flops=flops, bytes_accessed=moved, transcendentals=0),
    )(drop, *args, *passed)


def routed(x, step):
    size = lax.axis_size(RING)
    return lax.ppermute(x, RING, [(i, (i + step(i)) % size) for i in range(size) if step(i)])


def on_device(density, inverse_start, block_cols):
    rows, width, order, _ = density.shape
    half = width // 2
    ring = lax.axis_size(RING)
    total = rows * ring
    assert rows == half and half % 2 == 0 and ring % 2 == 0
    f = Frame(half, order)
    kind = density.dtype
    me = lax.axis_index(RING)

    def mate_step(i):
        return 1 - 2 * (i % 2)

    def cross_step(i):
        return 2 * (i % 2) - 1

    def to_mate(x):
        return routed(x, mate_step)

    def to_cross(x):
        return routed(x, cross_step)

    positions = block_cols - (me * rows + jnp.arange(rows, dtype=jnp.int32))[:, None] + half
    positions = positions + jnp.where(positions < 0, total, jnp.where(positions >= total, -total, 0))
    own_drop = width * (width + 1) // 2 - jnp.sum(positions, axis=1)

    density_cross, density_mate = to_cross(density), to_mate(density)
    cross_drop, mate_drop = to_cross(own_drop), to_mate(own_drop)
    even = (me & 1) == 0
    mark = jnp.reshape(me & 1, (1,))
    start_drop = jnp.concatenate([own_drop, mark])
    drop = jnp.concatenate(
        [jnp.where(even, cross_drop, mate_drop), own_drop, jnp.where(even, mate_drop, cross_drop), mark]
    )

    unit = 2 * f.t**3
    count = half * (half + 1) // 2
    square_group = jax.ShapeDtypeStruct((f.group, f.group), kind)
    columns = jax.ShapeDtypeStruct((3 * f.group, f.group), kind)
    band = jax.ShapeDtypeStruct((3 * f.group, (2 * f.p + 1) * f.t), kind)
    triangle = jax.ShapeDtypeStruct((count * order, order), kind)
    half_triangle = jax.ShapeDtypeStruct((count // 2 * order, order), kind)
    listed = jax.ShapeDtypeStruct((half * half * order, order), kind)
    both = jax.ShapeDtypeStruct(((count + half * half) * order, order), kind)
    partial_sums = jax.ShapeDtypeStruct((2 * f.group, f.group), jnp.float32)
    group_scratch = pltpu.VMEM((f.group, f.group), kind)
    whole_scratch = pltpu.VMEM((3 * f.group, f.group), kind)

    def run(kernel, outs, scratch, tiles, limit, *args, **kw):
        return call(functools.partial(kernel, f), outs, scratch, tiles * unit, limit, *args, **kw)

    corner, corner_cross, slab_mate, triangle_cross = run(
        slabs_kernel, [listed, listed, both, triangle], [], 0, 12, start_drop, inverse_start
    )
    from_mate = to_mate(slab_mate)
    forward_mate, forward_mate_too, forward_far, triangle_cross, corner_cross = run(
        forward_kernel, [half_triangle, half_triangle, triangle], [], 0, 12, drop, density_cross, density_mate, from_mate,
        passed=(triangle_cross, corner_cross),
    )
    far_mate, far_mate_too = to_mate(forward_mate), to_mate(forward_mate_too)
    far_far = routed(forward_far, lambda i: 3 * cross_step(i))
    cross_triangle = to_cross(triangle_cross)
    cross_corner = to_cross(corner_cross)

    both_corners = jax.ShapeDtypeStruct((2 * f.group, f.group), kind)
    square, shifted, reach, here, partial = run(
        square_kernel,
        [band, band, both_corners, both_corners, partial_sums],
        [pltpu.VMEM((3 * f.group, 5 * f.group), kind)],
        84, 26, drop, density, density_cross, density_mate,
    )
    square_corners, shifted_corners = run(
        corners_kernel,
        [both_corners, both_corners],
        [group_scratch] * 2,
        10, 16, drop, far_far, far_mate, far_mate_too, reach, here, partial, light=True,
    )
    correction, own, partial = run(
        first_sweep_kernel,
        [columns, square_group, partial_sums],
        [whole_scratch, group_scratch, group_scratch],
        66, 24, drop, shifted, shifted_corners, corner, slab_mate, triangle_cross, from_mate, cross_triangle, light=True,
    )
    corner_cross, corner_mate = to_cross(own), to_mate(own)
    low, high, edge_cross, edge_mate = run(
        first_edges_kernel,
        [square_group, square_group, triangle, triangle],
        [group_scratch] * 2,
        10, 16, drop, from_mate, cross_corner, correction, partial,
    )
    edge_cross, edge_mate = to_cross(edge_cross), to_mate(edge_mate)
    (correction,) = run(
        correction_kernel, [columns], [whole_scratch], 38, 16, drop, shifted, shifted_corners, low, own, high
    )
    new_low, new_high, inverse_cross, inverse_mate = run(
        second_edges_kernel,
        [square_group, square_group, triangle, triangle],
        [],
        20, 12, drop, corner_cross, corner_mate, correction, low, high,
    )
    inverse_cross, inverse_mate = to_cross(inverse_cross), to_mate(inverse_mate)
    whole, rim_cross, rim_mate, rim_mate_too = run(
        density_edges_kernel,
        [columns, triangle, half_triangle, half_triangle],
        [group_scratch] * 4,
        38, 20, drop, own, edge_mate, edge_cross, correction, new_low, new_high, square,
        square_corners,
    )
    rim_cross, rim_mates = to_cross(rim_cross), [to_mate(rim_mate), to_mate(rim_mate_too)]
    (density_own,) = run(density_own_kernel, [square_group], [], 18, 12, drop, square, whole)
    out = jax.ShapeDtypeStruct(density.shape, kind)

    def assembled(own, first, cross, mates):
        kernel = functools.partial(slots_kernel, f, first, len(mates))
        scratch = [pltpu.SemaphoreType.DMA(())]
        slots, early = call(kernel, [out, out], scratch, 0, 8, drop, own, *mates, light=True, off=1)
        scratch = [pltpu.VMEM(out.shape, kind), pltpu.SemaphoreType.DMA((half,))]
        kernel = functools.partial(last_slots_kernel, f)
        return call(kernel, [], scratch, 0, 8, drop, slots, cross, passed=(early,), light=True)[0]

    inverse_next = assembled(whole, half, inverse_cross, [inverse_mate])
    density_next = assembled(density_own, 0, rim_cross, rim_mates)
    return density_next, inverse_next


def solution(mesh):
    blocks = P(("grp", "row", "inner"), None, None, None)
    return jax.shard_map(
        on_device,
        mesh=mesh,
        in_specs=(blocks, blocks, P(("grp", "row", "inner"), None)),
        out_specs=(blocks, blocks),
        check_vma=False,
    )
```

```python
import functools

import jax
import jax.numpy as jnp
from jax import lax
from jax.experimental import pallas as pl
from jax.experimental.pallas import tpu as pltpu
from jax.sharding import PartitionSpec as P

RING = ("row", "inner")
MIB = 1024 * 1024


class Frame:
    def __init__(self, half, order):
        self.h = half
        self.b = order
        self.k = 2 * half
        self.p = half // 2
        self.t = 2 * order
        self.group = half * order
        self.pairs = 3 * self.p
        self.own_pairs = range(self.p, 2 * self.p)
        self.edge_rows = [*range(self.p), *range(2 * self.p, 3 * self.p)]

    def tiles(self, columns):
        for col in columns:
            for row in range(max(0, col - self.p), min(self.pairs, col + self.p + 1)):
                yield row, col

    def inner(self, row, col):
        return max(row, col) - self.p, min(row, col) + self.p + 1

    def clipped(self, row, col):
        lo, hi = self.inner(row, col)
        return max(lo, 0), min(hi, self.pairs)

    def on_corner(self, row, col):
        return max(row, col) < self.p or min(row, col) >= 2 * self.p

    def corner_place(self, row, col):
        r, c = (row, col) if row < self.p else (row - self.p, col - 2 * self.p)
        return r, r + 1, c, c + 1

    def split(self, row, col):
        lo, hi = self.clipped(row, col)
        for g in range(3):
            a, z = max(lo, g * self.p), min(hi, (g + 1) * self.p)
            if a < z:
                yield g, a - g * self.p, z - g * self.p


def under(h):
    return [(r, c) for r in range(h) for c in range(r + 1)]


def over(h):
    return [(r, c) for r in range(h) for c in range(r, h)]


def full(h):
    return [(r, c) for r in range(h) for c in range(h)]


def at(f, row_lo, row_hi, col_lo, col_hi):
    t = f.t
    return pl.ds(row_lo * t, (row_hi - row_lo) * t), pl.ds(col_lo * t, (col_hi - col_lo) * t)


def block(f, r, c):
    return pl.ds(r * f.b, f.b), pl.ds(c * f.b, f.b)


def banded(f, row, lo, hi):
    return at(f, row, row + 1, lo - row + f.p, hi - row + f.p)


def dot(a, b):
    return jnp.dot(a, b, preferred_element_type=jnp.float32)


def stored(rows, r, offset, dropped, slots=None):
    last = (rows.shape[1] if slots is None else slots) - 1
    slot = jnp.minimum(offset - (offset > dropped).astype(jnp.int32), last)
    value = rows[r, slot] if slots is None else rows((r, slot))
    return jnp.where(offset == dropped, jnp.zeros_like(value), value)


def masked(f, tile, row, col, drop_ref):
    b = f.b
    parts = []
    for i in range(2):
        r = 2 * row + i
        line = []
        for j in range(2):
            offset = 2 * col + j - r + f.h
            piece = tile[i * b : (i + 1) * b, j * b : (j + 1) * b]
            if 0 <= offset <= f.k:
                piece = jnp.where(drop_ref[r] == offset, 0.0, piece)
            else:
                piece = jnp.zeros_like(piece)
            line.append(piece)
        parts.append(jnp.concatenate(line, axis=1))
    return jnp.concatenate(parts, axis=0)


def odd_place(f, drop_ref):
    return drop_ref[3 * f.h] == 1


def indexed(f, ref, first=0):
    return lambda i: ref[block(f, first + i, 0)]


def plain(ref):
    return lambda place: ref[place]


def sides(f, drop_ref, mate, cross):
    odd = odd_place(f, drop_ref)

    def below(key):
        return jnp.where(odd, mate(key), cross(key))

    def above(key):
        return jnp.where(odd, cross(key), mate(key))

    return below, above


def spread(f, dest, row, col, read, places):
    index = {place: i for i, place in enumerate(places)}
    for r in range(f.h):
        for c in range(f.h):
            i = index.get((r, c))
            dest[block(f, row + r, col + c)] = jnp.zeros((f.b, f.b), dest.dtype) if i is None else read(i)


def pack_edges(f, drop_ref, low, high, to_cross, *to_mate):
    odd = odd_place(f, drop_ref)
    parts = len(to_mate)
    for i, (lower, upper) in enumerate(zip(under(f.h), over(f.h))):
        back, forth = low[block(f, *lower)], high[block(f, *upper)]
        to_cross[block(f, i, 0)] = jnp.where(odd, forth, back)
        to_mate[i % parts][block(f, i // parts, 0)] = jnp.where(odd, back, forth)


def slabs_kernel(f, drop_ref, own, corner, corner_again, to_mate, to_cross, to_cross_again):
    h = f.h
    odd = drop_ref[h] == 1
    n = len(under(h))
    for i, (lower, upper) in enumerate(zip(under(h), over(h))):
        (r, c), (s, d) = lower, upper
        forth = stored(own, r, 2 * h + c - r, drop_ref[r])
        back = stored(own, s, d - s, drop_ref[s])
        to_mate[block(f, i, 0)] = jnp.where(odd, back, forth)
        across = jnp.where(odd, forth, back)
        to_cross[block(f, i, 0)] = across
        to_cross_again[block(f, i, 0)] = across
    for i, (r, c) in enumerate(full(h)):
        value = stored(own, r, c - r + h, drop_ref[r])
        corner[block(f, i, 0)] = value
        corner_again[block(f, i, 0)] = value
        to_mate[block(f, n + i, 0)] = value


def forward_kernel(f, drop_ref, cross, *refs):
    h = f.h
    odd = odd_place(f, drop_ref)
    to_mate, to_far = refs[-4:-2]
    for i, (lower, upper) in enumerate(zip(under(h), over(h))):
        (r, c), (s, d) = lower, upper
        forth = stored(cross, r, 2 * h + c - r, jnp.where(odd, drop_ref[2 * h + r], drop_ref[r]))
        back = stored(cross, s, d - s, jnp.where(odd, drop_ref[2 * h + s], drop_ref[s]))
        to_mate[block(f, i, 0)] = jnp.where(odd, back, forth)
        to_far[block(f, i, 0)] = jnp.where(odd, forth, back)


def square_kernel(f, drop_ref, own, cross, mate, square, shifted, reach, here, partial, wide):
    h, p = f.h, f.p
    below, above = sides(f, drop_ref, plain(mate), plain(cross))
    for g, read in enumerate((below, plain(own), above)):
        for r in range(h):
            row = g * h + r
            first = 2 * (row // 2) - h
            for col in range(first, first + 2 * h + 2):
                offset = col - row + h
                if 0 <= offset <= f.k:
                    value = stored(read, r, offset, drop_ref[row], f.k)
                else:
                    value = jnp.zeros((f.b, f.b), wide.dtype)
                wide[block(f, row, col + h)] = value
    for i in range(h):
        for g, row in enumerate((i, 2 * h + i)):
            rows = pl.ds((g * h + i) * f.b, f.b)
            source = pl.ds(row * f.b, f.b)
            reach[rows, :] = wide[source, pl.ds(4 * g * f.group, f.group)]
            here[rows, :] = wide[source, pl.ds((2 * g + 1) * f.group, f.group)]
    unit = unit_tile(f)
    for row, col in f.tiles(range(f.pairs)):
        lo, hi = f.clipped(row, col)
        total = dot(
            wide[at(f, row, row + 1, lo + p, hi + p)], wide[at(f, lo, hi, col + p, col + p + 1)]
        )
        if f.on_corner(row, col):
            partial[at(f, *f.corner_place(row, col))] = total
            continue
        total = masked(f, total, row, col, drop_ref)
        place = banded(f, row, col, col + 1)
        tile = wide[at(f, row, row + 1, col + p, col + p + 1)].astype(jnp.float32)
        square[place] = total.astype(square.dtype)
        shifted[place] = moved(total, tile, unit if row == col else None).astype(shifted.dtype)


def unit_tile(f):
    rows = lax.broadcasted_iota(jnp.int32, (f.t, f.t), 0)
    return (rows == lax.broadcasted_iota(jnp.int32, (f.t, f.t), 1)).astype(jnp.float32)


def moved(total, tile, unit):
    value = 2.0 * total - 2.0 * tile
    return value if unit is None else value + unit


def corners_kernel(
    f, drop_ref, far_far, far_mate, reach, here, partial, unused, square, shifted, low, high
):
    p = f.p
    far_below, far_above = sides(f, drop_ref, indexed(f, far_mate), indexed(f, far_far))
    spread(f, low, 0, 0, far_below, under(f.h))
    spread(f, high, 0, 0, far_above, over(f.h))
    unit = unit_tile(f)
    for row, col in f.tiles(range(f.pairs)):
        if not f.on_corner(row, col):
            continue
        place = at(f, *f.corner_place(row, col))
        r, _, c, _ = f.corner_place(row, col)
        total = partial[place]
        if row < p:
            a, z, far = max(row, col), p, low
        else:
            a, z, far = 0, min(row, col) - 2 * p + 1, high
        if a < z:
            total = total + dot(reach[at(f, r, r + 1, a, z)], far[at(f, a, z, c, c + 1)])
        total = masked(f, total, row, col, drop_ref)
        tile = here[place].astype(jnp.float32)
        square[place] = total.astype(square.dtype)
        shifted[place] = moved(total, tile, unit if row == col else None).astype(shifted.dtype)


def right_tile(f, left, corners, right, row, col):
    lo, hi = f.clipped(row, col)
    total = None
    if row < f.p:
        inside = corners[at(f, row, row + 1, lo, f.p)]
        total = dot(inside, right[at(f, lo, f.p, col - f.p, col - f.p + 1)])
        lo = f.p
    elif row >= 2 * f.p:
        inside = corners[at(f, row - f.p, row - f.p + 1, 0, hi - 2 * f.p)]
        total = dot(inside, right[at(f, 2 * f.p, hi, col - f.p, col - f.p + 1)])
        hi = 2 * f.p
    rest = dot(left[banded(f, row, lo, hi)], right[at(f, lo, hi, col - f.p, col - f.p + 1)])
    return rest if total is None else total + rest


def first_sweep_kernel(
    f, drop_ref, shifted, corners, corner, sent_mate, sent_cross, mate, direct, turned,
    correction, fresh, partial, whole, before, after,
):
    h, p = f.h, f.p
    turning = drop_ref[3 * h + 1] == 1
    direct_block, turned_block = indexed(f, direct), indexed(f, turned)

    def cross(i):
        return jnp.where(turning, turned_block(i), direct_block(i))

    from_below, from_above = sides(f, drop_ref, indexed(f, mate), cross)
    down, up = sides(f, drop_ref, indexed(f, sent_mate), indexed(f, sent_cross))
    spread(f, whole, 0, 0, from_below, under(h))
    spread(f, whole, h, 0, indexed(f, corner), full(h))
    spread(f, whole, 2 * h, 0, from_above, over(h))
    spread(f, before, 0, 0, down, over(h))
    spread(f, after, 0, 0, up, under(h))
    for row, col in f.tiles(f.own_pairs):
        total = masked(f, right_tile(f, shifted, corners, whole, row, col), row, col, drop_ref)
        correction[at(f, row, row + 1, col - p, col - p + 1)] = total.astype(correction.dtype)
    for row, col in f.tiles(f.own_pairs):
        c = col - p
        own_row = row in f.own_pairs
        total = 2.0 * whole[at(f, row, row + 1, c, c + 1)].astype(jnp.float32)
        for g, a, z in f.split(row, col):
            if g == 1:
                left = whole[at(f, row, row + 1, a, z)]
            elif own_row:
                left = (before, None, after)[g][at(f, row - p, row - p + 1, a, z)]
            else:
                continue
            total = total - dot(left, correction[at(f, g * p + a, g * p + z, c, c + 1)])
        if own_row:
            total = masked(f, total, row, col, drop_ref)
            fresh[at(f, row - p, row - p + 1, c, c + 1)] = total.astype(fresh.dtype)
        else:
            place = row if row < p else row - p
            partial[at(f, place, place + 1, c, c + 1)] = total


def edges(f, drop_ref, corner_below, corner_above, correction, start, low, high):
    p = f.p
    for row, col in f.tiles(f.own_pairs):
        if row in f.own_pairs:
            continue
        c = col - p
        side = 0 if row < p else 2
        corner, dest = ((corner_below, low), None, (corner_above, high))[side]
        local = row - side * p
        total = start(row, col)
        for g, a, z in f.split(row, col):
            if g == side:
                total = total - dot(
                    corner(at(f, local, local + 1, a, z)), correction[at(f, g * p + a, g * p + z, c, c + 1)]
                )
        total = masked(f, total, row, col, drop_ref)
        dest[at(f, local, local + 1, c, c + 1)] = total.astype(dest.dtype)


def first_edges_kernel(
    f, drop_ref, mate, cross, correction, partial, low, high, to_cross, to_mate, before, after
):
    p = f.p
    below, above = sides(f, drop_ref, indexed(f, mate, len(under(f.h))), indexed(f, cross))
    spread(f, before, 0, 0, below, full(f.h))
    spread(f, after, 0, 0, above, full(f.h))

    def start(row, col):
        place = row if row < p else row - p
        return partial[at(f, place, place + 1, col - p, col - p + 1)]

    edges(f, drop_ref, plain(before), plain(after), correction, start, low, high)
    pack_edges(f, drop_ref, low, high, to_cross, to_mate)


def gather(f, whole, low, own, high):
    for g, source in enumerate((low, own, high)):
        for i in range(f.h):
            whole[pl.ds(g * f.group + i * f.b, f.b), :] = source[pl.ds(i * f.b, f.b), :]


def correction_kernel(f, drop_ref, shifted, corners, low, own, high, correction, whole):
    p = f.p
    gather(f, whole, low, own, high)
    for row, col in f.tiles(f.own_pairs):
        total = masked(f, right_tile(f, shifted, corners, whole, row, col), row, col, drop_ref)
        correction[at(f, row, row + 1, col - p, col - p + 1)] = total.astype(correction.dtype)


def second_edges_kernel(
    f, drop_ref, mate, cross, correction, low, high, new_low, new_high, to_cross, to_mate
):
    p = f.p

    def start(row, col):
        c = col - p
        source, local = (low, row) if row < p else (high, row - 2 * p)
        total = 2.0 * source[at(f, local, local + 1, c, c + 1)].astype(jnp.float32)
        for g, a, z in f.split(row, col):
            if g == 1:
                total = total - dot(
                    source[at(f, local, local + 1, a, z)], correction[at(f, p + a, p + z, c, c + 1)]
                )
        return total

    below, above = sides(f, drop_ref, plain(mate), plain(cross))
    edges(f, drop_ref, below, above, correction, start, new_low, new_high)
    pack_edges(f, drop_ref, new_low, new_high, to_cross, to_mate)


def density_edges_kernel(
    f, drop_ref, own, mate, cross, correction, new_low, new_high, square, corners, whole, to_cross, to_mate,
    to_mate_too, before, after, low, high,
):
    h, p = f.h, f.p
    below, above = sides(f, drop_ref, indexed(f, mate), indexed(f, cross))
    spread(f, before, 0, 0, below, over(h))
    spread(f, after, 0, 0, above, under(h))
    for row, col in f.tiles(f.own_pairs):
        if row not in f.own_pairs:
            continue
        c, local = col - p, row - p
        total = 2.0 * own[at(f, local, local + 1, c, c + 1)].astype(jnp.float32)
        for g, a, z in f.split(row, col):
            left = (before, own, after)[g][at(f, local, local + 1, a, z)]
            total = total - dot(left, correction[at(f, g * p + a, g * p + z, c, c + 1)])
        total = masked(f, total, row, col, drop_ref)
        whole[at(f, row, row + 1, c, c + 1)] = total.astype(whole.dtype)
    for i in range(h):
        rows = pl.ds(i * f.b, f.b)
        whole[pl.ds(i * f.b, f.b), :] = new_low[rows, :]
        whole[pl.ds(2 * f.group + i * f.b, f.b), :] = new_high[rows, :]
    for row, col in f.tiles(f.own_pairs):
        if row in f.own_pairs:
            continue
        total = masked(f, right_tile(f, square, corners, whole, row, col), row, col, drop_ref)
        dest, local = (low, row) if row < p else (high, row - 2 * p)
        dest[at(f, local, local + 1, col - p, col - p + 1)] = total.astype(dest.dtype)
    pack_edges(f, drop_ref, low, high, to_cross, to_mate, to_mate_too)


def density_own_kernel(f, drop_ref, square, whole, out):
    p = f.p
    for row, col in f.tiles(f.own_pairs):
        if row in f.own_pairs:
            total = masked(f, right_tile(f, square, None, whole, row, col), row, col, drop_ref)
            out[at(f, row - p, row - p + 1, col - p, col - p + 1)] = total.astype(out.dtype)


def slots_kernel(f, first, parts, drop_ref, own, *refs):
    h = f.h
    mates = [indexed(f, ref) for ref in refs[:parts]]
    slots, out, sem = refs[parts:]
    over_index = {place: i for i, place in enumerate(over(h))}
    under_index = {place: i for i, place in enumerate(under(h))}

    def mate_block(i):
        return mates[i % parts](i // parts)

    for r in range(h):
        dropped = drop_ref[h + r]

        def at_offset(offset, r=r):
            col = r + offset
            if col < h:
                return mate_block(over_index[r, col])
            if col < 2 * h:
                return own[block(f, first + r, col - h)]
            return mate_block(under_index[r, col - 2 * h])

        for s in range(f.k):
            slots[r, s] = jnp.where(dropped <= s, at_offset(s + 1), at_offset(s))
    copy = pltpu.make_async_copy(slots, out, sem)
    copy.start()
    copy.wait()


def last_slots_kernel(f, drop_ref, slots, cross, unused, out, side, sems):
    h, k = f.h, f.k
    odd = odd_place(f, drop_ref)
    cross_block = indexed(f, cross)
    over_index = {place: i for i, place in enumerate(over(h))}
    under_index = {place: i for i, place in enumerate(under(h))}

    def fill(low):
        copies = []
        for r in range(h):
            dropped = drop_ref[h + r]
            lo, hi = (0, h - r) if low else (k - 1 - r, k)
            for s in range(lo, hi):

                def at_offset(offset, r=r, s=s):
                    col = r + offset
                    if low and col < h:
                        return cross_block(over_index[r, col])
                    if not low and col >= 2 * h:
                        return cross_block(under_index[r, col - 2 * h])
                    return slots[r, s]

                side[r, s] = jnp.where(dropped <= s, at_offset(s + 1), at_offset(s))
            copy = pltpu.make_async_copy(
                side.at[r, pl.ds(lo, hi - lo)], out.at[r, pl.ds(lo, hi - lo)], sems.at[r]
            )
            copy.start()
            copies.append(copy)
        for copy in copies:
            copy.wait()

    @pl.when(odd)
    def _():
        fill(False)

    @pl.when(jnp.logical_not(odd))
    def _():
        fill(True)


VMEM = pl.BlockSpec(memory_space=pltpu.VMEM)
SMEM = pl.BlockSpec(memory_space=pltpu.SMEM)
ANY = pl.BlockSpec(memory_space=pl.ANY)


def call(kernel, outs, scratch, flops, limit, drop, *args, passed=(), light=False, off=0):
    moved = sum(a.size * a.dtype.itemsize for a in args) + sum(s.size * s.dtype.itemsize for s in outs)
    if light:
        flops = moved = 0
    n = len(args)
    return pl.pallas_call(
        kernel,
        out_shape=[*outs, *[jax.ShapeDtypeStruct(a.shape, a.dtype) for a in passed]],
        in_specs=[SMEM] + [VMEM] * n + [ANY] * len(passed),
        out_specs=[VMEM] * (len(outs) - off) + [ANY] * (off + len(passed)),
        scratch_shapes=scratch,
        input_output_aliases={1 + n + i: len(outs) + i for i in range(len(passed))},
        compiler_params=pltpu.CompilerParams(vmem_limit_bytes=limit * MIB),
        cost_estimate=pl.CostEstimate(flops=flops, bytes_accessed=moved, transcendentals=0),
    )(drop, *args, *passed)


def routed(x, step):
    size = lax.axis_size(RING)
    return lax.ppermute(x, RING, [(i, (i + step(i)) % size) for i in range(size) if step(i)])


def on_device(density, inverse_start, block_cols):
    rows, width, order, _ = density.shape
    half = width // 2
    ring, inner = lax.axis_size(RING), lax.axis_size(RING[1])
    total = rows * ring
    assert rows == half and half % 2 == 0 and inner % 2 == 0
    f = Frame(half, order)
    kind = density.dtype
    me = lax.axis_index(RING)

    def mate_step(i):
        return 1 - 2 * (i % 2)

    def cross_step(i):
        return 2 * (i % 2) - 1

    def to_mate(x):
        return routed(x, mate_step)

    def to_cross(x):
        return routed(x, cross_step)

    def turns(i):
        return i % inner in (0, inner - 1)

    positions = block_cols - (me * rows + jnp.arange(rows, dtype=jnp.int32))[:, None] + half
    positions = positions + jnp.where(positions < 0, total, jnp.where(positions >= total, -total, 0))
    own_drop = width * (width + 1) // 2 - jnp.sum(positions, axis=1)

    density_cross, density_mate = to_cross(density), to_mate(density)
    cross_drop, mate_drop = to_cross(own_drop), to_mate(own_drop)
    even = (me & 1) == 0
    place = lax.axis_index(RING[1])
    marks = jnp.stack([me & 1, ((place == 0) | (place == inner - 1)).astype(jnp.int32)])
    start_drop = jnp.concatenate([own_drop, marks[:1]])
    drop = jnp.concatenate(
        [jnp.where(even, cross_drop, mate_drop), own_drop, jnp.where(even, mate_drop, cross_drop), marks]
    )

    unit = 2 * f.t**3
    count = half * (half + 1) // 2
    square_group = jax.ShapeDtypeStruct((f.group, f.group), kind)
    columns = jax.ShapeDtypeStruct((3 * f.group, f.group), kind)
    band = jax.ShapeDtypeStruct((3 * f.group, (2 * f.p + 1) * f.t), kind)
    triangle = jax.ShapeDtypeStruct((count * order, order), kind)
    half_triangle = jax.ShapeDtypeStruct((count // 2 * order, order), kind)
    listed = jax.ShapeDtypeStruct((half * half * order, order), kind)
    both = jax.ShapeDtypeStruct(((count + half * half) * order, order), kind)
    partial_sums = jax.ShapeDtypeStruct((2 * f.group, f.group), jnp.float32)
    group_scratch = pltpu.VMEM((f.group, f.group), kind)
    whole_scratch = pltpu.VMEM((3 * f.group, f.group), kind)

    def run(kernel, outs, scratch, tiles, limit, *args, **kw):
        return call(functools.partial(kernel, f), outs, scratch, tiles * unit, limit, *args, **kw)

    corner, corner_cross, slab_mate, triangle_cross, triangle_turning = run(
        slabs_kernel, [listed, listed, both, triangle, triangle], [], 0, 12, start_drop, inverse_start
    )
    from_mate = to_mate(slab_mate)
    direct_triangle = routed(triangle_cross, lambda i: 0 if turns(i) else cross_step(i))
    forward_mate, forward_far, triangle_turning, corner_cross = run(
        forward_kernel, [triangle, triangle], [], 0, 12, drop, density_cross, density_mate, from_mate,
        passed=(triangle_turning, corner_cross),
    )
    far_mate = to_mate(forward_mate)
    far_far = routed(forward_far, lambda i: 3 * cross_step(i))
    turned_triangle = routed(triangle_turning, lambda i: cross_step(i) if turns(i) else 0)
    cross_corner = to_cross(corner_cross)

    both_corners = jax.ShapeDtypeStruct((2 * f.group, f.group), kind)
    square, shifted, reach, here, partial = run(
        square_kernel,
        [band, band, both_corners, both_corners, partial_sums],
        [pltpu.VMEM((3 * f.group, 5 * f.group), kind)],
        84, 26, drop, density, density_cross, density_mate, light=True,
    )
    square_corners, shifted_corners = run(
        corners_kernel,
        [both_corners, both_corners],
        [group_scratch] * 2,
        10, 16, drop, far_far, far_mate, reach, here, partial, direct_triangle, light=True,
    )
    correction, own, partial = run(
        first_sweep_kernel,
        [columns, square_group, partial_sums],
        [whole_scratch, group_scratch, group_scratch],
        66, 24, drop, shifted, shifted_corners, corner, slab_mate, triangle_cross, from_mate,
        direct_triangle, turned_triangle, light=True,
    )
    corner_cross, corner_mate = to_cross(own), to_mate(own)
    low, high, edge_cross, edge_mate = run(
        first_edges_kernel,
        [square_group, square_group, triangle, triangle],
        [group_scratch] * 2,
        10, 16, drop, from_mate, cross_corner, correction, partial,
    )
    edge_cross, edge_mate = to_cross(edge_cross), to_mate(edge_mate)
    (correction,) = run(
        correction_kernel, [columns], [whole_scratch], 38, 16, drop, shifted, shifted_corners, low, own, high
    )
    new_low, new_high, inverse_cross, inverse_mate = run(
        second_edges_kernel,
        [square_group, square_group, triangle, triangle],
        [],
        20, 12, drop, corner_mate, corner_cross, correction, low, high,
    )
    inverse_cross, inverse_mate = to_cross(inverse_cross), to_mate(inverse_mate)
    whole, rim_cross, rim_mate, rim_mate_too = run(
        density_edges_kernel,
        [columns, triangle, half_triangle, half_triangle],
        [group_scratch] * 4,
        38, 20, drop, own, edge_mate, edge_cross, correction, new_low, new_high, square,
        square_corners,
    )
    rim_cross, rim_mates = to_cross(rim_cross), [to_mate(rim_mate), to_mate(rim_mate_too)]
    (density_own,) = run(density_own_kernel, [square_group], [], 18, 12, drop, square, whole)
    out = jax.ShapeDtypeStruct(density.shape, kind)

    def assembled(own, first, cross, mates):
        kernel = functools.partial(slots_kernel, f, first, len(mates))
        scratch = [pltpu.SemaphoreType.DMA(())]
        slots, early = call(kernel, [out, out], scratch, 0, 8, drop, own, *mates, light=True, off=1)
        scratch = [pltpu.VMEM(out.shape, kind), pltpu.SemaphoreType.DMA((half,))]
        kernel = functools.partial(last_slots_kernel, f)
        return call(kernel, [], scratch, 0, 8, drop, slots, cross, passed=(early,), light=True)[0]

    inverse_next = assembled(whole, half, inverse_cross, [inverse_mate])
    density_next = assembled(density_own, 0, rim_cross, rim_mates)
    return density_next, inverse_next


def solution(mesh):
    blocks = P(("grp", "row", "inner"), None, None, None)
    return jax.shard_map(
        on_device,
        mesh=mesh,
        in_specs=(blocks, blocks, P(("grp", "row", "inner"), None)),
        out_specs=(blocks, blocks),
        check_vma=False,
    )
```

```python
import functools

import jax
import jax.numpy as jnp
from jax import lax
from jax.experimental import pallas as pl
from jax.experimental.pallas import tpu as pltpu
from jax.sharding import PartitionSpec as P

RING = ("row", "inner")
MIB = 1024 * 1024


class Frame:
    def __init__(self, half, order):
        self.h = half
        self.b = order
        self.k = 2 * half
        self.p = half // 2
        self.t = 2 * order
        self.group = half * order
        self.pairs = 3 * self.p
        self.own_pairs = range(self.p, 2 * self.p)
        self.edge_rows = [*range(self.p), *range(2 * self.p, 3 * self.p)]

    def tiles(self, columns):
        for col in columns:
            for row in range(max(0, col - self.p), min(self.pairs, col + self.p + 1)):
                yield row, col

    def inner(self, row, col):
        return max(row, col) - self.p, min(row, col) + self.p + 1

    def clipped(self, row, col):
        lo, hi = self.inner(row, col)
        return max(lo, 0), min(hi, self.pairs)

    def on_corner(self, row, col):
        return max(row, col) < self.p or min(row, col) >= 2 * self.p

    def corner_place(self, row, col):
        r, c = (row, col) if row < self.p else (row - self.p, col - 2 * self.p)
        return r, r + 1, c, c + 1

    def split(self, row, col):
        lo, hi = self.clipped(row, col)
        for g in range(3):
            a, z = max(lo, g * self.p), min(hi, (g + 1) * self.p)
            if a < z:
                yield g, a - g * self.p, z - g * self.p


def under(h):
    return [(r, c) for r in range(h) for c in range(r + 1)]


def over(h):
    return [(r, c) for r in range(h) for c in range(r, h)]


def full(h):
    return [(r, c) for r in range(h) for c in range(h)]


def at(f, row_lo, row_hi, col_lo, col_hi):
    t = f.t
    return pl.ds(row_lo * t, (row_hi - row_lo) * t), pl.ds(col_lo * t, (col_hi - col_lo) * t)


def block(f, r, c):
    return pl.ds(r * f.b, f.b), pl.ds(c * f.b, f.b)


def banded(f, row, lo, hi):
    return at(f, row, row + 1, lo - row + f.p, hi - row + f.p)


def dot(a, b):
    return jnp.dot(a, b, preferred_element_type=jnp.float32)


def stored(rows, r, offset, dropped, slots=None):
    last = (rows.shape[1] if slots is None else slots) - 1
    slot = jnp.minimum(offset - (offset > dropped).astype(jnp.int32), last)
    value = rows[r, slot] if slots is None else rows((r, slot))
    return jnp.where(offset == dropped, jnp.zeros_like(value), value)


def masked(f, tile, row, col, drop_ref):
    b = f.b
    parts = []
    for i in range(2):
        r = 2 * row + i
        line = []
        for j in range(2):
            offset = 2 * col + j - r + f.h
            piece = tile[i * b : (i + 1) * b, j * b : (j + 1) * b]
            if 0 <= offset <= f.k:
                piece = jnp.where(drop_ref[r] == offset, 0.0, piece)
            else:
                piece = jnp.zeros_like(piece)
            line.append(piece)
        parts.append(jnp.concatenate(line, axis=1))
    return jnp.concatenate(parts, axis=0)


def odd_place(f, drop_ref):
    return drop_ref[3 * f.h] == 1


def indexed(f, ref, first=0):
    return lambda i: ref[block(f, first + i, 0)]


def plain(ref):
    return lambda place: ref[place]


def sides(f, drop_ref, mate, cross):
    odd = odd_place(f, drop_ref)

    def below(key):
        return jnp.where(odd, mate(key), cross(key))

    def above(key):
        return jnp.where(odd, cross(key), mate(key))

    return below, above


def spread(f, dest, row, col, read, places):
    index = {place: i for i, place in enumerate(places)}
    for r in range(f.h):
        for c in range(f.h):
            i = index.get((r, c))
            dest[block(f, row + r, col + c)] = jnp.zeros((f.b, f.b), dest.dtype) if i is None else read(i)


def pack_edges(f, drop_ref, low, high, to_cross, *to_mate):
    odd = odd_place(f, drop_ref)
    parts = len(to_mate)
    for i, (lower, upper) in enumerate(zip(under(f.h), over(f.h))):
        back, forth = low[block(f, *lower)], high[block(f, *upper)]
        to_cross[block(f, i, 0)] = jnp.where(odd, forth, back)
        to_mate[i % parts][block(f, i // parts, 0)] = jnp.where(odd, back, forth)


def slabs_kernel(f, drop_ref, own, corner, corner_again, to_mate, to_cross, to_cross_again):
    h = f.h
    odd = drop_ref[h] == 1
    n = len(under(h))
    for i, (lower, upper) in enumerate(zip(under(h), over(h))):
        (r, c), (s, d) = lower, upper
        forth = stored(own, r, 2 * h + c - r, drop_ref[r])
        back = stored(own, s, d - s, drop_ref[s])
        to_mate[block(f, i, 0)] = jnp.where(odd, back, forth)
        across = jnp.where(odd, forth, back)
        to_cross[block(f, i, 0)] = across
        to_cross_again[block(f, i, 0)] = across
    for i, (r, c) in enumerate(full(h)):
        value = stored(own, r, c - r + h, drop_ref[r])
        corner[block(f, i, 0)] = value
        corner_again[block(f, i, 0)] = value
        to_mate[block(f, n + i, 0)] = value


def forward_kernel(f, drop_ref, cross, *refs):
    h = f.h
    odd = odd_place(f, drop_ref)
    to_mate, to_far = refs[-4:-2]
    for i, (lower, upper) in enumerate(zip(under(h), over(h))):
        (r, c), (s, d) = lower, upper
        forth = stored(cross, r, 2 * h + c - r, jnp.where(odd, drop_ref[2 * h + r], drop_ref[r]))
        back = stored(cross, s, d - s, jnp.where(odd, drop_ref[2 * h + s], drop_ref[s]))
        to_mate[block(f, i, 0)] = jnp.where(odd, back, forth)
        to_far[block(f, i, 0)] = jnp.where(odd, forth, back)


def square_kernel(f, drop_ref, own, cross, mate, square, shifted, reach, here, partial, wide):
    h, p = f.h, f.p
    below, above = sides(f, drop_ref, plain(mate), plain(cross))
    for g, read in enumerate((below, plain(own), above)):
        for r in range(h):
            row = g * h + r
            first = 2 * (row // 2) - h
            for col in range(first, first + 2 * h + 2):
                offset = col - row + h
                if 0 <= offset <= f.k:
                    value = stored(read, r, offset, drop_ref[row], f.k)
                else:
                    value = jnp.zeros((f.b, f.b), wide.dtype)
                wide[block(f, row, col + h)] = value
    for i in range(h):
        for g, row in enumerate((i, 2 * h + i)):
            rows = pl.ds((g * h + i) * f.b, f.b)
            source = pl.ds(row * f.b, f.b)
            reach[rows, :] = wide[source, pl.ds(4 * g * f.group, f.group)]
            here[rows, :] = wide[source, pl.ds((2 * g + 1) * f.group, f.group)]
    unit = unit_tile(f)
    for row, col in f.tiles(range(f.pairs)):
        lo, hi = f.clipped(row, col)
        total = dot(
            wide[at(f, row, row + 1, lo + p, hi + p)], wide[at(f, lo, hi, col + p, col + p + 1)]
        )
        if f.on_corner(row, col):
            partial[at(f, *f.corner_place(row, col))] = total
            continue
        total = masked(f, total, row, col, drop_ref)
        place = banded(f, row, col, col + 1)
        tile = wide[at(f, row, row + 1, col + p, col + p + 1)].astype(jnp.float32)
        square[place] = total.astype(square.dtype)
        shifted[place] = moved(total, tile, unit if row == col else None).astype(shifted.dtype)


def unit_tile(f):
    rows = lax.broadcasted_iota(jnp.int32, (f.t, f.t), 0)
    return (rows == lax.broadcasted_iota(jnp.int32, (f.t, f.t), 1)).astype(jnp.float32)


def moved(total, tile, unit):
    value = 2.0 * total - 2.0 * tile
    return value if unit is None else value + unit


def corners_kernel(
    f, drop_ref, far_far, far_mate, reach, here, partial, unused, square, shifted, low, high
):
    p = f.p
    far_below, far_above = sides(f, drop_ref, indexed(f, far_mate), indexed(f, far_far))
    spread(f, low, 0, 0, far_below, under(f.h))
    spread(f, high, 0, 0, far_above, over(f.h))
    unit = unit_tile(f)
    for row, col in f.tiles(range(f.pairs)):
        if not f.on_corner(row, col):
            continue
        place = at(f, *f.corner_place(row, col))
        r, _, c, _ = f.corner_place(row, col)
        total = partial[place]
        if row < p:
            a, z, far = max(row, col), p, low
        else:
            a, z, far = 0, min(row, col) - 2 * p + 1, high
        if a < z:
            total = total + dot(reach[at(f, r, r + 1, a, z)], far[at(f, a, z, c, c + 1)])
        total = masked(f, total, row, col, drop_ref)
        tile = here[place].astype(jnp.float32)
        square[place] = total.astype(square.dtype)
        shifted[place] = moved(total, tile, unit if row == col else None).astype(shifted.dtype)


def right_tile(f, left, corners, right, row, col):
    lo, hi = f.clipped(row, col)
    total = None
    if row < f.p:
        inside = corners[at(f, row, row + 1, lo, f.p)]
        total = dot(inside, right[at(f, lo, f.p, col - f.p, col - f.p + 1)])
        lo = f.p
    elif row >= 2 * f.p:
        inside = corners[at(f, row - f.p, row - f.p + 1, 0, hi - 2 * f.p)]
        total = dot(inside, right[at(f, 2 * f.p, hi, col - f.p, col - f.p + 1)])
        hi = 2 * f.p
    rest = dot(left[banded(f, row, lo, hi)], right[at(f, lo, hi, col - f.p, col - f.p + 1)])
    return rest if total is None else total + rest


def early_sweep_kernel(f, drop_ref, shifted, corner, mate, direct, turned, whole, early):
    h, p = f.h, f.p
    turning = drop_ref[3 * h + 1] == 1
    direct_block, turned_block = indexed(f, direct), indexed(f, turned)

    def cross(i):
        return jnp.where(turning, turned_block(i), direct_block(i))

    from_below, from_above = sides(f, drop_ref, indexed(f, mate), cross)
    spread(f, whole, 0, 0, from_below, under(h))
    spread(f, whole, h, 0, indexed(f, corner), full(h))
    spread(f, whole, 2 * h, 0, from_above, over(h))
    for row, col in f.tiles(f.own_pairs):
        lo, hi = f.clipped(row, col)
        lo = p if row < p else lo
        hi = 2 * p if row >= 2 * p else hi
        c = col - p
        early[at(f, row, row + 1, c, c + 1)] = dot(
            shifted[banded(f, row, lo, hi)], whole[at(f, lo, hi, c, c + 1)]
        )


def first_sweep_kernel(
    f, drop_ref, corners, early, whole, sent_mate, sent_cross, correction, fresh, before, after
):
    h, p = f.h, f.p
    down, up = sides(f, drop_ref, indexed(f, sent_mate), indexed(f, sent_cross))
    spread(f, before, 0, 0, down, over(h))
    spread(f, after, 0, 0, up, under(h))
    for row, col in f.tiles(f.own_pairs):
        lo, hi = f.clipped(row, col)
        c = col - p
        total = early[at(f, row, row + 1, c, c + 1)]
        if row < p:
            total = total + dot(corners[at(f, row, row + 1, lo, p)], whole[at(f, lo, p, c, c + 1)])
        elif row >= 2 * p:
            total = total + dot(
                corners[at(f, row - p, row - p + 1, 0, hi - 2 * p)], whole[at(f, 2 * p, hi, c, c + 1)]
            )
        total = masked(f, total, row, col, drop_ref)
        correction[at(f, row, row + 1, c, c + 1)] = total.astype(correction.dtype)
    for row, col in f.tiles(f.own_pairs):
        if row not in f.own_pairs:
            continue
        c, local = col - p, row - p
        total = 2.0 * whole[at(f, row, row + 1, c, c + 1)].astype(jnp.float32)
        for g, a, z in f.split(row, col):
            left = whole[at(f, row, row + 1, a, z)] if g == 1 else (before, None, after)[g][at(f, local, local + 1, a, z)]
            total = total - dot(left, correction[at(f, g * p + a, g * p + z, c, c + 1)])
        total = masked(f, total, row, col, drop_ref)
        fresh[at(f, local, local + 1, c, c + 1)] = total.astype(fresh.dtype)


def edges(f, drop_ref, corner_below, corner_above, correction, start, low, high):
    p = f.p
    for row, col in f.tiles(f.own_pairs):
        if row in f.own_pairs:
            continue
        c = col - p
        side = 0 if row < p else 2
        corner, dest = ((corner_below, low), None, (corner_above, high))[side]
        local = row - side * p
        total = start(row, col)
        for g, a, z in f.split(row, col):
            if g == side:
                total = total - dot(
                    corner(at(f, local, local + 1, a, z)), correction[at(f, g * p + a, g * p + z, c, c + 1)]
                )
        total = masked(f, total, row, col, drop_ref)
        dest[at(f, local, local + 1, c, c + 1)] = total.astype(dest.dtype)


def first_edges_kernel(
    f, drop_ref, mate, cross, correction, whole, low, high, to_cross, to_mate, before, after
):
    p = f.p
    below, above = sides(f, drop_ref, indexed(f, mate, len(under(f.h))), indexed(f, cross))
    spread(f, before, 0, 0, below, full(f.h))
    spread(f, after, 0, 0, above, full(f.h))

    def start(row, col):
        c = col - p
        total = 2.0 * whole[at(f, row, row + 1, c, c + 1)].astype(jnp.float32)
        for g, a, z in f.split(row, col):
            if g == 1:
                total = total - dot(
                    whole[at(f, row, row + 1, a, z)], correction[at(f, p + a, p + z, c, c + 1)]
                )
        return total

    edges(f, drop_ref, plain(before), plain(after), correction, start, low, high)
    pack_edges(f, drop_ref, low, high, to_cross, to_mate)


def gather(f, whole, low, own, high):
    for g, source in enumerate((low, own, high)):
        for i in range(f.h):
            whole[pl.ds(g * f.group + i * f.b, f.b), :] = source[pl.ds(i * f.b, f.b), :]


def correction_kernel(f, drop_ref, shifted, corners, low, own, high, correction, whole):
    p = f.p
    gather(f, whole, low, own, high)
    for row, col in f.tiles(f.own_pairs):
        total = masked(f, right_tile(f, shifted, corners, whole, row, col), row, col, drop_ref)
        correction[at(f, row, row + 1, col - p, col - p + 1)] = total.astype(correction.dtype)


def second_edges_kernel(
    f, drop_ref, mate, cross, correction, low, high, new_low, new_high, to_cross, to_mate
):
    p = f.p

    def start(row, col):
        c = col - p
        source, local = (low, row) if row < p else (high, row - 2 * p)
        total = 2.0 * source[at(f, local, local + 1, c, c + 1)].astype(jnp.float32)
        for g, a, z in f.split(row, col):
            if g == 1:
                total = total - dot(
                    source[at(f, local, local + 1, a, z)], correction[at(f, p + a, p + z, c, c + 1)]
                )
        return total

    below, above = sides(f, drop_ref, plain(mate), plain(cross))
    edges(f, drop_ref, below, above, correction, start, new_low, new_high)
    pack_edges(f, drop_ref, new_low, new_high, to_cross, to_mate)


def density_edges_kernel(
    f, drop_ref, own, mate, cross, correction, new_low, new_high, square, corners, whole, to_cross, to_mate,
    to_mate_too, before, after, low, high,
):
    h, p = f.h, f.p
    below, above = sides(f, drop_ref, indexed(f, mate), indexed(f, cross))
    spread(f, before, 0, 0, below, over(h))
    spread(f, after, 0, 0, above, under(h))
    for row, col in f.tiles(f.own_pairs):
        if row not in f.own_pairs:
            continue
        c, local = col - p, row - p
        total = 2.0 * own[at(f, local, local + 1, c, c + 1)].astype(jnp.float32)
        for g, a, z in f.split(row, col):
            left = (before, own, after)[g][at(f, local, local + 1, a, z)]
            total = total - dot(left, correction[at(f, g * p + a, g * p + z, c, c + 1)])
        total = masked(f, total, row, col, drop_ref)
        whole[at(f, row, row + 1, c, c + 1)] = total.astype(whole.dtype)
    for i in range(h):
        rows = pl.ds(i * f.b, f.b)
        whole[pl.ds(i * f.b, f.b), :] = new_low[rows, :]
        whole[pl.ds(2 * f.group + i * f.b, f.b), :] = new_high[rows, :]
    for row, col in f.tiles(f.own_pairs):
        if row in f.own_pairs:
            continue
        total = masked(f, right_tile(f, square, corners, whole, row, col), row, col, drop_ref)
        dest, local = (low, row) if row < p else (high, row - 2 * p)
        dest[at(f, local, local + 1, col - p, col - p + 1)] = total.astype(dest.dtype)
    pack_edges(f, drop_ref, low, high, to_cross, to_mate, to_mate_too)


def density_own_kernel(f, drop_ref, square, whole, out):
    p = f.p
    for row, col in f.tiles(f.own_pairs):
        if row in f.own_pairs:
            total = masked(f, right_tile(f, square, None, whole, row, col), row, col, drop_ref)
            out[at(f, row - p, row - p + 1, col - p, col - p + 1)] = total.astype(out.dtype)


def slots_kernel(f, first, parts, drop_ref, own, *refs):
    h = f.h
    mates = [indexed(f, ref) for ref in refs[:parts]]
    slots, out, sem = refs[parts:]
    over_index = {place: i for i, place in enumerate(over(h))}
    under_index = {place: i for i, place in enumerate(under(h))}

    def mate_block(i):
        return mates[i % parts](i // parts)

    for r in range(h):
        dropped = drop_ref[h + r]

        def at_offset(offset, r=r):
            col = r + offset
            if col < h:
                return mate_block(over_index[r, col])
            if col < 2 * h:
                return own[block(f, first + r, col - h)]
            return mate_block(under_index[r, col - 2 * h])

        for s in range(f.k):
            slots[r, s] = jnp.where(dropped <= s, at_offset(s + 1), at_offset(s))
    copy = pltpu.make_async_copy(slots, out, sem)
    copy.start()
    copy.wait()


def last_slots_kernel(f, drop_ref, slots, cross, unused, out, side, sems):
    h, k = f.h, f.k
    odd = odd_place(f, drop_ref)
    cross_block = indexed(f, cross)
    over_index = {place: i for i, place in enumerate(over(h))}
    under_index = {place: i for i, place in enumerate(under(h))}

    def fill(low):
        copies = []
        for r in range(h):
            dropped = drop_ref[h + r]
            lo, hi = (0, h - r) if low else (k - 1 - r, k)
            for s in range(lo, hi):

                def at_offset(offset, r=r, s=s):
                    col = r + offset
                    if low and col < h:
                        return cross_block(over_index[r, col])
                    if not low and col >= 2 * h:
                        return cross_block(under_index[r, col - 2 * h])
                    return slots[r, s]

                side[r, s] = jnp.where(dropped <= s, at_offset(s + 1), at_offset(s))
            copy = pltpu.make_async_copy(
                side.at[r, pl.ds(lo, hi - lo)], out.at[r, pl.ds(lo, hi - lo)], sems.at[r]
            )
            copy.start()
            copies.append(copy)
        for copy in copies:
            copy.wait()

    @pl.when(odd)
    def _():
        fill(False)

    @pl.when(jnp.logical_not(odd))
    def _():
        fill(True)


VMEM = pl.BlockSpec(memory_space=pltpu.VMEM)
SMEM = pl.BlockSpec(memory_space=pltpu.SMEM)
ANY = pl.BlockSpec(memory_space=pl.ANY)


def call(kernel, outs, scratch, flops, limit, drop, *args, passed=(), light=False, off=0):
    moved = sum(a.size * a.dtype.itemsize for a in args) + sum(s.size * s.dtype.itemsize for s in outs)
    if light:
        flops = moved = 0
    n = len(args)
    return pl.pallas_call(
        kernel,
        out_shape=[*outs, *[jax.ShapeDtypeStruct(a.shape, a.dtype) for a in passed]],
        in_specs=[SMEM] + [VMEM] * n + [ANY] * len(passed),
        out_specs=[VMEM] * (len(outs) - off) + [ANY] * (off + len(passed)),
        scratch_shapes=scratch,
        input_output_aliases={1 + n + i: len(outs) + i for i in range(len(passed))},
        compiler_params=pltpu.CompilerParams(vmem_limit_bytes=limit * MIB),
        cost_estimate=pl.CostEstimate(flops=flops, bytes_accessed=moved, transcendentals=0),
    )(drop, *args, *passed)


def routed(x, step):
    size = lax.axis_size(RING)
    return lax.ppermute(x, RING, [(i, (i + step(i)) % size) for i in range(size) if step(i)])


def on_device(density, inverse_start, block_cols):
    rows, width, order, _ = density.shape
    half = width // 2
    ring, inner = lax.axis_size(RING), lax.axis_size(RING[1])
    total = rows * ring
    assert rows == half and half % 2 == 0 and inner % 2 == 0
    f = Frame(half, order)
    kind = density.dtype
    me = lax.axis_index(RING)

    def mate_step(i):
        return 1 - 2 * (i % 2)

    def cross_step(i):
        return 2 * (i % 2) - 1

    def to_mate(x):
        return routed(x, mate_step)

    def to_cross(x):
        return routed(x, cross_step)

    def turns(i):
        return i % inner in (0, inner - 1)

    positions = block_cols - (me * rows + jnp.arange(rows, dtype=jnp.int32))[:, None] + half
    positions = positions + jnp.where(positions < 0, total, jnp.where(positions >= total, -total, 0))
    own_drop = width * (width + 1) // 2 - jnp.sum(positions, axis=1)

    density_cross, density_mate = to_cross(density), to_mate(density)
    cross_drop, mate_drop = to_cross(own_drop), to_mate(own_drop)
    even = (me & 1) == 0
    place = lax.axis_index(RING[1])
    marks = jnp.stack([me & 1, ((place == 0) | (place == inner - 1)).astype(jnp.int32)])
    start_drop = jnp.concatenate([own_drop, marks[:1]])
    drop = jnp.concatenate(
        [jnp.where(even, cross_drop, mate_drop), own_drop, jnp.where(even, mate_drop, cross_drop), marks]
    )

    unit = 2 * f.t**3
    count = half * (half + 1) // 2
    square_group = jax.ShapeDtypeStruct((f.group, f.group), kind)
    columns = jax.ShapeDtypeStruct((3 * f.group, f.group), kind)
    band = jax.ShapeDtypeStruct((3 * f.group, (2 * f.p + 1) * f.t), kind)
    triangle = jax.ShapeDtypeStruct((count * order, order), kind)
    half_triangle = jax.ShapeDtypeStruct((count // 2 * order, order), kind)
    listed = jax.ShapeDtypeStruct((half * half * order, order), kind)
    both = jax.ShapeDtypeStruct(((count + half * half) * order, order), kind)
    partial_sums = jax.ShapeDtypeStruct((2 * f.group, f.group), jnp.float32)
    group_scratch = pltpu.VMEM((f.group, f.group), kind)
    whole_scratch = pltpu.VMEM((3 * f.group, f.group), kind)

    def run(kernel, outs, scratch, tiles, limit, *args, **kw):
        return call(functools.partial(kernel, f), outs, scratch, tiles * unit, limit, *args, **kw)

    corner, corner_cross, slab_mate, triangle_cross, triangle_turning = run(
        slabs_kernel, [listed, listed, both, triangle, triangle], [], 0, 12, start_drop, inverse_start
    )
    from_mate = to_mate(slab_mate)
    direct_triangle = routed(triangle_cross, lambda i: 0 if turns(i) else cross_step(i))
    forward_mate, forward_far, triangle_turning, corner_cross = run(
        forward_kernel, [triangle, triangle], [], 0, 12, drop, density_cross, density_mate, from_mate,
        passed=(triangle_turning, corner_cross),
    )
    far_mate = to_mate(forward_mate)
    far_far = routed(forward_far, lambda i: 3 * cross_step(i))
    turned_triangle = routed(triangle_turning, lambda i: cross_step(i) if turns(i) else 0)
    cross_corner = to_cross(corner_cross)

    both_corners = jax.ShapeDtypeStruct((2 * f.group, f.group), kind)
    square, shifted, reach, here, partial = run(
        square_kernel,
        [band, band, both_corners, both_corners, partial_sums],
        [pltpu.VMEM((3 * f.group, 5 * f.group), kind)],
        84, 26, drop, density, density_cross, density_mate, light=True,
    )
    early_sums = jax.ShapeDtypeStruct((3 * f.group, f.group), jnp.float32)
    columns_start, early = run(
        early_sweep_kernel,
        [columns, early_sums],
        [],
        28, 16, drop, shifted, corner, from_mate, direct_triangle, turned_triangle, light=True,
    )
    square_corners, shifted_corners = run(
        corners_kernel,
        [both_corners, both_corners],
        [group_scratch] * 2,
        10, 16, drop, far_far, far_mate, reach, here, partial, early, light=True,
    )
    correction, own = run(
        first_sweep_kernel,
        [columns, square_group],
        [group_scratch, group_scratch],
        28, 20, drop, shifted_corners, early, columns_start, slab_mate, triangle_cross, light=True,
    )
    corner_cross, corner_mate = to_cross(own), to_mate(own)
    low, high, edge_cross, edge_mate = run(
        first_edges_kernel,
        [square_group, square_group, triangle, triangle],
        [group_scratch] * 2,
        20, 16, drop, from_mate, cross_corner, correction, columns_start,
    )
    edge_cross, edge_mate = to_cross(edge_cross), to_mate(edge_mate)
    (correction,) = run(
        correction_kernel, [columns], [whole_scratch], 38, 16, drop, shifted, shifted_corners, low, own, high
    )
    new_low, new_high, inverse_cross, inverse_mate = run(
        second_edges_kernel,
        [square_group, square_group, triangle, triangle],
        [],
        20, 12, drop, corner_mate, corner_cross, correction, low, high,
    )
    inverse_cross, inverse_mate = to_cross(inverse_cross), to_mate(inverse_mate)
    whole, rim_cross, rim_mate, rim_mate_too = run(
        density_edges_kernel,
        [columns, triangle, half_triangle, half_triangle],
        [group_scratch] * 4,
        38, 20, drop, own, edge_mate, edge_cross, correction, new_low, new_high, square,
        square_corners,
    )
    rim_cross, rim_mates = to_cross(rim_cross), [to_mate(rim_mate), to_mate(rim_mate_too)]
    (density_own,) = run(density_own_kernel, [square_group], [], 18, 12, drop, square, whole)
    out = jax.ShapeDtypeStruct(density.shape, kind)

    def assembled(own, first, cross, mates):
        kernel = functools.partial(slots_kernel, f, first, len(mates))
        scratch = [pltpu.SemaphoreType.DMA(())]
        slots, early = call(kernel, [out, out], scratch, 0, 8, drop, own, *mates, light=True, off=1)
        scratch = [pltpu.VMEM(out.shape, kind), pltpu.SemaphoreType.DMA((half,))]
        kernel = functools.partial(last_slots_kernel, f)
        return call(kernel, [], scratch, 0, 8, drop, slots, cross, passed=(early,), light=True)[0]

    inverse_next = assembled(whole, half, inverse_cross, [inverse_mate])
    density_next = assembled(density_own, 0, rim_cross, rim_mates)
    return density_next, inverse_next


def solution(mesh):
    blocks = P(("grp", "row", "inner"), None, None, None)
    return jax.shard_map(
        on_device,
        mesh=mesh,
        in_specs=(blocks, blocks, P(("grp", "row", "inner"), None)),
        out_specs=(blocks, blocks),
        check_vma=False,
    )
```

```python
import functools

import jax
import jax.numpy as jnp
from jax import lax
from jax.experimental import pallas as pl
from jax.experimental.pallas import tpu as pltpu
from jax.sharding import PartitionSpec as P

RING = ("row", "inner")
MIB = 1024 * 1024


class Frame:
    def __init__(self, half, order):
        self.h = half
        self.b = order
        self.k = 2 * half
        self.p = half // 2
        self.t = 2 * order
        self.group = half * order
        self.pairs = 3 * self.p
        self.own_pairs = range(self.p, 2 * self.p)
        self.edge_rows = [*range(self.p), *range(2 * self.p, 3 * self.p)]

    def tiles(self, columns):
        for col in columns:
            for row in range(max(0, col - self.p), min(self.pairs, col + self.p + 1)):
                yield row, col

    def inner(self, row, col):
        return max(row, col) - self.p, min(row, col) + self.p + 1

    def clipped(self, row, col):
        lo, hi = self.inner(row, col)
        return max(lo, 0), min(hi, self.pairs)

    def on_corner(self, row, col):
        return max(row, col) < self.p or min(row, col) >= 2 * self.p

    def corner_place(self, row, col):
        r, c = (row, col) if row < self.p else (row - self.p, col - 2 * self.p)
        return r, r + 1, c, c + 1

    def split(self, row, col):
        lo, hi = self.clipped(row, col)
        for g in range(3):
            a, z = max(lo, g * self.p), min(hi, (g + 1) * self.p)
            if a < z:
                yield g, a - g * self.p, z - g * self.p


def under(h):
    return [(r, c) for r in range(h) for c in range(r + 1)]


def over(h):
    return [(r, c) for r in range(h) for c in range(r, h)]


def full(h):
    return [(r, c) for r in range(h) for c in range(h)]


def at(f, row_lo, row_hi, col_lo, col_hi):
    t = f.t
    return pl.ds(row_lo * t, (row_hi - row_lo) * t), pl.ds(col_lo * t, (col_hi - col_lo) * t)


def block(f, r, c):
    return pl.ds(r * f.b, f.b), pl.ds(c * f.b, f.b)


def banded(f, row, lo, hi):
    return at(f, row, row + 1, lo - row + f.p, hi - row + f.p)


def dot(a, b):
    return jnp.dot(a, b, preferred_element_type=jnp.float32)


def stored(rows, r, offset, dropped, slots=None):
    last = (rows.shape[1] if slots is None else slots) - 1
    slot = jnp.minimum(offset - (offset > dropped).astype(jnp.int32), last)
    value = rows[r, slot] if slots is None else rows((r, slot))
    return jnp.where(offset == dropped, jnp.zeros_like(value), value)


def masked(f, tile, row, col, drop_ref):
    b = f.b
    parts = []
    for i in range(2):
        r = 2 * row + i
        line = []
        for j in range(2):
            offset = 2 * col + j - r + f.h
            piece = tile[i * b : (i + 1) * b, j * b : (j + 1) * b]
            if 0 <= offset <= f.k:
                piece = jnp.where(drop_ref[r] == offset, 0.0, piece)
            else:
                piece = jnp.zeros_like(piece)
            line.append(piece)
        parts.append(jnp.concatenate(line, axis=1))
    return jnp.concatenate(parts, axis=0)


def odd_place(f, drop_ref):
    return drop_ref[3 * f.h] == 1


def indexed(f, ref, first=0):
    return lambda i: ref[block(f, first + i, 0)]


def plain(ref):
    return lambda place: ref[place]


def sides(f, drop_ref, mate, cross):
    odd = odd_place(f, drop_ref)

    def below(key):
        return jnp.where(odd, mate(key), cross(key))

    def above(key):
        return jnp.where(odd, cross(key), mate(key))

    return below, above


def spread(f, dest, row, col, read, places):
    index = {place: i for i, place in enumerate(places)}
    for r in range(f.h):
        for c in range(f.h):
            i = index.get((r, c))
            dest[block(f, row + r, col + c)] = jnp.zeros((f.b, f.b), dest.dtype) if i is None else read(i)


def pack_edges(f, drop_ref, low, high, to_cross, *to_mate):
    odd = odd_place(f, drop_ref)
    parts = len(to_mate)
    for i, (lower, upper) in enumerate(zip(under(f.h), over(f.h))):
        back, forth = low[block(f, *lower)], high[block(f, *upper)]
        to_cross[block(f, i, 0)] = jnp.where(odd, forth, back)
        to_mate[i % parts][block(f, i // parts, 0)] = jnp.where(odd, back, forth)


def slabs_kernel(f, drop_ref, own, corner, corner_again, to_mate, to_cross, to_cross_again):
    h = f.h
    odd = drop_ref[h] == 1
    n = len(under(h))
    for i, (lower, upper) in enumerate(zip(under(h), over(h))):
        (r, c), (s, d) = lower, upper
        forth = stored(own, r, 2 * h + c - r, drop_ref[r])
        back = stored(own, s, d - s, drop_ref[s])
        to_mate[block(f, i, 0)] = jnp.where(odd, back, forth)
        across = jnp.where(odd, forth, back)
        to_cross[block(f, i, 0)] = across
        to_cross_again[block(f, i, 0)] = across
    for i, (r, c) in enumerate(full(h)):
        value = stored(own, r, c - r + h, drop_ref[r])
        corner[block(f, i, 0)] = value
        corner_again[block(f, i, 0)] = value
        to_mate[block(f, n + i, 0)] = value


def forward_kernel(f, drop_ref, cross, *refs):
    h = f.h
    odd = odd_place(f, drop_ref)
    to_mate, to_far = refs[-4:-2]
    for i, (lower, upper) in enumerate(zip(under(h), over(h))):
        (r, c), (s, d) = lower, upper
        forth = stored(cross, r, 2 * h + c - r, jnp.where(odd, drop_ref[2 * h + r], drop_ref[r]))
        back = stored(cross, s, d - s, jnp.where(odd, drop_ref[2 * h + s], drop_ref[s]))
        to_mate[block(f, i, 0)] = jnp.where(odd, back, forth)
        to_far[block(f, i, 0)] = jnp.where(odd, forth, back)


def square_kernel(f, drop_ref, own, cross, mate, square, shifted, reach, here, partial, wide):
    h, p = f.h, f.p
    below, above = sides(f, drop_ref, plain(mate), plain(cross))
    for g, read in enumerate((below, plain(own), above)):
        for r in range(h):
            row = g * h + r
            first = 2 * (row // 2) - h
            for col in range(first, first + 2 * h + 2):
                offset = col - row + h
                if 0 <= offset <= f.k:
                    value = stored(read, r, offset, drop_ref[row], f.k)
                else:
                    value = jnp.zeros((f.b, f.b), wide.dtype)
                wide[block(f, row, col + h)] = value
    for i in range(h):
        for g, row in enumerate((i, 2 * h + i)):
            rows = pl.ds((g * h + i) * f.b, f.b)
            source = pl.ds(row * f.b, f.b)
            reach[rows, :] = wide[source, pl.ds(4 * g * f.group, f.group)]
            here[rows, :] = wide[source, pl.ds((2 * g + 1) * f.group, f.group)]
    unit = unit_tile(f)
    for row, col in f.tiles(range(f.pairs)):
        lo, hi = f.clipped(row, col)
        total = dot(
            wide[at(f, row, row + 1, lo + p, hi + p)], wide[at(f, lo, hi, col + p, col + p + 1)]
        )
        if f.on_corner(row, col):
            partial[at(f, *f.corner_place(row, col))] = total
            continue
        total = masked(f, total, row, col, drop_ref)
        place = banded(f, row, col, col + 1)
        tile = wide[at(f, row, row + 1, col + p, col + p + 1)].astype(jnp.float32)
        square[place] = total.astype(square.dtype)
        shifted[place] = moved(total, tile, unit if row == col else None).astype(shifted.dtype)


def unit_tile(f):
    rows = lax.broadcasted_iota(jnp.int32, (f.t, f.t), 0)
    return (rows == lax.broadcasted_iota(jnp.int32, (f.t, f.t), 1)).astype(jnp.float32)


def moved(total, tile, unit):
    value = 2.0 * total - 2.0 * tile
    return value if unit is None else value + unit


def corners_kernel(
    f, drop_ref, far_far, far_mate, reach, here, partial, unused, square, shifted, low, high
):
    p = f.p
    far_below, far_above = sides(f, drop_ref, indexed(f, far_mate), indexed(f, far_far))
    spread(f, low, 0, 0, far_below, under(f.h))
    spread(f, high, 0, 0, far_above, over(f.h))
    unit = unit_tile(f)
    for row, col in f.tiles(range(f.pairs)):
        if not f.on_corner(row, col):
            continue
        place = at(f, *f.corner_place(row, col))
        r, _, c, _ = f.corner_place(row, col)
        total = partial[place]
        if row < p:
            a, z, far = max(row, col), p, low
        else:
            a, z, far = 0, min(row, col) - 2 * p + 1, high
        if a < z:
            total = total + dot(reach[at(f, r, r + 1, a, z)], far[at(f, a, z, c, c + 1)])
        total = masked(f, total, row, col, drop_ref)
        tile = here[place].astype(jnp.float32)
        square[place] = total.astype(square.dtype)
        shifted[place] = moved(total, tile, unit if row == col else None).astype(shifted.dtype)


def right_tile(f, left, corners, right, row, col):
    lo, hi = f.clipped(row, col)
    total = None
    if row < f.p:
        inside = corners[at(f, row, row + 1, lo, f.p)]
        total = dot(inside, right[at(f, lo, f.p, col - f.p, col - f.p + 1)])
        lo = f.p
    elif row >= 2 * f.p:
        inside = corners[at(f, row - f.p, row - f.p + 1, 0, hi - 2 * f.p)]
        total = dot(inside, right[at(f, 2 * f.p, hi, col - f.p, col - f.p + 1)])
        hi = 2 * f.p
    rest = dot(left[banded(f, row, lo, hi)], right[at(f, lo, hi, col - f.p, col - f.p + 1)])
    return rest if total is None else total + rest


def first_sweep_kernel(
    f, drop_ref, shifted, corners, corner, sent_mate, sent_cross, mate, direct, turned,
    correction, fresh, whole, before, after,
):
    h, p = f.h, f.p
    turning = drop_ref[3 * h + 1] == 1
    direct_block, turned_block = indexed(f, direct), indexed(f, turned)

    def cross(i):
        return jnp.where(turning, turned_block(i), direct_block(i))

    from_below, from_above = sides(f, drop_ref, indexed(f, mate), cross)
    down, up = sides(f, drop_ref, indexed(f, sent_mate), indexed(f, sent_cross))
    spread(f, whole, 0, 0, from_below, under(h))
    spread(f, whole, h, 0, indexed(f, corner), full(h))
    spread(f, whole, 2 * h, 0, from_above, over(h))
    spread(f, before, 0, 0, down, over(h))
    spread(f, after, 0, 0, up, under(h))
    for row, col in f.tiles(f.own_pairs):
        total = masked(f, right_tile(f, shifted, corners, whole, row, col), row, col, drop_ref)
        correction[at(f, row, row + 1, col - p, col - p + 1)] = total.astype(correction.dtype)
    for row, col in f.tiles(f.own_pairs):
        if row not in f.own_pairs:
            continue
        c, local = col - p, row - p
        total = 2.0 * whole[at(f, row, row + 1, c, c + 1)].astype(jnp.float32)
        for g, a, z in f.split(row, col):
            source, first = (before, local) if g == 0 else (whole, row) if g == 1 else (after, local)
            left = source[at(f, first, first + 1, a, z)]
            total = total - dot(left, correction[at(f, g * p + a, g * p + z, c, c + 1)])
        total = masked(f, total, row, col, drop_ref)
        fresh[at(f, local, local + 1, c, c + 1)] = total.astype(fresh.dtype)


def edges(f, drop_ref, corner_below, corner_above, correction, start, low, high):
    p = f.p
    for row, col in f.tiles(f.own_pairs):
        if row in f.own_pairs:
            continue
        c = col - p
        side = 0 if row < p else 2
        corner, dest = ((corner_below, low), None, (corner_above, high))[side]
        local = row - side * p
        total = start(row, col)
        for g, a, z in f.split(row, col):
            if g == side:
                total = total - dot(
                    corner(at(f, local, local + 1, a, z)), correction[at(f, g * p + a, g * p + z, c, c + 1)]
                )
        total = masked(f, total, row, col, drop_ref)
        dest[at(f, local, local + 1, c, c + 1)] = total.astype(dest.dtype)


def first_edges_kernel(
    f, drop_ref, mate, cross, correction, whole, low, high, to_cross, to_mate, before, after
):
    p = f.p
    below, above = sides(f, drop_ref, indexed(f, mate, len(under(f.h))), indexed(f, cross))
    spread(f, before, 0, 0, below, full(f.h))
    spread(f, after, 0, 0, above, full(f.h))

    def start(row, col):
        c = col - p
        total = 2.0 * whole[at(f, row, row + 1, c, c + 1)].astype(jnp.float32)
        for g, a, z in f.split(row, col):
            if g == 1:
                total = total - dot(
                    whole[at(f, row, row + 1, a, z)], correction[at(f, p + a, p + z, c, c + 1)]
                )
        return total

    edges(f, drop_ref, plain(before), plain(after), correction, start, low, high)
    pack_edges(f, drop_ref, low, high, to_cross, to_mate)


def gather(f, whole, low, own, high):
    for g, source in enumerate((low, own, high)):
        for i in range(f.h):
            whole[pl.ds(g * f.group + i * f.b, f.b), :] = source[pl.ds(i * f.b, f.b), :]


def correction_kernel(f, drop_ref, shifted, corners, low, own, high, correction, whole):
    p = f.p
    gather(f, whole, low, own, high)
    for row, col in f.tiles(f.own_pairs):
        total = masked(f, right_tile(f, shifted, corners, whole, row, col), row, col, drop_ref)
        correction[at(f, row, row + 1, col - p, col - p + 1)] = total.astype(correction.dtype)


def second_edges_kernel(
    f, drop_ref, mate, cross, correction, low, high, new_low, new_high, to_cross, to_mate
):
    p = f.p

    def start(row, col):
        c = col - p
        source, local = (low, row) if row < p else (high, row - 2 * p)
        total = 2.0 * source[at(f, local, local + 1, c, c + 1)].astype(jnp.float32)
        for g, a, z in f.split(row, col):
            if g == 1:
                total = total - dot(
                    source[at(f, local, local + 1, a, z)], correction[at(f, p + a, p + z, c, c + 1)]
                )
        return total

    below, above = sides(f, drop_ref, plain(mate), plain(cross))
    edges(f, drop_ref, below, above, correction, start, new_low, new_high)
    pack_edges(f, drop_ref, new_low, new_high, to_cross, to_mate)


def density_edges_kernel(
    f, drop_ref, own, mate, cross, correction, new_low, new_high, square, corners, whole, to_cross, to_mate,
    to_mate_too, before, after, low, high,
):
    h, p = f.h, f.p
    below, above = sides(f, drop_ref, indexed(f, mate), indexed(f, cross))
    spread(f, before, 0, 0, below, over(h))
    spread(f, after, 0, 0, above, under(h))
    for row, col in f.tiles(f.own_pairs):
        if row not in f.own_pairs:
            continue
        c, local = col - p, row - p
        total = 2.0 * own[at(f, local, local + 1, c, c + 1)].astype(jnp.float32)
        for g, a, z in f.split(row, col):
            left = (before, own, after)[g][at(f, local, local + 1, a, z)]
            total = total - dot(left, correction[at(f, g * p + a, g * p + z, c, c + 1)])
        total = masked(f, total, row, col, drop_ref)
        whole[at(f, row, row + 1, c, c + 1)] = total.astype(whole.dtype)
    for i in range(h):
        rows = pl.ds(i * f.b, f.b)
        whole[pl.ds(i * f.b, f.b), :] = new_low[rows, :]
        whole[pl.ds(2 * f.group + i * f.b, f.b), :] = new_high[rows, :]
    for row, col in f.tiles(f.own_pairs):
        if row in f.own_pairs:
            continue
        total = masked(f, right_tile(f, square, corners, whole, row, col), row, col, drop_ref)
        dest, local = (low, row) if row < p else (high, row - 2 * p)
        dest[at(f, local, local + 1, col - p, col - p + 1)] = total.astype(dest.dtype)
    pack_edges(f, drop_ref, low, high, to_cross, to_mate, to_mate_too)


def density_own_kernel(f, drop_ref, square, whole, out):
    p = f.p
    for row, col in f.tiles(f.own_pairs):
        if row in f.own_pairs:
            total = masked(f, right_tile(f, square, None, whole, row, col), row, col, drop_ref)
            out[at(f, row - p, row - p + 1, col - p, col - p + 1)] = total.astype(out.dtype)


def slots_kernel(f, first, parts, drop_ref, own, *refs):
    h = f.h
    mates = [indexed(f, ref) for ref in refs[:parts]]
    slots, out, sem = refs[parts:]
    over_index = {place: i for i, place in enumerate(over(h))}
    under_index = {place: i for i, place in enumerate(under(h))}

    def mate_block(i):
        return mates[i % parts](i // parts)

    for r in range(h):
        dropped = drop_ref[h + r]

        def at_offset(offset, r=r):
            col = r + offset
            if col < h:
                return mate_block(over_index[r, col])
            if col < 2 * h:
                return own[block(f, first + r, col - h)]
            return mate_block(under_index[r, col - 2 * h])

        for s in range(f.k):
            slots[r, s] = jnp.where(dropped <= s, at_offset(s + 1), at_offset(s))
    copy = pltpu.make_async_copy(slots, out, sem)
    copy.start()
    copy.wait()


def last_slots_kernel(f, drop_ref, slots, cross, unused, out, side, sems):
    h, k = f.h, f.k
    odd = odd_place(f, drop_ref)
    cross_block = indexed(f, cross)
    over_index = {place: i for i, place in enumerate(over(h))}
    under_index = {place: i for i, place in enumerate(under(h))}

    def fill(low):
        copies = []
        for r in range(h):
            dropped = drop_ref[h + r]
            lo, hi = (0, h - r) if low else (k - 1 - r, k)
            for s in range(lo, hi):

                def at_offset(offset, r=r, s=s):
                    col = r + offset
                    if low and col < h:
                        return cross_block(over_index[r, col])
                    if not low and col >= 2 * h:
                        return cross_block(under_index[r, col - 2 * h])
                    return slots[r, s]

                side[r, s] = jnp.where(dropped <= s, at_offset(s + 1), at_offset(s))
            copy = pltpu.make_async_copy(
                side.at[r, pl.ds(lo, hi - lo)], out.at[r, pl.ds(lo, hi - lo)], sems.at[r]
            )
            copy.start()
            copies.append(copy)
        for copy in copies:
            copy.wait()

    @pl.when(odd)
    def _():
        fill(False)

    @pl.when(jnp.logical_not(odd))
    def _():
        fill(True)


VMEM = pl.BlockSpec(memory_space=pltpu.VMEM)
SMEM = pl.BlockSpec(memory_space=pltpu.SMEM)
ANY = pl.BlockSpec(memory_space=pl.ANY)


def call(kernel, outs, scratch, flops, limit, drop, *args, passed=(), light=False, off=0):
    moved = sum(a.size * a.dtype.itemsize for a in args) + sum(s.size * s.dtype.itemsize for s in outs)
    if light:
        flops = moved = 0
    n = len(args)
    return pl.pallas_call(
        kernel,
        out_shape=[*outs, *[jax.ShapeDtypeStruct(a.shape, a.dtype) for a in passed]],
        in_specs=[SMEM] + [VMEM] * n + [ANY] * len(passed),
        out_specs=[VMEM] * (len(outs) - off) + [ANY] * (off + len(passed)),
        scratch_shapes=scratch,
        input_output_aliases={1 + n + i: len(outs) + i for i in range(len(passed))},
        compiler_params=pltpu.CompilerParams(vmem_limit_bytes=limit * MIB),
        cost_estimate=pl.CostEstimate(flops=flops, bytes_accessed=moved, transcendentals=0),
    )(drop, *args, *passed)


def routed(x, step):
    size = lax.axis_size(RING)
    return lax.ppermute(x, RING, [(i, (i + step(i)) % size) for i in range(size) if step(i)])


def on_device(density, inverse_start, block_cols):
    rows, width, order, _ = density.shape
    half = width // 2
    ring, inner = lax.axis_size(RING), lax.axis_size(RING[1])
    total = rows * ring
    assert rows == half and half % 2 == 0 and inner % 2 == 0
    f = Frame(half, order)
    kind = density.dtype
    me = lax.axis_index(RING)

    def mate_step(i):
        return 1 - 2 * (i % 2)

    def cross_step(i):
        return 2 * (i % 2) - 1

    def to_mate(x):
        return routed(x, mate_step)

    def to_cross(x):
        return routed(x, cross_step)

    def turns(i):
        return i % inner in (0, inner - 1)

    positions = block_cols - (me * rows + jnp.arange(rows, dtype=jnp.int32))[:, None] + half
    positions = positions + jnp.where(positions < 0, total, jnp.where(positions >= total, -total, 0))
    own_drop = width * (width + 1) // 2 - jnp.sum(positions, axis=1)

    density_cross, density_mate = to_cross(density), to_mate(density)
    cross_drop, mate_drop = to_cross(own_drop), to_mate(own_drop)
    even = (me & 1) == 0
    place = lax.axis_index(RING[1])
    marks = jnp.stack([me & 1, ((place == 0) | (place == inner - 1)).astype(jnp.int32)])
    start_drop = jnp.concatenate([own_drop, marks[:1]])
    drop = jnp.concatenate(
        [jnp.where(even, cross_drop, mate_drop), own_drop, jnp.where(even, mate_drop, cross_drop), marks]
    )

    unit = 2 * f.t**3
    count = half * (half + 1) // 2
    square_group = jax.ShapeDtypeStruct((f.group, f.group), kind)
    columns = jax.ShapeDtypeStruct((3 * f.group, f.group), kind)
    band = jax.ShapeDtypeStruct((3 * f.group, (2 * f.p + 1) * f.t), kind)
    triangle = jax.ShapeDtypeStruct((count * order, order), kind)
    half_triangle = jax.ShapeDtypeStruct((count // 2 * order, order), kind)
    listed = jax.ShapeDtypeStruct((half * half * order, order), kind)
    both = jax.ShapeDtypeStruct(((count + half * half) * order, order), kind)
    partial_sums = jax.ShapeDtypeStruct((2 * f.group, f.group), jnp.float32)
    group_scratch = pltpu.VMEM((f.group, f.group), kind)
    whole_scratch = pltpu.VMEM((3 * f.group, f.group), kind)

    def run(kernel, outs, scratch, tiles, limit, *args, **kw):
        return call(functools.partial(kernel, f), outs, scratch, tiles * unit, limit, *args, **kw)

    corner, corner_cross, slab_mate, triangle_cross, triangle_turning = run(
        slabs_kernel, [listed, listed, both, triangle, triangle], [], 0, 12, start_drop, inverse_start
    )
    from_mate = to_mate(slab_mate)
    direct_triangle = routed(triangle_cross, lambda i: 0 if turns(i) else cross_step(i))
    forward_mate, forward_far, triangle_turning, corner_cross = run(
        forward_kernel, [triangle, triangle], [], 0, 12, drop, density_cross, density_mate, from_mate,
        passed=(triangle_turning, corner_cross),
    )
    far_mate = to_mate(forward_mate)
    far_far = routed(forward_far, lambda i: 3 * cross_step(i))
    turned_triangle = routed(triangle_turning, lambda i: cross_step(i) if turns(i) else 0)
    cross_corner = to_cross(corner_cross)

    both_corners = jax.ShapeDtypeStruct((2 * f.group, f.group), kind)
    square, shifted, reach, here, partial = run(
        square_kernel,
        [band, band, both_corners, both_corners, partial_sums],
        [pltpu.VMEM((3 * f.group, 5 * f.group), kind)],
        84, 26, drop, density, density_cross, density_mate, light=True,
    )
    square_corners, shifted_corners = run(
        corners_kernel,
        [both_corners, both_corners],
        [group_scratch] * 2,
        10, 16, drop, far_far, far_mate, reach, here, partial, direct_triangle, light=True,
    )
    correction, own, columns_start = run(
        first_sweep_kernel,
        [columns, square_group, columns],
        [group_scratch, group_scratch],
        56, 24, drop, shifted, shifted_corners, corner, slab_mate, triangle_cross, from_mate,
        direct_triangle, turned_triangle, light=True,
    )
    corner_cross, corner_mate = to_cross(own), to_mate(own)
    low, high, edge_cross, edge_mate = run(
        first_edges_kernel,
        [square_group, square_group, triangle, triangle],
        [group_scratch] * 2,
        20, 16, drop, from_mate, cross_corner, correction, columns_start,
    )
    edge_cross, edge_mate = to_cross(edge_cross), to_mate(edge_mate)
    (correction,) = run(
        correction_kernel, [columns], [whole_scratch], 38, 16, drop, shifted, shifted_corners, low, own, high
    )
    new_low, new_high, inverse_cross, inverse_mate = run(
        second_edges_kernel,
        [square_group, square_group, triangle, triangle],
        [],
        20, 12, drop, corner_mate, corner_cross, correction, low, high,
    )
    inverse_cross, inverse_mate = to_cross(inverse_cross), to_mate(inverse_mate)
    whole, rim_cross, rim_mate, rim_mate_too = run(
        density_edges_kernel,
        [columns, triangle, half_triangle, half_triangle],
        [group_scratch] * 4,
        38, 20, drop, own, edge_mate, edge_cross, correction, new_low, new_high, square,
        square_corners,
    )
    rim_cross, rim_mates = to_cross(rim_cross), [to_mate(rim_mate), to_mate(rim_mate_too)]
    (density_own,) = run(density_own_kernel, [square_group], [], 18, 12, drop, square, whole)
    out = jax.ShapeDtypeStruct(density.shape, kind)

    def assembled(own, first, cross, mates):
        kernel = functools.partial(slots_kernel, f, first, len(mates))
        scratch = [pltpu.SemaphoreType.DMA(())]
        slots, early = call(kernel, [out, out], scratch, 0, 8, drop, own, *mates, light=True, off=1)
        scratch = [pltpu.VMEM(out.shape, kind), pltpu.SemaphoreType.DMA((half,))]
        kernel = functools.partial(last_slots_kernel, f)
        return call(kernel, [], scratch, 0, 8, drop, slots, cross, passed=(early,), light=True)[0]

    inverse_next = assembled(whole, half, inverse_cross, [inverse_mate])
    density_next = assembled(density_own, 0, rim_cross, rim_mates)
    return density_next, inverse_next


def solution(mesh):
    blocks = P(("grp", "row", "inner"), None, None, None)
    return jax.shard_map(
        on_device,
        mesh=mesh,
        in_specs=(blocks, blocks, P(("grp", "row", "inner"), None)),
        out_specs=(blocks, blocks),
        check_vma=False,
    )
```

```python
import functools

import jax
import jax.numpy as jnp
from jax import lax
from jax.experimental import pallas as pl
from jax.experimental.pallas import tpu as pltpu
from jax.sharding import PartitionSpec as P

RING = ("row", "inner")
MIB = 1024 * 1024


class Frame:
    def __init__(self, half, order):
        self.h = half
        self.b = order
        self.k = 2 * half
        self.p = half // 2
        self.t = 2 * order
        self.group = half * order
        self.pairs = 3 * self.p
        self.own_pairs = range(self.p, 2 * self.p)
        self.edge_rows = [*range(self.p), *range(2 * self.p, 3 * self.p)]

    def tiles(self, columns):
        for col in columns:
            for row in range(max(0, col - self.p), min(self.pairs, col + self.p + 1)):
                yield row, col

    def inner(self, row, col):
        return max(row, col) - self.p, min(row, col) + self.p + 1

    def clipped(self, row, col):
        lo, hi = self.inner(row, col)
        return max(lo, 0), min(hi, self.pairs)

    def on_corner(self, row, col):
        return max(row, col) < self.p or min(row, col) >= 2 * self.p

    def corner_place(self, row, col):
        r, c = (row, col) if row < self.p else (row - self.p, col - 2 * self.p)
        return r, r + 1, c, c + 1

    def split(self, row, col):
        lo, hi = self.clipped(row, col)
        for g in range(3):
            a, z = max(lo, g * self.p), min(hi, (g + 1) * self.p)
            if a < z:
                yield g, a - g * self.p, z - g * self.p


def under(h):
    return [(r, c) for r in range(h) for c in range(r + 1)]


def over(h):
    return [(r, c) for r in range(h) for c in range(r, h)]


def full(h):
    return [(r, c) for r in range(h) for c in range(h)]


def at(f, row_lo, row_hi, col_lo, col_hi):
    t = f.t
    return pl.ds(row_lo * t, (row_hi - row_lo) * t), pl.ds(col_lo * t, (col_hi - col_lo) * t)


def block(f, r, c):
    return pl.ds(r * f.b, f.b), pl.ds(c * f.b, f.b)


def banded(f, row, lo, hi):
    return at(f, row, row + 1, lo - row + f.p, hi - row + f.p)


def dot(a, b):
    return jnp.dot(a, b, preferred_element_type=jnp.float32)


def stored(rows, r, offset, dropped, slots=None):
    last = (rows.shape[1] if slots is None else slots) - 1
    slot = jnp.minimum(offset - (offset > dropped).astype(jnp.int32), last)
    value = rows[r, slot] if slots is None else rows((r, slot))
    return jnp.where(offset == dropped, jnp.zeros_like(value), value)


def masked(f, tile, row, col, drop_ref):
    b = f.b
    parts = []
    for i in range(2):
        r = 2 * row + i
        line = []
        for j in range(2):
            offset = 2 * col + j - r + f.h
            piece = tile[i * b : (i + 1) * b, j * b : (j + 1) * b]
            if 0 <= offset <= f.k:
                piece = jnp.where(drop_ref[r] == offset, 0.0, piece)
            else:
                piece = jnp.zeros_like(piece)
            line.append(piece)
        parts.append(jnp.concatenate(line, axis=1))
    return jnp.concatenate(parts, axis=0)


def odd_place(f, drop_ref):
    return drop_ref[3 * f.h] == 1


def indexed(f, ref, first=0):
    return lambda i: ref[block(f, first + i, 0)]


def plain(ref):
    return lambda place: ref[place]


def sides(f, drop_ref, mate, cross):
    odd = odd_place(f, drop_ref)

    def below(key):
        return jnp.where(odd, mate(key), cross(key))

    def above(key):
        return jnp.where(odd, cross(key), mate(key))

    return below, above


def spread(f, dest, row, col, read, places):
    index = {place: i for i, place in enumerate(places)}
    for r in range(f.h):
        for c in range(f.h):
            i = index.get((r, c))
            dest[block(f, row + r, col + c)] = jnp.zeros((f.b, f.b), dest.dtype) if i is None else read(i)


def pack_edges(f, drop_ref, low, high, to_cross, *to_mate):
    odd = odd_place(f, drop_ref)
    parts = len(to_mate)
    for i, (lower, upper) in enumerate(zip(under(f.h), over(f.h))):
        back, forth = low[block(f, *lower)], high[block(f, *upper)]
        to_cross[block(f, i, 0)] = jnp.where(odd, forth, back)
        to_mate[i % parts][block(f, i // parts, 0)] = jnp.where(odd, back, forth)


def slabs_kernel(f, drop_ref, own, corner, corner_again, to_mate, to_cross):
    h = f.h
    odd = drop_ref[h] == 1
    n = len(under(h))
    for i, (lower, upper) in enumerate(zip(under(h), over(h))):
        (r, c), (s, d) = lower, upper
        forth = stored(own, r, 2 * h + c - r, drop_ref[r])
        back = stored(own, s, d - s, drop_ref[s])
        to_mate[block(f, i, 0)] = jnp.where(odd, back, forth)
        to_cross[block(f, i, 0)] = jnp.where(odd, forth, back)
    for i, (r, c) in enumerate(full(h)):
        value = stored(own, r, c - r + h, drop_ref[r])
        corner[block(f, i, 0)] = value
        corner_again[block(f, i, 0)] = value
        to_mate[block(f, n + i, 0)] = value


def forward_kernel(f, drop_ref, cross, *refs):
    h = f.h
    odd = odd_place(f, drop_ref)
    to_mate, to_far = refs[-5:-3], refs[-3]
    for i, (lower, upper) in enumerate(zip(under(h), over(h))):
        (r, c), (s, d) = lower, upper
        forth = stored(cross, r, 2 * h + c - r, jnp.where(odd, drop_ref[2 * h + r], drop_ref[r]))
        back = stored(cross, s, d - s, jnp.where(odd, drop_ref[2 * h + s], drop_ref[s]))
        part, place = i % 2, i // 2
        to_mate[part][block(f, place, 0)] = jnp.where(odd, back, forth)
        to_far[block(f, i, 0)] = jnp.where(odd, forth, back)


def square_kernel(f, drop_ref, own, cross, mate, square, shifted, reach, here, partial, wide):
    h, p = f.h, f.p
    below, above = sides(f, drop_ref, plain(mate), plain(cross))
    for g, read in enumerate((below, plain(own), above)):
        for r in range(h):
            row = g * h + r
            first = 2 * (row // 2) - h
            for col in range(first, first + 2 * h + 2):
                offset = col - row + h
                if 0 <= offset <= f.k:
                    value = stored(read, r, offset, drop_ref[row], f.k)
                else:
                    value = jnp.zeros((f.b, f.b), wide.dtype)
                wide[block(f, row, col + h)] = value
    for i in range(h):
        for g, row in enumerate((i, 2 * h + i)):
            rows = pl.ds((g * h + i) * f.b, f.b)
            source = pl.ds(row * f.b, f.b)
            reach[rows, :] = wide[source, pl.ds(4 * g * f.group, f.group)]
            here[rows, :] = wide[source, pl.ds((2 * g + 1) * f.group, f.group)]
    unit = unit_tile(f)
    for row, col in f.tiles(range(f.pairs)):
        lo, hi = f.clipped(row, col)
        total = dot(
            wide[at(f, row, row + 1, lo + p, hi + p)], wide[at(f, lo, hi, col + p, col + p + 1)]
        )
        if f.on_corner(row, col):
            partial[at(f, *f.corner_place(row, col))] = total
            continue
        total = masked(f, total, row, col, drop_ref)
        place = banded(f, row, col, col + 1)
        tile = wide[at(f, row, row + 1, col + p, col + p + 1)].astype(jnp.float32)
        square[place] = total.astype(square.dtype)
        shifted[place] = moved(total, tile, unit if row == col else None).astype(shifted.dtype)


def unit_tile(f):
    rows = lax.broadcasted_iota(jnp.int32, (f.t, f.t), 0)
    return (rows == lax.broadcasted_iota(jnp.int32, (f.t, f.t), 1)).astype(jnp.float32)


def moved(total, tile, unit):
    value = 2.0 * total - 2.0 * tile
    return value if unit is None else value + unit


def corners_kernel(
    f, drop_ref, far_far, far_mate, far_mate_too, reach, here, partial, square, shifted, low, high
):
    p = f.p
    far_mates = [indexed(f, far_mate), indexed(f, far_mate_too)]
    far_below, far_above = sides(f, drop_ref, lambda i: far_mates[i % 2](i // 2), indexed(f, far_far))
    spread(f, low, 0, 0, far_below, under(f.h))
    spread(f, high, 0, 0, far_above, over(f.h))
    unit = unit_tile(f)
    for row, col in f.tiles(range(f.pairs)):
        if not f.on_corner(row, col):
            continue
        place = at(f, *f.corner_place(row, col))
        r, _, c, _ = f.corner_place(row, col)
        total = partial[place]
        if row < p:
            a, z, far = max(row, col), p, low
        else:
            a, z, far = 0, min(row, col) - 2 * p + 1, high
        if a < z:
            total = total + dot(reach[at(f, r, r + 1, a, z)], far[at(f, a, z, c, c + 1)])
        total = masked(f, total, row, col, drop_ref)
        tile = here[place].astype(jnp.float32)
        square[place] = total.astype(square.dtype)
        shifted[place] = moved(total, tile, unit if row == col else None).astype(shifted.dtype)


def right_tile(f, left, corners, right, row, col):
    lo, hi = f.clipped(row, col)
    total = None
    if row < f.p:
        inside = corners[at(f, row, row + 1, lo, f.p)]
        total = dot(inside, right[at(f, lo, f.p, col - f.p, col - f.p + 1)])
        lo = f.p
    elif row >= 2 * f.p:
        inside = corners[at(f, row - f.p, row - f.p + 1, 0, hi - 2 * f.p)]
        total = dot(inside, right[at(f, 2 * f.p, hi, col - f.p, col - f.p + 1)])
        hi = 2 * f.p
    rest = dot(left[banded(f, row, lo, hi)], right[at(f, lo, hi, col - f.p, col - f.p + 1)])
    return rest if total is None else total + rest


def first_sweep_kernel(
    f, drop_ref, shifted, corners, corner, sent_mate, sent_cross, mate, cross,
    correction, fresh, whole, before, after,
):
    h, p = f.h, f.p
    from_below, from_above = sides(f, drop_ref, indexed(f, mate), indexed(f, cross))
    down, up = sides(f, drop_ref, indexed(f, sent_mate), indexed(f, sent_cross))
    spread(f, whole, 0, 0, from_below, under(h))
    spread(f, whole, h, 0, indexed(f, corner), full(h))
    spread(f, whole, 2 * h, 0, from_above, over(h))
    spread(f, before, 0, 0, down, over(h))
    spread(f, after, 0, 0, up, under(h))
    for row, col in f.tiles(f.own_pairs):
        total = masked(f, right_tile(f, shifted, corners, whole, row, col), row, col, drop_ref)
        correction[at(f, row, row + 1, col - p, col - p + 1)] = total.astype(correction.dtype)
    for row, col in f.tiles(f.own_pairs):
        if row not in f.own_pairs:
            continue
        c, local = col - p, row - p
        total = 2.0 * whole[at(f, row, row + 1, c, c + 1)].astype(jnp.float32)
        for g, a, z in f.split(row, col):
            source, first = (before, local) if g == 0 else (whole, row) if g == 1 else (after, local)
            left = source[at(f, first, first + 1, a, z)]
            total = total - dot(left, correction[at(f, g * p + a, g * p + z, c, c + 1)])
        total = masked(f, total, row, col, drop_ref)
        fresh[at(f, local, local + 1, c, c + 1)] = total.astype(fresh.dtype)


def edges(f, drop_ref, corner_below, corner_above, correction, start, low, high):
    p = f.p
    for row, col in f.tiles(f.own_pairs):
        if row in f.own_pairs:
            continue
        c = col - p
        side = 0 if row < p else 2
        corner, dest = ((corner_below, low), None, (corner_above, high))[side]
        local = row - side * p
        total = start(row, col)
        for g, a, z in f.split(row, col):
            if g == side:
                total = total - dot(
                    corner(at(f, local, local + 1, a, z)), correction[at(f, g * p + a, g * p + z, c, c + 1)]
                )
        total = masked(f, total, row, col, drop_ref)
        dest[at(f, local, local + 1, c, c + 1)] = total.astype(dest.dtype)


def first_edges_kernel(
    f, drop_ref, mate, cross, correction, whole, low, high, to_cross, to_mate, before, after
):
    p = f.p
    below, above = sides(f, drop_ref, indexed(f, mate, len(under(f.h))), indexed(f, cross))
    spread(f, before, 0, 0, below, full(f.h))
    spread(f, after, 0, 0, above, full(f.h))

    def start(row, col):
        c = col - p
        total = 2.0 * whole[at(f, row, row + 1, c, c + 1)].astype(jnp.float32)
        for g, a, z in f.split(row, col):
            if g == 1:
                total = total - dot(
                    whole[at(f, row, row + 1, a, z)], correction[at(f, p + a, p + z, c, c + 1)]
                )
        return total

    edges(f, drop_ref, plain(before), plain(after), correction, start, low, high)
    pack_edges(f, drop_ref, low, high, to_cross, to_mate)


def gather(f, whole, low, own, high):
    for g, source in enumerate((low, own, high)):
        for i in range(f.h):
            whole[pl.ds(g * f.group + i * f.b, f.b), :] = source[pl.ds(i * f.b, f.b), :]


def correction_kernel(f, drop_ref, shifted, corners, low, own, high, correction, whole):
    p = f.p
    gather(f, whole, low, own, high)
    for row, col in f.tiles(f.own_pairs):
        total = masked(f, right_tile(f, shifted, corners, whole, row, col), row, col, drop_ref)
        correction[at(f, row, row + 1, col - p, col - p + 1)] = total.astype(correction.dtype)


def second_edges_kernel(
    f, drop_ref, cross, mate, correction, low, high, new_low, new_high, to_cross, to_mate
):
    p = f.p

    def start(row, col):
        c = col - p
        source, local = (low, row) if row < p else (high, row - 2 * p)
        total = 2.0 * source[at(f, local, local + 1, c, c + 1)].astype(jnp.float32)
        for g, a, z in f.split(row, col):
            if g == 1:
                total = total - dot(
                    source[at(f, local, local + 1, a, z)], correction[at(f, p + a, p + z, c, c + 1)]
                )
        return total

    below, above = sides(f, drop_ref, plain(mate), plain(cross))
    edges(f, drop_ref, below, above, correction, start, new_low, new_high)
    pack_edges(f, drop_ref, new_low, new_high, to_cross, to_mate)


def density_edges_kernel(
    f, drop_ref, own, cross, mate, correction, new_low, new_high, square, corners, whole, to_cross, to_mate,
    to_mate_too, before, after, low, high,
):
    h, p = f.h, f.p
    below, above = sides(f, drop_ref, indexed(f, mate), indexed(f, cross))
    spread(f, before, 0, 0, below, over(h))
    spread(f, after, 0, 0, above, under(h))
    for row, col in f.tiles(f.own_pairs):
        if row not in f.own_pairs:
            continue
        c, local = col - p, row - p
        total = 2.0 * own[at(f, local, local + 1, c, c + 1)].astype(jnp.float32)
        for g, a, z in f.split(row, col):
            left = (before, own, after)[g][at(f, local, local + 1, a, z)]
            total = total - dot(left, correction[at(f, g * p + a, g * p + z, c, c + 1)])
        total = masked(f, total, row, col, drop_ref)
        whole[at(f, row, row + 1, c, c + 1)] = total.astype(whole.dtype)
    for i in range(h):
        rows = pl.ds(i * f.b, f.b)
        whole[pl.ds(i * f.b, f.b), :] = new_low[rows, :]
        whole[pl.ds(2 * f.group + i * f.b, f.b), :] = new_high[rows, :]
    for row, col in f.tiles(f.own_pairs):
        if row in f.own_pairs:
            continue
        total = masked(f, right_tile(f, square, corners, whole, row, col), row, col, drop_ref)
        dest, local = (low, row) if row < p else (high, row - 2 * p)
        dest[at(f, local, local + 1, col - p, col - p + 1)] = total.astype(dest.dtype)
    pack_edges(f, drop_ref, low, high, to_cross, to_mate, to_mate_too)


def density_own_kernel(f, drop_ref, square, whole, out):
    p = f.p
    for row, col in f.tiles(f.own_pairs):
        if row in f.own_pairs:
            total = masked(f, right_tile(f, square, None, whole, row, col), row, col, drop_ref)
            out[at(f, row - p, row - p + 1, col - p, col - p + 1)] = total.astype(out.dtype)


def slots_kernel(f, first, parts, drop_ref, own, *refs):
    h = f.h
    mates = [indexed(f, ref) for ref in refs[:parts]]
    slots, out, sem = refs[parts:]
    over_index = {place: i for i, place in enumerate(over(h))}
    under_index = {place: i for i, place in enumerate(under(h))}

    def mate_block(i):
        return mates[i % parts](i // parts)

    for r in range(h):
        dropped = drop_ref[h + r]

        def at_offset(offset, r=r):
            col = r + offset
            if col < h:
                return mate_block(over_index[r, col])
            if col < 2 * h:
                return own[block(f, first + r, col - h)]
            return mate_block(under_index[r, col - 2 * h])

        for s in range(f.k):
            slots[r, s] = jnp.where(dropped <= s, at_offset(s + 1), at_offset(s))
    copy = pltpu.make_async_copy(slots, out, sem)
    copy.start()
    copy.wait()


def last_slots_kernel(f, drop_ref, slots, cross, unused, out, side, sems):
    h, k = f.h, f.k
    odd = odd_place(f, drop_ref)
    cross_block = indexed(f, cross)
    over_index = {place: i for i, place in enumerate(over(h))}
    under_index = {place: i for i, place in enumerate(under(h))}

    def fill(low):
        copies = []
        for r in range(h):
            dropped = drop_ref[h + r]
            lo, hi = (0, h - r) if low else (k - 1 - r, k)
            for s in range(lo, hi):

                def at_offset(offset, r=r, s=s):
                    col = r + offset
                    if low and col < h:
                        return cross_block(over_index[r, col])
                    if not low and col >= 2 * h:
                        return cross_block(under_index[r, col - 2 * h])
                    return slots[r, s]

                side[r, s] = jnp.where(dropped <= s, at_offset(s + 1), at_offset(s))
            copy = pltpu.make_async_copy(
                side.at[r, pl.ds(lo, hi - lo)], out.at[r, pl.ds(lo, hi - lo)], sems.at[r]
            )
            copy.start()
            copies.append(copy)
        for copy in copies:
            copy.wait()

    @pl.when(odd)
    def _():
        fill(False)

    @pl.when(jnp.logical_not(odd))
    def _():
        fill(True)


VMEM = pl.BlockSpec(memory_space=pltpu.VMEM)
SMEM = pl.BlockSpec(memory_space=pltpu.SMEM)
ANY = pl.BlockSpec(memory_space=pl.ANY)


def call(kernel, outs, scratch, flops, limit, drop, *args, passed=(), light=False, off=0):
    moved = sum(a.size * a.dtype.itemsize for a in args) + sum(s.size * s.dtype.itemsize for s in outs)
    if light:
        flops = moved = 0
    n = len(args)
    return pl.pallas_call(
        kernel,
        out_shape=[*outs, *[jax.ShapeDtypeStruct(a.shape, a.dtype) for a in passed]],
        in_specs=[SMEM] + [VMEM] * n + [ANY] * len(passed),
        out_specs=[VMEM] * (len(outs) - off) + [ANY] * (off + len(passed)),
        scratch_shapes=scratch,
        input_output_aliases={1 + n + i: len(outs) + i for i in range(len(passed))},
        compiler_params=pltpu.CompilerParams(vmem_limit_bytes=limit * MIB),
        cost_estimate=pl.CostEstimate(flops=flops, bytes_accessed=moved, transcendentals=0),
    )(drop, *args, *passed)


def routed(x, step):
    size = lax.axis_size(RING)
    return lax.ppermute(x, RING, [(i, (i + step(i)) % size) for i in range(size) if step(i)])


def on_device(density, inverse_start, block_cols):
    rows, width, order, _ = density.shape
    half = width // 2
    ring = lax.axis_size(RING)
    total = rows * ring
    assert rows == half and half % 2 == 0 and ring % 2 == 0
    f = Frame(half, order)
    kind = density.dtype
    me = lax.axis_index(RING)

    def mate_step(i):
        return 1 - 2 * (i % 2)

    def cross_step(i):
        return 2 * (i % 2) - 1

    def to_mate(x):
        return routed(x, mate_step)

    def to_cross(x):
        return routed(x, cross_step)

    positions = block_cols - (me * rows + jnp.arange(rows, dtype=jnp.int32))[:, None] + half
    positions = positions + jnp.where(positions < 0, total, jnp.where(positions >= total, -total, 0))
    own_drop = width * (width + 1) // 2 - jnp.sum(positions, axis=1)

    density_cross, density_mate = to_cross(density), to_mate(density)
    cross_drop, mate_drop = to_cross(own_drop), to_mate(own_drop)
    even = (me & 1) == 0
    mark = jnp.reshape(me & 1, (1,))
    start_drop = jnp.concatenate([own_drop, mark])
    drop = jnp.concatenate(
        [jnp.where(even, cross_drop, mate_drop), own_drop, jnp.where(even, mate_drop, cross_drop), mark]
    )

    unit = 2 * f.t**3
    count = half * (half + 1) // 2
    square_group = jax.ShapeDtypeStruct((f.group, f.group), kind)
    columns = jax.ShapeDtypeStruct((3 * f.group, f.group), kind)
    band = jax.ShapeDtypeStruct((3 * f.group, (2 * f.p + 1) * f.t), kind)
    triangle = jax.ShapeDtypeStruct((count * order, order), kind)
    half_triangle = jax.ShapeDtypeStruct((count // 2 * order, order), kind)
    listed = jax.ShapeDtypeStruct((half * half * order, order), kind)
    both = jax.ShapeDtypeStruct(((count + half * half) * order, order), kind)
    partial_sums = jax.ShapeDtypeStruct((2 * f.group, f.group), jnp.float32)
    group_scratch = pltpu.VMEM((f.group, f.group), kind)
    whole_scratch = pltpu.VMEM((3 * f.group, f.group), kind)

    def run(kernel, outs, scratch, tiles, limit, *args, **kw):
        return call(functools.partial(kernel, f), outs, scratch, tiles * unit, limit, *args, **kw)

    corner, corner_cross, slab_mate, triangle_cross = run(
        slabs_kernel, [listed, listed, both, triangle], [], 0, 12, start_drop, inverse_start
    )
    from_mate = to_mate(slab_mate)
    forward_mate, forward_mate_too, forward_far, triangle_cross, corner_cross = run(
        forward_kernel, [half_triangle, half_triangle, triangle], [], 0, 12, drop, density_cross, density_mate, from_mate,
        passed=(triangle_cross, corner_cross),
    )
    far_mate, far_mate_too = to_mate(forward_mate), to_mate(forward_mate_too)
    far_far = routed(forward_far, lambda i: 3 * cross_step(i))
    cross_triangle = to_cross(triangle_cross)
    cross_corner = to_cross(corner_cross)

    both_corners = jax.ShapeDtypeStruct((2 * f.group, f.group), kind)
    square, shifted, reach, here, partial = run(
        square_kernel,
        [band, band, both_corners, both_corners, partial_sums],
        [pltpu.VMEM((3 * f.group, 5 * f.group), kind)],
        84, 26, drop, density, density_cross, density_mate,
    )
    square_corners, shifted_corners = run(
        corners_kernel,
        [both_corners, both_corners],
        [group_scratch] * 2,
        10, 16, drop, far_far, far_mate, far_mate_too, reach, here, partial, light=True,
    )
    correction, own, columns_start = run(
        first_sweep_kernel,
        [columns, square_group, columns],
        [group_scratch, group_scratch],
        56, 24, drop, shifted, shifted_corners, corner, slab_mate, triangle_cross, from_mate, cross_triangle, light=True,
    )
    corner_cross, corner_mate = to_cross(own), to_mate(own)
    low, high, edge_cross, edge_mate = run(
        first_edges_kernel,
        [square_group, square_group, triangle, triangle],
        [group_scratch] * 2,
        20, 16, drop, from_mate, cross_corner, correction, columns_start,
    )
    edge_cross, edge_mate = to_cross(edge_cross), to_mate(edge_mate)
    (correction,) = run(
        correction_kernel, [columns], [whole_scratch], 38, 16, drop, shifted, shifted_corners, low, own, high
    )
    new_low, new_high, inverse_cross, inverse_mate = run(
        second_edges_kernel,
        [square_group, square_group, triangle, triangle],
        [],
        20, 12, drop, corner_cross, corner_mate, correction, low, high,
    )
    inverse_cross, inverse_mate = to_cross(inverse_cross), to_mate(inverse_mate)
    whole, rim_cross, rim_mate, rim_mate_too = run(
        density_edges_kernel,
        [columns, triangle, half_triangle, half_triangle],
        [group_scratch] * 4,
        38, 20, drop, own, edge_cross, edge_mate, correction, new_low, new_high, square,
        square_corners,
    )
    rim_cross, rim_mates = to_cross(rim_cross), [to_mate(rim_mate), to_mate(rim_mate_too)]
    (density_own,) = run(density_own_kernel, [square_group], [], 18, 12, drop, square, whole)
    out = jax.ShapeDtypeStruct(density.shape, kind)

    def assembled(own, first, cross, mates):
        kernel = functools.partial(slots_kernel, f, first, len(mates))
        scratch = [pltpu.SemaphoreType.DMA(())]
        slots, early = call(kernel, [out, out], scratch, 0, 8, drop, own, *mates, light=True, off=1)
        scratch = [pltpu.VMEM(out.shape, kind), pltpu.SemaphoreType.DMA((half,))]
        kernel = functools.partial(last_slots_kernel, f)
        return call(kernel, [], scratch, 0, 8, drop, slots, cross, passed=(early,), light=True)[0]

    inverse_next = assembled(whole, half, inverse_cross, [inverse_mate])
    density_next = assembled(density_own, 0, rim_cross, rim_mates)
    return density_next, inverse_next


def solution(mesh):
    blocks = P(("grp", "row", "inner"), None, None, None)
    return jax.shard_map(
        on_device,
        mesh=mesh,
        in_specs=(blocks, blocks, P(("grp", "row", "inner"), None)),
        out_specs=(blocks, blocks),
        check_vma=False,
    )
```

```python
import functools

import jax
import jax.numpy as jnp
from jax import lax
from jax.experimental import pallas as pl
from jax.experimental.pallas import tpu as pltpu
from jax.sharding import PartitionSpec as P

RING = ("row", "inner")
MIB = 1024 * 1024


class Frame:
    def __init__(self, half, order):
        self.h = half
        self.b = order
        self.k = 2 * half
        self.p = half // 2
        self.t = 2 * order
        self.group = half * order
        self.pairs = 3 * self.p
        self.own_pairs = range(self.p, 2 * self.p)
        self.edge_rows = [*range(self.p), *range(2 * self.p, 3 * self.p)]

    def tiles(self, columns):
        for col in columns:
            for row in range(max(0, col - self.p), min(self.pairs, col + self.p + 1)):
                yield row, col

    def inner(self, row, col):
        return max(row, col) - self.p, min(row, col) + self.p + 1

    def clipped(self, row, col):
        lo, hi = self.inner(row, col)
        return max(lo, 0), min(hi, self.pairs)

    def on_corner(self, row, col):
        return max(row, col) < self.p or min(row, col) >= 2 * self.p

    def corner_place(self, row, col):
        r, c = (row, col) if row < self.p else (row - self.p, col - 2 * self.p)
        return r, r + 1, c, c + 1

    def split(self, row, col):
        lo, hi = self.clipped(row, col)
        for g in range(3):
            a, z = max(lo, g * self.p), min(hi, (g + 1) * self.p)
            if a < z:
                yield g, a - g * self.p, z - g * self.p


def under(h):
    return [(r, c) for r in range(h) for c in range(r + 1)]


def over(h):
    return [(r, c) for r in range(h) for c in range(r, h)]


def full(h):
    return [(r, c) for r in range(h) for c in range(h)]


def at(f, row_lo, row_hi, col_lo, col_hi):
    t = f.t
    return pl.ds(row_lo * t, (row_hi - row_lo) * t), pl.ds(col_lo * t, (col_hi - col_lo) * t)


def block(f, r, c):
    return pl.ds(r * f.b, f.b), pl.ds(c * f.b, f.b)


def banded(f, row, lo, hi):
    return at(f, row, row + 1, lo - row + f.p, hi - row + f.p)


def dot(a, b):
    return jnp.dot(a, b, preferred_element_type=jnp.float32)


def stored(rows, r, offset, dropped, slots=None):
    last = (rows.shape[1] if slots is None else slots) - 1
    slot = jnp.minimum(offset - (offset > dropped).astype(jnp.int32), last)
    value = rows[r, slot] if slots is None else rows((r, slot))
    return jnp.where(offset == dropped, jnp.zeros_like(value), value)


def masked(f, tile, row, col, drop_ref):
    b = f.b
    parts = []
    for i in range(2):
        r = 2 * row + i
        line = []
        for j in range(2):
            offset = 2 * col + j - r + f.h
            piece = tile[i * b : (i + 1) * b, j * b : (j + 1) * b]
            if 0 <= offset <= f.k:
                piece = jnp.where(drop_ref[r] == offset, 0.0, piece)
            else:
                piece = jnp.zeros_like(piece)
            line.append(piece)
        parts.append(jnp.concatenate(line, axis=1))
    return jnp.concatenate(parts, axis=0)


def odd_place(f, drop_ref):
    return drop_ref[3 * f.h] == 1


def indexed(f, ref, first=0):
    return lambda i: ref[block(f, first + i, 0)]


def plain(ref):
    return lambda place: ref[place]


def sides(f, drop_ref, mate, cross):
    odd = odd_place(f, drop_ref)

    def below(key):
        return jnp.where(odd, mate(key), cross(key))

    def above(key):
        return jnp.where(odd, cross(key), mate(key))

    return below, above


def spread(f, dest, row, col, read, places):
    index = {place: i for i, place in enumerate(places)}
    for r in range(f.h):
        for c in range(f.h):
            i = index.get((r, c))
            dest[block(f, row + r, col + c)] = jnp.zeros((f.b, f.b), dest.dtype) if i is None else read(i)


def pack_edges(f, drop_ref, low, high, to_cross, *to_mate):
    odd = odd_place(f, drop_ref)
    parts = len(to_mate)
    for i, (lower, upper) in enumerate(zip(under(f.h), over(f.h))):
        back, forth = low[block(f, *lower)], high[block(f, *upper)]
        to_cross[block(f, i, 0)] = jnp.where(odd, forth, back)
        to_mate[i % parts][block(f, i // parts, 0)] = jnp.where(odd, back, forth)


def slabs_kernel(f, drop_ref, own, corner, corner_again, to_mate, to_cross):
    h = f.h
    odd = drop_ref[h] == 1
    n = len(under(h))
    for i, (lower, upper) in enumerate(zip(under(h), over(h))):
        (r, c), (s, d) = lower, upper
        forth = stored(own, r, 2 * h + c - r, drop_ref[r])
        back = stored(own, s, d - s, drop_ref[s])
        to_mate[block(f, i, 0)] = jnp.where(odd, back, forth)
        to_cross[block(f, i, 0)] = jnp.where(odd, forth, back)
    for i, (r, c) in enumerate(full(h)):
        value = stored(own, r, c - r + h, drop_ref[r])
        corner[block(f, i, 0)] = value
        corner_again[block(f, i, 0)] = value
        to_mate[block(f, n + i, 0)] = value


def forward_kernel(f, drop_ref, cross, *refs):
    h = f.h
    odd = odd_place(f, drop_ref)
    to_mate, to_far = refs[-5:-3], refs[-3]
    for i, (lower, upper) in enumerate(zip(under(h), over(h))):
        (r, c), (s, d) = lower, upper
        forth = stored(cross, r, 2 * h + c - r, jnp.where(odd, drop_ref[2 * h + r], drop_ref[r]))
        back = stored(cross, s, d - s, jnp.where(odd, drop_ref[2 * h + s], drop_ref[s]))
        part, place = i % 2, i // 2
        to_mate[part][block(f, place, 0)] = jnp.where(odd, back, forth)
        to_far[block(f, i, 0)] = jnp.where(odd, forth, back)


def square_kernel(f, drop_ref, own, cross, mate, square, shifted, reach, here, partial, wide):
    h, p = f.h, f.p
    below, above = sides(f, drop_ref, plain(mate), plain(cross))
    for g, read in enumerate((below, plain(own), above)):
        for r in range(h):
            row = g * h + r
            first = 2 * (row // 2) - h
            for col in range(first, first + 2 * h + 2):
                offset = col - row + h
                if 0 <= offset <= f.k:
                    value = stored(read, r, offset, drop_ref[row], f.k)
                else:
                    value = jnp.zeros((f.b, f.b), wide.dtype)
                wide[block(f, row, col + h)] = value
    for i in range(h):
        for g, row in enumerate((i, 2 * h + i)):
            rows = pl.ds((g * h + i) * f.b, f.b)
            source = pl.ds(row * f.b, f.b)
            reach[rows, :] = wide[source, pl.ds(4 * g * f.group, f.group)]
            here[rows, :] = wide[source, pl.ds((2 * g + 1) * f.group, f.group)]
    unit = unit_tile(f)
    for row, col in f.tiles(range(f.pairs)):
        lo, hi = f.clipped(row, col)
        total = dot(
            wide[at(f, row, row + 1, lo + p, hi + p)], wide[at(f, lo, hi, col + p, col + p + 1)]
        )
        if f.on_corner(row, col):
            partial[at(f, *f.corner_place(row, col))] = total
            continue
        total = masked(f, total, row, col, drop_ref)
        place = banded(f, row, col, col + 1)
        tile = wide[at(f, row, row + 1, col + p, col + p + 1)].astype(jnp.float32)
        square[place] = total.astype(square.dtype)
        shifted[place] = moved(total, tile, unit if row == col else None).astype(shifted.dtype)


def unit_tile(f):
    rows = lax.broadcasted_iota(jnp.int32, (f.t, f.t), 0)
    return (rows == lax.broadcasted_iota(jnp.int32, (f.t, f.t), 1)).astype(jnp.float32)


def moved(total, tile, unit):
    value = 2.0 * total - 2.0 * tile
    return value if unit is None else value + unit


def corners_kernel(
    f, drop_ref, far_far, far_mate, far_mate_too, reach, here, partial, square, shifted, low, high
):
    p = f.p
    far_mates = [indexed(f, far_mate), indexed(f, far_mate_too)]
    far_below, far_above = sides(f, drop_ref, lambda i: far_mates[i % 2](i // 2), indexed(f, far_far))
    spread(f, low, 0, 0, far_below, under(f.h))
    spread(f, high, 0, 0, far_above, over(f.h))
    unit = unit_tile(f)
    for row, col in f.tiles(range(f.pairs)):
        if not f.on_corner(row, col):
            continue
        place = at(f, *f.corner_place(row, col))
        r, _, c, _ = f.corner_place(row, col)
        total = partial[place]
        if row < p:
            a, z, far = max(row, col), p, low
        else:
            a, z, far = 0, min(row, col) - 2 * p + 1, high
        if a < z:
            total = total + dot(reach[at(f, r, r + 1, a, z)], far[at(f, a, z, c, c + 1)])
        total = masked(f, total, row, col, drop_ref)
        tile = here[place].astype(jnp.float32)
        square[place] = total.astype(square.dtype)
        shifted[place] = moved(total, tile, unit if row == col else None).astype(shifted.dtype)


def right_tile(f, left, corners, right, row, col):
    lo, hi = f.clipped(row, col)
    total = None
    if row < f.p:
        inside = corners[at(f, row, row + 1, lo, f.p)]
        total = dot(inside, right[at(f, lo, f.p, col - f.p, col - f.p + 1)])
        lo = f.p
    elif row >= 2 * f.p:
        inside = corners[at(f, row - f.p, row - f.p + 1, 0, hi - 2 * f.p)]
        total = dot(inside, right[at(f, 2 * f.p, hi, col - f.p, col - f.p + 1)])
        hi = 2 * f.p
    rest = dot(left[banded(f, row, lo, hi)], right[at(f, lo, hi, col - f.p, col - f.p + 1)])
    return rest if total is None else total + rest


def first_sweep_kernel(
    f, drop_ref, shifted, corners, corner, sent_mate, sent_cross, mate, cross,
    correction, fresh, partial, whole, before, after,
):
    h, p = f.h, f.p
    from_below, from_above = sides(f, drop_ref, indexed(f, mate), indexed(f, cross))
    down, up = sides(f, drop_ref, indexed(f, sent_mate), indexed(f, sent_cross))
    spread(f, whole, 0, 0, from_below, under(h))
    spread(f, whole, h, 0, indexed(f, corner), full(h))
    spread(f, whole, 2 * h, 0, from_above, over(h))
    spread(f, before, 0, 0, down, over(h))
    spread(f, after, 0, 0, up, under(h))
    for row, col in f.tiles(f.own_pairs):
        total = masked(f, right_tile(f, shifted, corners, whole, row, col), row, col, drop_ref)
        correction[at(f, row, row + 1, col - p, col - p + 1)] = total.astype(correction.dtype)
    for row, col in f.tiles(f.own_pairs):
        c = col - p
        own_row = row in f.own_pairs
        total = 2.0 * whole[at(f, row, row + 1, c, c + 1)].astype(jnp.float32)
        for g, a, z in f.split(row, col):
            if g == 1:
                left = whole[at(f, row, row + 1, a, z)]
            elif own_row:
                left = (before, None, after)[g][at(f, row - p, row - p + 1, a, z)]
            else:
                continue
            total = total - dot(left, correction[at(f, g * p + a, g * p + z, c, c + 1)])
        if own_row:
            total = masked(f, total, row, col, drop_ref)
            fresh[at(f, row - p, row - p + 1, c, c + 1)] = total.astype(fresh.dtype)
        else:
            place = row if row < p else row - p
            partial[at(f, place, place + 1, c, c + 1)] = total


def edges(f, drop_ref, corner_below, corner_above, correction, start, low, high):
    p = f.p
    for row, col in f.tiles(f.own_pairs):
        if row in f.own_pairs:
            continue
        c = col - p
        side = 0 if row < p else 2
        corner, dest = ((corner_below, low), None, (corner_above, high))[side]
        local = row - side * p
        total = start(row, col)
        for g, a, z in f.split(row, col):
            if g == side:
                total = total - dot(
                    corner(at(f, local, local + 1, a, z)), correction[at(f, g * p + a, g * p + z, c, c + 1)]
                )
        total = masked(f, total, row, col, drop_ref)
        dest[at(f, local, local + 1, c, c + 1)] = total.astype(dest.dtype)


def first_edges_kernel(
    f, drop_ref, mate, cross, correction, partial, low, high, to_cross, to_mate, before, after
):
    p = f.p
    below, above = sides(f, drop_ref, indexed(f, mate, len(under(f.h))), indexed(f, cross))
    spread(f, before, 0, 0, below, full(f.h))
    spread(f, after, 0, 0, above, full(f.h))

    def start(row, col):
        place = row if row < p else row - p
        return partial[at(f, place, place + 1, col - p, col - p + 1)]

    edges(f, drop_ref, plain(before), plain(after), correction, start, low, high)
    pack_edges(f, drop_ref, low, high, to_cross, to_mate)


def gather(f, whole, low, own, high):
    for g, source in enumerate((low, own, high)):
        for i in range(f.h):
            whole[pl.ds(g * f.group + i * f.b, f.b), :] = source[pl.ds(i * f.b, f.b), :]


def correction_kernel(f, drop_ref, shifted, corners, low, own, high, correction, whole):
    p = f.p
    gather(f, whole, low, own, high)
    for row, col in f.tiles(f.own_pairs):
        total = masked(f, right_tile(f, shifted, corners, whole, row, col), row, col, drop_ref)
        correction[at(f, row, row + 1, col - p, col - p + 1)] = total.astype(correction.dtype)


def second_edges_kernel(
    f, drop_ref, cross, mate, correction, low, high, new_low, new_high, to_cross, to_mate
):
    p = f.p

    def start(row, col):
        c = col - p
        source, local = (low, row) if row < p else (high, row - 2 * p)
        total = 2.0 * source[at(f, local, local + 1, c, c + 1)].astype(jnp.float32)
        for g, a, z in f.split(row, col):
            if g == 1:
                total = total - dot(
                    source[at(f, local, local + 1, a, z)], correction[at(f, p + a, p + z, c, c + 1)]
                )
        return total

    below, above = sides(f, drop_ref, plain(mate), plain(cross))
    edges(f, drop_ref, below, above, correction, start, new_low, new_high)
    pack_edges(f, drop_ref, new_low, new_high, to_cross, to_mate)


def density_edges_kernel(
    f, drop_ref, own, cross, mate, correction, new_low, new_high, square, corners, whole, to_cross, to_mate,
    to_mate_too, before, after, low, high,
):
    h, p = f.h, f.p
    below, above = sides(f, drop_ref, indexed(f, mate), indexed(f, cross))
    spread(f, before, 0, 0, below, over(h))
    spread(f, after, 0, 0, above, under(h))
    for row, col in f.tiles(f.own_pairs):
        if row not in f.own_pairs:
            continue
        c, local = col - p, row - p
        total = 2.0 * own[at(f, local, local + 1, c, c + 1)].astype(jnp.float32)
        for g, a, z in f.split(row, col):
            left = (before, own, after)[g][at(f, local, local + 1, a, z)]
            total = total - dot(left, correction[at(f, g * p + a, g * p + z, c, c + 1)])
        total = masked(f, total, row, col, drop_ref)
        whole[at(f, row, row + 1, c, c + 1)] = total.astype(whole.dtype)
    for i in range(h):
        rows = pl.ds(i * f.b, f.b)
        whole[pl.ds(i * f.b, f.b), :] = new_low[rows, :]
        whole[pl.ds(2 * f.group + i * f.b, f.b), :] = new_high[rows, :]
    for row, col in f.tiles(f.own_pairs):
        if row in f.own_pairs:
            continue
        total = masked(f, right_tile(f, square, corners, whole, row, col), row, col, drop_ref)
        dest, local = (low, row) if row < p else (high, row - 2 * p)
        dest[at(f, local, local + 1, col - p, col - p + 1)] = total.astype(dest.dtype)
    pack_edges(f, drop_ref, low, high, to_cross, to_mate, to_mate_too)


def density_own_kernel(f, drop_ref, square, whole, out):
    p = f.p
    for row, col in f.tiles(f.own_pairs):
        if row in f.own_pairs:
            total = masked(f, right_tile(f, square, None, whole, row, col), row, col, drop_ref)
            out[at(f, row - p, row - p + 1, col - p, col - p + 1)] = total.astype(out.dtype)


def slots_kernel(f, first, parts, drop_ref, own, *refs):
    h = f.h
    mates = [indexed(f, ref) for ref in refs[:parts]]
    slots, out, sem = refs[parts:]
    over_index = {place: i for i, place in enumerate(over(h))}
    under_index = {place: i for i, place in enumerate(under(h))}

    def mate_block(i):
        return mates[i % parts](i // parts)

    for r in range(h):
        dropped = drop_ref[h + r]

        def at_offset(offset, r=r):
            col = r + offset
            if col < h:
                return mate_block(over_index[r, col])
            if col < 2 * h:
                return own[block(f, first + r, col - h)]
            return mate_block(under_index[r, col - 2 * h])

        for s in range(f.k):
            slots[r, s] = jnp.where(dropped <= s, at_offset(s + 1), at_offset(s))
    copy = pltpu.make_async_copy(slots, out, sem)
    copy.start()
    copy.wait()


def last_slots_kernel(f, drop_ref, slots, cross, unused, out, side, sems):
    h, k = f.h, f.k
    odd = odd_place(f, drop_ref)
    cross_block = indexed(f, cross)
    over_index = {place: i for i, place in enumerate(over(h))}
    under_index = {place: i for i, place in enumerate(under(h))}

    def fill(low):
        copies = []
        for r in range(h) if low else reversed(range(h)):
            dropped = drop_ref[h + r]
            lo, hi = (0, h - r) if low else (k - 1 - r, k)
            for s in range(lo, hi):

                def at_offset(offset, r=r, s=s):
                    col = r + offset
                    if low and col < h:
                        return cross_block(over_index[r, col])
                    if not low and col >= 2 * h:
                        return cross_block(under_index[r, col - 2 * h])
                    return slots[r, s]

                side[r, s] = jnp.where(dropped <= s, at_offset(s + 1), at_offset(s))
            copy = pltpu.make_async_copy(
                side.at[r, pl.ds(lo, hi - lo)], out.at[r, pl.ds(lo, hi - lo)], sems.at[r]
            )
            copy.start()
            copies.append(copy)
        for copy in copies:
            copy.wait()

    @pl.when(odd)
    def _():
        fill(False)

    @pl.when(jnp.logical_not(odd))
    def _():
        fill(True)


VMEM = pl.BlockSpec(memory_space=pltpu.VMEM)
SMEM = pl.BlockSpec(memory_space=pltpu.SMEM)
ANY = pl.BlockSpec(memory_space=pl.ANY)


def call(kernel, outs, scratch, flops, limit, drop, *args, passed=(), light=False, off=0):
    moved = sum(a.size * a.dtype.itemsize for a in args) + sum(s.size * s.dtype.itemsize for s in outs)
    if light:
        flops = moved = 0
    n = len(args)
    return pl.pallas_call(
        kernel,
        out_shape=[*outs, *[jax.ShapeDtypeStruct(a.shape, a.dtype) for a in passed]],
        in_specs=[SMEM] + [VMEM] * n + [ANY] * len(passed),
        out_specs=[VMEM] * (len(outs) - off) + [ANY] * (off + len(passed)),
        scratch_shapes=scratch,
        input_output_aliases={1 + n + i: len(outs) + i for i in range(len(passed))},
        compiler_params=pltpu.CompilerParams(vmem_limit_bytes=limit * MIB),
        cost_estimate=pl.CostEstimate(flops=flops, bytes_accessed=moved, transcendentals=0),
    )(drop, *args, *passed)


def routed(x, step):
    size = lax.axis_size(RING)
    return lax.ppermute(x, RING, [(i, (i + step(i)) % size) for i in range(size) if step(i)])


def on_device(density, inverse_start, block_cols):
    rows, width, order, _ = density.shape
    half = width // 2
    ring = lax.axis_size(RING)
    total = rows * ring
    assert rows == half and half % 2 == 0 and ring % 2 == 0
    f = Frame(half, order)
    kind = density.dtype
    me = lax.axis_index(RING)

    def mate_step(i):
        return 1 - 2 * (i % 2)

    def cross_step(i):
        return 2 * (i % 2) - 1

    def to_mate(x):
        return routed(x, mate_step)

    def to_cross(x):
        return routed(x, cross_step)

    positions = block_cols - (me * rows + jnp.arange(rows, dtype=jnp.int32))[:, None] + half
    positions = positions + jnp.where(positions < 0, total, jnp.where(positions >= total, -total, 0))
    own_drop = width * (width + 1) // 2 - jnp.sum(positions, axis=1)

    density_cross, density_mate = to_cross(density), to_mate(density)
    cross_drop, mate_drop = to_cross(own_drop), to_mate(own_drop)
    even = (me & 1) == 0
    mark = jnp.reshape(me & 1, (1,))
    start_drop = jnp.concatenate([own_drop, mark])
    drop = jnp.concatenate(
        [jnp.where(even, cross_drop, mate_drop), own_drop, jnp.where(even, mate_drop, cross_drop), mark]
    )

    unit = 2 * f.t**3
    count = half * (half + 1) // 2
    square_group = jax.ShapeDtypeStruct((f.group, f.group), kind)
    columns = jax.ShapeDtypeStruct((3 * f.group, f.group), kind)
    band = jax.ShapeDtypeStruct((3 * f.group, (2 * f.p + 1) * f.t), kind)
    triangle = jax.ShapeDtypeStruct((count * order, order), kind)
    half_triangle = jax.ShapeDtypeStruct((count // 2 * order, order), kind)
    listed = jax.ShapeDtypeStruct((half * half * order, order), kind)
    both = jax.ShapeDtypeStruct(((count + half * half) * order, order), kind)
    partial_sums = jax.ShapeDtypeStruct((2 * f.group, f.group), jnp.float32)
    group_scratch = pltpu.VMEM((f.group, f.group), kind)
    whole_scratch = pltpu.VMEM((3 * f.group, f.group), kind)

    def run(kernel, outs, scratch, tiles, limit, *args, **kw):
        return call(functools.partial(kernel, f), outs, scratch, tiles * unit, limit, *args, **kw)

    corner, corner_cross, slab_mate, triangle_cross = run(
        slabs_kernel, [listed, listed, both, triangle], [], 0, 12, start_drop, inverse_start
    )
    from_mate = to_mate(slab_mate)
    forward_mate, forward_mate_too, forward_far, triangle_cross, corner_cross = run(
        forward_kernel, [half_triangle, half_triangle, triangle], [], 0, 12, drop, density_cross, density_mate, from_mate,
        passed=(triangle_cross, corner_cross),
    )
    far_mate, far_mate_too = to_mate(forward_mate), to_mate(forward_mate_too)
    far_far = routed(forward_far, lambda i: 3 * cross_step(i))
    cross_triangle = to_cross(triangle_cross)
    cross_corner = to_cross(corner_cross)

    both_corners = jax.ShapeDtypeStruct((2 * f.group, f.group), kind)
    square, shifted, reach, here, partial = run(
        square_kernel,
        [band, band, both_corners, both_corners, partial_sums],
        [pltpu.VMEM((3 * f.group, 5 * f.group), kind)],
        84, 26, drop, density, density_cross, density_mate,
    )
    square_corners, shifted_corners = run(
        corners_kernel,
        [both_corners, both_corners],
        [group_scratch] * 2,
        10, 16, drop, far_far, far_mate, far_mate_too, reach, here, partial, light=True,
    )
    correction, own, partial = run(
        first_sweep_kernel,
        [columns, square_group, partial_sums],
        [whole_scratch, group_scratch, group_scratch],
        66, 24, drop, shifted, shifted_corners, corner, slab_mate, triangle_cross, from_mate, cross_triangle, light=True,
    )
    corner_cross, corner_mate = to_cross(own), to_mate(own)
    low, high, edge_cross, edge_mate = run(
        first_edges_kernel,
        [square_group, square_group, triangle, triangle],
        [group_scratch] * 2,
        10, 16, drop, from_mate, cross_corner, correction, partial,
    )
    edge_cross, edge_mate = to_cross(edge_cross), to_mate(edge_mate)
    (correction,) = run(
        correction_kernel, [columns], [whole_scratch], 38, 16, drop, shifted, shifted_corners, low, own, high
    )
    new_low, new_high, inverse_cross, inverse_mate = run(
        second_edges_kernel,
        [square_group, square_group, triangle, triangle],
        [],
        20, 12, drop, corner_cross, corner_mate, correction, low, high,
    )
    inverse_cross, inverse_mate = to_cross(inverse_cross), to_mate(inverse_mate)
    whole, rim_cross, rim_mate, rim_mate_too = run(
        density_edges_kernel,
        [columns, triangle, half_triangle, half_triangle],
        [group_scratch] * 4,
        38, 20, drop, own, edge_cross, edge_mate, correction, new_low, new_high, square,
        square_corners,
    )
    rim_cross, rim_mates = to_cross(rim_cross), [to_mate(rim_mate), to_mate(rim_mate_too)]
    (density_own,) = run(density_own_kernel, [square_group], [], 18, 12, drop, square, whole)
    out = jax.ShapeDtypeStruct(density.shape, kind)

    def assembled(own, first, cross, mates):
        kernel = functools.partial(slots_kernel, f, first, len(mates))
        scratch = [pltpu.SemaphoreType.DMA(())]
        slots, early = call(kernel, [out, out], scratch, 0, 8, drop, own, *mates, light=True, off=1)
        scratch = [pltpu.VMEM(out.shape, kind), pltpu.SemaphoreType.DMA((half,))]
        kernel = functools.partial(last_slots_kernel, f)
        return call(kernel, [], scratch, 0, 8, drop, slots, cross, passed=(early,), light=True)[0]

    inverse_next = assembled(whole, half, inverse_cross, [inverse_mate])
    density_next = assembled(density_own, 0, rim_cross, rim_mates)
    return density_next, inverse_next


def solution(mesh):
    blocks = P(("grp", "row", "inner"), None, None, None)
    return jax.shard_map(
        on_device,
        mesh=mesh,
        in_specs=(blocks, blocks, P(("grp", "row", "inner"), None)),
        out_specs=(blocks, blocks),
        check_vma=False,
    )
```

```python
import functools

import jax
import jax.numpy as jnp
from jax import lax
from jax.experimental import pallas as pl
from jax.experimental.pallas import tpu as pltpu
from jax.sharding import PartitionSpec as P

RING = ("row", "inner")
MIB = 1024 * 1024


class Frame:
    def __init__(self, half, order):
        self.h = half
        self.b = order
        self.k = 2 * half
        self.p = half // 2
        self.t = 2 * order
        self.group = half * order
        self.pairs = 3 * self.p
        self.own_pairs = range(self.p, 2 * self.p)
        self.edge_rows = [*range(self.p), *range(2 * self.p, 3 * self.p)]

    def tiles(self, columns):
        for col in columns:
            for row in range(max(0, col - self.p), min(self.pairs, col + self.p + 1)):
                yield row, col

    def inner(self, row, col):
        return max(row, col) - self.p, min(row, col) + self.p + 1

    def clipped(self, row, col):
        lo, hi = self.inner(row, col)
        return max(lo, 0), min(hi, self.pairs)

    def on_corner(self, row, col):
        return max(row, col) < self.p or min(row, col) >= 2 * self.p

    def corner_place(self, row, col):
        r, c = (row, col) if row < self.p else (row - self.p, col - 2 * self.p)
        return r, r + 1, c, c + 1

    def split(self, row, col):
        lo, hi = self.clipped(row, col)
        for g in range(3):
            a, z = max(lo, g * self.p), min(hi, (g + 1) * self.p)
            if a < z:
                yield g, a - g * self.p, z - g * self.p


def under(h):
    return [(r, c) for r in range(h) for c in range(r + 1)]


def over(h):
    return [(r, c) for r in range(h) for c in range(r, h)]


def full(h):
    return [(r, c) for r in range(h) for c in range(h)]


def at(f, row_lo, row_hi, col_lo, col_hi):
    t = f.t
    return pl.ds(row_lo * t, (row_hi - row_lo) * t), pl.ds(col_lo * t, (col_hi - col_lo) * t)


def block(f, r, c):
    return pl.ds(r * f.b, f.b), pl.ds(c * f.b, f.b)


def banded(f, row, lo, hi):
    return at(f, row, row + 1, lo - row + f.p, hi - row + f.p)


def dot(a, b):
    return jnp.dot(a, b, preferred_element_type=jnp.float32)


def stored(rows, r, offset, dropped, slots=None):
    last = (rows.shape[1] if slots is None else slots) - 1
    slot = jnp.minimum(offset - (offset > dropped).astype(jnp.int32), last)
    value = rows[r, slot] if slots is None else rows((r, slot))
    return jnp.where(offset == dropped, jnp.zeros_like(value), value)


def masked(f, tile, row, col, drop_ref):
    b = f.b
    parts = []
    for i in range(2):
        r = 2 * row + i
        line = []
        for j in range(2):
            offset = 2 * col + j - r + f.h
            piece = tile[i * b : (i + 1) * b, j * b : (j + 1) * b]
            if 0 <= offset <= f.k:
                piece = jnp.where(drop_ref[r] == offset, 0.0, piece)
            else:
                piece = jnp.zeros_like(piece)
            line.append(piece)
        parts.append(jnp.concatenate(line, axis=1))
    return jnp.concatenate(parts, axis=0)


def odd_place(f, drop_ref):
    return drop_ref[3 * f.h] == 1


def indexed(f, ref, first=0):
    return lambda i: ref[block(f, first + i, 0)]


def plain(ref):
    return lambda place: ref[place]


def sides(f, drop_ref, mate, cross):
    odd = odd_place(f, drop_ref)

    def below(key):
        return jnp.where(odd, mate(key), cross(key))

    def above(key):
        return jnp.where(odd, cross(key), mate(key))

    return below, above


def spread(f, dest, row, col, read, places):
    index = {place: i for i, place in enumerate(places)}
    for r in range(f.h):
        for c in range(f.h):
            i = index.get((r, c))
            dest[block(f, row + r, col + c)] = jnp.zeros((f.b, f.b), dest.dtype) if i is None else read(i)


def pack_edges(f, drop_ref, low, high, to_cross, *to_mate):
    odd = odd_place(f, drop_ref)
    parts = len(to_mate)
    for i, (lower, upper) in enumerate(zip(under(f.h), over(f.h))):
        back, forth = low[block(f, *lower)], high[block(f, *upper)]
        to_cross[block(f, i, 0)] = jnp.where(odd, forth, back)
        to_mate[i % parts][block(f, i // parts, 0)] = jnp.where(odd, back, forth)


def slabs_kernel(f, drop_ref, own, corner, corner_again, to_mate, to_cross):
    h = f.h
    odd = drop_ref[h] == 1
    n = len(under(h))
    for i, (lower, upper) in enumerate(zip(under(h), over(h))):
        (r, c), (s, d) = lower, upper
        forth = stored(own, r, 2 * h + c - r, drop_ref[r])
        back = stored(own, s, d - s, drop_ref[s])
        to_mate[block(f, i, 0)] = jnp.where(odd, back, forth)
        to_cross[block(f, i, 0)] = jnp.where(odd, forth, back)
    for i, (r, c) in enumerate(full(h)):
        value = stored(own, r, c - r + h, drop_ref[r])
        corner[block(f, i, 0)] = value
        corner_again[block(f, i, 0)] = value
        to_mate[block(f, n + i, 0)] = value


def forward_kernel(f, drop_ref, cross, *refs):
    h = f.h
    odd = odd_place(f, drop_ref)
    to_mate, to_far = refs[-5:-3], refs[-3]
    for i, (lower, upper) in enumerate(zip(under(h), over(h))):
        (r, c), (s, d) = lower, upper
        forth = stored(cross, r, 2 * h + c - r, jnp.where(odd, drop_ref[2 * h + r], drop_ref[r]))
        back = stored(cross, s, d - s, jnp.where(odd, drop_ref[2 * h + s], drop_ref[s]))
        part, place = i % 2, i // 2
        to_mate[part][block(f, place, 0)] = jnp.where(odd, back, forth)
        to_far[block(f, i, 0)] = jnp.where(odd, forth, back)


def square_kernel(f, drop_ref, own, cross, mate, square, shifted, reach, here, partial, wide):
    h, p = f.h, f.p
    below, above = sides(f, drop_ref, plain(mate), plain(cross))
    for g, read in enumerate((below, plain(own), above)):
        for r in range(h):
            row = g * h + r
            first = 2 * (row // 2) - h
            for col in range(first, first + 2 * h + 2):
                offset = col - row + h
                if 0 <= offset <= f.k:
                    value = stored(read, r, offset, drop_ref[row], f.k)
                else:
                    value = jnp.zeros((f.b, f.b), wide.dtype)
                wide[block(f, row, col + h)] = value
    for i in range(h):
        for g, row in enumerate((i, 2 * h + i)):
            rows = pl.ds((g * h + i) * f.b, f.b)
            source = pl.ds(row * f.b, f.b)
            reach[rows, :] = wide[source, pl.ds(4 * g * f.group, f.group)]
            here[rows, :] = wide[source, pl.ds((2 * g + 1) * f.group, f.group)]
    unit = unit_tile(f)
    for row, col in f.tiles(range(f.pairs)):
        lo, hi = f.clipped(row, col)
        total = dot(
            wide[at(f, row, row + 1, lo + p, hi + p)], wide[at(f, lo, hi, col + p, col + p + 1)]
        )
        if f.on_corner(row, col):
            partial[at(f, *f.corner_place(row, col))] = total
            continue
        total = masked(f, total, row, col, drop_ref)
        place = banded(f, row, col, col + 1)
        tile = wide[at(f, row, row + 1, col + p, col + p + 1)].astype(jnp.float32)
        square[place] = total.astype(square.dtype)
        shifted[place] = moved(total, tile, unit if row == col else None).astype(shifted.dtype)


def unit_tile(f):
    rows = lax.broadcasted_iota(jnp.int32, (f.t, f.t), 0)
    return (rows == lax.broadcasted_iota(jnp.int32, (f.t, f.t), 1)).astype(jnp.float32)


def moved(total, tile, unit):
    value = 2.0 * total - 2.0 * tile
    return value if unit is None else value + unit


def corners_kernel(
    f, drop_ref, far_far, far_mate, far_mate_too, reach, here, partial, square, shifted, low, high
):
    p = f.p
    far_mates = [indexed(f, far_mate), indexed(f, far_mate_too)]
    far_below, far_above = sides(f, drop_ref, lambda i: far_mates[i % 2](i // 2), indexed(f, far_far))
    spread(f, low, 0, 0, far_below, under(f.h))
    spread(f, high, 0, 0, far_above, over(f.h))
    unit = unit_tile(f)
    for row, col in f.tiles(range(f.pairs)):
        if not f.on_corner(row, col):
            continue
        place = at(f, *f.corner_place(row, col))
        r, _, c, _ = f.corner_place(row, col)
        total = partial[place]
        if row < p:
            a, z, far = max(row, col), p, low
        else:
            a, z, far = 0, min(row, col) - 2 * p + 1, high
        if a < z:
            total = total + dot(reach[at(f, r, r + 1, a, z)], far[at(f, a, z, c, c + 1)])
        total = masked(f, total, row, col, drop_ref)
        tile = here[place].astype(jnp.float32)
        square[place] = total.astype(square.dtype)
        shifted[place] = moved(total, tile, unit if row == col else None).astype(shifted.dtype)


def right_tile(f, left, corners, right, row, col):
    lo, hi = f.clipped(row, col)
    total = None
    if row < f.p:
        inside = corners[at(f, row, row + 1, lo, f.p)]
        total = dot(inside, right[at(f, lo, f.p, col - f.p, col - f.p + 1)])
        lo = f.p
    elif row >= 2 * f.p:
        inside = corners[at(f, row - f.p, row - f.p + 1, 0, hi - 2 * f.p)]
        total = dot(inside, right[at(f, 2 * f.p, hi, col - f.p, col - f.p + 1)])
        hi = 2 * f.p
    rest = dot(left[banded(f, row, lo, hi)], right[at(f, lo, hi, col - f.p, col - f.p + 1)])
    return rest if total is None else total + rest


def first_sweep_kernel(
    f, drop_ref, shifted, corners, corner, sent_mate, sent_cross, mate, cross,
    correction, fresh, whole, before, after,
):
    h, p = f.h, f.p
    from_below, from_above = sides(f, drop_ref, indexed(f, mate), indexed(f, cross))
    down, up = sides(f, drop_ref, indexed(f, sent_mate), indexed(f, sent_cross))
    spread(f, whole, 0, 0, from_below, under(h))
    spread(f, whole, h, 0, indexed(f, corner), full(h))
    spread(f, whole, 2 * h, 0, from_above, over(h))
    spread(f, before, 0, 0, down, over(h))
    spread(f, after, 0, 0, up, under(h))
    for row, col in f.tiles(f.own_pairs):
        total = masked(f, right_tile(f, shifted, corners, whole, row, col), row, col, drop_ref)
        correction[at(f, row, row + 1, col - p, col - p + 1)] = total.astype(correction.dtype)
    for row, col in f.tiles(f.own_pairs):
        if row not in f.own_pairs:
            continue
        c, local = col - p, row - p
        total = 2.0 * whole[at(f, row, row + 1, c, c + 1)].astype(jnp.float32)
        for g, a, z in f.split(row, col):
            source, first = (before, local) if g == 0 else (whole, row) if g == 1 else (after, local)
            left = source[at(f, first, first + 1, a, z)]
            total = total - dot(left, correction[at(f, g * p + a, g * p + z, c, c + 1)])
        total = masked(f, total, row, col, drop_ref)
        fresh[at(f, local, local + 1, c, c + 1)] = total.astype(fresh.dtype)


def edges(f, drop_ref, corner_below, corner_above, correction, start, low, high):
    p = f.p
    for row, col in f.tiles(f.own_pairs):
        if row in f.own_pairs:
            continue
        c = col - p
        side = 0 if row < p else 2
        corner, dest = ((corner_below, low), None, (corner_above, high))[side]
        local = row - side * p
        total = start(row, col)
        for g, a, z in f.split(row, col):
            if g == side:
                total = total - dot(
                    corner(at(f, local, local + 1, a, z)), correction[at(f, g * p + a, g * p + z, c, c + 1)]
                )
        total = masked(f, total, row, col, drop_ref)
        dest[at(f, local, local + 1, c, c + 1)] = total.astype(dest.dtype)


def first_edges_kernel(
    f, drop_ref, mate, cross, correction, whole, low, high, to_cross, to_mate, before, after
):
    p = f.p
    below, above = sides(f, drop_ref, indexed(f, mate, len(under(f.h))), indexed(f, cross))
    spread(f, before, 0, 0, below, full(f.h))
    spread(f, after, 0, 0, above, full(f.h))

    def start(row, col):
        c = col - p
        total = 2.0 * whole[at(f, row, row + 1, c, c + 1)].astype(jnp.float32)
        for g, a, z in f.split(row, col):
            if g == 1:
                total = total - dot(
                    whole[at(f, row, row + 1, a, z)], correction[at(f, p + a, p + z, c, c + 1)]
                )
        return total

    edges(f, drop_ref, plain(before), plain(after), correction, start, low, high)
    pack_edges(f, drop_ref, low, high, to_cross, to_mate)


def gather(f, whole, low, own, high):
    for g, source in enumerate((low, own, high)):
        for i in range(f.h):
            whole[pl.ds(g * f.group + i * f.b, f.b), :] = source[pl.ds(i * f.b, f.b), :]


def correction_kernel(f, drop_ref, shifted, corners, low, own, high, correction, whole):
    p = f.p
    gather(f, whole, low, own, high)
    for row, col in f.tiles(f.own_pairs):
        total = masked(f, right_tile(f, shifted, corners, whole, row, col), row, col, drop_ref)
        correction[at(f, row, row + 1, col - p, col - p + 1)] = total.astype(correction.dtype)


def second_edges_kernel(
    f, drop_ref, cross, mate, correction, low, high, new_low, new_high, to_cross, to_mate
):
    p = f.p

    def start(row, col):
        c = col - p
        source, local = (low, row) if row < p else (high, row - 2 * p)
        total = 2.0 * source[at(f, local, local + 1, c, c + 1)].astype(jnp.float32)
        for g, a, z in f.split(row, col):
            if g == 1:
                total = total - dot(
                    source[at(f, local, local + 1, a, z)], correction[at(f, p + a, p + z, c, c + 1)]
                )
        return total

    below, above = sides(f, drop_ref, plain(mate), plain(cross))
    edges(f, drop_ref, below, above, correction, start, new_low, new_high)
    pack_edges(f, drop_ref, new_low, new_high, to_cross, to_mate)


def density_edges_kernel(
    f, drop_ref, own, mate, cross, correction, new_low, new_high, square, corners, whole, to_cross, to_mate,
    to_mate_too, before, after, low, high,
):
    h, p = f.h, f.p
    below, above = sides(f, drop_ref, indexed(f, mate), indexed(f, cross))
    spread(f, before, 0, 0, below, over(h))
    spread(f, after, 0, 0, above, under(h))
    for row, col in f.tiles(f.own_pairs):
        if row not in f.own_pairs:
            continue
        c, local = col - p, row - p
        total = 2.0 * own[at(f, local, local + 1, c, c + 1)].astype(jnp.float32)
        for g, a, z in f.split(row, col):
            left = (before, own, after)[g][at(f, local, local + 1, a, z)]
            total = total - dot(left, correction[at(f, g * p + a, g * p + z, c, c + 1)])
        total = masked(f, total, row, col, drop_ref)
        whole[at(f, row, row + 1, c, c + 1)] = total.astype(whole.dtype)
    for i in range(h):
        rows = pl.ds(i * f.b, f.b)
        whole[pl.ds(i * f.b, f.b), :] = new_low[rows, :]
        whole[pl.ds(2 * f.group + i * f.b, f.b), :] = new_high[rows, :]
    for row, col in f.tiles(f.own_pairs):
        if row in f.own_pairs:
            continue
        total = masked(f, right_tile(f, square, corners, whole, row, col), row, col, drop_ref)
        dest, local = (low, row) if row < p else (high, row - 2 * p)
        dest[at(f, local, local + 1, col - p, col - p + 1)] = total.astype(dest.dtype)
    pack_edges(f, drop_ref, low, high, to_cross, to_mate, to_mate_too)


def density_own_kernel(f, drop_ref, square, whole, out):
    p = f.p
    for row, col in f.tiles(f.own_pairs):
        if row in f.own_pairs:
            total = masked(f, right_tile(f, square, None, whole, row, col), row, col, drop_ref)
            out[at(f, row - p, row - p + 1, col - p, col - p + 1)] = total.astype(out.dtype)


def slots_kernel(f, first, parts, drop_ref, own, *refs):
    h = f.h
    mates = [indexed(f, ref) for ref in refs[:parts]]
    slots, out, sem = refs[parts:]
    over_index = {place: i for i, place in enumerate(over(h))}
    under_index = {place: i for i, place in enumerate(under(h))}

    def mate_block(i):
        return mates[i % parts](i // parts)

    for r in range(h):
        dropped = drop_ref[h + r]

        def at_offset(offset, r=r):
            col = r + offset
            if col < h:
                return mate_block(over_index[r, col])
            if col < 2 * h:
                return own[block(f, first + r, col - h)]
            return mate_block(under_index[r, col - 2 * h])

        for s in range(f.k):
            slots[r, s] = jnp.where(dropped <= s, at_offset(s + 1), at_offset(s))
    copy = pltpu.make_async_copy(slots, out, sem)
    copy.start()
    copy.wait()


def last_slots_kernel(f, drop_ref, slots, cross, unused, out, side, sems):
    h, k = f.h, f.k
    odd = odd_place(f, drop_ref)
    cross_block = indexed(f, cross)
    over_index = {place: i for i, place in enumerate(over(h))}
    under_index = {place: i for i, place in enumerate(under(h))}

    def fill(low):
        copies = []
        for r in range(h):
            dropped = drop_ref[h + r]
            lo, hi = (0, h - r) if low else (k - 1 - r, k)
            for s in range(lo, hi):

                def at_offset(offset, r=r, s=s):
                    col = r + offset
                    if low and col < h:
                        return cross_block(over_index[r, col])
                    if not low and col >= 2 * h:
                        return cross_block(under_index[r, col - 2 * h])
                    return slots[r, s]

                side[r, s] = jnp.where(dropped <= s, at_offset(s + 1), at_offset(s))
            copy = pltpu.make_async_copy(
                side.at[r, pl.ds(lo, hi - lo)], out.at[r, pl.ds(lo, hi - lo)], sems.at[r]
            )
            copy.start()
            copies.append(copy)
        for copy in copies:
            copy.wait()

    @pl.when(odd)
    def _():
        fill(False)

    @pl.when(jnp.logical_not(odd))
    def _():
        fill(True)


VMEM = pl.BlockSpec(memory_space=pltpu.VMEM)
SMEM = pl.BlockSpec(memory_space=pltpu.SMEM)
ANY = pl.BlockSpec(memory_space=pl.ANY)


def call(kernel, outs, scratch, flops, limit, drop, *args, passed=(), light=False, off=0):
    moved = sum(a.size * a.dtype.itemsize for a in args) + sum(s.size * s.dtype.itemsize for s in outs)
    if light:
        flops = moved = 0
    n = len(args)
    return pl.pallas_call(
        kernel,
        out_shape=[*outs, *[jax.ShapeDtypeStruct(a.shape, a.dtype) for a in passed]],
        in_specs=[SMEM] + [VMEM] * n + [ANY] * len(passed),
        out_specs=[VMEM] * (len(outs) - off) + [ANY] * (off + len(passed)),
        scratch_shapes=scratch,
        input_output_aliases={1 + n + i: len(outs) + i for i in range(len(passed))},
        compiler_params=pltpu.CompilerParams(vmem_limit_bytes=limit * MIB),
        cost_estimate=pl.CostEstimate(flops=flops, bytes_accessed=moved, transcendentals=0),
    )(drop, *args, *passed)


def routed(x, step):
    size = lax.axis_size(RING)
    return lax.ppermute(x, RING, [(i, (i + step(i)) % size) for i in range(size) if step(i)])


def on_device(density, inverse_start, block_cols):
    rows, width, order, _ = density.shape
    half = width // 2
    ring = lax.axis_size(RING)
    total = rows * ring
    assert rows == half and half % 2 == 0 and ring % 2 == 0
    f = Frame(half, order)
    kind = density.dtype
    me = lax.axis_index(RING)

    def mate_step(i):
        return 1 - 2 * (i % 2)

    def cross_step(i):
        return 2 * (i % 2) - 1

    def to_mate(x):
        return routed(x, mate_step)

    def to_cross(x):
        return routed(x, cross_step)

    positions = block_cols - (me * rows + jnp.arange(rows, dtype=jnp.int32))[:, None] + half
    positions = positions + jnp.where(positions < 0, total, jnp.where(positions >= total, -total, 0))
    own_drop = width * (width + 1) // 2 - jnp.sum(positions, axis=1)

    density_cross, density_mate = to_cross(density), to_mate(density)
    cross_drop, mate_drop = to_cross(own_drop), to_mate(own_drop)
    even = (me & 1) == 0
    mark = jnp.reshape(me & 1, (1,))
    start_drop = jnp.concatenate([own_drop, mark])
    drop = jnp.concatenate(
        [jnp.where(even, cross_drop, mate_drop), own_drop, jnp.where(even, mate_drop, cross_drop), mark]
    )

    unit = 2 * f.t**3
    count = half * (half + 1) // 2
    square_group = jax.ShapeDtypeStruct((f.group, f.group), kind)
    columns = jax.ShapeDtypeStruct((3 * f.group, f.group), kind)
    band = jax.ShapeDtypeStruct((3 * f.group, (2 * f.p + 1) * f.t), kind)
    triangle = jax.ShapeDtypeStruct((count * order, order), kind)
    half_triangle = jax.ShapeDtypeStruct((count // 2 * order, order), kind)
    listed = jax.ShapeDtypeStruct((half * half * order, order), kind)
    both = jax.ShapeDtypeStruct(((count + half * half) * order, order), kind)
    partial_sums = jax.ShapeDtypeStruct((2 * f.group, f.group), jnp.float32)
    group_scratch = pltpu.VMEM((f.group, f.group), kind)
    whole_scratch = pltpu.VMEM((3 * f.group, f.group), kind)

    def run(kernel, outs, scratch, tiles, limit, *args, **kw):
        return call(functools.partial(kernel, f), outs, scratch, tiles * unit, limit, *args, **kw)

    corner, corner_cross, slab_mate, triangle_cross = run(
        slabs_kernel, [listed, listed, both, triangle], [], 0, 12, start_drop, inverse_start
    )
    from_mate = to_mate(slab_mate)
    forward_mate, forward_mate_too, forward_far, triangle_cross, corner_cross = run(
        forward_kernel, [half_triangle, half_triangle, triangle], [], 0, 12, drop, density_cross, density_mate, from_mate,
        passed=(triangle_cross, corner_cross),
    )
    far_mate, far_mate_too = to_mate(forward_mate), to_mate(forward_mate_too)
    far_far = routed(forward_far, lambda i: 3 * cross_step(i))
    cross_triangle = to_cross(triangle_cross)
    cross_corner = to_cross(corner_cross)

    both_corners = jax.ShapeDtypeStruct((2 * f.group, f.group), kind)
    square, shifted, reach, here, partial = run(
        square_kernel,
        [band, band, both_corners, both_corners, partial_sums],
        [pltpu.VMEM((3 * f.group, 5 * f.group), kind)],
        84, 26, drop, density, density_cross, density_mate,
    )
    square_corners, shifted_corners = run(
        corners_kernel,
        [both_corners, both_corners],
        [group_scratch] * 2,
        10, 16, drop, far_far, far_mate, far_mate_too, reach, here, partial, light=True,
    )
    correction, own, columns_start = run(
        first_sweep_kernel,
        [columns, square_group, columns],
        [group_scratch, group_scratch],
        56, 24, drop, shifted, shifted_corners, corner, slab_mate, triangle_cross, from_mate, cross_triangle, light=True,
    )
    corner_cross, corner_mate = to_cross(own), to_mate(own)
    low, high, edge_cross, edge_mate = run(
        first_edges_kernel,
        [square_group, square_group, triangle, triangle],
        [group_scratch] * 2,
        20, 16, drop, from_mate, cross_corner, correction, columns_start,
    )
    edge_cross, edge_mate = to_cross(edge_cross), to_mate(edge_mate)
    (correction,) = run(
        correction_kernel, [columns], [whole_scratch], 38, 16, drop, shifted, shifted_corners, low, own, high
    )
    new_low, new_high, inverse_cross, inverse_mate = run(
        second_edges_kernel,
        [square_group, square_group, triangle, triangle],
        [],
        20, 12, drop, corner_cross, corner_mate, correction, low, high,
    )
    inverse_cross, inverse_mate = to_cross(inverse_cross), to_mate(inverse_mate)
    whole, rim_cross, rim_mate, rim_mate_too = run(
        density_edges_kernel,
        [columns, triangle, half_triangle, half_triangle],
        [group_scratch] * 4,
        38, 20, drop, own, edge_mate, edge_cross, correction, new_low, new_high, square,
        square_corners,
    )
    rim_cross, rim_mates = to_cross(rim_cross), [to_mate(rim_mate), to_mate(rim_mate_too)]
    (density_own,) = run(density_own_kernel, [square_group], [], 18, 12, drop, square, whole)
    out = jax.ShapeDtypeStruct(density.shape, kind)

    def assembled(own, first, cross, mates):
        kernel = functools.partial(slots_kernel, f, first, len(mates))
        scratch = [pltpu.SemaphoreType.DMA(())]
        slots, early = call(kernel, [out, out], scratch, 0, 8, drop, own, *mates, light=True, off=1)
        scratch = [pltpu.VMEM(out.shape, kind), pltpu.SemaphoreType.DMA((half,))]
        kernel = functools.partial(last_slots_kernel, f)
        return call(kernel, [], scratch, 0, 8, drop, slots, cross, passed=(early,), light=True)[0]

    inverse_next = assembled(whole, half, inverse_cross, [inverse_mate])
    density_next = assembled(density_own, 0, rim_cross, rim_mates)
    return density_next, inverse_next


def solution(mesh):
    blocks = P(("grp", "row", "inner"), None, None, None)
    return jax.shard_map(
        on_device,
        mesh=mesh,
        in_specs=(blocks, blocks, P(("grp", "row", "inner"), None)),
        out_specs=(blocks, blocks),
        check_vma=False,
    )
```
